32 devices in a mesh: chan: 8 (over z, y), batch: 4 (over x, core).
Axes of the slice: x: 2, y: 2, z: 4, core: 2. Of those that a mesh axis runs over, the one named last changes fastest.
Arguments:
- images: bfloat16 [1536, 49, 2048], P('batch', None, 'chan'), may hold values from -6 to 6
- pixel_mask: int32 [1536, 49], P('batch'), may hold values from 0 to 1, as said below
- labels: int32 [1536], P('batch'), may hold values from 0 to 999
- reduce_weight: float32 [512, 2048], P('chan'), may hold values from -0.1875 to 0.1875
- reduce_mask: int32 [512, 2048], P('chan'), may hold values 0 or 1
- spatial_weight: float32 [512, 4608], P('chan'), may hold values from -0.125 to 0.125
- spatial_mask: int32 [512, 4608], P('chan'), may hold values 0 or 1
- head_weight: float32 [512, 1000], P('chan'), may hold values from -1 to 1
- head_bias: float32 [1000], replicated, may hold values from -3 to 3
- norm_params: float32 [4, 512], P(None, 'chan')
- left_stats: float32 [13, 512, 512], P(None, 'chan')
- right_stats: float32 [13, 512, 512], P(None, 'chan')
- left_root: float32 [13, 512, 512], P(None, 'chan'), as said below
- input_side_roots: float32 [13, 512, 512], P(None, 'chan'), as said below
- head_first: float32 [512, 1000], P('chan'), may hold values from -0.0024414062 to 0.0024414062
- head_second: float32 [512, 1000], P('chan'), may hold values from 2.6041667e-09 to 1.0416667e-08
- bias_first: float32 [1000], replicated, may hold values from -0.0048828125 to 0.0048828125
- bias_second: float32 [1000], replicated, may hold values from 1.0416667e-08 to 4.1666667e-08
- norm_first: float32 [4, 512], P(None, 'chan'), may hold values from -0.046875 to 0.046875
- norm_second: float32 [4, 512], P(None, 'chan'), may hold values from 9.375e-07 to 3.75e-06
Outputs:
- loss_sum: float32 [], replicated
- slot_count: float32 [], replicated
- reduce_grad: float32 [512, 2048], P('chan')
- spatial_grad: float32 [512, 4608], P('chan')
- reduce_new: float32 [512, 2048], P('chan')
- spatial_new: float32 [512, 4608], P('chan')
- left_new: float32 [13, 512, 512], P(None, 'chan')
- right_new: float32 [13, 512, 512], P(None, 'chan')
- head_new: float32 [512, 1000], P('chan')
- head_first_new: float32 [512, 1000], P('chan')
- head_second_new: float32 [512, 1000], P('chan')
- bias_new: float32 [1000], replicated
- bias_first_new: float32 [1000], replicated
- bias_second_new: float32 [1000], replicated
- norm_new: float32 [4, 512], P(None, 'chan')
- norm_first_new: float32 [4, 512], P(None, 'chan')
- norm_second_new: float32 [4, 512], P(None, 'chan')
The draws below stay inside these ranges and needn't reach their ends.
Inputs may be any that keep to these rules, and one draw needn't show every extreme that they name: `pixel_mask`: the last of every 384 slots in a row is used; every used slot has its centre pixel valid. `left_root`: symmetric. `input_side_roots`: symmetric.
All inputs are finite; a program needn't handle non-finite values. No bound on the sum of `reduce_mask` or of `spatial_mask` on one device may be relied on, other than what follows from the above.
Results may differ from the reference program's by a relative error of at most 0.0045.
The reference program's roundings to bfloat16 on the way count: a program that leaves them out, or rounds other values in their place, can miss the bound.
Values may be sent and summed in bfloat16 or wider, within the bound.
A program may use at most 640 MiB of HBM per device.

```python
import math
import jax
import jax.numpy as jnp
from jax import lax

C_IN = 2048
WIDTH = 512
CLASSES = 1000
SIDE = 7
SLOTS_DEV = 384
STEP = 10
PIXELS = 49
SLOTS = 1536
TILES = 13
N_BATCH = 4


def symmetric_matrix(key, diagonal, offscale):
    noise = jax.random.normal(key, (TILES, WIDTH, WIDTH), jnp.float32) * offscale
    noise = 0.5 * (noise + jnp.swapaxes(noise, 1, 2))
    onto = jnp.arange(WIDTH)[:, None] == jnp.arange(WIDTH)[None, :]
    return jnp.where(onto[None, :, :], diagonal[:, :, None], noise)


def draw_pixel_mask(key, part):
    key = jax.random.fold_in(key, 1)
    first_key, second_key = jax.random.split(key)
    slot = jnp.arange(SLOTS, dtype=jnp.int32)[:, None]
    used = jax.random.randint(first_key, (SLOTS, 1), 0, 100) < 30 + 60 * slot // SLOTS
    used = used | (slot % SLOTS_DEV == SLOTS_DEV - 1)
    pixel_bits = jax.random.randint(second_key, (SLOTS, PIXELS), 0, 10) < 8
    centre = jnp.arange(PIXELS, dtype=jnp.int32)[None, :] == PIXELS // 2
    return (used & (pixel_bits | centre)).astype(jnp.int32)


def draw_norm_params(key, part):
    key = jax.random.fold_in(key, 2)
    values = jax.random.uniform(key, (4, WIDTH), jnp.float32)
    row = jnp.arange(4)[:, None]
    return jnp.where(row % 2 == 0, 0.6 + 0.8 * values, values - 0.5)


def stats_draw(key):
    first_key, second_key = jax.random.split(key)
    level = 0.02 * WIDTH * N_BATCH / SLOTS_DEV
    diagonal = level * jnp.exp(jax.random.uniform(first_key, (TILES, WIDTH), jnp.float32, 0.0, math.log(4.0)))
    return symmetric_matrix(second_key, diagonal, 0.2 * level / math.sqrt(WIDTH))


def draw_left_stats(key, part):
    return stats_draw(jax.random.fold_in(key, 3))


def draw_right_stats(key, part):
    return stats_draw(jax.random.fold_in(key, 4))


def draw_left_root(key, part):
    key = jax.random.fold_in(key, 5)
    first_key, second_key = jax.random.split(key)
    rising = 3.0 ** (jnp.arange(WIDTH, dtype=jnp.float32) / WIDTH)
    diagonal = rising[None, :] * jnp.exp(jax.random.uniform(first_key, (TILES, WIDTH), jnp.float32, math.log(0.6), math.log(2.4)))
    return symmetric_matrix(second_key, diagonal, 0.5 / math.sqrt(WIDTH))


def draw_input_side_roots(key, part):
    key = jax.random.fold_in(key, 6)
    first_key, second_key = jax.random.split(key)
    diagonal = jnp.exp(jax.random.uniform(first_key, (TILES, WIDTH), jnp.float32, math.log(0.3), math.log(3.0)))
    return symmetric_matrix(second_key, diagonal, 0.5 / math.sqrt(WIDTH))


def set_ends(array, rng, smallest, high):
    longest = array.shape.index(max(array.shape))
    spots = []
    for shift in (0, 1):
        where = [jax.random.randint(jax.random.fold_in(rng, axis), (), 0, length) for axis, length in enumerate(array.shape)]
        where[longest] = (where[longest] + shift) % array.shape[longest]
        spots.append(tuple(where))
    return array.at[spots[0]].set(smallest).at[spots[1]].set(high)


def shard_levels(stream_key, shape, pieces, smallest, high):
    def one(dim, blocks):
        steps = jax.random.uniform(jax.random.fold_in(jax.random.fold_in(stream_key, 6), dim), (blocks,), jnp.float32, smallest / len(pieces), high / len(pieces))
        return jnp.repeat(jnp.exp(steps), shape[dim] // blocks).reshape((-1,) + (1,) * (len(shape) - dim - 1))

    level = one(*pieces[0])
    for cut in pieces[1:]:
        level = level * one(*cut)
    return level


def normal_values(own_key, extent, spread, most, cuts=(), held_as=jnp.bfloat16):
    result = jax.random.normal(own_key, extent, jnp.float32) * spread
    if len(cuts) > 0:
        result = shard_levels(own_key, extent, cuts, -0.22, 0.18) * result
    return jnp.clip(result, min=-most, max=most).astype(held_as)


def setup_inputs(seed: int = 0) -> dict:
    key_list = jax.random.split(jax.random.key(seed), 21)
    images = normal_values(key_list[0], (SLOTS, PIXELS, C_IN), 1.0, 6.0, ((0, 4), (2, 8)))
    pixel_mask = draw_pixel_mask(jax.random.fold_in(key_list[20], 71), 0)
    labels = set_ends(jax.random.randint(key_list[2], (SLOTS,), 0, CLASSES), jax.random.fold_in(key_list[2], 1), 0, CLASSES - 1).astype(jnp.int32)
    reduce_weight = normal_values(key_list[3], (WIDTH, C_IN), (C_IN // 2) ** -0.5, 0.1875, ((0, 8),), jnp.float32)
    reduce_mask = set_ends((jax.random.randint(key_list[4], (WIDTH, C_IN), 0, 2) < 1).astype(jnp.int32), jax.random.fold_in(key_list[4], 1), 0, 1)
    spatial_weight = normal_values(key_list[5], (WIDTH, 9 * WIDTH), (9 * WIDTH // 2) ** -0.5, 0.125, ((0, 8),), jnp.float32)
    spatial_mask = set_ends((jax.random.randint(key_list[6], (WIDTH, 9 * WIDTH), 0, 2) < 1).astype(jnp.int32), jax.random.fold_in(key_list[6], 1), 0, 1)
    head_weight = normal_values(key_list[7], (WIDTH, CLASSES), (WIDTH // 16) ** -0.5, 1.0, ((0, 8),), jnp.float32)
    head_bias = normal_values(key_list[8], (CLASSES,), 0.5, 3.0, (), jnp.float32)
    norm_params = draw_norm_params(jax.random.fold_in(key_list[20], 71), 0)
    left_stats = draw_left_stats(jax.random.fold_in(key_list[20], 71), 0)
    right_stats = draw_right_stats(jax.random.fold_in(key_list[20], 71), 0)
    left_root = draw_left_root(jax.random.fold_in(key_list[20], 71), 0)
    input_side_roots = draw_input_side_roots(jax.random.fold_in(key_list[20], 71), 0)
    head_first = normal_values(key_list[14], (WIDTH, CLASSES), (0.055 * (N_BATCH / (CLASSES * SLOTS_DEV)) ** 0.5), 0.0024414062, ((0, 8),), jnp.float32)
    head_second = jnp.clip(jnp.exp(math.log(1.0416666640367112e-08) - 1.3862944 * jax.random.uniform(key_list[15], (WIDTH, CLASSES), jnp.float32) ** shard_levels(key_list[15], (WIDTH, CLASSES), ((0, 8),), -0.2, 0.2)), 2.604166660091778e-09, 1.0416666640367112e-08)
    bias_first = normal_values(key_list[16], (CLASSES,), (0.11 * (N_BATCH / (CLASSES * SLOTS_DEV)) ** 0.5), 0.0048828125, (), jnp.float32)
    bias_second = jnp.clip(jnp.exp(jax.random.uniform(key_list[17], (CLASSES,), jnp.float32, math.log(1.0416666640367112e-08), math.log(4.1666666561468446e-08))), 1.0416666640367112e-08, 4.1666666561468446e-08)
    norm_first = normal_values(key_list[18], (4, WIDTH), (0.033 * (N_BATCH / SLOTS_DEV) ** 0.5), 0.046875, ((1, 8),), jnp.float32)
    norm_second = jnp.clip(jnp.exp(math.log(3.749999905267032e-06) - 1.3862944 * jax.random.uniform(key_list[19], (4, WIDTH), jnp.float32) ** shard_levels(key_list[19], (4, WIDTH), ((1, 8),), -0.2, 0.2)), 9.37499976316758e-07, 3.749999905267032e-06)
    return {"images": images, "pixel_mask": pixel_mask, "labels": labels, "reduce_weight": reduce_weight, "reduce_mask": reduce_mask, "spatial_weight": spatial_weight, "spatial_mask": spatial_mask, "head_weight": head_weight, "head_bias": head_bias, "norm_params": norm_params, "left_stats": left_stats, "right_stats": right_stats, "left_root": left_root, "input_side_roots": input_side_roots, "head_first": head_first, "head_second": head_second, "bias_first": bias_first, "bias_second": bias_second, "norm_first": norm_first, "norm_second": norm_second}


FULL_PRECISION = lax.Precision.HIGHEST
EPS = 1e-05

@jax.custom_vjp
def low(v):
    return lax.optimization_barrier(v.astype(jnp.bfloat16)).astype(jnp.float32)

@jax.custom_vjp
def low_back(v):
    return v

def low_keep(v):
    return (low(v), None)

def reduced_precision_pass(kept, grad):
    return (grad,)

def back_keep(v):
    return (v, None)

def back_low(kept, grad):
    return (low(grad),)
low.defvjp(low_keep, reduced_precision_pass)
low_back.defvjp(back_keep, back_low)

def norm_act(z, gain, shift, valid):
    count = jnp.sum(valid)
    mean = lax.optimization_barrier(jnp.sum(z * valid, axis=(0, 1))) / count
    var = lax.optimization_barrier(jnp.sum(z * z * valid, axis=(0, 1))) / count - mean * mean
    pre = gain * ((z - mean) * lax.rsqrt(var + EPS)) + shift
    return jax.nn.silu(pre) * valid

def shift_grid(grid, dy, dx):
    padded = jnp.pad(grid, ((0, 0), (1, 1), (1, 1), (0, 0)))
    return padded[:, 1 + dy:1 + dy + SIDE, 1 + dx:1 + dx + SIDE, :]

def spatial_conv(hidden, taps):
    grid = hidden.reshape(hidden.shape[0], SIDE, SIDE, hidden.shape[2])
    total = jnp.zeros((hidden.shape[0], SIDE, SIDE, taps.shape[0]), jnp.float32)
    for dy in (-1, 0, 1):
        for dx in (-1, 0, 1):
            total = total + jnp.einsum('syxi,oi->syxo', shift_grid(grid, dy, dx), taps[:, 3 * (dy + 1) + dx + 1, :], precision=FULL_PRECISION)
    return total.reshape(hidden.shape[0], PIXELS, taps.shape[0])

def adam_step(param, grad, first, second, rate, decay):
    first = 0.9 * first + 0.1 * grad
    second = 0.999 * second + 0.001 * grad * grad
    mhat = first / (1.0 - 0.9 ** STEP)
    vhat = second / (1.0 - 0.999 ** STEP)
    return (param - rate * (mhat / (jnp.sqrt(vhat) + 1e-08) + decay * param), first, second)

def reference(images, pixel_mask, labels, reduce_weight, reduce_mask, spatial_weight, spatial_mask, head_weight, head_bias, norm_params, left_stats, right_stats, left_root, input_side_roots, head_first, head_second, bias_first, bias_second, norm_first, norm_second):
    inputs = images.astype(jnp.float32)
    valid = pixel_mask.astype(jnp.float32)[:, :, None]
    filled = lax.optimization_barrier(jnp.sum(valid[:, :, 0], axis=1))
    divisor = jnp.maximum(filled, 1.0)
    used = (filled > 0.0).astype(jnp.float32)
    reduce_float = reduce_mask.astype(jnp.float32)
    spatial_float = spatial_mask.astype(jnp.float32)
    onehot = jnp.arange(CLASSES)[None, :] == labels[:, None]

    def forward(reduce_w, spatial_w, head_w, bias_matrix, norm_w):
        first_pre = low_back(jnp.einsum('spc,oc->spo', inputs, low(reduce_w * reduce_float), precision=FULL_PRECISION))
        hidden = low(norm_act(first_pre, norm_w[0], norm_w[1], valid))
        taps = low(spatial_w * spatial_float).reshape(WIDTH, 9, WIDTH)
        second_pre = low_back(spatial_conv(hidden, taps))
        second_act = norm_act(second_pre, norm_w[2], norm_w[3], valid)
        pooled = low(lax.optimization_barrier(jnp.sum(second_act, axis=1)) / divisor[:, None])
        logits = low_back(jnp.dot(pooled, low(head_w), precision=FULL_PRECISION) + bias_matrix)
        lse = jax.nn.logsumexp(logits, axis=1)
        picked = lax.optimization_barrier(jnp.sum(jnp.where(onehot, logits, 0.0), axis=1))
        loss = jnp.sum(used * (lse - picked))
        return (loss / SLOTS_DEV, loss)
    objective, pullback, loss_sum = jax.vjp(forward, reduce_weight, spatial_weight, head_weight, head_bias, norm_params, has_aux=True)
    reduce_grad, spatial_grad, head_grad, bias_grad, norm_gain_gradient = pullback(jnp.float32(1.0))
    tiles_one = C_IN // WIDTH
    blocks = jnp.concatenate([reduce_grad.reshape(WIDTH, tiles_one, WIDTH).transpose(1, 0, 2), spatial_grad.reshape(WIDTH, 9, WIDTH).transpose(1, 0, 2)], axis=0)
    left_new = 0.95 * left_stats + jnp.einsum('tak,tbk->tab', blocks, blocks, precision=FULL_PRECISION)
    right_new = 0.95 * right_stats + jnp.einsum('tki,tkb->tib', blocks, blocks, precision=FULL_PRECISION)
    matrix_product = jnp.einsum('tak,tkb->tab', left_root, blocks, precision=FULL_PRECISION)
    matrix_product = jnp.einsum('ghk,gkl->ghl', matrix_product, input_side_roots, precision=FULL_PRECISION)
    step = matrix_product / jnp.sqrt(lax.optimization_barrier(jnp.mean(matrix_product * matrix_product, axis=(1, 2))) + 1e-06)[:, None, None]
    step_one = step[:tiles_one].transpose(1, 0, 2).reshape(WIDTH, C_IN)
    step_two = step[tiles_one:].transpose(1, 0, 2).reshape(WIDTH, 9 * WIDTH)
    reduce_new = reduce_weight - 0.02 * reduce_float * (step_one + 0.1 * reduce_weight)
    spatial_new = spatial_weight - 0.02 * spatial_float * (step_two + 0.1 * spatial_weight)
    head_new, head_first_new, head_second_new = adam_step(head_weight, head_grad, head_first, head_second, 0.04, 0.1)
    bias_new, bias_first_new, bias_second_new = adam_step(head_bias, bias_grad, bias_first, bias_second, 0.1, 0.0)
    norm_new, norm_first_new, norm_second_new = adam_step(norm_params, norm_gain_gradient, norm_first, norm_second, 0.1, 0.0)
    slot_count = jnp.sum(used)
    return (loss_sum, slot_count, reduce_grad, spatial_grad, reduce_new, spatial_new, left_new, right_new, head_new, head_first_new, head_second_new, bias_new, bias_first_new, bias_second_new, norm_new, norm_first_new, norm_second_new)
```

```python
import functools

import jax
import jax.numpy as jnp
from jax import lax
from jax.experimental import pallas as pl
from jax.experimental.pallas import tpu as pltpu
from jax.sharding import PartitionSpec as P

SIDE = 7
SLOTS_DEV = 384
STEP = 10

WIDTH = 512
EPS = 1e-05
MESH = pl.DeviceIdType.MESH
ANY = pl.BlockSpec(memory_space=pl.ANY)
VMEM = pl.BlockSpec(memory_space=pltpu.VMEM)
DMA = pltpu.SemaphoreType.DMA
SMALL = 8


def place():
    c, b = lax.axis_index("chan"), lax.axis_index("batch")
    nz, nx = lax.axis_size("chan") // 2, lax.axis_size("batch") // 2
    return (c // 2, lax.rem(c, 2), b // 2, lax.rem(b, 2)), (nz, 2, nx, 2)


def at(z, y, x, core):
    return {"chan": z * 2 + y, "batch": x * 2 + core}


def turned(index, size):
    return [lax.rem(index + k, size) for k in range(1, size)]


def greet(peers):
    barrier = pltpu.get_barrier_semaphore()
    for peer in peers:
        pl.semaphore_signal(barrier, inc=1, device_id=peer, device_id_type=MESH)
    pl.semaphore_wait(barrier, len(peers))


class Copies:
    def __init__(self, send, recv):
        self.send, self.recv, self.used = send, recv, 0

    def start(self, source, target, peer):
        copy = pltpu.make_async_remote_copy(
            source, target, self.send.at[self.used], self.recv.at[self.used],
            device_id=peer, device_id_type=MESH,
        )
        self.used += 1
        copy.start()
        return copy


def small_sum_kernel(own, total, held, send, recv):
    (z, y, x, core), (nz, ny, nx, nc) = place()
    peers = [
        at(lax.rem(z + i, nz), lax.rem(y + j, ny), lax.rem(x + k, nx), lax.rem(core + m, nc))
        for i in range(nz) for j in range(ny) for k in range(nx) for m in range(nc) if i + j + k + m
    ]
    greet(peers)
    copies = Copies(send, recv)
    started = [copies.start(own, held.at[k + 1], peer) for k, peer in enumerate(peers)]
    held[0] = own[...]
    for copy in started:
        copy.wait()
    total[...] = jnp.sum(held[...], axis=0)


def small_sum(rows, cid):
    n = lax.axis_size("chan") * lax.axis_size("batch")
    return pl.pallas_call(
        small_sum_kernel,
        out_shape=jax.ShapeDtypeStruct(rows.shape, jnp.float32),
        in_specs=[VMEM],
        out_specs=VMEM,
        scratch_shapes=[pltpu.VMEM((n,) + rows.shape, jnp.float32), DMA((n - 1,)), DMA((n - 1,))],
        compiler_params=pltpu.CompilerParams(collective_id=cid, has_side_effects=True),
        name="small_sum",
    )(rows)


def chan_sum_kernel(own, total, held, send, recv):
    c, n = lax.axis_index("chan"), lax.axis_size("chan")
    peers = [{"chan": other} for other in turned(c, n)]
    greet(peers)
    copies = Copies(send, recv)
    started = [copies.start(own, held.at[k + 1], peer) for k, peer in enumerate(peers)]
    held[0] = own[...]
    for copy in started:
        copy.wait()
    total[...] = jnp.sum(held[...], axis=0)


def chan_sum(rows, cid):
    n = lax.axis_size("chan")
    return pl.pallas_call(
        chan_sum_kernel,
        out_shape=jax.ShapeDtypeStruct(rows.shape, jnp.float32),
        in_specs=[VMEM],
        out_specs=VMEM,
        scratch_shapes=[pltpu.VMEM((n,) + rows.shape, jnp.float32), DMA((n - 1,)), DMA((n - 1,))],
        compiler_params=pltpu.CompilerParams(collective_id=cid, has_side_effects=True),
        name="chan_sum",
    )(rows)


def spread_kernel(images, weights, norms, images_out, weights_out, norms_out, send, recv, local):
    (z, y, x, core), (nz, ny, nx, nc) = place()
    c, n = lax.axis_index("chan"), lax.axis_size("chan")
    others = turned(c, n)
    greet([{"chan": k} for k in others] + [at(z, y, k, core) for k in turned(x, nx)] + [at(z, y, x, 1 - core)])
    copies = Copies(send, recv)
    quarter = pltpu.make_async_copy(weights.at[x, core], weights_out.at[z, y, x, core], local.at[0])
    quarter.start()
    along_z = [
        copies.start(weights.at[x, core], weights_out.at[z, y, x, core], at(k, y, x, core)) for k in turned(z, nz)
    ]
    rest = [copies.start(norms, norms_out.at[c], {"chan": k}) for k in others]
    rest += [copies.start(images.at[k], images_out.at[c], {"chan": k}) for k in others]
    own = pltpu.make_async_copy(images.at[c], images_out.at[c], local.at[1])
    own.start()
    own_norms = pltpu.make_async_copy(norms, norms_out.at[c], local.at[2])
    own_norms.start()
    quarter.wait()
    for copy in along_z:
        copy.wait()
    part = weights_out.at[:, y, x, core]
    copies.start(part, part, at(z, 1 - y, x, core)).wait()
    part = weights_out.at[:, :, x, core]
    along_x = [copies.start(part, part, at(z, y, k, core)) for k in turned(x, nx)]
    for copy in along_x:
        copy.wait()
    part = weights_out.at[:, :, :, core]
    copies.start(part, part, at(z, y, x, 1 - core)).wait()
    own.wait()
    own_norms.wait()
    for copy in rest:
        copy.wait()


def spread(images, weights, norms):
    nz, nx = lax.axis_size("chan") // 2, lax.axis_size("batch") // 2
    n = lax.axis_size("chan")
    count = (nz - 1) + 2 * (n - 1) + 1 + (nx - 1) + 1
    rows, columns = weights.shape[0] // (2 * nx), weights.shape[1]
    images_out, weights_out, norms_out = pl.pallas_call(
        spread_kernel,
        out_shape=(
            jax.ShapeDtypeStruct(images.shape, images.dtype),
            jax.ShapeDtypeStruct((nz, 2, nx, 2, rows, columns), weights.dtype),
            jax.ShapeDtypeStruct((n,) + norms.shape, norms.dtype),
        ),
        in_specs=[ANY] * 3,
        out_specs=(ANY,) * 3,
        scratch_shapes=[DMA((count,)), DMA((count,)), DMA((3,))],
        compiler_params=pltpu.CompilerParams(collective_id=0, has_side_effects=True),
        name="spread",
    )(images, weights.reshape(nx, 2, rows, columns), norms)
    return images_out, weights_out.reshape(n * weights.shape[0], columns), norms_out


def settle_kernel(wire, spatial, reduce, head, mask, full, own, sums_a, sums_b, core_a, core_b, x_a, x_b, y_a, y_b,
                  z_a, z_b, sx_a, sx_b, sy_a, sy_b, sz_a, sz_b, final, final_low, send, recv, local):
    (z, y, x, core), (nz, ny, nx, nc) = place()
    greet([at(k, y, x, core) for k in turned(z, nz)] + [at(z, 1 - y, x, core)]
          + [at(z, y, k, core) for k in turned(x, nx)] + [at(z, y, x, 1 - core)])
    copies = Copies(send, recv)
    half = sums_a.shape[-1]
    tail = spatial.shape[-1] - half
    mate, mate_y = at(z, y, x, 1 - core), at(z, 1 - y, x, core)
    mates_x, mates_z = turned(x, nx), turned(z, nz)
    groups = [(i, j, k) for i in range(nz) for j in range(ny) for k in range(nx)]
    pieces_a = [(spatial.at[:, :, :, :, :, pl.ds(0, half)], 0, half)]
    pieces_b = [(spatial.at[:, :, :, :, :, pl.ds(half, tail)], 0, tail), (reduce, tail, reduce.shape[-1]),
                (head, tail + reduce.shape[-1], head.shape[-1])]

    def begin(pieces, sums, landing, sem):
        remote, kept = [], []
        for source, start, size in pieces:
            columns = pl.ds(start, size)
            remote.append(copies.start(source.at[:, :, :, 1 - core], landing.at[:, :, :, :, columns], mate))
            copy = pltpu.make_async_copy(source.at[:, :, :, core], sums.at[:, :, :, :, columns], local.at[sem + len(kept)])
            copy.start()
            kept.append(copy)
        return remote + kept

    def ship(source, staged, landing, peer):
        if staged.dtype == jnp.float32:
            return copies.start(source, landing, peer)
        for i in range(staged.shape[0]):
            staged[i] = source[i].astype(staged.dtype)
        return copies.start(staged, landing, peer)

    def add(sums, landing):
        for i in range(landing.shape[0]):
            sums[i] += landing[i].astype(jnp.float32)

    first_a = begin(pieces_a, sums_a, core_a, 0)
    first_b = begin(pieces_b, sums_b, core_b, len(pieces_a))
    for first, sums, landing in ((first_a, sums_a, core_a), (first_b, sums_b, core_b)):
        for copy in first:
            copy.wait()
        for i, j, k in groups:
            sums[i, j, k] += landing[i, j, k]
        if sums is sums_a:
            going_a = []
            for t, k in enumerate(mates_x):
                for j in range(ny):
                    going_a.append(ship(sums.at[:, j, k], sx_a.at[t, j], x_a.at[t, j], at(z, y, k, core)))
        else:
            going_b = [ship(sums.at[:, 1 - y, k], sy_b.at[k], y_b.at[k], mate_y) for k in range(nx)]
    for copy in going_a:
        copy.wait()
    for t in range(nx - 1):
        for j in range(ny):
            add(sums_a.at[:, j, x], x_a.at[t, j])
    going_a = [ship(sums_a.at[:, 1 - y, x], sy_a, y_a, mate_y)]
    for copy in going_b:
        copy.wait()
    for k in range(nx):
        add(sums_b.at[:, y, k], y_b.at[k])
    going_b = [ship(sums_b.at[:, y, k], sx_b.at[t], x_b.at[t], at(z, y, k, core)) for t, k in enumerate(mates_x)]
    for copy in going_a:
        copy.wait()
    add(sums_a.at[:, y, x], y_a)
    going_a = [ship(sums_a.at[pl.ds(k, 1), y, x], sz_a.at[pl.ds(t, 1)], z_a.at[pl.ds(t, 1)], at(k, y, x, core))
               for t, k in enumerate(mates_z)]
    for copy in going_b:
        copy.wait()
    for t in range(nx - 1):
        add(sums_b.at[:, y, x], x_b.at[t])
    going_b = [ship(sums_b.at[pl.ds(k, 1), y, x], sz_b.at[pl.ds(t, 1)], z_b.at[pl.ds(t, 1)], at(k, y, x, core))
               for t, k in enumerate(mates_z)]
    for going, sums, landing, start in ((going_a, sums_a, z_a, 0), (going_b, sums_b, z_b, half)):
        for copy in going:
            copy.wait()
        value = sums[z, y, x]
        for t in range(nz - 1):
            value = value + landing[t].astype(jnp.float32)
        columns = pl.ds(start, half)
        final[:, columns] = value * mask[:, columns]

    wide = full.shape[-1]
    final_low[...] = final[:, :wide].astype(final_low.dtype)
    keep = pltpu.make_async_copy(final_low, full.at[z, y, x, core], local.at[4])
    keep.start()
    keep_own = pltpu.make_async_copy(final, own.at[x, core], local.at[5])
    keep_own.start()
    up = [copies.start(final_low, full.at[z, y, x, core], at(k, y, x, core)) for k in mates_z]
    rows_x = [copies.start(final, own.at[x, core], at(z, y, k, core)) for k in mates_x]
    keep.wait()
    for copy in up:
        copy.wait()
    left, right = pl.ds(0, wide // 2), pl.ds(wide // 2, wide // 2)
    part = full.at[:, y, x, core, :, left]
    going_a = [copies.start(part, part, at(z, y, k, core)) for k in mates_x]
    part = full.at[:, y, x, core, :, right]
    going_b = [copies.start(part, part, mate_y)]
    keep_own.wait()
    for copy in rows_x:
        copy.wait()
    part = own.at[:, core]
    rows_core = copies.start(part, part, mate)
    for copy in going_a:
        copy.wait()
    part = full.at[:, y, :, core, :, left]
    going_a = [copies.start(part, part, mate_y)]
    for copy in going_b:
        copy.wait()
    part = full.at[:, :, x, core, :, right]
    going_b = [copies.start(part, part, at(z, y, k, core)) for k in mates_x]
    for copy in going_a:
        copy.wait()
    part = full.at[:, :, :, core, :, left]
    last = [copies.start(part, part, mate)]
    for copy in going_b:
        copy.wait()
    part = full.at[:, :, :, core, :, right]
    last += [copies.start(part, part, mate), rows_core]
    for copy in last:
        copy.wait()


def settle(spatial, reduce, head, mask, wire):
    nz, nx = lax.axis_size("chan") // 2, lax.axis_size("batch") // 2
    width = spatial.shape[0]
    rows = width // (4 * nz * nx)
    total = spatial.shape[1] + reduce.shape[1] + head.shape[1]
    wide, half = spatial.shape[1] + reduce.shape[1], total // 2
    split = lambda a: a.reshape(nz, 2, nx, 2, rows, a.shape[1])
    f32 = jnp.float32
    big = pltpu.VMEM((nz, 2, nx, rows, half), f32)
    shapes = [(nx - 1, 2, nz, rows, half), (nx - 1, nz, rows, half), (nz, rows, half), (nx, nz, rows, half),
              (nz - 1, rows, half), (nz - 1, rows, half)]
    landing = [pltpu.VMEM(s, wire) for s in shapes]
    staging = [pltpu.VMEM(s if wire != f32 else s[:-2] + (8, 128), wire) for s in shapes]
    count = 4 + 2 * (nx - 1) + nx + 1 + (nx - 1) + 2 * (nz - 1) + (nz - 1) + (nx - 1) + 2 * nx + 1 + 2
    full, own = pl.pallas_call(
        functools.partial(settle_kernel, wire),
        out_shape=(
            jax.ShapeDtypeStruct((nz, 2, nx, 2, rows, wide), jnp.bfloat16),
            jax.ShapeDtypeStruct((nx, 2, rows, total), f32),
        ),
        in_specs=[ANY, ANY, ANY, VMEM],
        out_specs=(ANY, ANY),
        scratch_shapes=[big, big, big, big] + landing + staging
        + [pltpu.VMEM((rows, total), f32), pltpu.VMEM((rows, wide), jnp.bfloat16), DMA((count,)), DMA((count,)), DMA((6,))],
        compiler_params=pltpu.CompilerParams(collective_id=1, has_side_effects=True, vmem_limit_bytes=56 << 20),
        name="settle",
    )(split(spatial), split(reduce), split(head), mask)
    return full.reshape(width, wide), own.reshape(2 * nx * rows, total)


def silu_slope(pre):
    sigma = jax.nn.sigmoid(pre)
    return sigma * (1.0 + pre * (1.0 - sigma))


def adam_step(param, grad, first, second, rate, decay):
    first = 0.9 * first + 0.1 * grad
    second = 0.999 * second + 0.001 * grad * grad
    mhat = first / (1.0 - 0.9**STEP)
    vhat = second / (1.0 - 0.999**STEP)
    return (param - rate * (mhat / (jnp.sqrt(vhat) + 1e-08) + decay * param), first, second)


def own_part(array, axis, name="chan"):
    size = array.shape[axis] // lax.axis_size(name)
    return lax.dynamic_slice_in_dim(array, lax.axis_index(name) * size, size, axis)


def stacked(rows):
    width = rows[0].shape[0]
    rows = [jnp.pad(r, (0, width - r.shape[0])) for r in rows]
    rows += [jnp.zeros((width,), jnp.float32)] * (SMALL - len(rows))
    return jnp.stack(rows)


def two_parts(array):
    high = array.astype(jnp.bfloat16)
    return high, (array - high.astype(jnp.float32)).astype(jnp.bfloat16)


def product(spec, left, right):
    return jnp.einsum(spec, left, right, preferred_element_type=jnp.float32)


def conv_grid(grid, taps, spec):
    return lax.conv_general_dilated(
        grid, taps, (1, 1), ((1, 1), (1, 1)), dimension_numbers=spec, preferred_element_type=jnp.float32
    )


def body(
    images,
    pixel_mask,
    labels,
    reduce_weight,
    reduce_mask,
    spatial_weight,
    spatial_mask,
    head_weight,
    head_bias,
    norm_params,
    left_stats,
    right_stats,
    left_root,
    input_side_roots,
    head_first,
    head_second,
    bias_first,
    bias_second,
    norm_first,
    norm_second,
):
    n = lax.axis_size("chan")
    pixels, channels = images.shape[1:]
    side = SIDE
    rows_out, c_in = reduce_weight.shape
    width = left_stats.shape[2]
    classes = head_weight.shape[1]
    padded = 1024
    slots = images.shape[0] // n
    low = jnp.bfloat16
    f32 = jnp.float32
    reduce_float = reduce_mask.astype(f32)
    spatial_float = spatial_mask.astype(f32)

    by_pixel = images.reshape(n, slots, pixels, channels).transpose(0, 2, 1, 3)
    weights = jnp.concatenate(
        [(spatial_weight * spatial_float).astype(low), (reduce_weight * reduce_float).astype(low),
         jnp.pad(head_weight.astype(low), ((0, 0), (0, padded - classes)))], axis=1)
    norms = jnp.pad(norm_params, ((0, 4), (0, 128 - rows_out)))
    own_images, weights_full, norms_full = spread(by_pixel, weights, norms)
    taps = weights_full[:, : 9 * width].reshape(width, 3, 3, width)
    reduce_low = weights_full[:, 9 * width : 9 * width + c_in]
    head_low = weights_full[:, 9 * width + c_in : 9 * width + c_in + classes]
    norm_full = norms_full[:, :4, :rows_out].transpose(1, 0, 2).reshape(4, width)

    mask_own = own_part(pixel_mask, 0).astype(f32)
    valid = mask_own.T[:, :, None]
    own_labels = own_part(labels, 0)
    filled = jnp.sum(mask_own, axis=1)
    divisor = jnp.maximum(filled, 1.0)
    used = (filled > 0.0).astype(f32)

    first_pre = product("npsc,onc->pso", own_images, reduce_low.reshape(width, n, channels))
    roots_low, _ = lax.optimization_barrier((input_side_roots.astype(low), first_pre[0, 0, 0]))
    right_full = lax.all_gather(roots_low, "chan", axis=1, tiled=True)

    def sums_of(value):
        return jnp.sum(value * valid, axis=(0, 1)), jnp.sum(value * value * valid, axis=(0, 1))

    def forward(pre_norm, sums, count, gain, shift):
        mean = sums[0] / count
        scale = lax.rsqrt(sums[1] / count - mean * mean + EPS)
        normed = (pre_norm - mean) * scale
        pre = gain * normed + shift
        return normed, pre, scale

    stats = small_sum(stacked([*sums_of(first_pre), jnp.full((width,), jnp.sum(valid))]), 2)
    count = stats[2, 0]
    normed_one, pre_one, scale_one = forward(first_pre, stats, count, norm_full[0], norm_full[1])
    hidden = (jax.nn.silu(pre_one) * valid).astype(low).reshape(side, side, slots, width)
    second_pre = conv_grid(hidden, taps, ("HWNC", "OHWI", "HWNC")).reshape(pixels, slots, width)
    stats = small_sum(stacked([*sums_of(second_pre)]), 3)
    normed_two, pre_two, scale_two = forward(second_pre, stats, count, norm_full[2], norm_full[3])
    second_act = jax.nn.silu(pre_two) * valid
    pooled = (jnp.sum(second_act, axis=0) / divisor[:, None]).astype(low)
    logits = jnp.dot(pooled, head_low, preferred_element_type=f32) + head_bias
    onehot = (jnp.arange(classes)[None, :] == own_labels[:, None]).astype(f32)
    log_total = jax.nn.logsumexp(logits, axis=1)
    picked = jnp.sum(onehot * logits, axis=1)
    loss_local = jnp.sum(used * (log_total - picked))
    d_logits = (used[:, None] * (jnp.exp(logits - log_total[:, None]) - onehot) / SLOTS_DEV).astype(low)
    head_local = product("so,sc->oc", pooled, d_logits)
    bias_local = jnp.sum(d_logits.astype(f32), axis=0)
    d_pooled = product("sc,oc->so", d_logits, head_low)
    d_act = jnp.broadcast_to((d_pooled / divisor[:, None])[None], second_act.shape)

    def backward(d_act, normed, pre, scale, gain, cid, extra):
        d_pre = d_act * valid * silu_slope(pre)
        sums = small_sum(
            stacked([jnp.sum(d_pre, axis=(0, 1)), jnp.sum(d_pre * normed, axis=(0, 1))] + extra), cid)
        d_z = gain * scale / count * (count * d_pre - sums[0] - normed * sums[1]) * valid
        return d_z.astype(low), sums

    half = padded // 2
    bias_padded = jnp.pad(bias_local, (0, padded - classes))
    misc = jnp.zeros((width,), f32).at[0].set(loss_local).at[1].set(jnp.sum(used))
    d_second, sums_two = backward(d_act, normed_two, pre_two, scale_two, norm_full[2], 4,
                                  [bias_padded[:half], bias_padded[half:], misc])
    d_second = d_second.reshape(side, side, slots, width)
    spatial_local = lax.conv_general_dilated(
        hidden, d_second, (1, 1), ((1, 1), (1, 1)), dimension_numbers=("HWCN", "HWIO", "HWNC"),
        preferred_element_type=f32,
    )
    spatial_local = spatial_local.transpose(3, 0, 1, 2).reshape(width, 9 * width)
    d_hidden = conv_grid(
        d_second, taps[:, ::-1, ::-1, :], ("HWNC", "IHWO", "HWNC")
    ).reshape(pixels, slots, width)
    d_first, sums_one = backward(d_hidden, normed_one, pre_one, scale_one, norm_full[0], 5, [])
    reduce_local = product("npsc,pso->onc", own_images, d_first).reshape(width, c_in)

    mask_rows = jnp.concatenate([spatial_float, reduce_float, jnp.ones((rows_out, padded), f32)], axis=1)
    full, own = settle(spatial_local, reduce_local, jnp.pad(head_local, ((0, 0), (0, padded - classes))),
                       own_part(mask_rows, 0, "batch"), jnp.float32)
    spatial_grad = own[:, : 9 * width]
    reduce_grad = own[:, 9 * width : 9 * width + c_in]
    head_grad = own[:, 9 * width + c_in : 9 * width + c_in + classes]
    loss_sum, slot_count = sums_two[4, 0], sums_two[4, 1]
    bias_grad = jnp.concatenate([sums_two[2], sums_two[3]])[:classes]
    norm_gain_gradient = own_part(jnp.stack([sums_one[1], sums_one[0], sums_two[1], sums_two[0]]), 1)

    tiles_one = c_in // width
    blocks_of = lambda a: a.reshape(a.shape[0], -1, width).transpose(1, 0, 2)
    in_order = lambda a: jnp.concatenate([a[9:], a[:9]], axis=0)
    blocks = in_order(blocks_of(own[:, : 9 * width + c_in])).astype(low)
    blocks_full = in_order(blocks_of(full))
    left_new = 0.95 * left_stats + product("tak,tbk->tab", blocks, blocks_full)
    right_new = 0.95 * right_stats + product("tki,tkb->tib", own_part(blocks_full, 2), blocks_full)
    left_high, left_rest = two_parts(left_root)
    inner = product("tak,tkb->tab", left_high, blocks_full) + product("tak,tkb->tab", left_rest, blocks_full)
    inner_high, inner_rest = two_parts(inner)
    outer = product("tak,tkb->tab", inner_high, right_full) + product("tak,tkb->tab", inner_rest, right_full)
    squares = jnp.pad(jnp.sum(outer * outer, axis=(1, 2))[:, None] * jnp.ones((1, 128), f32), ((0, 3), (0, 0)))
    squares = chan_sum(squares, 6)[: 9 + tiles_one, 0]
    step = outer / jnp.sqrt(squares / (width * width) + 1e-06)[:, None, None]
    step_one = step[:tiles_one].transpose(1, 0, 2).reshape(rows_out, c_in)
    step_two = step[tiles_one:].transpose(1, 0, 2).reshape(rows_out, 9 * width)
    reduce_new = reduce_weight - 0.02 * reduce_float * (step_one + 0.1 * reduce_weight)
    spatial_new = spatial_weight - 0.02 * spatial_float * (step_two + 0.1 * spatial_weight)
    head_new, head_first_new, head_second_new = adam_step(head_weight, head_grad, head_first, head_second, 0.04, 0.1)
    bias_new, bias_first_new, bias_second_new = adam_step(head_bias, bias_grad, bias_first, bias_second, 0.1, 0.0)
    norm_new, norm_first_new, norm_second_new = adam_step(
        norm_params, norm_gain_gradient, norm_first, norm_second, 0.1, 0.0)
    return (
        loss_sum,
        slot_count,
        reduce_grad,
        spatial_grad,
        reduce_new,
        spatial_new,
        left_new,
        right_new,
        head_new,
        head_first_new,
        head_second_new,
        bias_new,
        bias_first_new,
        bias_second_new,
        norm_new,
        norm_first_new,
        norm_second_new,
    )


FULL_PRECISION = lax.Precision.HIGHEST
BOTH = ("chan", "batch")


def plain_norm_forward(pre_norm, gain, shift, valid):
    first_sum = jnp.sum(pre_norm * valid, axis=(0, 1))
    second_sum = jnp.sum(pre_norm * pre_norm * valid, axis=(0, 1))
    first_sum, second_sum, count = lax.psum((first_sum, second_sum, jnp.sum(valid)), BOTH)
    mean = first_sum / count
    scale = lax.rsqrt(second_sum / count - mean * mean + EPS)
    normed = (pre_norm - mean) * scale
    pre = gain * normed + shift
    return (jax.nn.silu(pre) * valid, (normed, pre, scale, count))


def plain_norm_backward(grad_act, kept, gain, valid):
    normed, pre, scale, count = kept
    d_pre = grad_act * valid * silu_slope(pre)
    shift_gradient, gain_grad = lax.psum(
        (jnp.sum(d_pre, axis=(0, 1)), jnp.sum(d_pre * normed, axis=(0, 1))), BOTH
    )
    d_input = gain * scale / count * (count * d_pre - shift_gradient - normed * gain_grad) * valid
    return (d_input, gain_grad, shift_gradient)


def plain_own_part(array, parts, axis=0):
    size = array.shape[axis] // parts
    return lax.dynamic_slice_in_dim(array, lax.axis_index("chan") * size, size, axis)


def plain_body(
    images,
    pixel_mask,
    labels,
    reduce_weight,
    reduce_mask,
    spatial_weight,
    spatial_mask,
    head_weight,
    head_bias,
    norm_params,
    left_stats,
    right_stats,
    left_root,
    input_side_roots,
    head_first,
    head_second,
    bias_first,
    bias_second,
    norm_first,
    norm_second,
):
    parts = lax.axis_size("chan")
    pixels = images.shape[1]
    side = SIDE
    rows_out = reduce_weight.shape[0]
    width = left_stats.shape[2]
    classes = head_weight.shape[1]
    own_images = lax.all_to_all(images, "chan", 0, 2, tiled=True)
    slots = own_images.shape[0]
    reduce_float = reduce_mask.astype(jnp.float32)
    spatial_float = spatial_mask.astype(jnp.float32)
    gather = lambda a, axis: lax.all_gather(a, "chan", axis=axis, tiled=True)
    reduce_low = gather((reduce_weight * reduce_float).astype(jnp.bfloat16), 0)
    spatial_low = gather((spatial_weight * spatial_float).astype(jnp.bfloat16), 0)
    head_low = gather(head_weight.astype(jnp.bfloat16), 0)
    norm_full = gather(norm_params, 1)
    right_factor_full = gather(input_side_roots, 1)
    valid = plain_own_part(pixel_mask, parts).astype(jnp.float32)[:, :, None]
    own_labels = plain_own_part(labels, parts)
    filled = jnp.sum(valid[:, :, 0], axis=1)
    divisor = jnp.maximum(filled, 1.0)
    used = (filled > 0.0).astype(jnp.float32)
    taps = spatial_low.reshape(width, 3, 3, width)
    first_pre = jnp.einsum("spc,oc->spo", own_images, reduce_low, preferred_element_type=jnp.float32)
    first_act, first_kept = plain_norm_forward(first_pre, norm_full[0], norm_full[1], valid)
    hidden = first_act.astype(jnp.bfloat16).reshape(slots, side, side, width)
    second_pre = conv_grid(hidden, taps, ("NHWC", "OHWI", "NHWC")).reshape(slots, pixels, width)
    second_act, second_kept = plain_norm_forward(second_pre, norm_full[2], norm_full[3], valid)
    pooled = (jnp.sum(second_act, axis=1) / divisor[:, None]).astype(jnp.bfloat16)
    logits = jnp.dot(pooled, head_low, preferred_element_type=jnp.float32) + head_bias
    onehot = (jnp.arange(classes)[None, :] == own_labels[:, None]).astype(jnp.float32)
    log_total = jax.nn.logsumexp(logits, axis=1)
    picked = jnp.sum(onehot * logits, axis=1)
    loss_local = jnp.sum(used * (log_total - picked))
    d_logits = (used[:, None] * (jnp.exp(logits - log_total[:, None]) - onehot) / SLOTS_DEV).astype(
        jnp.bfloat16
    )
    head_grad = jnp.einsum("so,sc->oc", pooled, d_logits, preferred_element_type=jnp.float32)
    bias_grad = jnp.sum(d_logits.astype(jnp.float32), axis=0)
    d_pooled = jnp.einsum("sc,oc->so", d_logits, head_low, preferred_element_type=jnp.float32)
    d_act = jnp.broadcast_to((d_pooled / divisor[:, None])[:, None, :], second_act.shape)
    d_second, gain_two, shift_two = plain_norm_backward(d_act, second_kept, norm_full[2], valid)
    d_second = d_second.astype(jnp.bfloat16).reshape(slots, side, side, width)
    spatial_local = lax.conv_general_dilated(
        hidden, d_second, (1, 1), ((1, 1), (1, 1)), dimension_numbers=("CHWN", "IHWO", "NHWC"),
        preferred_element_type=jnp.float32,
    )
    spatial_local = spatial_local.transpose(3, 1, 2, 0).reshape(width, 9 * width)
    d_hidden = conv_grid(
        d_second, taps[:, ::-1, ::-1, :], ("NHWC", "IHWO", "NHWC")
    ).reshape(slots, pixels, width)
    d_first, gain_one, shift_one = plain_norm_backward(d_hidden, first_kept, norm_full[0], valid)
    d_first = d_first.astype(jnp.bfloat16)
    reduce_local = jnp.einsum("spc,spo->oc", own_images, d_first, preferred_element_type=jnp.float32)
    scatter = lambda a: lax.psum_scatter(a, "chan", scatter_dimension=0, tiled=True)
    reduce_grad, spatial_grad, head_grad = scatter(reduce_local), scatter(spatial_local), scatter(head_grad)
    reduce_grad, spatial_grad, head_grad = lax.psum((reduce_grad, spatial_grad, head_grad), "batch")
    reduce_grad = reduce_grad * reduce_float
    spatial_grad = spatial_grad * spatial_float
    bias_grad, loss_sum, slot_count = lax.psum((bias_grad, loss_local, jnp.sum(used)), BOTH)
    norm_gain_gradient = plain_own_part(jnp.stack([gain_one, shift_one, gain_two, shift_two], axis=0), parts, 1)
    tiles_one = reduce_weight.shape[1] // width
    blocks = jnp.concatenate(
        [
            reduce_grad.reshape(rows_out, tiles_one, width).transpose(1, 0, 2),
            spatial_grad.reshape(rows_out, 9, width).transpose(1, 0, 2),
        ],
        axis=0,
    )
    blocks_full = gather(blocks, 1)
    left_new = 0.95 * left_stats + jnp.einsum(
        "tak,tbk->tab", blocks, blocks_full, precision=FULL_PRECISION
    )
    own_columns = plain_own_part(blocks_full, parts, 2)
    right_new = 0.95 * right_stats + jnp.einsum(
        "tki,tkb->tib", own_columns, blocks_full, precision=FULL_PRECISION
    )
    matrix_product = jnp.einsum("tak,tkb->tab", left_root, blocks_full, precision=FULL_PRECISION)
    matrix_product = jnp.einsum(
        "ghk,gkl->ghl", matrix_product, right_factor_full, precision=FULL_PRECISION
    )
    squares = lax.psum(jnp.sum(matrix_product * matrix_product, axis=(1, 2)), "chan")
    step = matrix_product / jnp.sqrt(squares / (width * width) + 1e-06)[:, None, None]
    step_one = step[:tiles_one].transpose(1, 0, 2).reshape(rows_out, tiles_one * width)
    step_two = step[tiles_one:].transpose(1, 0, 2).reshape(rows_out, 9 * width)
    reduce_new = reduce_weight - 0.02 * reduce_float * (step_one + 0.1 * reduce_weight)
    spatial_new = spatial_weight - 0.02 * spatial_float * (step_two + 0.1 * spatial_weight)
    head_new, head_first_new, head_second_new = adam_step(
        head_weight, head_grad, head_first, head_second, 0.04, 0.1
    )
    bias_new, bias_first_new, bias_second_new = adam_step(
        head_bias, bias_grad, bias_first, bias_second, 0.1, 0.0
    )
    norm_new, norm_first_new, norm_second_new = adam_step(
        norm_params, norm_gain_gradient, norm_first, norm_second, 0.1, 0.0
    )
    return (
        loss_sum,
        slot_count,
        reduce_grad,
        spatial_grad,
        reduce_new,
        spatial_new,
        left_new,
        right_new,
        head_new,
        head_first_new,
        head_second_new,
        bias_new,
        bias_first_new,
        bias_second_new,
        norm_new,
        norm_first_new,
        norm_second_new,
    )


def solution(mesh):
    in_specs = (
        P("batch", None, "chan"),
        P("batch", None),
        P("batch"),
        P("chan", None),
        P("chan", None),
        P("chan", None),
        P("chan", None),
        P("chan", None),
        P(),
        P(None, "chan"),
        P(None, "chan", None),
        P(None, "chan", None),
        P(None, "chan", None),
        P(None, "chan", None),
        P("chan", None),
        P("chan", None),
        P(),
        P(),
        P(None, "chan"),
        P(None, "chan"),
    )
    out_specs = (
        P(),
        P(),
        P("chan", None),
        P("chan", None),
        P("chan", None),
        P("chan", None),
        P(None, "chan", None),
        P(None, "chan", None),
        P("chan", None),
        P("chan", None),
        P("chan", None),
        P(),
        P(),
        P(),
        P(None, "chan"),
        P(None, "chan"),
        P(None, "chan"),
    )
    chan, batch = mesh.shape["chan"], mesh.shape["batch"]
    fits = chan % 2 == 0 and batch % 2 == 0 and WIDTH % (16 * chan * batch) == 0 and SLOTS_DEV % (16 * chan) == 0
    return jax.shard_map(body if fits else plain_body, mesh=mesh, in_specs=in_specs, out_specs=out_specs, check_vma=False)
```

```python
import functools

import jax
import jax.numpy as jnp
from jax import lax
from jax.experimental import pallas as pl
from jax.experimental.pallas import tpu as pltpu
from jax.sharding import PartitionSpec as P

SIDE = 7
SLOTS_DEV = 384
STEP = 10

WIDTH = 512
EPS = 1e-05
MESH = pl.DeviceIdType.MESH
ANY = pl.BlockSpec(memory_space=pl.ANY)
VMEM = pl.BlockSpec(memory_space=pltpu.VMEM)
DMA = pltpu.SemaphoreType.DMA
SMALL = 8


def place():
    c, b = lax.axis_index("chan"), lax.axis_index("batch")
    nz, nx = lax.axis_size("chan") // 2, lax.axis_size("batch") // 2
    return (c // 2, lax.rem(c, 2), b // 2, lax.rem(b, 2)), (nz, 2, nx, 2)


def at(z, y, x, core):
    return {"chan": z * 2 + y, "batch": x * 2 + core}


def turned(index, size):
    return [lax.rem(index + k, size) for k in range(1, size)]


def greet(peers):
    barrier = pltpu.get_barrier_semaphore()
    for peer in peers:
        pl.semaphore_signal(barrier, inc=1, device_id=peer, device_id_type=MESH)
    pl.semaphore_wait(barrier, len(peers))


class Copies:
    def __init__(self, send, recv):
        self.send, self.recv, self.used = send, recv, 0

    def start(self, source, target, peer):
        copy = pltpu.make_async_remote_copy(
            source, target, self.send.at[self.used], self.recv.at[self.used],
            device_id=peer, device_id_type=MESH,
        )
        self.used += 1
        copy.start()
        return copy


def chan_sum_kernel(own, total, held, send, recv):
    c, n = lax.axis_index("chan"), lax.axis_size("chan")
    peers = [{"chan": other} for other in turned(c, n)]
    greet(peers)
    copies = Copies(send, recv)
    started = [copies.start(own, held.at[k + 1], peer) for k, peer in enumerate(peers)]
    held[0] = own[...]
    for copy in started:
        copy.wait()
    total[...] = jnp.sum(held[...], axis=0)


def chan_sum(rows, cid):
    n = lax.axis_size("chan")
    return pl.pallas_call(
        chan_sum_kernel,
        out_shape=jax.ShapeDtypeStruct(rows.shape, jnp.float32),
        in_specs=[VMEM],
        out_specs=VMEM,
        scratch_shapes=[pltpu.VMEM((n,) + rows.shape, jnp.float32), DMA((n - 1,)), DMA((n - 1,))],
        compiler_params=pltpu.CompilerParams(collective_id=cid, has_side_effects=True),
        name="chan_sum",
    )(rows)


def dot(left, right, left_dim, right_dim):
    return lax.dot_general(left, right, (((left_dim,), (right_dim,)), ((), ())), preferred_element_type=jnp.float32)


def sigmoid(value):
    return 1.0 / (1.0 + jnp.exp(-value))


def packed(row):
    return jnp.concatenate([row[:, i : i + 128] for i in range(0, row.shape[1], 128)], axis=0)


def unpacked(block):
    return jnp.concatenate([block[i : i + 1] for i in range(block.shape[0])], axis=1)


def step_kernel(
    images, weights, roots, norms, valid, labels, used, divisor, bias,
    spatial_out, reduce_out, head_out, totals_out, weights_out, roots_out,
    own_images, first, second, hidden_pad, grad_pad, turned_grad, taps, reduce_low, head_low,
    norms_held, pack_one, pack_two, pack_three, pack_four, held_one, held_two, held_three, held_four,
    partial, pooled_low, d_logits, d_act, head_buf, grad_buf, send, recv, local,
):
    (z, y, x, core), (nz, ny, nx, nc) = place()
    c, n = lax.axis_index("chan"), lax.axis_size("chan")
    f32, low = jnp.float32, jnp.bfloat16
    slots = used.shape[0]
    side = SIDE
    line = side * slots
    wide_line = (side + 1) * slots
    pixels = side * side
    rim = (side + 2) * slots
    body_rows = side * wide_line
    width = first.shape[1]
    depth = own_images.shape[-1]
    everyone = [
        at(lax.rem(z + i, nz), lax.rem(y + j, ny), lax.rem(x + k, nx), lax.rem(core + m, nc))
        for i in range(nz) for j in range(ny) for k in range(nx) for m in range(nc) if i + j + k + m
    ]
    greet(everyone)
    copies = Copies(send, recv)
    others = turned(c, n)
    sources = ((weights, weights_out), (roots, roots_out))

    quarters = []
    for i, (source, target) in enumerate(sources):
        copy = pltpu.make_async_copy(source.at[x, core], target.at[z, y, x, core], local.at[i])
        copy.start()
        quarters.append(copy)
    along_z = [[copies.start(source.at[x, core], target.at[z, y, x, core], at(k, y, x, core)) for k in turned(z, nz)]
               for source, target in sources[:1]]
    norm_copies = [copies.start(norms, norms_held.at[k + 1], {"chan": other}) for k, other in enumerate(others)]
    image_copies = [copies.start(images.at[k], own_images.at[c, :, pl.ds(0, line)], {"chan": k}) for k in others]
    along_z += [[copies.start(source.at[x, core], target.at[z, y, x, core], at(k, y, x, core)) for k in turned(z, nz)]
                for source, target in sources[1:]]
    own = pltpu.make_async_copy(images.at[c], own_images.at[c, :, pl.ds(0, line)], local.at[2])
    own.start()
    norms_held[0] = norms[...]

    def clear(i, _):
        rows = pl.ds(pl.multiple_of(i * slots, slots), slots)
        hidden_pad[rows, :] = jnp.zeros((slots, width), low)
        grad_pad[rows, :] = jnp.zeros((slots, width), low)
        return 0

    lax.fori_loop(0, hidden_pad.shape[0] // slots, clear, 0)
    for k in range(n):
        for j in range(side):
            own_images[k, j, pl.ds(line, slots), :] = jnp.zeros((slots, depth), low)

    for i, (source, target) in enumerate(sources):
        quarters[i].wait()
        for copy in along_z[i]:
            copy.wait()
        part = target.at[:, y, x, core]
        along_y = copies.start(part, part, at(z, 1 - y, x, core))
        along_y.wait()
        part = target.at[:, :, x, core]
        along_x = [copies.start(part, part, at(z, y, k, core)) for k in turned(x, nx)]
        for copy in along_x:
            copy.wait()
        part = target.at[:, :, :, core]
        copies.start(part, part, at(z, y, x, 1 - core)).wait()
        if i == 0:
            fetched = []
            start = 0
            for j, held in enumerate((taps, reduce_low, head_low)):
                size = held.shape[-1]
                copy = pltpu.make_async_copy(target.at[:, :, :, :, :, pl.ds(start, size)], held, local.at[3 + j])
                copy.start()
                fetched.append(copy)
                start += size
            for copy in fetched:
                copy.wait()
    taps, reduce_low, head_low = (held.reshape(width, held.shape[-1]) for held in (taps, reduce_low, head_low))
    for copy in norm_copies:
        copy.wait()
    norm_rows = jnp.sum(norms_held[...], axis=0)
    gain_one, shift_one, gain_two, shift_two = (norm_rows[i : i + 1] for i in range(4))

    def line_rows(j):
        return pl.ds(pl.multiple_of(j * line, slots), line)

    def pixel_rows(p):
        return pl.ds(pl.multiple_of(p * slots, slots), slots)

    def padded_pixel(p):
        j = p // side
        return pl.ds(pl.multiple_of(rim + (p + j) * slots, slots), slots)

    def across(block):
        return jnp.concatenate([block] * (width // 128), axis=1)

    def fold(value):
        return jnp.sum(value.reshape(-1, 8, width), axis=0)

    def total_of(index):
        return jnp.sum(partial[index], axis=0, keepdims=True)

    def exchange(pack, held):
        pack_copies = [copies.start(pack, held.at[k + 1], peer) for k, peer in enumerate(everyone)]
        held[0] = pack[...]
        return pack_copies

    def settled(pack_copies, held):
        for copy in pack_copies:
            copy.wait()
        return jnp.sum(held[...], axis=0)

    for k in range(n):
        source = lax.rem(c + n - k, n)
        if k == 0:
            own.wait()
        else:
            image_copies[k - 1].wait()
        columns = pl.ds(pl.multiple_of(source * depth, depth), depth)

        def reduce_line(j, _, k=k, source=source, columns=columns):
            value = dot(own_images[source, j, pl.ds(0, line), :], reduce_low[:, columns], 1, 1)
            if k:
                value = first[line_rows(j), :] + value
            first[line_rows(j), :] = value
            return 0

        lax.fori_loop(0, side, reduce_line, 0)

    def norm_sums(ref):
        partial[...] = jnp.zeros(partial.shape, f32)

        def add(p, _):
            value = ref[pixel_rows(p), :]
            kept = value * across(valid[pixel_rows(p), :])
            partial[0] += fold(kept)
            partial[1] += fold(kept * value)
            return 0

        lax.fori_loop(0, pixels, add, 0)

    norm_sums(first)
    all_valid = jnp.sum(valid[...], axis=0, keepdims=True)
    pack_one[...] = jnp.concatenate(
        [packed(total_of(0)), packed(total_of(1)), all_valid, jnp.zeros((7, 128), f32)], axis=0)
    stats = settled(exchange(pack_one, held_one), held_one)
    rows = width // 128
    count = jnp.concatenate([stats[2 * rows : 2 * rows + 1]] * rows, axis=1)

    def norm_of(stats):
        mean = unpacked(stats[:rows]) / count
        scale = lax.rsqrt(unpacked(stats[rows : 2 * rows]) / count - mean * mean + EPS)
        return mean, scale

    mean_one, scale_one = norm_of(stats)

    def activate(p, _):
        normed = (first[pixel_rows(p), :] - mean_one) * scale_one
        pre = gain_one * normed + shift_one
        act = pre * sigmoid(pre) * across(valid[pixel_rows(p), :])
        hidden_pad[padded_pixel(p), :] = act.astype(low)
        return 0

    lax.fori_loop(0, pixels, activate, 0)

    def conv_line(j, _):
        value = None
        for t in range(9):
            offset = (t // 3 - 1) * wide_line + (t % 3 - 1) * slots
            rows_in = pl.ds(pl.multiple_of(rim + j * wide_line + offset, slots), line)
            term = dot(hidden_pad[rows_in, :], taps[:, t * width : (t + 1) * width], 1, 1)
            value = term if value is None else value + term
        second[line_rows(j), :] = value
        return 0

    lax.fori_loop(0, side, conv_line, 0)
    norm_sums(second)
    pack_two[...] = jnp.concatenate([packed(total_of(0)), packed(total_of(1))], axis=0)
    stats = settled(exchange(pack_two, held_two), held_two)
    mean_two, scale_two = norm_of(stats)

    def pool(p, sums):
        pooled, slopes, slopes_normed = sums
        normed = (second[pixel_rows(p), :] - mean_two) * scale_two
        pre = gain_two * normed + shift_two
        sigma = sigmoid(pre)
        kept = across(valid[pixel_rows(p), :])
        slope = sigma * (1.0 + pre * (1.0 - sigma)) * kept
        return pooled + pre * sigma * kept, slopes + slope, slopes_normed + slope * normed

    nothing = jnp.zeros((slots, width), f32)
    pooled, slopes, slopes_normed = lax.fori_loop(0, pixels, pool, (nothing, nothing, nothing))
    divide = across(divisor[...])
    pooled_low[...] = (pooled / divide).astype(low)
    logits = dot(pooled_low[...], head_low[...], 1, 0) + bias[...]
    classes = logits.shape[1]
    index = lax.broadcasted_iota(jnp.int32, (slots, classes), 1)
    onehot = (index == labels[:, :1]).astype(f32)
    top = jnp.max(logits, axis=1, keepdims=True)
    log_total = jnp.log(jnp.sum(jnp.exp(logits - top), axis=1, keepdims=True)) + top
    picked = jnp.sum(onehot * logits, axis=1, keepdims=True)
    use = used[:, :1]
    loss = jnp.sum(use * (log_total - picked))
    d_logits[...] = (use * (jnp.exp(logits - log_total) - onehot) / SLOTS_DEV).astype(low)
    bias_sum = jnp.sum(d_logits[...].astype(f32), axis=0, keepdims=True)
    half = width // 2

    def to_pooled(m, _):
        rows_in = pl.ds(pl.multiple_of(m * half, half), half)
        d_act[:, rows_in] = dot(d_logits[...], head_low[rows_in, :], 1, 1) / across(divisor[...])[:, :half]
        return 0

    lax.fori_loop(0, 2, to_pooled, 0)
    at_class = lax.broadcasted_iota(jnp.int32, (1, classes), 1)
    bias_sum = jnp.where(at_class == classes - 1, loss, jnp.where(at_class == classes - 2, jnp.sum(use), bias_sum))
    pack_three[...] = jnp.concatenate(
        [packed(jnp.sum(d_act[...] * slopes, axis=0, keepdims=True)),
         packed(jnp.sum(d_act[...] * slopes_normed, axis=0, keepdims=True)), packed(bias_sum)], axis=0)
    going = exchange(pack_three, held_three)

    def to_head(m, _):
        columns = pl.ds(pl.multiple_of(m * (classes // 2), 128), classes // 2)
        head_buf[:, columns] = dot(pooled_low[...], d_logits[:, columns], 0, 0)
        return 0

    lax.fori_loop(0, 2, to_head, 0)
    head_copy = pltpu.make_async_copy(head_buf, head_out, local.at[6])
    head_copy.start()
    totals_two = settled(going, held_three)
    shift_grad, gain_grad = unpacked(totals_two[:rows]), unpacked(totals_two[rows : 2 * rows])
    factor = gain_two * scale_two / count

    def leave_second(p, _):
        normed = (second[pixel_rows(p), :] - mean_two) * scale_two
        pre = gain_two * normed + shift_two
        sigma = sigmoid(pre)
        kept = across(valid[pixel_rows(p), :])
        d_pre = d_act[...] * kept * (sigma * (1.0 + pre * (1.0 - sigma)))
        d_z = factor * (count * d_pre - shift_grad - normed * gain_grad) * kept
        grad_pad[padded_pixel(p), :] = d_z.astype(low)
        return 0

    lax.fori_loop(0, pixels, leave_second, 0)

    partial[...] = jnp.zeros(partial.shape, f32)

    def spread_line(j, _):
        value = None
        for t in range(9):
            offset = (t // 3 - 1) * wide_line + (t % 3 - 1) * slots
            rows_in = pl.ds(pl.multiple_of(rim + j * wide_line - offset, slots), line)
            term = dot(grad_pad[rows_in, :], taps[:, t * width : (t + 1) * width], 1, 0)
            value = term if value is None else value + term
        second[line_rows(j), :] = value
        return 0

    lax.fori_loop(0, side, spread_line, 0)

    def enter_first(p, _):
        normed = (first[pixel_rows(p), :] - mean_one) * scale_one
        pre = gain_one * normed + shift_one
        sigma = sigmoid(pre)
        d_pre = second[pixel_rows(p), :] * across(valid[pixel_rows(p), :]) * (sigma * (1.0 + pre * (1.0 - sigma)))
        second[pixel_rows(p), :] = d_pre
        partial[0] += fold(d_pre)
        partial[1] += fold(d_pre * normed)
        return 0

    lax.fori_loop(0, pixels, enter_first, 0)
    pack_four[...] = jnp.concatenate([packed(total_of(0)), packed(total_of(1))], axis=0)
    going = exchange(pack_four, held_four)

    def turn(j, _):
        rows_in = pl.ds(pl.multiple_of(rim + j * wide_line, slots), wide_line)
        turned_grad[:, pl.ds(pl.multiple_of(j * wide_line, 128), wide_line)] = grad_pad[rows_in, :].T
        return 0

    lax.fori_loop(0, side, turn, 0)

    def leave(slot, target, sem):
        copy = pltpu.make_async_copy(grad_buf.at[slot], target, local.at[sem])
        copy.start()
        return copy

    leaving = []
    for t in range(9):
        offset = (t // 3 - 1) * wide_line + (t % 3 - 1) * slots
        slot = t % 2
        if t >= 2:
            leaving[t - 2].wait()
        shifted = hidden_pad.at[pl.ds(rim + offset, body_rows)]

        def tap_rows(m, _, slot=slot, shifted=shifted):
            rows_out = pl.ds(pl.multiple_of(m * 256, 256), 256)
            grad_buf[slot, rows_out, :] = dot(turned_grad[rows_out, :], shifted[...], 1, 0)
            return 0

        lax.fori_loop(0, width // 256, tap_rows, 0)
        leaving.append(leave(slot, spatial_out.at[:, pl.ds(t * width, width)], 7 + slot))

    totals_one = settled(going, held_four)
    shift_sum, gain_sum = unpacked(totals_one[:rows]), unpacked(totals_one[rows : 2 * rows])
    factor_one = gain_one * scale_one / count

    def leave_first(p, _):
        normed = (first[pixel_rows(p), :] - mean_one) * scale_one
        kept = across(valid[pixel_rows(p), :])
        d_z = factor_one * (count * second[pixel_rows(p), :] - shift_sum - normed * gain_sum) * kept
        grad_pad[padded_pixel(p), :] = d_z.astype(low)
        return 0

    lax.fori_loop(0, pixels, leave_first, 0)
    lax.fori_loop(0, side, turn, 0)
    per = width // depth
    for t in range(n // per):
        slot = (9 + t) % 2
        leaving[9 + t - 2].wait()

        def source_rows(m, _, slot=slot, t=t):
            rows_out = pl.ds(pl.multiple_of(m * 256, 256), 256)
            for k in range(per):
                block = own_images[t * per + k].reshape(body_rows, depth)
                grad_buf[slot, rows_out, k * depth : (k + 1) * depth] = dot(turned_grad[rows_out, :], block, 1, 0)
            return 0

        lax.fori_loop(0, width // 256, source_rows, 0)
        leaving.append(leave(slot, reduce_out.at[:, pl.ds(t * width, width)], 7 + slot))
    totals_out[...] = jnp.concatenate([totals_two, totals_one], axis=0)
    head_copy.wait()
    for copy in leaving[-2:]:
        copy.wait()


def local_step(images, weights, roots, norms, valid, labels, used, divisor, bias):
    n, nb = lax.axis_size("chan"), lax.axis_size("batch")
    nz, nx = n // 2, nb // 2
    slots, width = used.shape[0], norms.shape[1]
    line, depth, classes = SIDE * slots, images.shape[-1], bias.shape[1]
    f32, low = jnp.float32, jnp.bfloat16
    rows = weights.shape[0] // nb
    grids = ((SIDE * (SIDE + 1) + 2 * (SIDE + 2)) * slots, width)
    shape = jax.ShapeDtypeStruct
    gathered = lambda a: shape((nz, 2, nx, 2, rows, a.shape[1]), a.dtype)
    quarters = lambda a: a.reshape(nx, 2, rows, a.shape[1])
    held = lambda k: pltpu.VMEM((n * nb, k, 128), f32)
    pack = lambda k: pltpu.VMEM((k, 128), f32)
    count = 2 * (nz - 1) + 2 * (n - 1) + 2 * (1 + (nx - 1) + 1) + 4 * (n * nb - 1)
    two = 2 * width // 128
    three = two + classes // 128
    weight = lambda size: pltpu.VMEM((nz, 2, nx, 2, rows, size), low)
    spatial, reduce, head, totals, weights_full, roots_full = pl.pallas_call(
        step_kernel,
        out_shape=(
            shape((width, 9 * width), f32),
            shape((width, n * depth), f32),
            shape((width, classes), f32),
            shape((two + three, 128), f32),
            gathered(weights),
            gathered(roots),
        ),
        in_specs=[ANY, ANY, ANY, VMEM, VMEM, VMEM, VMEM, VMEM, VMEM],
        out_specs=(ANY, ANY, ANY, VMEM, ANY, ANY),
        scratch_shapes=[
            pltpu.VMEM((n, SIDE, line + slots, depth), low),
            pltpu.VMEM((SIDE * line, width), f32),
            pltpu.VMEM((SIDE * line, width), f32),
            pltpu.VMEM(grids, low),
            pltpu.VMEM(grids, low),
            pltpu.VMEM((width, SIDE * (line + slots)), low),
            weight(9 * width), weight(n * depth), weight(classes),
            pltpu.VMEM((n,) + norms.shape, f32),
            pack(two + 8), pack(two), pack(three), pack(two),
            held(two + 8), held(two), held(three), held(two),
            pltpu.VMEM((2, 8, width), f32),
            pltpu.VMEM((slots, width), low),
            pltpu.VMEM((slots, classes), low),
            pltpu.VMEM((slots, width), f32),
            pltpu.VMEM((width, classes), f32),
            pltpu.VMEM((2, width, width), f32),
            DMA((count,)), DMA((count,)), DMA((9,)),
        ],
        compiler_params=pltpu.CompilerParams(collective_id=0, has_side_effects=True, vmem_limit_bytes=60 << 20),
        name="step",
    )(images.reshape(n, SIDE, line, depth), quarters(weights), quarters(roots), norms, valid, labels, used, divisor, bias)
    return spatial, reduce, head, totals[:three], totals[three:], roots_full.reshape(width, roots.shape[1])


def settle_kernel(wire, spatial, reduce, head, mask, full, own, sums_a, sums_b, core_a, core_b, x_a, x_b, y_a, y_b,
                  z_a, z_b, sx_a, sx_b, sy_a, sy_b, sz_a, sz_b, final, final_low, send, recv, local):
    (z, y, x, core), (nz, ny, nx, nc) = place()
    greet([at(k, y, x, core) for k in turned(z, nz)] + [at(z, 1 - y, x, core)]
          + [at(z, y, k, core) for k in turned(x, nx)] + [at(z, y, x, 1 - core)])
    copies = Copies(send, recv)
    half = sums_a.shape[-1]
    tail = spatial.shape[-1] - half
    mate, mate_y = at(z, y, x, 1 - core), at(z, 1 - y, x, core)
    mates_x, mates_z = turned(x, nx), turned(z, nz)
    groups = [(i, j, k) for i in range(nz) for j in range(ny) for k in range(nx)]
    pieces_a = [(spatial.at[:, :, :, :, :, pl.ds(0, half)], 0, half)]
    pieces_b = [(spatial.at[:, :, :, :, :, pl.ds(half, tail)], 0, tail), (reduce, tail, reduce.shape[-1]),
                (head, tail + reduce.shape[-1], head.shape[-1])]

    def begin(pieces, sums, landing, sem):
        remote, kept = [], []
        for source, start, size in pieces:
            columns = pl.ds(start, size)
            remote.append(copies.start(source.at[:, :, :, 1 - core], landing.at[:, :, :, :, columns], mate))
            copy = pltpu.make_async_copy(source.at[:, :, :, core], sums.at[:, :, :, :, columns], local.at[sem + len(kept)])
            copy.start()
            kept.append(copy)
        return remote + kept

    def ship(source, staged, landing, peer):
        if staged.dtype == jnp.float32:
            return copies.start(source, landing, peer)
        for i in range(staged.shape[0]):
            staged[i] = source[i].astype(staged.dtype)
        return copies.start(staged, landing, peer)

    def add(sums, landing):
        for i in range(landing.shape[0]):
            sums[i] += landing[i].astype(jnp.float32)

    first_a = begin(pieces_a, sums_a, core_a, 0)
    first_b = begin(pieces_b, sums_b, core_b, len(pieces_a))
    for first, sums, landing in ((first_a, sums_a, core_a), (first_b, sums_b, core_b)):
        for copy in first:
            copy.wait()
        for i, j, k in groups:
            sums[i, j, k] += landing[i, j, k]
        if sums is sums_a:
            going_a = []
            for t, k in enumerate(mates_x):
                for j in range(ny):
                    going_a.append(ship(sums.at[:, j, k], sx_a.at[t, j], x_a.at[t, j], at(z, y, k, core)))
        else:
            going_b = [ship(sums.at[:, 1 - y, k], sy_b.at[k], y_b.at[k], mate_y) for k in range(nx)]
    for copy in going_a:
        copy.wait()
    for t in range(nx - 1):
        for j in range(ny):
            add(sums_a.at[:, j, x], x_a.at[t, j])
    going_a = [ship(sums_a.at[:, 1 - y, x], sy_a, y_a, mate_y)]
    for copy in going_b:
        copy.wait()
    for k in range(nx):
        add(sums_b.at[:, y, k], y_b.at[k])
    going_b = [ship(sums_b.at[:, y, k], sx_b.at[t], x_b.at[t], at(z, y, k, core)) for t, k in enumerate(mates_x)]
    for copy in going_a:
        copy.wait()
    add(sums_a.at[:, y, x], y_a)
    going_a = [ship(sums_a.at[pl.ds(k, 1), y, x], sz_a.at[pl.ds(t, 1)], z_a.at[pl.ds(t, 1)], at(k, y, x, core))
               for t, k in enumerate(mates_z)]
    for copy in going_b:
        copy.wait()
    for t in range(nx - 1):
        add(sums_b.at[:, y, x], x_b.at[t])
    going_b = [ship(sums_b.at[pl.ds(k, 1), y, x], sz_b.at[pl.ds(t, 1)], z_b.at[pl.ds(t, 1)], at(k, y, x, core))
               for t, k in enumerate(mates_z)]
    for going, sums, landing, start in ((going_a, sums_a, z_a, 0), (going_b, sums_b, z_b, half)):
        for copy in going:
            copy.wait()
        value = sums[z, y, x]
        for t in range(nz - 1):
            value = value + landing[t].astype(jnp.float32)
        columns = pl.ds(start, half)
        final[:, columns] = value * mask[:, columns]

    wide = full.shape[-1]
    final_low[...] = final[:, :wide].astype(final_low.dtype)
    keep = pltpu.make_async_copy(final_low, full.at[z, y, x, core], local.at[4])
    keep.start()
    keep_own = pltpu.make_async_copy(final, own.at[x, core], local.at[5])
    keep_own.start()
    up = [copies.start(final_low, full.at[z, y, x, core], at(k, y, x, core)) for k in mates_z]
    rows_x = [copies.start(final, own.at[x, core], at(z, y, k, core)) for k in mates_x]
    keep.wait()
    for copy in up:
        copy.wait()
    left, right = pl.ds(0, wide // 2), pl.ds(wide // 2, wide // 2)
    part = full.at[:, y, x, core, :, left]
    going_a = [copies.start(part, part, at(z, y, k, core)) for k in mates_x]
    part = full.at[:, y, x, core, :, right]
    going_b = [copies.start(part, part, mate_y)]
    keep_own.wait()
    for copy in rows_x:
        copy.wait()
    part = own.at[:, core]
    rows_core = copies.start(part, part, mate)
    for copy in going_a:
        copy.wait()
    part = full.at[:, y, :, core, :, left]
    going_a = [copies.start(part, part, mate_y)]
    for copy in going_b:
        copy.wait()
    part = full.at[:, :, x, core, :, right]
    going_b = [copies.start(part, part, at(z, y, k, core)) for k in mates_x]
    for copy in going_a:
        copy.wait()
    part = full.at[:, :, :, core, :, left]
    last = [copies.start(part, part, mate)]
    for copy in going_b:
        copy.wait()
    part = full.at[:, :, :, core, :, right]
    last += [copies.start(part, part, mate), rows_core]
    for copy in last:
        copy.wait()


def settle(spatial, reduce, head, mask, wire):
    nz, nx = lax.axis_size("chan") // 2, lax.axis_size("batch") // 2
    width = spatial.shape[0]
    rows = width // (4 * nz * nx)
    total = spatial.shape[1] + reduce.shape[1] + head.shape[1]
    wide, half = spatial.shape[1] + reduce.shape[1], total // 2
    split = lambda a: a.reshape(nz, 2, nx, 2, rows, a.shape[1])
    f32 = jnp.float32
    big = pltpu.VMEM((nz, 2, nx, rows, half), f32)
    shapes = [(nx - 1, 2, nz, rows, half), (nx - 1, nz, rows, half), (nz, rows, half), (nx, nz, rows, half),
              (nz - 1, rows, half), (nz - 1, rows, half)]
    landing = [pltpu.VMEM(s, wire) for s in shapes]
    staging = [pltpu.VMEM(s if wire != f32 else s[:-2] + (8, 128), wire) for s in shapes]
    count = 4 + 2 * (nx - 1) + nx + 1 + (nx - 1) + 2 * (nz - 1) + (nz - 1) + (nx - 1) + 2 * nx + 1 + 2
    full, own = pl.pallas_call(
        functools.partial(settle_kernel, wire),
        out_shape=(
            jax.ShapeDtypeStruct((nz, 2, nx, 2, rows, wide), jnp.bfloat16),
            jax.ShapeDtypeStruct((nx, 2, rows, total), f32),
        ),
        in_specs=[ANY, ANY, ANY, VMEM],
        out_specs=(ANY, ANY),
        scratch_shapes=[big, big, big, big] + landing + staging
        + [pltpu.VMEM((rows, total), f32), pltpu.VMEM((rows, wide), jnp.bfloat16), DMA((count,)), DMA((count,)), DMA((6,))],
        compiler_params=pltpu.CompilerParams(collective_id=1, has_side_effects=True, vmem_limit_bytes=56 << 20),
        name="settle",
    )(split(spatial), split(reduce), split(head), mask)
    return full.reshape(width, wide), own.reshape(2 * nx * rows, total)


def silu_slope(pre):
    sigma = jax.nn.sigmoid(pre)
    return sigma * (1.0 + pre * (1.0 - sigma))


def adam_step(param, grad, first, second, rate, decay):
    first = 0.9 * first + 0.1 * grad
    second = 0.999 * second + 0.001 * grad * grad
    mhat = first / (1.0 - 0.9**STEP)
    vhat = second / (1.0 - 0.999**STEP)
    return (param - rate * (mhat / (jnp.sqrt(vhat) + 1e-08) + decay * param), first, second)


def own_part(array, axis, name="chan"):
    size = array.shape[axis] // lax.axis_size(name)
    return lax.dynamic_slice_in_dim(array, lax.axis_index(name) * size, size, axis)


def two_parts(array):
    high = array.astype(jnp.bfloat16)
    return high, (array - high.astype(jnp.float32)).astype(jnp.bfloat16)


def product(spec, left, right):
    return jnp.einsum(spec, left, right, preferred_element_type=jnp.float32)


def conv_grid(grid, taps, spec):
    return lax.conv_general_dilated(
        grid, taps, (1, 1), ((1, 1), (1, 1)), dimension_numbers=spec, preferred_element_type=jnp.float32
    )


def body(
    images,
    pixel_mask,
    labels,
    reduce_weight,
    reduce_mask,
    spatial_weight,
    spatial_mask,
    head_weight,
    head_bias,
    norm_params,
    left_stats,
    right_stats,
    left_root,
    input_side_roots,
    head_first,
    head_second,
    bias_first,
    bias_second,
    norm_first,
    norm_second,
):
    n = lax.axis_size("chan")
    pixels, channels = images.shape[1:]
    side = SIDE
    rows_out, c_in = reduce_weight.shape
    width = left_stats.shape[2]
    classes = head_weight.shape[1]
    padded = 1024
    slots = images.shape[0] // n
    low = jnp.bfloat16
    f32 = jnp.float32
    reduce_float = reduce_mask.astype(f32)
    spatial_float = spatial_mask.astype(f32)

    spread_out = lambda a: jnp.broadcast_to(a[:, None], (a.shape[0], 128))
    by_pixel = images.reshape(n, slots, pixels, channels).transpose(0, 2, 1, 3)
    weights = jnp.concatenate(
        [(spatial_weight * spatial_float).astype(low), (reduce_weight * reduce_float).astype(low),
         jnp.pad(head_weight.astype(low), ((0, 0), (0, padded - classes)))], axis=1)
    roots = input_side_roots.astype(low).transpose(1, 0, 2).reshape(rows_out, -1)
    norms = lax.dynamic_update_slice_in_dim(
        jnp.zeros((8, width), f32), jnp.pad(norm_params, ((0, 4), (0, 0))), lax.axis_index("chan") * rows_out, 1)
    mask_own = own_part(pixel_mask, 0).astype(f32)
    filled = jnp.sum(mask_own, axis=1)
    spatial_local, reduce_local, head_local, sums_two, sums_one, roots_full = local_step(
        by_pixel, weights, roots, norms, spread_out(mask_own.T.reshape(-1)), spread_out(own_part(labels, 0)),
        spread_out((filled > 0.0).astype(f32)), spread_out(jnp.maximum(filled, 1.0)),
        jnp.pad(head_bias, (0, padded - classes), constant_values=-1e30)[None])

    mask_rows = jnp.concatenate([spatial_float, reduce_float, jnp.ones((rows_out, padded), f32)], axis=1)
    full, own = settle(spatial_local, reduce_local, head_local, own_part(mask_rows, 0, "batch"), jnp.float32)
    spatial_grad = own[:, : 9 * width]
    reduce_grad = own[:, 9 * width : 9 * width + c_in]
    head_grad = own[:, 9 * width + c_in : 9 * width + c_in + classes]
    of_norms = jnp.stack([a.reshape(-1) for a in (sums_one[4:], sums_one[:4], sums_two[4:8], sums_two[:4])])
    norm_gain_gradient = own_part(of_norms, 1)
    of_head = sums_two[8:].reshape(-1)
    bias_grad = of_head[:classes]
    loss_sum, slot_count = of_head[-1], of_head[-2]
    right_full = roots_full.reshape(width, -1, width)

    tiles_one = c_in // width
    blocks_of = lambda a: a.reshape(a.shape[0], -1, width).transpose(1, 0, 2)
    in_order = lambda a: jnp.concatenate([a[9:], a[:9]], axis=0)
    blocks = in_order(blocks_of(own[:, : 9 * width + c_in])).astype(low)
    blocks_full = in_order(blocks_of(full))
    left_new = 0.95 * left_stats + product("tak,tbk->tab", blocks, blocks_full)
    right_new = 0.95 * right_stats + product("tki,tkb->tib", own_part(blocks_full, 2), blocks_full)
    left_high, left_rest = two_parts(left_root)
    inner = product("tak,tkb->tab", left_high, blocks_full) + product("tak,tkb->tab", left_rest, blocks_full)
    inner_high, inner_rest = two_parts(inner)
    outer = product("tak,ktb->tab", inner_high, right_full) + product("tak,ktb->tab", inner_rest, right_full)
    squares = jnp.pad(jnp.sum(outer * outer, axis=(1, 2))[:, None] * jnp.ones((1, 128), f32), ((0, 3), (0, 0)))
    squares = chan_sum(squares, 6)[: 9 + tiles_one, 0]
    step = outer / jnp.sqrt(squares / (width * width) + 1e-06)[:, None, None]
    step_one = step[:tiles_one].transpose(1, 0, 2).reshape(rows_out, c_in)
    step_two = step[tiles_one:].transpose(1, 0, 2).reshape(rows_out, 9 * width)
    reduce_new = reduce_weight - 0.02 * reduce_float * (step_one + 0.1 * reduce_weight)
    spatial_new = spatial_weight - 0.02 * spatial_float * (step_two + 0.1 * spatial_weight)
    head_new, head_first_new, head_second_new = adam_step(head_weight, head_grad, head_first, head_second, 0.04, 0.1)
    bias_new, bias_first_new, bias_second_new = adam_step(head_bias, bias_grad, bias_first, bias_second, 0.1, 0.0)
    norm_new, norm_first_new, norm_second_new = adam_step(
        norm_params, norm_gain_gradient, norm_first, norm_second, 0.1, 0.0)
    return (
        loss_sum,
        slot_count,
        reduce_grad,
        spatial_grad,
        reduce_new,
        spatial_new,
        left_new,
        right_new,
        head_new,
        head_first_new,
        head_second_new,
        bias_new,
        bias_first_new,
        bias_second_new,
        norm_new,
        norm_first_new,
        norm_second_new,
    )


FULL_PRECISION = lax.Precision.HIGHEST
BOTH = ("chan", "batch")


def plain_norm_forward(pre_norm, gain, shift, valid):
    first_sum = jnp.sum(pre_norm * valid, axis=(0, 1))
    second_sum = jnp.sum(pre_norm * pre_norm * valid, axis=(0, 1))
    first_sum, second_sum, count = lax.psum((first_sum, second_sum, jnp.sum(valid)), BOTH)
    mean = first_sum / count
    scale = lax.rsqrt(second_sum / count - mean * mean + EPS)
    normed = (pre_norm - mean) * scale
    pre = gain * normed + shift
    return (jax.nn.silu(pre) * valid, (normed, pre, scale, count))


def plain_norm_backward(grad_act, kept, gain, valid):
    normed, pre, scale, count = kept
    d_pre = grad_act * valid * silu_slope(pre)
    shift_gradient, gain_grad = lax.psum(
        (jnp.sum(d_pre, axis=(0, 1)), jnp.sum(d_pre * normed, axis=(0, 1))), BOTH
    )
    d_input = gain * scale / count * (count * d_pre - shift_gradient - normed * gain_grad) * valid
    return (d_input, gain_grad, shift_gradient)


def plain_own_part(array, parts, axis=0):
    size = array.shape[axis] // parts
    return lax.dynamic_slice_in_dim(array, lax.axis_index("chan") * size, size, axis)


def plain_body(
    images,
    pixel_mask,
    labels,
    reduce_weight,
    reduce_mask,
    spatial_weight,
    spatial_mask,
    head_weight,
    head_bias,
    norm_params,
    left_stats,
    right_stats,
    left_root,
    input_side_roots,
    head_first,
    head_second,
    bias_first,
    bias_second,
    norm_first,
    norm_second,
):
    parts = lax.axis_size("chan")
    pixels = images.shape[1]
    side = SIDE
    rows_out = reduce_weight.shape[0]
    width = left_stats.shape[2]
    classes = head_weight.shape[1]
    own_images = lax.all_to_all(images, "chan", 0, 2, tiled=True)
    slots = own_images.shape[0]
    reduce_float = reduce_mask.astype(jnp.float32)
    spatial_float = spatial_mask.astype(jnp.float32)
    gather = lambda a, axis: lax.all_gather(a, "chan", axis=axis, tiled=True)
    reduce_low = gather((reduce_weight * reduce_float).astype(jnp.bfloat16), 0)
    spatial_low = gather((spatial_weight * spatial_float).astype(jnp.bfloat16), 0)
    head_low = gather(head_weight.astype(jnp.bfloat16), 0)
    norm_full = gather(norm_params, 1)
    right_factor_full = gather(input_side_roots, 1)
    valid = plain_own_part(pixel_mask, parts).astype(jnp.float32)[:, :, None]
    own_labels = plain_own_part(labels, parts)
    filled = jnp.sum(valid[:, :, 0], axis=1)
    divisor = jnp.maximum(filled, 1.0)
    used = (filled > 0.0).astype(jnp.float32)
    taps = spatial_low.reshape(width, 3, 3, width)
    first_pre = jnp.einsum("spc,oc->spo", own_images, reduce_low, preferred_element_type=jnp.float32)
    first_act, first_kept = plain_norm_forward(first_pre, norm_full[0], norm_full[1], valid)
    hidden = first_act.astype(jnp.bfloat16).reshape(slots, side, side, width)
    second_pre = conv_grid(hidden, taps, ("NHWC", "OHWI", "NHWC")).reshape(slots, pixels, width)
    second_act, second_kept = plain_norm_forward(second_pre, norm_full[2], norm_full[3], valid)
    pooled = (jnp.sum(second_act, axis=1) / divisor[:, None]).astype(jnp.bfloat16)
    logits = jnp.dot(pooled, head_low, preferred_element_type=jnp.float32) + head_bias
    onehot = (jnp.arange(classes)[None, :] == own_labels[:, None]).astype(jnp.float32)
    log_total = jax.nn.logsumexp(logits, axis=1)
    picked = jnp.sum(onehot * logits, axis=1)
    loss_local = jnp.sum(used * (log_total - picked))
    d_logits = (used[:, None] * (jnp.exp(logits - log_total[:, None]) - onehot) / SLOTS_DEV).astype(
        jnp.bfloat16
    )
    head_grad = jnp.einsum("so,sc->oc", pooled, d_logits, preferred_element_type=jnp.float32)
    bias_grad = jnp.sum(d_logits.astype(jnp.float32), axis=0)
    d_pooled = jnp.einsum("sc,oc->so", d_logits, head_low, preferred_element_type=jnp.float32)
    d_act = jnp.broadcast_to((d_pooled / divisor[:, None])[:, None, :], second_act.shape)
    d_second, gain_two, shift_two = plain_norm_backward(d_act, second_kept, norm_full[2], valid)
    d_second = d_second.astype(jnp.bfloat16).reshape(slots, side, side, width)
    spatial_local = lax.conv_general_dilated(
        hidden, d_second, (1, 1), ((1, 1), (1, 1)), dimension_numbers=("CHWN", "IHWO", "NHWC"),
        preferred_element_type=jnp.float32,
    )
    spatial_local = spatial_local.transpose(3, 1, 2, 0).reshape(width, 9 * width)
    d_hidden = conv_grid(
        d_second, taps[:, ::-1, ::-1, :], ("NHWC", "IHWO", "NHWC")
    ).reshape(slots, pixels, width)
    d_first, gain_one, shift_one = plain_norm_backward(d_hidden, first_kept, norm_full[0], valid)
    d_first = d_first.astype(jnp.bfloat16)
    reduce_local = jnp.einsum("spc,spo->oc", own_images, d_first, preferred_element_type=jnp.float32)
    scatter = lambda a: lax.psum_scatter(a, "chan", scatter_dimension=0, tiled=True)
    reduce_grad, spatial_grad, head_grad = scatter(reduce_local), scatter(spatial_local), scatter(head_grad)
    reduce_grad, spatial_grad, head_grad = lax.psum((reduce_grad, spatial_grad, head_grad), "batch")
    reduce_grad = reduce_grad * reduce_float
    spatial_grad = spatial_grad * spatial_float
    bias_grad, loss_sum, slot_count = lax.psum((bias_grad, loss_local, jnp.sum(used)), BOTH)
    norm_gain_gradient = plain_own_part(jnp.stack([gain_one, shift_one, gain_two, shift_two], axis=0), parts, 1)
    tiles_one = reduce_weight.shape[1] // width
    blocks = jnp.concatenate(
        [
            reduce_grad.reshape(rows_out, tiles_one, width).transpose(1, 0, 2),
            spatial_grad.reshape(rows_out, 9, width).transpose(1, 0, 2),
        ],
        axis=0,
    )
    blocks_full = gather(blocks, 1)
    left_new = 0.95 * left_stats + jnp.einsum(
        "tak,tbk->tab", blocks, blocks_full, precision=FULL_PRECISION
    )
    own_columns = plain_own_part(blocks_full, parts, 2)
    right_new = 0.95 * right_stats + jnp.einsum(
        "tki,tkb->tib", own_columns, blocks_full, precision=FULL_PRECISION
    )
    matrix_product = jnp.einsum("tak,tkb->tab", left_root, blocks_full, precision=FULL_PRECISION)
    matrix_product = jnp.einsum(
        "ghk,gkl->ghl", matrix_product, right_factor_full, precision=FULL_PRECISION
    )
    squares = lax.psum(jnp.sum(matrix_product * matrix_product, axis=(1, 2)), "chan")
    step = matrix_product / jnp.sqrt(squares / (width * width) + 1e-06)[:, None, None]
    step_one = step[:tiles_one].transpose(1, 0, 2).reshape(rows_out, tiles_one * width)
    step_two = step[tiles_one:].transpose(1, 0, 2).reshape(rows_out, 9 * width)
    reduce_new = reduce_weight - 0.02 * reduce_float * (step_one + 0.1 * reduce_weight)
    spatial_new = spatial_weight - 0.02 * spatial_float * (step_two + 0.1 * spatial_weight)
    head_new, head_first_new, head_second_new = adam_step(
        head_weight, head_grad, head_first, head_second, 0.04, 0.1
    )
    bias_new, bias_first_new, bias_second_new = adam_step(
        head_bias, bias_grad, bias_first, bias_second, 0.1, 0.0
    )
    norm_new, norm_first_new, norm_second_new = adam_step(
        norm_params, norm_gain_gradient, norm_first, norm_second, 0.1, 0.0
    )
    return (
        loss_sum,
        slot_count,
        reduce_grad,
        spatial_grad,
        reduce_new,
        spatial_new,
        left_new,
        right_new,
        head_new,
        head_first_new,
        head_second_new,
        bias_new,
        bias_first_new,
        bias_second_new,
        norm_new,
        norm_first_new,
        norm_second_new,
    )


def solution(mesh):
    in_specs = (
        P("batch", None, "chan"),
        P("batch", None),
        P("batch"),
        P("chan", None),
        P("chan", None),
        P("chan", None),
        P("chan", None),
        P("chan", None),
        P(),
        P(None, "chan"),
        P(None, "chan", None),
        P(None, "chan", None),
        P(None, "chan", None),
        P(None, "chan", None),
        P("chan", None),
        P("chan", None),
        P(),
        P(),
        P(None, "chan"),
        P(None, "chan"),
    )
    out_specs = (
        P(),
        P(),
        P("chan", None),
        P("chan", None),
        P("chan", None),
        P("chan", None),
        P(None, "chan", None),
        P(None, "chan", None),
        P("chan", None),
        P("chan", None),
        P("chan", None),
        P(),
        P(),
        P(),
        P(None, "chan"),
        P(None, "chan"),
        P(None, "chan"),
    )
    chan, batch = mesh.shape["chan"], mesh.shape["batch"]
    fits = chan % 2 == 0 and batch % 2 == 0 and WIDTH % (16 * chan * batch) == 0 and SLOTS_DEV % (16 * chan) == 0
    return jax.shard_map(body if fits else plain_body, mesh=mesh, in_specs=in_specs, out_specs=out_specs, check_vma=False)
```

```python
import functools

import jax
import jax.numpy as jnp
from jax import lax
from jax.experimental import pallas as pl
from jax.experimental.pallas import tpu as pltpu
from jax.sharding import PartitionSpec as P

SIDE = 7
SLOTS_DEV = 384
STEP = 10

WIDTH = 512
EPS = 1e-05
MESH = pl.DeviceIdType.MESH
ANY = pl.BlockSpec(memory_space=pl.ANY)
VMEM = pl.BlockSpec(memory_space=pltpu.VMEM)
DMA = pltpu.SemaphoreType.DMA
SMALL = 8


def place():
    c, b = lax.axis_index("chan"), lax.axis_index("batch")
    nz, nx = lax.axis_size("chan") // 2, lax.axis_size("batch") // 2
    return (c // 2, lax.rem(c, 2), b // 2, lax.rem(b, 2)), (nz, 2, nx, 2)


def at(z, y, x, core):
    return {"chan": z * 2 + y, "batch": x * 2 + core}


def turned(index, size):
    return [lax.rem(index + k, size) for k in range(1, size)]


def greet(peers):
    barrier = pltpu.get_barrier_semaphore()
    for peer in peers:
        pl.semaphore_signal(barrier, inc=1, device_id=peer, device_id_type=MESH)
    pl.semaphore_wait(barrier, len(peers))


class Copies:
    def __init__(self, send, recv):
        self.send, self.recv, self.used = send, recv, 0

    def start(self, source, target, peer):
        copy = pltpu.make_async_remote_copy(
            source, target, self.send.at[self.used], self.recv.at[self.used],
            device_id=peer, device_id_type=MESH,
        )
        self.used += 1
        copy.start()
        return copy


def chan_sum_kernel(own, total, held, send, recv):
    c, n = lax.axis_index("chan"), lax.axis_size("chan")
    peers = [{"chan": other} for other in turned(c, n)]
    greet(peers)
    copies = Copies(send, recv)
    started = [copies.start(own, held.at[k + 1], peer) for k, peer in enumerate(peers)]
    held[0] = own[...]
    for copy in started:
        copy.wait()
    total[...] = jnp.sum(held[...], axis=0)


def chan_sum(rows, cid):
    n = lax.axis_size("chan")
    return pl.pallas_call(
        chan_sum_kernel,
        out_shape=jax.ShapeDtypeStruct(rows.shape, jnp.float32),
        in_specs=[VMEM],
        out_specs=VMEM,
        scratch_shapes=[pltpu.VMEM((n,) + rows.shape, jnp.float32), DMA((n - 1,)), DMA((n - 1,))],
        compiler_params=pltpu.CompilerParams(collective_id=cid, has_side_effects=True),
        name="chan_sum",
    )(rows)


def dot(left, right, left_dim, right_dim):
    return lax.dot_general(left, right, (((left_dim,), (right_dim,)), ((), ())), preferred_element_type=jnp.float32)


def sigmoid(value):
    return 1.0 / (1.0 + jnp.exp(-value))


def packed(row):
    return jnp.concatenate([row[:, i : i + 128] for i in range(0, row.shape[1], 128)], axis=0)


def unpacked(block):
    return jnp.concatenate([block[i : i + 1] for i in range(block.shape[0])], axis=1)


def step_kernel(
    images, weights, roots, norms, valid, labels, used, divisor, bias,
    spatial_out, reduce_out, head_out, totals_out, weights_out, roots_out,
    own_images, first, second, hidden_pad, grad_pad, turned_grad, taps, reduce_low, head_low,
    norms_held, pack_one, pack_two, pack_three, pack_four, held_one, held_two, held_three, held_four,
    partial, pooling, pooled_low, d_logits, d_act, head_buf, grad_buf, send, recv, local,
):
    (z, y, x, core), (nz, ny, nx, nc) = place()
    c, n = lax.axis_index("chan"), lax.axis_size("chan")
    f32, low = jnp.float32, jnp.bfloat16
    slots = used.shape[0]
    side = SIDE
    line = side * slots
    wide_line = (side + 1) * slots
    pixels = side * side
    rim = (side + 2) * slots
    body_rows = side * wide_line
    width = first.shape[1]
    depth = own_images.shape[-1]
    everyone = [
        at(lax.rem(z + i, nz), lax.rem(y + j, ny), lax.rem(x + k, nx), lax.rem(core + m, nc))
        for i in range(nz) for j in range(ny) for k in range(nx) for m in range(nc) if i + j + k + m
    ]
    greet(everyone)
    copies = Copies(send, recv)
    others = turned(c, n)
    across_z = lax.rem(z + nz // 2, nz)
    near_z = [z // (nz // 2) * (nz // 2) + lax.rem(lax.rem(z, nz // 2) + k, nz // 2) for k in range(1, nz // 2)]
    mate, mate_y = at(z, y, x, 1 - core), at(z, 1 - y, x, core)
    mates_x = [at(z, y, k, core) for k in turned(x, nx)]

    def begin_z(source, target, sem):
        keep = pltpu.make_async_copy(source.at[x, core], target.at[z, y, x, core], local.at[sem])
        keep.start()
        peers = [at(k, y, x, core) for k in [across_z] + near_z]
        return [keep] + [copies.start(source.at[x, core], target.at[z, y, x, core], peer) for peer in peers]

    def pass_z(target, begun):
        for copy in begun:
            copy.wait()
        part = target.at[across_z, y, x, core]
        return [copies.start(part, part, at(k, y, x, core)) for k in near_z]

    weights_z = pass_z(weights_out, begin_z(weights, weights_out, 0))
    norm_copies = [copies.start(norms, norms_held.at[k + 1], {"chan": other}) for k, other in enumerate(others)]
    image_copies = [copies.start(images.at[k], own_images.at[c, :, pl.ds(0, line)], {"chan": k}) for k in others]
    own = pltpu.make_async_copy(images.at[c], own_images.at[c, :, pl.ds(0, line)], local.at[2])
    own.start()
    norms_held[0] = norms[...]

    def clear(i, _):
        rows = pl.ds(pl.multiple_of(i * slots, slots), slots)
        hidden_pad[rows, :] = jnp.zeros((slots, width), low)
        grad_pad[rows, :] = jnp.zeros((slots, width), low)
        return 0

    lax.fori_loop(0, hidden_pad.shape[0] // slots, clear, 0)
    for k in range(n):
        for j in range(side):
            own_images[k, j, pl.ds(line, slots), :] = jnp.zeros((slots, depth), low)

    for copy in weights_z:
        copy.wait()
    part = weights_out.at[:, y, x, core]
    copies.start(part, part, mate_y).wait()
    part = weights_out.at[:, :, x, core]
    along_x = [copies.start(part, part, peer) for peer in mates_x]
    for copy in along_x:
        copy.wait()
    part = weights_out.at[:, :, :, core]
    copies.start(part, part, mate).wait()
    fetched = []
    start = 0
    for j, held in enumerate((taps, reduce_low, head_low)):
        size = held.shape[-1]
        copy = pltpu.make_async_copy(weights_out.at[:, :, :, :, :, pl.ds(start, size)], held, local.at[3 + j])
        copy.start()
        fetched.append(copy)
        start += size
    for copy in fetched:
        copy.wait()
    taps, reduce_low, head_low = (held.reshape(width, held.shape[-1]) for held in (taps, reduce_low, head_low))
    for copy in norm_copies:
        copy.wait()
    norm_rows = jnp.sum(norms_held[...], axis=0)
    gain_one, shift_one, gain_two, shift_two = (norm_rows[i : i + 1] for i in range(4))

    def line_rows(j):
        return pl.ds(pl.multiple_of(j * line, slots), line)

    def pixel_rows(p):
        return pl.ds(pl.multiple_of(p * slots, slots), slots)

    def padded_pixel(p):
        j = p // side
        return pl.ds(pl.multiple_of(rim + (p + j) * slots, slots), slots)

    def across(block):
        return jnp.concatenate([block] * (width // 128), axis=1)

    def fold(value):
        return jnp.sum(value.reshape(-1, 8, width), axis=0)

    def total_of(index):
        return jnp.sum(partial[index], axis=0, keepdims=True)

    def exchange(pack, held):
        pack_copies = [copies.start(pack, held.at[k + 1], peer) for k, peer in enumerate(everyone)]
        held[0] = pack[...]
        return pack_copies

    def settled(pack_copies, held):
        for copy in pack_copies:
            copy.wait()
        return jnp.sum(held[...], axis=0)

    for k in range(n):
        source = lax.rem(c + n - k, n)
        if k == 0:
            own.wait()
        else:
            image_copies[k - 1].wait()
        columns = pl.ds(pl.multiple_of(source * depth, depth), depth)

        def reduce_line(j, _, k=k, source=source, columns=columns):
            value = dot(own_images[source, j, pl.ds(0, line), :], reduce_low[:, columns], 1, 1)
            if k:
                value = first[line_rows(j), :] + value
            first[line_rows(j), :] = value
            return 0

        lax.fori_loop(0, side, reduce_line, 0)

    def norm_sums(ref):
        partial[...] = jnp.zeros(partial.shape, f32)

        def add(p, _):
            value = ref[pixel_rows(p), :]
            kept = value * across(valid[pixel_rows(p), :])
            partial[0] += fold(kept)
            partial[1] += fold(kept * value)
            return 0

        lax.fori_loop(0, pixels, add, 0)

    norm_sums(first)
    all_valid = jnp.sum(valid[...], axis=0, keepdims=True)
    pack_one[...] = jnp.concatenate(
        [packed(total_of(0)), packed(total_of(1)), all_valid, jnp.zeros((7, 128), f32)], axis=0)
    stats = settled(exchange(pack_one, held_one), held_one)
    rows = width // 128
    count = jnp.concatenate([stats[2 * rows : 2 * rows + 1]] * rows, axis=1)

    def norm_of(stats):
        mean = unpacked(stats[:rows]) / count
        scale = lax.rsqrt(unpacked(stats[rows : 2 * rows]) / count - mean * mean + EPS)
        return mean, scale

    mean_one, scale_one = norm_of(stats)
    roots_z = begin_z(roots, roots_out, 1)

    def activate(p, _):
        normed = (first[pixel_rows(p), :] - mean_one) * scale_one
        pre = gain_one * normed + shift_one
        act = pre * sigmoid(pre) * across(valid[pixel_rows(p), :])
        hidden_pad[padded_pixel(p), :] = act.astype(low)
        return 0

    lax.fori_loop(0, pixels, activate, 0)

    def conv_line(j, _):
        value = None
        for t in range(9):
            offset = (t // 3 - 1) * wide_line + (t % 3 - 1) * slots
            rows_in = pl.ds(pl.multiple_of(rim + j * wide_line + offset, slots), line)
            term = dot(hidden_pad[rows_in, :], taps[:, t * width : (t + 1) * width], 1, 1)
            value = term if value is None else value + term
        second[line_rows(j), :] = value
        return 0

    lax.fori_loop(0, side, conv_line, 0)
    roots_z = pass_z(roots_out, roots_z)
    norm_sums(second)
    pack_two[...] = jnp.concatenate([packed(total_of(0)), packed(total_of(1))], axis=0)
    stats = settled(exchange(pack_two, held_two), held_two)
    mean_two, scale_two = norm_of(stats)
    for copy in roots_z:
        copy.wait()
    across_half = roots_out.shape[-1] // 2
    left, right = pl.ds(0, across_half), pl.ds(across_half, across_half)
    part = roots_out.at[:, y, x, core, :, left]
    roots_a = [copies.start(part, part, peer) for peer in mates_x]
    part = roots_out.at[:, y, x, core, :, right]
    roots_b = [copies.start(part, part, mate_y)]

    pooling[...] = jnp.zeros(pooling.shape, f32)

    def pool(p, _):
        normed = (second[pixel_rows(p), :] - mean_two) * scale_two
        pre = gain_two * normed + shift_two
        sigma = sigmoid(pre)
        kept = across(valid[pixel_rows(p), :])
        slope = sigma * (1.0 + pre * (1.0 - sigma)) * kept
        pooling[0] += pre * sigma * kept
        pooling[1] += slope
        pooling[2] += slope * normed
        return 0

    lax.fori_loop(0, pixels, pool, 0)
    divide = across(divisor[...])
    pooled_low[...] = (pooling[0] / divide).astype(low)
    logits = dot(pooled_low[...], head_low[...], 1, 0) + bias[...]
    classes = logits.shape[1]
    index = lax.broadcasted_iota(jnp.int32, (slots, classes), 1)
    onehot = (index == labels[:, :1]).astype(f32)
    top = jnp.max(logits, axis=1, keepdims=True)
    log_total = jnp.log(jnp.sum(jnp.exp(logits - top), axis=1, keepdims=True)) + top
    picked = jnp.sum(onehot * logits, axis=1, keepdims=True)
    use = used[:, :1]
    loss = jnp.sum(use * (log_total - picked))
    d_logits[...] = (use * (jnp.exp(logits - log_total) - onehot) / SLOTS_DEV).astype(low)
    bias_sum = jnp.sum(d_logits[...].astype(f32), axis=0, keepdims=True)
    half = width // 2

    def to_pooled(m, _):
        rows_in = pl.ds(pl.multiple_of(m * half, half), half)
        d_act[:, rows_in] = dot(d_logits[...], head_low[rows_in, :], 1, 1) / across(divisor[...])[:, :half]
        return 0

    lax.fori_loop(0, 2, to_pooled, 0)
    at_class = lax.broadcasted_iota(jnp.int32, (1, classes), 1)
    bias_sum = jnp.where(at_class == classes - 1, loss, jnp.where(at_class == classes - 2, jnp.sum(use), bias_sum))
    pack_three[...] = jnp.concatenate(
        [packed(jnp.sum(d_act[...] * pooling[1], axis=0, keepdims=True)),
         packed(jnp.sum(d_act[...] * pooling[2], axis=0, keepdims=True)), packed(bias_sum)], axis=0)
    going = exchange(pack_three, held_three)

    def to_head(m, _):
        columns = pl.ds(pl.multiple_of(m * (classes // 2), 128), classes // 2)
        head_buf[:, columns] = dot(pooled_low[...], d_logits[:, columns], 0, 0)
        return 0

    lax.fori_loop(0, 2, to_head, 0)
    head_copy = pltpu.make_async_copy(head_buf, head_out, local.at[6])
    head_copy.start()
    totals_two = settled(going, held_three)
    shift_grad, gain_grad = unpacked(totals_two[:rows]), unpacked(totals_two[rows : 2 * rows])
    factor = gain_two * scale_two / count
    for copy in roots_a:
        copy.wait()
    part = roots_out.at[:, y, :, core, :, left]
    roots_a = [copies.start(part, part, mate_y)]
    for copy in roots_b:
        copy.wait()
    part = roots_out.at[:, :, x, core, :, right]
    roots_b = [copies.start(part, part, peer) for peer in mates_x]

    def leave_second(p, _):
        normed = (second[pixel_rows(p), :] - mean_two) * scale_two
        pre = gain_two * normed + shift_two
        sigma = sigmoid(pre)
        kept = across(valid[pixel_rows(p), :])
        d_pre = d_act[...] * kept * (sigma * (1.0 + pre * (1.0 - sigma)))
        d_z = factor * (count * d_pre - shift_grad - normed * gain_grad) * kept
        grad_pad[padded_pixel(p), :] = d_z.astype(low)
        return 0

    lax.fori_loop(0, pixels, leave_second, 0)

    partial[...] = jnp.zeros(partial.shape, f32)

    def spread_line(j, _):
        value = None
        for t in range(9):
            offset = (t // 3 - 1) * wide_line + (t % 3 - 1) * slots
            rows_in = pl.ds(pl.multiple_of(rim + j * wide_line - offset, slots), line)
            term = dot(grad_pad[rows_in, :], taps[:, t * width : (t + 1) * width], 1, 0)
            value = term if value is None else value + term
        second[line_rows(j), :] = value
        return 0

    lax.fori_loop(0, side, spread_line, 0)
    for copy in roots_a + roots_b:
        copy.wait()
    part = roots_out.at[:, :, :, core]
    roots_core = copies.start(part, part, mate)

    def enter_first(p, _):
        normed = (first[pixel_rows(p), :] - mean_one) * scale_one
        pre = gain_one * normed + shift_one
        sigma = sigmoid(pre)
        d_pre = second[pixel_rows(p), :] * across(valid[pixel_rows(p), :]) * (sigma * (1.0 + pre * (1.0 - sigma)))
        second[pixel_rows(p), :] = d_pre
        partial[0] += fold(d_pre)
        partial[1] += fold(d_pre * normed)
        return 0

    lax.fori_loop(0, pixels, enter_first, 0)
    pack_four[...] = jnp.concatenate([packed(total_of(0)), packed(total_of(1))], axis=0)
    going = exchange(pack_four, held_four)

    def turn(j, _):
        rows_in = pl.ds(pl.multiple_of(rim + j * wide_line, slots), wide_line)
        turned_grad[:, pl.ds(pl.multiple_of(j * wide_line, 128), wide_line)] = grad_pad[rows_in, :].T
        return 0

    lax.fori_loop(0, side, turn, 0)

    def leave(slot, target, sem):
        copy = pltpu.make_async_copy(grad_buf.at[slot], target, local.at[sem])
        copy.start()
        return copy

    leaving = []
    for t in range(9):
        offset = (t // 3 - 1) * wide_line + (t % 3 - 1) * slots
        slot = t % 2
        if t >= 2:
            leaving[t - 2].wait()
        shifted = hidden_pad.at[pl.ds(rim + offset, body_rows)]

        grad_buf[slot] = dot(turned_grad[...], shifted[...], 1, 0)
        leaving.append(leave(slot, spatial_out.at[:, pl.ds(t * width, width)], 7 + slot))

    totals_one = settled(going, held_four)
    shift_sum, gain_sum = unpacked(totals_one[:rows]), unpacked(totals_one[rows : 2 * rows])
    factor_one = gain_one * scale_one / count

    def leave_first(p, _):
        normed = (first[pixel_rows(p), :] - mean_one) * scale_one
        kept = across(valid[pixel_rows(p), :])
        d_z = factor_one * (count * second[pixel_rows(p), :] - shift_sum - normed * gain_sum) * kept
        grad_pad[padded_pixel(p), :] = d_z.astype(low)
        return 0

    lax.fori_loop(0, pixels, leave_first, 0)
    lax.fori_loop(0, side, turn, 0)
    per = width // depth
    for t in range(n // per):
        slot = (9 + t) % 2
        leaving[9 + t - 2].wait()

        def source_rows(m, _, slot=slot, t=t):
            rows_out = pl.ds(pl.multiple_of(m * 256, 256), 256)
            for k in range(per):
                block = own_images[t * per + k].reshape(body_rows, depth)
                grad_buf[slot, rows_out, k * depth : (k + 1) * depth] = dot(turned_grad[rows_out, :], block, 1, 0)
            return 0

        lax.fori_loop(0, width // 256, source_rows, 0)
        leaving.append(leave(slot, reduce_out.at[:, pl.ds(t * width, width)], 7 + slot))
    totals_out[...] = jnp.concatenate([totals_two, totals_one], axis=0)
    head_copy.wait()
    roots_core.wait()
    for copy in leaving[-2:]:
        copy.wait()


def local_step(images, weights, roots, norms, valid, labels, used, divisor, bias):
    n, nb = lax.axis_size("chan"), lax.axis_size("batch")
    nz, nx = n // 2, nb // 2
    slots, width = used.shape[0], norms.shape[1]
    line, depth, classes = SIDE * slots, images.shape[-1], bias.shape[1]
    f32, low = jnp.float32, jnp.bfloat16
    rows = weights.shape[0] // nb
    grids = ((SIDE * (SIDE + 1) + 2 * (SIDE + 2)) * slots, width)
    shape = jax.ShapeDtypeStruct
    gathered = lambda a: shape((nz, 2, nx, 2, rows, a.shape[1]), a.dtype)
    quarters = lambda a: a.reshape(nx, 2, rows, a.shape[1])
    held = lambda k: pltpu.VMEM((n * nb, k, 128), f32)
    pack = lambda k: pltpu.VMEM((k, 128), f32)
    count = 2 * (nz - 1) + 2 * (n - 1) + (1 + (nx - 1) + 1) + (2 * nx + 1) + 4 * (n * nb - 1)
    two = 2 * width // 128
    three = two + classes // 128
    weight = lambda size: pltpu.VMEM((nz, 2, nx, 2, rows, size), low)
    spatial, reduce, head, totals, weights_full, roots_full = pl.pallas_call(
        step_kernel,
        out_shape=(
            shape((width, 9 * width), f32),
            shape((width, n * depth), f32),
            shape((width, classes), f32),
            shape((two + three, 128), f32),
            gathered(weights),
            gathered(roots),
        ),
        in_specs=[ANY, ANY, ANY, VMEM, VMEM, VMEM, VMEM, VMEM, VMEM],
        out_specs=(ANY, ANY, ANY, VMEM, ANY, ANY),
        scratch_shapes=[
            pltpu.VMEM((n, SIDE, line + slots, depth), low),
            pltpu.VMEM((SIDE * line, width), f32),
            pltpu.VMEM((SIDE * line, width), f32),
            pltpu.VMEM(grids, low),
            pltpu.VMEM(grids, low),
            pltpu.VMEM((width, SIDE * (line + slots)), low),
            weight(9 * width), weight(n * depth), weight(classes),
            pltpu.VMEM((n,) + norms.shape, f32),
            pack(two + 8), pack(two), pack(three), pack(two),
            held(two + 8), held(two), held(three), held(two),
            pltpu.VMEM((2, 8, width), f32),
            pltpu.VMEM((3, slots, width), f32),
            pltpu.VMEM((slots, width), low),
            pltpu.VMEM((slots, classes), low),
            pltpu.VMEM((slots, width), f32),
            pltpu.VMEM((width, classes), f32),
            pltpu.VMEM((2, width, width), f32),
            DMA((count,)), DMA((count,)), DMA((9,)),
        ],
        compiler_params=pltpu.CompilerParams(collective_id=0, has_side_effects=True, vmem_limit_bytes=60 << 20),
        name="step",
    )(images.reshape(n, SIDE, line, depth), quarters(weights), quarters(roots), norms, valid, labels, used, divisor, bias)
    return spatial, reduce, head, totals[:three], totals[three:], roots_full.reshape(width, roots.shape[1])


def settle_kernel(
    chunks, spatial, reduce, head, mask, full, own, sums, core_in, first_in, first_out, second_in, near_in, across_in,
    final, final_low, send, recv, local,
):
    (z, y, x, core), (nz, ny, nx, nc) = place()
    half = nz // 2
    across_z = lax.rem(z + half, nz)
    base_z = z // half * half
    near_z = [base_z + lax.rem(lax.rem(z, half) + k, half) for k in range(1, half)]
    others_x = turned(x, nx)
    mate, mate_y = at(z, y, x, 1 - core), at(z, 1 - y, x, core)
    mates_x = [at(z, y, k, core) for k in others_x]
    mates_near = [at(k, y, x, core) for k in near_z]
    mate_across = at(across_z, y, x, core)
    greet([mate, mate_y, mate_across] + mates_x + mates_near)
    copies = Copies(send, recv)
    f32 = jnp.float32
    sources = ((spatial, 0), (reduce, spatial.shape[-1]), (head, spatial.shape[-1] + reduce.shape[-1]))
    wide = full.shape[-1]
    used_local = [0]

    def keep(source, target):
        copy = pltpu.make_async_copy(source, target, local.at[used_local[0]])
        used_local[0] += 1
        copy.start()
        return copy

    def wait(going):
        for copy in going:
            copy.wait()

    def chunk(start, size, x_first):
        columns = pl.ds(start, size)
        going = []
        for source, first_column in sources:
            begin, end = max(start, first_column), min(start + size, first_column + source.shape[-1])
            if begin < end:
                taken, landed = pl.ds(begin - first_column, end - begin), pl.ds(begin, end - begin)
                going.append(copies.start(source.at[:, :, :, 1 - core, :, taken], core_in.at[:, :, :, :, landed], mate))
                going.append(keep(source.at[:, :, :, core, :, taken], sums.at[:, :, :, :, landed]))
        yield
        wait(going)
        for i in range(nz):
            for j in range(ny):
                for k in range(nx):
                    sums[i, j, k, :, columns] += core_in[i, j, k, :, columns]
        going = []
        if x_first:
            for t, k in enumerate(others_x):
                for i in range(nz):
                    for j in range(ny):
                        first_out[t, i, j, :, columns] = sums[i, j, k, :, columns].astype(first_out.dtype)
                going.append(copies.start(first_out.at[t, :, :, :, columns], first_in.at[t, :, :, :, columns], mates_x[t]))
        else:
            for i in range(nz):
                for k in range(nx):
                    first_out[k // ny, i, k % ny, :, columns] = sums[i, 1 - y, k, :, columns].astype(first_out.dtype)
            for t in range(nx // ny):
                going.append(copies.start(first_out.at[t, :, :, :, columns], first_in.at[t, :, :, :, columns], mate_y))
        yield
        wait(going)
        going = []
        if x_first:
            for t in range(nx - 1):
                for i in range(nz):
                    for j in range(ny):
                        sums[i, j, x, :, columns] += first_in[t, i, j, :, columns].astype(f32)
            going.append(copies.start(sums.at[:, 1 - y, x, :, columns], second_in.at[0, :, :, columns], mate_y))
        else:
            for i in range(nz):
                for k in range(nx):
                    sums[i, y, k, :, columns] += first_in[k // ny, i, k % ny, :, columns].astype(f32)
            for t, k in enumerate(others_x):
                going.append(copies.start(sums.at[:, y, k, :, columns], second_in.at[t, :, :, columns], mates_x[t]))
        yield
        wait(going)
        for t in range(1 if x_first else nx - 1):
            for i in range(nz):
                sums[i, y, x, :, columns] += second_in[t, i, :, columns]
        going = []
        for t, k in enumerate(near_z):
            for h in range(2):
                there = lax.rem(k + h * half, nz)
                going.append(copies.start(sums.at[there, y, x, :, columns], near_in.at[t, h, :, columns], mates_near[t]))
        yield
        wait(going)
        for t in range(half - 1):
            for h in range(2):
                sums[lax.rem(z + h * half, nz), y, x, :, columns] += near_in[t, h, :, columns]
        going = [copies.start(sums.at[across_z, y, x, :, columns], across_in.at[:, columns], mate_across)]
        yield
        wait(going)
        total = (sums[z, y, x, :, columns] + across_in[:, columns]) * mask[:, columns]
        final[:, columns] = total
        kept = keep(final.at[:, columns], own.at[x, core, :, columns])
        rows_x = [copies.start(final.at[:, columns], own.at[x, core, :, columns], peer) for peer in mates_x]
        low_size = min(start + size, wide) - start
        if low_size > 0:
            low_columns = pl.ds(start, low_size)
            final_low[:, low_columns] = total[:, :low_size].astype(final_low.dtype)
            source = final_low.at[:, low_columns]
            place_at = full.at[z, y, x, core, :, low_columns]
            going = [keep(source, place_at)] + [copies.start(source, place_at, peer) for peer in [mate_across] + mates_near]
        yield
        wait([kept] + rows_x)
        part = own.at[:, core, :, columns]
        rows_core = [copies.start(part, part, mate)]
        if low_size > 0:
            wait(going)
            part = full.at[across_z, y, x, core, :, low_columns]
            going = [copies.start(part, part, peer) for peer in mates_near]
            yield
            wait(going)
            part = full.at[:, y, x, core, :, low_columns]
            going = [copies.start(part, part, peer) for peer in (mates_x if x_first else [mate_y])]
            yield
            wait(going)
            part = full.at[:, y, :, core, :, low_columns] if x_first else full.at[:, :, x, core, :, low_columns]
            going = [copies.start(part, part, peer) for peer in ([mate_y] if x_first else mates_x)]
            yield
            wait(going)
            part = full.at[:, :, :, core, :, low_columns]
            rows_core.append(copies.start(part, part, mate))
        yield
        wait(rows_core)

    waiting, active = [chunk(*c) for c in chunks], []
    while waiting or active:
        for _ in range(2):
            if waiting:
                active.append(waiting.pop(0))
        for going in list(active):
            try:
                next(going)
            except StopIteration:
                active.remove(going)


def settle(spatial, reduce, head, mask, wire, pairs):
    nz, nx = lax.axis_size("chan") // 2, lax.axis_size("batch") // 2
    width = spatial.shape[0]
    rows = width // (4 * nz * nx)
    total = spatial.shape[1] + reduce.shape[1] + head.shape[1]
    wide = spatial.shape[1] + reduce.shape[1]
    split = lambda a: a.reshape(nz, 2, nx, 2, rows, a.shape[1])
    f32, low = jnp.float32, jnp.bfloat16
    cuts = [128 * (total // 128 * i // (2 * pairs)) for i in range(2 * pairs + 1)]
    chunks = [(a, b - a, i % 2 == 0) for i, (a, b) in enumerate(zip(cuts[:-1], cuts[1:]))]
    first = max(nx - 1, nx // 2)
    near = nz // 2 - 1
    count = len(chunks) * (max(nx - 1, nx // 2) + max(nx - 1, 1) + 2 * near + 1 + (nx - 1) + 1 + near + 1 + near + nx + 1)
    count += len(chunks) + 3
    full, own = pl.pallas_call(
        functools.partial(settle_kernel, chunks),
        out_shape=(
            jax.ShapeDtypeStruct((nz, 2, nx, 2, rows, wide), low),
            jax.ShapeDtypeStruct((nx, 2, rows, total), f32),
        ),
        in_specs=[ANY, ANY, ANY, VMEM],
        out_specs=(ANY, ANY),
        scratch_shapes=[
            pltpu.VMEM((nz, 2, nx, rows, total), f32),
            pltpu.VMEM((nz, 2, nx, rows, total), f32),
            pltpu.VMEM((first, nz, 2, rows, total), wire),
            pltpu.VMEM((first, nz, 2, rows, total), wire),
            pltpu.VMEM((max(nx - 1, 1), nz, rows, total), f32),
            pltpu.VMEM((near, 2, rows, total), f32),
            pltpu.VMEM((rows, total), f32),
            pltpu.VMEM((rows, total), f32),
            pltpu.VMEM((rows, wide), low),
            DMA((count,)), DMA((count,)), DMA((3 * len(chunks) + 3,)),
        ],
        compiler_params=pltpu.CompilerParams(collective_id=1, has_side_effects=True, vmem_limit_bytes=58 << 20),
        name="settle",
    )(split(spatial), split(reduce), split(head), mask)
    return full.reshape(width, wide), own.reshape(2 * nx * rows, total)


def silu_slope(pre):
    sigma = jax.nn.sigmoid(pre)
    return sigma * (1.0 + pre * (1.0 - sigma))


def adam_step(param, grad, first, second, rate, decay):
    first = 0.9 * first + 0.1 * grad
    second = 0.999 * second + 0.001 * grad * grad
    mhat = first / (1.0 - 0.9**STEP)
    vhat = second / (1.0 - 0.999**STEP)
    return (param - rate * (mhat / (jnp.sqrt(vhat) + 1e-08) + decay * param), first, second)


def own_part(array, axis, name="chan"):
    size = array.shape[axis] // lax.axis_size(name)
    return lax.dynamic_slice_in_dim(array, lax.axis_index(name) * size, size, axis)


def two_parts(array):
    high = array.astype(jnp.bfloat16)
    return high, (array - high.astype(jnp.float32)).astype(jnp.bfloat16)


def product(spec, left, right):
    return jnp.einsum(spec, left, right, preferred_element_type=jnp.float32)


def conv_grid(grid, taps, spec):
    return lax.conv_general_dilated(
        grid, taps, (1, 1), ((1, 1), (1, 1)), dimension_numbers=spec, preferred_element_type=jnp.float32
    )


def body(
    images,
    pixel_mask,
    labels,
    reduce_weight,
    reduce_mask,
    spatial_weight,
    spatial_mask,
    head_weight,
    head_bias,
    norm_params,
    left_stats,
    right_stats,
    left_root,
    input_side_roots,
    head_first,
    head_second,
    bias_first,
    bias_second,
    norm_first,
    norm_second,
):
    n = lax.axis_size("chan")
    pixels, channels = images.shape[1:]
    side = SIDE
    rows_out, c_in = reduce_weight.shape
    width = left_stats.shape[2]
    classes = head_weight.shape[1]
    padded = 1024
    slots = images.shape[0] // n
    low = jnp.bfloat16
    f32 = jnp.float32
    reduce_float = reduce_mask.astype(f32)
    spatial_float = spatial_mask.astype(f32)

    spread_out = lambda a: jnp.broadcast_to(a[:, None], (a.shape[0], 128))
    by_pixel = images.reshape(n, slots, pixels, channels).transpose(0, 2, 1, 3)
    weights = jnp.concatenate(
        [(spatial_weight * spatial_float).astype(low), (reduce_weight * reduce_float).astype(low),
         jnp.pad(head_weight.astype(low), ((0, 0), (0, padded - classes)))], axis=1)
    roots = input_side_roots.astype(low).transpose(1, 0, 2).reshape(rows_out, -1)
    norms = lax.dynamic_update_slice_in_dim(
        jnp.zeros((8, width), f32), jnp.pad(norm_params, ((0, 4), (0, 0))), lax.axis_index("chan") * rows_out, 1)
    mask_own = own_part(pixel_mask, 0).astype(f32)
    filled = jnp.sum(mask_own, axis=1)
    spatial_local, reduce_local, head_local, sums_two, sums_one, roots_full = local_step(
        by_pixel, weights, roots, norms, spread_out(mask_own.T.reshape(-1)), spread_out(own_part(labels, 0)),
        spread_out((filled > 0.0).astype(f32)), spread_out(jnp.maximum(filled, 1.0)),
        jnp.pad(head_bias, (0, padded - classes), constant_values=-1e30)[None])

    mask_rows = jnp.concatenate([spatial_float, reduce_float, jnp.ones((rows_out, padded), f32)], axis=1)
    full, own = settle(spatial_local, reduce_local, head_local, own_part(mask_rows, 0, "batch"), jnp.float32, 6)
    spatial_grad = own[:, : 9 * width]
    reduce_grad = own[:, 9 * width : 9 * width + c_in]
    head_grad = own[:, 9 * width + c_in : 9 * width + c_in + classes]
    of_norms = jnp.stack([a.reshape(-1) for a in (sums_one[4:], sums_one[:4], sums_two[4:8], sums_two[:4])])
    norm_gain_gradient = own_part(of_norms, 1)
    of_head = sums_two[8:].reshape(-1)
    bias_grad = of_head[:classes]
    loss_sum, slot_count = of_head[-1], of_head[-2]
    right_full = roots_full.reshape(width, -1, width)

    tiles_one = c_in // width
    blocks_of = lambda a: a.reshape(a.shape[0], -1, width).transpose(1, 0, 2)
    in_order = lambda a: jnp.concatenate([a[9:], a[:9]], axis=0)
    blocks = in_order(blocks_of(own[:, : 9 * width + c_in])).astype(low)
    blocks_full = in_order(blocks_of(full))
    left_new = 0.95 * left_stats + product("tak,tbk->tab", blocks, blocks_full)
    right_new = 0.95 * right_stats + product("tki,tkb->tib", own_part(blocks_full, 2), blocks_full)
    left_high, left_rest = two_parts(left_root)
    inner = product("tak,tkb->tab", left_high, blocks_full) + product("tak,tkb->tab", left_rest, blocks_full)
    inner_high, inner_rest = two_parts(inner)
    outer = product("tak,ktb->tab", inner_high, right_full) + product("tak,ktb->tab", inner_rest, right_full)
    squares = jnp.pad(jnp.sum(outer * outer, axis=(1, 2))[:, None] * jnp.ones((1, 128), f32), ((0, 3), (0, 0)))
    squares = chan_sum(squares, 6)[: 9 + tiles_one, 0]
    step = outer / jnp.sqrt(squares / (width * width) + 1e-06)[:, None, None]
    step_one = step[:tiles_one].transpose(1, 0, 2).reshape(rows_out, c_in)
    step_two = step[tiles_one:].transpose(1, 0, 2).reshape(rows_out, 9 * width)
    reduce_new = reduce_weight - 0.02 * reduce_float * (step_one + 0.1 * reduce_weight)
    spatial_new = spatial_weight - 0.02 * spatial_float * (step_two + 0.1 * spatial_weight)
    head_new, head_first_new, head_second_new = adam_step(head_weight, head_grad, head_first, head_second, 0.04, 0.1)
    bias_new, bias_first_new, bias_second_new = adam_step(head_bias, bias_grad, bias_first, bias_second, 0.1, 0.0)
    norm_new, norm_first_new, norm_second_new = adam_step(
        norm_params, norm_gain_gradient, norm_first, norm_second, 0.1, 0.0)
    return (
        loss_sum,
        slot_count,
        reduce_grad,
        spatial_grad,
        reduce_new,
        spatial_new,
        left_new,
        right_new,
        head_new,
        head_first_new,
        head_second_new,
        bias_new,
        bias_first_new,
        bias_second_new,
        norm_new,
        norm_first_new,
        norm_second_new,
    )


FULL_PRECISION = lax.Precision.HIGHEST
BOTH = ("chan", "batch")


def plain_norm_forward(pre_norm, gain, shift, valid):
    first_sum = jnp.sum(pre_norm * valid, axis=(0, 1))
    second_sum = jnp.sum(pre_norm * pre_norm * valid, axis=(0, 1))
    first_sum, second_sum, count = lax.psum((first_sum, second_sum, jnp.sum(valid)), BOTH)
    mean = first_sum / count
    scale = lax.rsqrt(second_sum / count - mean * mean + EPS)
    normed = (pre_norm - mean) * scale
    pre = gain * normed + shift
    return (jax.nn.silu(pre) * valid, (normed, pre, scale, count))


def plain_norm_backward(grad_act, kept, gain, valid):
    normed, pre, scale, count = kept
    d_pre = grad_act * valid * silu_slope(pre)
    shift_gradient, gain_grad = lax.psum(
        (jnp.sum(d_pre, axis=(0, 1)), jnp.sum(d_pre * normed, axis=(0, 1))), BOTH
    )
    d_input = gain * scale / count * (count * d_pre - shift_gradient - normed * gain_grad) * valid
    return (d_input, gain_grad, shift_gradient)


def plain_own_part(array, parts, axis=0):
    size = array.shape[axis] // parts
    return lax.dynamic_slice_in_dim(array, lax.axis_index("chan") * size, size, axis)


def plain_body(
    images,
    pixel_mask,
    labels,
    reduce_weight,
    reduce_mask,
    spatial_weight,
    spatial_mask,
    head_weight,
    head_bias,
    norm_params,
    left_stats,
    right_stats,
    left_root,
    input_side_roots,
    head_first,
    head_second,
    bias_first,
    bias_second,
    norm_first,
    norm_second,
):
    parts = lax.axis_size("chan")
    pixels = images.shape[1]
    side = SIDE
    rows_out = reduce_weight.shape[0]
    width = left_stats.shape[2]
    classes = head_weight.shape[1]
    own_images = lax.all_to_all(images, "chan", 0, 2, tiled=True)
    slots = own_images.shape[0]
    reduce_float = reduce_mask.astype(jnp.float32)
    spatial_float = spatial_mask.astype(jnp.float32)
    gather = lambda a, axis: lax.all_gather(a, "chan", axis=axis, tiled=True)
    reduce_low = gather((reduce_weight * reduce_float).astype(jnp.bfloat16), 0)
    spatial_low = gather((spatial_weight * spatial_float).astype(jnp.bfloat16), 0)
    head_low = gather(head_weight.astype(jnp.bfloat16), 0)
    norm_full = gather(norm_params, 1)
    right_factor_full = gather(input_side_roots, 1)
    valid = plain_own_part(pixel_mask, parts).astype(jnp.float32)[:, :, None]
    own_labels = plain_own_part(labels, parts)
    filled = jnp.sum(valid[:, :, 0], axis=1)
    divisor = jnp.maximum(filled, 1.0)
    used = (filled > 0.0).astype(jnp.float32)
    taps = spatial_low.reshape(width, 3, 3, width)
    first_pre = jnp.einsum("spc,oc->spo", own_images, reduce_low, preferred_element_type=jnp.float32)
    first_act, first_kept = plain_norm_forward(first_pre, norm_full[0], norm_full[1], valid)
    hidden = first_act.astype(jnp.bfloat16).reshape(slots, side, side, width)
    second_pre = conv_grid(hidden, taps, ("NHWC", "OHWI", "NHWC")).reshape(slots, pixels, width)
    second_act, second_kept = plain_norm_forward(second_pre, norm_full[2], norm_full[3], valid)
    pooled = (jnp.sum(second_act, axis=1) / divisor[:, None]).astype(jnp.bfloat16)
    logits = jnp.dot(pooled, head_low, preferred_element_type=jnp.float32) + head_bias
    onehot = (jnp.arange(classes)[None, :] == own_labels[:, None]).astype(jnp.float32)
    log_total = jax.nn.logsumexp(logits, axis=1)
    picked = jnp.sum(onehot * logits, axis=1)
    loss_local = jnp.sum(used * (log_total - picked))
    d_logits = (used[:, None] * (jnp.exp(logits - log_total[:, None]) - onehot) / SLOTS_DEV).astype(
        jnp.bfloat16
    )
    head_grad = jnp.einsum("so,sc->oc", pooled, d_logits, preferred_element_type=jnp.float32)
    bias_grad = jnp.sum(d_logits.astype(jnp.float32), axis=0)
    d_pooled = jnp.einsum("sc,oc->so", d_logits, head_low, preferred_element_type=jnp.float32)
    d_act = jnp.broadcast_to((d_pooled / divisor[:, None])[:, None, :], second_act.shape)
    d_second, gain_two, shift_two = plain_norm_backward(d_act, second_kept, norm_full[2], valid)
    d_second = d_second.astype(jnp.bfloat16).reshape(slots, side, side, width)
    spatial_local = lax.conv_general_dilated(
        hidden, d_second, (1, 1), ((1, 1), (1, 1)), dimension_numbers=("CHWN", "IHWO", "NHWC"),
        preferred_element_type=jnp.float32,
    )
    spatial_local = spatial_local.transpose(3, 1, 2, 0).reshape(width, 9 * width)
    d_hidden = conv_grid(
        d_second, taps[:, ::-1, ::-1, :], ("NHWC", "IHWO", "NHWC")
    ).reshape(slots, pixels, width)
    d_first, gain_one, shift_one = plain_norm_backward(d_hidden, first_kept, norm_full[0], valid)
    d_first = d_first.astype(jnp.bfloat16)
    reduce_local = jnp.einsum("spc,spo->oc", own_images, d_first, preferred_element_type=jnp.float32)
    scatter = lambda a: lax.psum_scatter(a, "chan", scatter_dimension=0, tiled=True)
    reduce_grad, spatial_grad, head_grad = scatter(reduce_local), scatter(spatial_local), scatter(head_grad)
    reduce_grad, spatial_grad, head_grad = lax.psum((reduce_grad, spatial_grad, head_grad), "batch")
    reduce_grad = reduce_grad * reduce_float
    spatial_grad = spatial_grad * spatial_float
    bias_grad, loss_sum, slot_count = lax.psum((bias_grad, loss_local, jnp.sum(used)), BOTH)
    norm_gain_gradient = plain_own_part(jnp.stack([gain_one, shift_one, gain_two, shift_two], axis=0), parts, 1)
    tiles_one = reduce_weight.shape[1] // width
    blocks = jnp.concatenate(
        [
            reduce_grad.reshape(rows_out, tiles_one, width).transpose(1, 0, 2),
            spatial_grad.reshape(rows_out, 9, width).transpose(1, 0, 2),
        ],
        axis=0,
    )
    blocks_full = gather(blocks, 1)
    left_new = 0.95 * left_stats + jnp.einsum(
        "tak,tbk->tab", blocks, blocks_full, precision=FULL_PRECISION
    )
    own_columns = plain_own_part(blocks_full, parts, 2)
    right_new = 0.95 * right_stats + jnp.einsum(
        "tki,tkb->tib", own_columns, blocks_full, precision=FULL_PRECISION
    )
    matrix_product = jnp.einsum("tak,tkb->tab", left_root, blocks_full, precision=FULL_PRECISION)
    matrix_product = jnp.einsum(
        "ghk,gkl->ghl", matrix_product, right_factor_full, precision=FULL_PRECISION
    )
    squares = lax.psum(jnp.sum(matrix_product * matrix_product, axis=(1, 2)), "chan")
    step = matrix_product / jnp.sqrt(squares / (width * width) + 1e-06)[:, None, None]
    step_one = step[:tiles_one].transpose(1, 0, 2).reshape(rows_out, tiles_one * width)
    step_two = step[tiles_one:].transpose(1, 0, 2).reshape(rows_out, 9 * width)
    reduce_new = reduce_weight - 0.02 * reduce_float * (step_one + 0.1 * reduce_weight)
    spatial_new = spatial_weight - 0.02 * spatial_float * (step_two + 0.1 * spatial_weight)
    head_new, head_first_new, head_second_new = adam_step(
        head_weight, head_grad, head_first, head_second, 0.04, 0.1
    )
    bias_new, bias_first_new, bias_second_new = adam_step(
        head_bias, bias_grad, bias_first, bias_second, 0.1, 0.0
    )
    norm_new, norm_first_new, norm_second_new = adam_step(
        norm_params, norm_gain_gradient, norm_first, norm_second, 0.1, 0.0
    )
    return (
        loss_sum,
        slot_count,
        reduce_grad,
        spatial_grad,
        reduce_new,
        spatial_new,
        left_new,
        right_new,
        head_new,
        head_first_new,
        head_second_new,
        bias_new,
        bias_first_new,
        bias_second_new,
        norm_new,
        norm_first_new,
        norm_second_new,
    )


def solution(mesh):
    in_specs = (
        P("batch", None, "chan"),
        P("batch", None),
        P("batch"),
        P("chan", None),
        P("chan", None),
        P("chan", None),
        P("chan", None),
        P("chan", None),
        P(),
        P(None, "chan"),
        P(None, "chan", None),
        P(None, "chan", None),
        P(None, "chan", None),
        P(None, "chan", None),
        P("chan", None),
        P("chan", None),
        P(),
        P(),
        P(None, "chan"),
        P(None, "chan"),
    )
    out_specs = (
        P(),
        P(),
        P("chan", None),
        P("chan", None),
        P("chan", None),
        P("chan", None),
        P(None, "chan", None),
        P(None, "chan", None),
        P("chan", None),
        P("chan", None),
        P("chan", None),
        P(),
        P(),
        P(),
        P(None, "chan"),
        P(None, "chan"),
        P(None, "chan"),
    )
    chan, batch = mesh.shape["chan"], mesh.shape["batch"]
    fits = chan % 4 == 0 and batch % 2 == 0 and WIDTH % (16 * chan * batch) == 0 and SLOTS_DEV % (16 * chan) == 0
    return jax.shard_map(body if fits else plain_body, mesh=mesh, in_specs=in_specs, out_specs=out_specs, check_vma=False)
```

```python
import functools

import jax
import jax.numpy as jnp
from jax import lax
from jax.experimental import pallas as pl
from jax.experimental.pallas import tpu as pltpu
from jax.sharding import PartitionSpec as P

SIDE = 7
SLOTS_DEV = 384
STEP = 10
ORDERS = ("xyz", "xy")

WIDTH = 512
EPS = 1e-05
MESH = pl.DeviceIdType.MESH
ANY = pl.BlockSpec(memory_space=pl.ANY)
VMEM = pl.BlockSpec(memory_space=pltpu.VMEM)
DMA = pltpu.SemaphoreType.DMA
SMALL = 8


def place():
    c, b = lax.axis_index("chan"), lax.axis_index("batch")
    nz, nx = lax.axis_size("chan") // 2, lax.axis_size("batch") // 2
    return (c // 2, lax.rem(c, 2), b // 2, lax.rem(b, 2)), (nz, 2, nx, 2)


def at(z, y, x, core):
    return {"chan": z * 2 + y, "batch": x * 2 + core}


def turned(index, size):
    return [lax.rem(index + k, size) for k in range(1, size)]


def greet(peers):
    barrier = pltpu.get_barrier_semaphore()
    for peer in peers:
        pl.semaphore_signal(barrier, inc=1, device_id=peer, device_id_type=MESH)
    pl.semaphore_wait(barrier, len(peers))


class Copies:
    def __init__(self, send, recv):
        self.send, self.recv, self.used = send, recv, 0

    def start(self, source, target, peer):
        copy = pltpu.make_async_remote_copy(
            source, target, self.send.at[self.used], self.recv.at[self.used],
            device_id=peer, device_id_type=MESH,
        )
        self.used += 1
        copy.start()
        return copy


def dot(left, right, left_dim, right_dim):
    return lax.dot_general(left, right, (((left_dim,), (right_dim,)), ((), ())), preferred_element_type=jnp.float32)


def sigmoid(value):
    return 1.0 / (1.0 + jnp.exp(-value))


def packed(row):
    return jnp.concatenate([row[:, i : i + 128] for i in range(0, row.shape[1], 128)], axis=0)


def unpacked(block):
    return jnp.concatenate([block[i : i + 1] for i in range(block.shape[0])], axis=1)


def step_kernel(
    images, weights, roots, norms, valid, labels, used, divisor, bias,
    spatial_out, reduce_out, head_out, totals_out, weights_out, roots_out,
    own_images, first, second, hidden_pad, grad_pad, turned_grad, taps, reduce_low, head_low,
    norms_held, pack_one, pack_two, pack_three, pack_four, held_one, held_two, held_three, held_four,
    partial, pooling, pooled_low, d_logits, d_act, head_buf, grad_buf, send, recv, local,
):
    (z, y, x, core), (nz, ny, nx, nc) = place()
    c, n = lax.axis_index("chan"), lax.axis_size("chan")
    f32, low = jnp.float32, jnp.bfloat16
    slots = used.shape[0]
    side = SIDE
    line = side * slots
    wide_line = (side + 1) * slots
    pixels = side * side
    rim = (side + 2) * slots
    body_rows = side * wide_line
    width = first.shape[1]
    depth = own_images.shape[-1]
    everyone = [
        at(lax.rem(z + i, nz), lax.rem(y + j, ny), lax.rem(x + k, nx), lax.rem(core + m, nc))
        for i in range(nz) for j in range(ny) for k in range(nx) for m in range(nc) if i + j + k + m
    ]
    greet(everyone)
    copies = Copies(send, recv)
    others = turned(c, n)
    across_z = lax.rem(z + nz // 2, nz)
    near_z = [z // (nz // 2) * (nz // 2) + lax.rem(lax.rem(z, nz // 2) + k, nz // 2) for k in range(1, nz // 2)]
    mate, mate_y = at(z, y, x, 1 - core), at(z, 1 - y, x, core)
    mates_x = [at(z, y, k, core) for k in turned(x, nx)]

    def begin_z(source, target, sem):
        keep = pltpu.make_async_copy(source.at[x, core], target.at[z, y, x, core], local.at[sem])
        keep.start()
        peers = [at(k, y, x, core) for k in [across_z] + near_z]
        return [keep] + [copies.start(source.at[x, core], target.at[z, y, x, core], peer) for peer in peers]

    def pass_z(target, begun):
        for copy in begun:
            copy.wait()
        part = target.at[across_z, y, x, core]
        return [copies.start(part, part, at(k, y, x, core)) for k in near_z]

    weights_z = pass_z(weights_out, begin_z(weights, weights_out, 0))
    norm_copies = [copies.start(norms, norms_held.at[k + 1], {"chan": other}) for k, other in enumerate(others)]
    image_copies = [[copies.start(images.at[k, j], own_images.at[c, j, pl.ds(0, line)], {"chan": k}) for k in others]
                    for j in range(side)]
    own = pltpu.make_async_copy(images.at[c], own_images.at[c, :, pl.ds(0, line)], local.at[2])
    own.start()
    norms_held[0] = norms[...]

    def clear(i, _):
        rows = pl.ds(pl.multiple_of(i * slots, slots), slots)
        hidden_pad[rows, :] = jnp.zeros((slots, width), low)
        grad_pad[rows, :] = jnp.zeros((slots, width), low)
        return 0

    lax.fori_loop(0, hidden_pad.shape[0] // slots, clear, 0)
    for k in range(n):
        for j in range(side):
            own_images[k, j, pl.ds(line, slots), :] = jnp.zeros((slots, depth), low)

    for copy in weights_z:
        copy.wait()
    part = weights_out.at[:, y, x, core]
    copies.start(part, part, mate_y).wait()
    part = weights_out.at[:, :, x, core]
    along_x = [copies.start(part, part, peer) for peer in mates_x]
    for copy in along_x:
        copy.wait()
    part = weights_out.at[:, :, :, core]
    copies.start(part, part, mate).wait()
    fetched = []
    start = 0
    for j, held in enumerate((taps, reduce_low, head_low)):
        size = held.shape[-1]
        copy = pltpu.make_async_copy(weights_out.at[:, :, :, :, :, pl.ds(start, size)], held, local.at[3 + j])
        copy.start()
        fetched.append(copy)
        start += size
    for copy in fetched:
        copy.wait()
    taps, reduce_low, head_low = (held.reshape(width, held.shape[-1]) for held in (taps, reduce_low, head_low))
    for copy in norm_copies:
        copy.wait()
    norm_rows = jnp.sum(norms_held[...], axis=0)
    gain_one, shift_one, gain_two, shift_two = (norm_rows[i : i + 1] for i in range(4))

    def line_rows(j):
        return pl.ds(pl.multiple_of(j * line, slots), line)

    def pixel_rows(p):
        return pl.ds(pl.multiple_of(p * slots, slots), slots)

    def padded_pixel(p):
        j = p // side
        return pl.ds(pl.multiple_of(rim + (p + j) * slots, slots), slots)

    def across(block):
        return jnp.concatenate([block] * (width // 128), axis=1)

    def fold(value):
        return jnp.sum(value.reshape(-1, 8, width), axis=0)

    def total_of(index):
        return jnp.sum(partial[index], axis=0, keepdims=True)

    def exchange(pack, held):
        pack_copies = [copies.start(pack, held.at[k + 1], peer) for k, peer in enumerate(everyone)]
        held[0] = pack[...]
        return pack_copies

    def settled(pack_copies, held):
        for copy in pack_copies:
            copy.wait()
        return jnp.sum(held[...], axis=0)

    def add_to_sums(ref):
        def add(p, _):
            value = ref[pixel_rows(p), :]
            kept = value * across(valid[pixel_rows(p), :])
            partial[0] += fold(kept)
            partial[1] += fold(kept * value)
            return 0

        return add

    own.wait()
    partial[...] = jnp.zeros(partial.shape, f32)
    for j in range(side):
        for copy in image_copies[j]:
            copy.wait()
        block = jnp.concatenate([own_images[k, j, pl.ds(0, line), :] for k in range(n)], axis=1)
        first[pl.ds(j * line, line), :] = dot(block, reduce_low[...], 1, 1)
        lax.fori_loop(j * side, (j + 1) * side, add_to_sums(first), 0)
    all_valid = jnp.sum(valid[...], axis=0, keepdims=True)
    pack_one[...] = jnp.concatenate(
        [packed(total_of(0)), packed(total_of(1)), all_valid, jnp.zeros((7, 128), f32)], axis=0)
    stats = settled(exchange(pack_one, held_one), held_one)
    rows = width // 128
    count = jnp.concatenate([stats[2 * rows : 2 * rows + 1]] * rows, axis=1)

    def norm_of(stats):
        mean = unpacked(stats[:rows]) / count
        scale = lax.rsqrt(unpacked(stats[rows : 2 * rows]) / count - mean * mean + EPS)
        return mean, scale

    mean_one, scale_one = norm_of(stats)
    roots_z = begin_z(roots, roots_out, 1)

    def activate(p, _):
        normed = (first[pixel_rows(p), :] - mean_one) * scale_one
        pre = gain_one * normed + shift_one
        act = pre * sigmoid(pre) * across(valid[pixel_rows(p), :])
        hidden_pad[padded_pixel(p), :] = act.astype(low)
        return 0

    lax.fori_loop(0, pixels, activate, 0)

    def conv_line(j, _):
        value = None
        for t in range(9):
            offset = (t // 3 - 1) * wide_line + (t % 3 - 1) * slots
            rows_in = pl.ds(pl.multiple_of(rim + j * wide_line + offset, slots), line)
            term = dot(hidden_pad[rows_in, :], taps[:, t * width : (t + 1) * width], 1, 1)
            value = term if value is None else value + term
        second[line_rows(j), :] = value
        return 0

    lax.fori_loop(0, side, conv_line, 0)
    roots_z = pass_z(roots_out, roots_z)
    partial[...] = jnp.zeros(partial.shape, f32)
    lax.fori_loop(0, pixels, add_to_sums(second), 0)
    pack_two[...] = jnp.concatenate([packed(total_of(0)), packed(total_of(1))], axis=0)
    stats = settled(exchange(pack_two, held_two), held_two)
    mean_two, scale_two = norm_of(stats)
    for copy in roots_z:
        copy.wait()
    across_half = roots_out.shape[-1] // 2
    left, right = pl.ds(0, across_half), pl.ds(across_half, across_half)
    part = roots_out.at[:, y, x, core, :, left]
    roots_a = [copies.start(part, part, peer) for peer in mates_x]
    part = roots_out.at[:, y, x, core, :, right]
    roots_b = [copies.start(part, part, mate_y)]

    pooling[...] = jnp.zeros(pooling.shape, f32)

    def pool(p, _):
        normed = (second[pixel_rows(p), :] - mean_two) * scale_two
        pre = gain_two * normed + shift_two
        sigma = sigmoid(pre)
        kept = across(valid[pixel_rows(p), :])
        slope = sigma * (1.0 + pre * (1.0 - sigma)) * kept
        pooling[0] += pre * sigma * kept
        pooling[1] += slope
        pooling[2] += slope * normed
        return 0

    lax.fori_loop(0, pixels, pool, 0)
    divide = across(divisor[...])
    pooled_low[...] = (pooling[0] / divide).astype(low)
    logits = dot(pooled_low[...], head_low[...], 1, 0) + bias[...]
    classes = logits.shape[1]
    index = lax.broadcasted_iota(jnp.int32, (slots, classes), 1)
    onehot = (index == labels[:, :1]).astype(f32)
    top = jnp.max(logits, axis=1, keepdims=True)
    log_total = jnp.log(jnp.sum(jnp.exp(logits - top), axis=1, keepdims=True)) + top
    picked = jnp.sum(onehot * logits, axis=1, keepdims=True)
    use = used[:, :1]
    loss = jnp.sum(use * (log_total - picked))
    d_logits[...] = (use * (jnp.exp(logits - log_total) - onehot) / SLOTS_DEV).astype(low)
    bias_sum = jnp.sum(d_logits[...].astype(f32), axis=0, keepdims=True)
    half = width // 2

    def to_pooled(m, _):
        rows_in = pl.ds(pl.multiple_of(m * half, half), half)
        d_act[:, rows_in] = dot(d_logits[...], head_low[rows_in, :], 1, 1) / across(divisor[...])[:, :half]
        return 0

    lax.fori_loop(0, 2, to_pooled, 0)
    at_class = lax.broadcasted_iota(jnp.int32, (1, classes), 1)
    bias_sum = jnp.where(at_class == classes - 1, loss, jnp.where(at_class == classes - 2, jnp.sum(use), bias_sum))
    pack_three[...] = jnp.concatenate(
        [packed(jnp.sum(d_act[...] * pooling[1], axis=0, keepdims=True)),
         packed(jnp.sum(d_act[...] * pooling[2], axis=0, keepdims=True)), packed(bias_sum)], axis=0)
    going = exchange(pack_three, held_three)

    def to_head(m, _):
        columns = pl.ds(pl.multiple_of(m * (classes // 2), 128), classes // 2)
        head_buf[:, columns] = dot(pooled_low[...], d_logits[:, columns], 0, 0)
        return 0

    lax.fori_loop(0, 2, to_head, 0)
    head_copy = pltpu.make_async_copy(head_buf, head_out, local.at[6])
    head_copy.start()
    totals_two = settled(going, held_three)
    shift_grad, gain_grad = unpacked(totals_two[:rows]), unpacked(totals_two[rows : 2 * rows])
    factor = gain_two * scale_two / count
    for copy in roots_a:
        copy.wait()
    part = roots_out.at[:, y, :, core, :, left]
    roots_a = [copies.start(part, part, mate_y)]
    for copy in roots_b:
        copy.wait()
    part = roots_out.at[:, :, x, core, :, right]
    roots_b = [copies.start(part, part, peer) for peer in mates_x]

    def leave_second(p, _):
        normed = (second[pixel_rows(p), :] - mean_two) * scale_two
        pre = gain_two * normed + shift_two
        sigma = sigmoid(pre)
        kept = across(valid[pixel_rows(p), :])
        d_pre = d_act[...] * kept * (sigma * (1.0 + pre * (1.0 - sigma)))
        d_z = factor * (count * d_pre - shift_grad - normed * gain_grad) * kept
        grad_pad[padded_pixel(p), :] = d_z.astype(low)
        return 0

    lax.fori_loop(0, pixels, leave_second, 0)

    partial[...] = jnp.zeros(partial.shape, f32)

    def spread_line(j, _):
        value = None
        for t in range(9):
            offset = (t // 3 - 1) * wide_line + (t % 3 - 1) * slots
            rows_in = pl.ds(pl.multiple_of(rim + j * wide_line - offset, slots), line)
            term = dot(grad_pad[rows_in, :], taps[:, t * width : (t + 1) * width], 1, 0)
            value = term if value is None else value + term
        second[line_rows(j), :] = value
        return 0

    lax.fori_loop(0, side, spread_line, 0)
    for copy in roots_a + roots_b:
        copy.wait()
    part = roots_out.at[:, :, :, core]
    roots_core = copies.start(part, part, mate)

    def enter_first(p, _):
        normed = (first[pixel_rows(p), :] - mean_one) * scale_one
        pre = gain_one * normed + shift_one
        sigma = sigmoid(pre)
        d_pre = second[pixel_rows(p), :] * across(valid[pixel_rows(p), :]) * (sigma * (1.0 + pre * (1.0 - sigma)))
        second[pixel_rows(p), :] = d_pre
        partial[0] += fold(d_pre)
        partial[1] += fold(d_pre * normed)
        return 0

    lax.fori_loop(0, pixels, enter_first, 0)
    pack_four[...] = jnp.concatenate([packed(total_of(0)), packed(total_of(1))], axis=0)
    going = exchange(pack_four, held_four)

    def turn(j, _):
        rows_in = pl.ds(pl.multiple_of(rim + j * wide_line, slots), wide_line)
        turned_grad[:, pl.ds(pl.multiple_of(j * wide_line, 128), wide_line)] = grad_pad[rows_in, :].T
        return 0

    lax.fori_loop(0, side, turn, 0)

    def leave(slot, target, sem):
        copy = pltpu.make_async_copy(grad_buf.at[slot], target, local.at[sem])
        copy.start()
        return copy

    leaving = []
    for t in range(9):
        offset = (t // 3 - 1) * wide_line + (t % 3 - 1) * slots
        slot = t % 2
        if t >= 2:
            leaving[t - 2].wait()
        shifted = hidden_pad.at[pl.ds(rim + offset, body_rows)]

        grad_buf[slot] = dot(turned_grad[...], shifted[...], 1, 0)
        leaving.append(leave(slot, spatial_out.at[:, pl.ds(t * width, width)], 7 + slot))

    totals_one = settled(going, held_four)
    shift_sum, gain_sum = unpacked(totals_one[:rows]), unpacked(totals_one[rows : 2 * rows])
    factor_one = gain_one * scale_one / count

    def leave_first(p, _):
        normed = (first[pixel_rows(p), :] - mean_one) * scale_one
        kept = across(valid[pixel_rows(p), :])
        d_z = factor_one * (count * second[pixel_rows(p), :] - shift_sum - normed * gain_sum) * kept
        grad_pad[padded_pixel(p), :] = d_z.astype(low)
        return 0

    lax.fori_loop(0, pixels, leave_first, 0)
    lax.fori_loop(0, side, turn, 0)
    per = width // depth
    for t in range(n // per):
        slot = (9 + t) % 2
        leaving[9 + t - 2].wait()

        def source_rows(m, _, slot=slot, t=t):
            rows_out = pl.ds(pl.multiple_of(m * 256, 256), 256)
            for k in range(per):
                block = own_images[t * per + k].reshape(body_rows, depth)
                grad_buf[slot, rows_out, k * depth : (k + 1) * depth] = dot(turned_grad[rows_out, :], block, 1, 0)
            return 0

        lax.fori_loop(0, width // 256, source_rows, 0)
        leaving.append(leave(slot, reduce_out.at[:, pl.ds(t * width, width)], 7 + slot))
    totals_out[...] = jnp.concatenate([totals_two, totals_one], axis=0)
    head_copy.wait()
    roots_core.wait()
    for copy in leaving[-2:]:
        copy.wait()


def local_step(images, weights, roots, norms, valid, labels, used, divisor, bias):
    n, nb = lax.axis_size("chan"), lax.axis_size("batch")
    nz, nx = n // 2, nb // 2
    slots, width = used.shape[0], norms.shape[1]
    line, depth, classes = SIDE * slots, images.shape[-1], bias.shape[1]
    f32, low = jnp.float32, jnp.bfloat16
    rows = weights.shape[0] // nb
    grids = ((SIDE * (SIDE + 1) + 2 * (SIDE + 2)) * slots, width)
    shape = jax.ShapeDtypeStruct
    gathered = lambda a: shape((nz, 2, nx, 2, rows, a.shape[1]), a.dtype)
    quarters = lambda a: a.reshape(nx, 2, rows, a.shape[1])
    held = lambda k: pltpu.VMEM((n * nb, k, 128), f32)
    pack = lambda k: pltpu.VMEM((k, 128), f32)
    count = 2 * (nz - 1) + (SIDE + 1) * (n - 1) + (1 + (nx - 1) + 1) + (2 * nx + 1) + 4 * (n * nb - 1)
    two = 2 * width // 128
    three = two + classes // 128
    weight = lambda size: pltpu.VMEM((nz, 2, nx, 2, rows, size), low)
    spatial, reduce, head, totals, weights_full, roots_full = pl.pallas_call(
        step_kernel,
        out_shape=(
            shape((width, 9 * width), f32),
            shape((width, n * depth), f32),
            shape((width, classes), f32),
            shape((two + three, 128), f32),
            gathered(weights),
            gathered(roots),
        ),
        in_specs=[ANY, ANY, ANY, VMEM, VMEM, VMEM, VMEM, VMEM, VMEM],
        out_specs=(ANY, ANY, ANY, VMEM, ANY, ANY),
        scratch_shapes=[
            pltpu.VMEM((n, SIDE, line + slots, depth), low),
            pltpu.VMEM((SIDE * line, width), f32),
            pltpu.VMEM((SIDE * line, width), f32),
            pltpu.VMEM(grids, low),
            pltpu.VMEM(grids, low),
            pltpu.VMEM((width, SIDE * (line + slots)), low),
            weight(9 * width), weight(n * depth), weight(classes),
            pltpu.VMEM((n,) + norms.shape, f32),
            pack(two + 8), pack(two), pack(three), pack(two),
            held(two + 8), held(two), held(three), held(two),
            pltpu.VMEM((2, 8, width), f32),
            pltpu.VMEM((3, slots, width), f32),
            pltpu.VMEM((slots, width), low),
            pltpu.VMEM((slots, classes), low),
            pltpu.VMEM((slots, width), f32),
            pltpu.VMEM((width, classes), f32),
            pltpu.VMEM((2, width, width), f32),
            DMA((count,)), DMA((count,)), DMA((9,)),
        ],
        compiler_params=pltpu.CompilerParams(collective_id=0, has_side_effects=True, vmem_limit_bytes=60 << 20),
        name="step",
    )(images.reshape(n, SIDE, line, depth), quarters(weights), quarters(roots), norms, valid, labels, used, divisor, bias)
    return spatial, reduce, head, totals[:three], totals[three:], roots_full.reshape(width, roots.shape[1])


def settle_kernel(
    chunks, spatial, reduce, head, mask, left_root, roots, own, left_part, right_part, outer_out, size,
    full, factors, lefts, rights, outers, squares, held, sums, core_in, first_in, second_in, near_in, across_in,
    final, final_low, send, recv, local,
):
    (z, y, x, core), (nz, ny, nx, nc) = place()
    half = nz // 2
    across_z = lax.rem(z + half, nz)
    base_z = z // half * half
    near_z = [base_z + lax.rem(lax.rem(z, half) + k, half) for k in range(1, half)]
    others_x = turned(x, nx)
    mate, mate_y = at(z, y, x, 1 - core), at(z, 1 - y, x, core)
    mates_x = [at(z, y, k, core) for k in others_x]
    mates_near = [at(k, y, x, core) for k in near_z]
    mate_across = at(across_z, y, x, core)
    c, n = lax.axis_index("chan"), lax.axis_size("chan")
    others = [{"chan": k} for k in turned(c, n)]
    greet(others + mates_x + [mate])
    copies = Copies(send, recv)
    f32, low = jnp.float32, jnp.bfloat16
    rows, width = left_root.shape[1:]
    tiles_one = reduce.shape[-1] // width
    sources = ((spatial, 0), (reduce, spatial.shape[-1]), (head, spatial.shape[-1] + reduce.shape[-1]))
    wide = full.shape[-1]
    used_local = [0]

    def keep(source, target):
        copy = pltpu.make_async_copy(source, target, local.at[used_local[0]])
        used_local[0] += 1
        copy.start()
        return copy

    roots_in = [keep(roots, factors)]
    pick = (lax.broadcasted_iota(jnp.int32, (rows, width), 1)
            == lax.broadcasted_iota(jnp.int32, (rows, width), 0) + c * rows).astype(low)
    squares[...] = jnp.zeros(squares.shape, f32)
    outgoing = []

    def two_parts(value):
        high = value.astype(low)
        return [high, (value - high.astype(f32)).astype(low)]

    def multiply(t, columns):
        grad = full[:, :, :, :, :, columns].reshape(width, width)
        mine = full[z, y, :, :, :, columns].reshape(rows, width)
        first = dot(jnp.concatenate([mine, pick], axis=0), grad, 1, 1)
        lefts[t] = first[:rows]
        second = dot(jnp.concatenate([first[rows:].astype(low)] + two_parts(left_root[t]), axis=0), grad, 1, 0)
        rights[t] = second[:rows]
        inner = second[rows : 2 * rows] + second[2 * rows :]
        third = dot(jnp.concatenate(two_parts(inner), axis=0), factors[:, t * width : (t + 1) * width], 1, 0)
        value = third[:rows] + third[rows:]
        outers[t] = value
        squares[t : t + 1, :] = jnp.full((1, 128), jnp.sum(value * value), f32)
        outgoing.extend(keep(a.at[t], b.at[t]) for a, b in ((lefts, left_part), (rights, right_part), (outers, outer_out)))

    def wait(going):
        for copy in going:
            copy.wait()

    def enter(start, size):
        columns = pl.ds(start, size)
        going = []
        for source, first_column in sources:
            begin, end = max(start, first_column), min(start + size, first_column + source.shape[-1])
            if begin < end:
                taken, landed = pl.ds(begin - first_column, end - begin), pl.ds(begin, end - begin)
                going.append(copies.start(source.at[:, :, :, 1 - core, :, taken], core_in.at[:, :, :, :, landed], mate))
                going.append(keep(source.at[:, :, :, core, :, taken], sums.at[:, :, :, :, landed]))
        yield
        wait(going)
        for i in range(nz):
            for j in range(ny):
                for k in range(nx):
                    sums[i, j, k, :, columns] += core_in[i, j, k, :, columns]

    def settled(start, last_in, columns):
        total = (sums[z, y, x, :, columns] + last_in) * mask[:, columns]
        final[:, columns] = total
        kept = [keep(final.at[:, columns], own.at[x, core, :, columns])]
        kept += [copies.start(final.at[:, columns], own.at[x, core, :, columns], peer) for peer in mates_x]
        if start < wide:
            final_low[:, columns] = total.astype(low)
            return kept, [keep(final_low.at[:, columns], full.at[z, y, x, core, :, columns])]
        return kept, []

    def own_core(kept, columns):
        wait(kept)
        part = own.at[:, core, :, columns]
        return copies.start(part, part, mate)

    def block_of(start, columns):
        t = start // width
        if roots_in:
            roots_in.pop().wait()
        taps = spatial.shape[-1] // width
        multiply(t + tiles_one if t < taps else t - taps, columns)

    def chunk_z(start, size):
        columns = pl.ds(start, size)
        yield from enter(start, size)
        going = []
        for t, k in enumerate(near_z):
            for h in range(2):
                there = lax.rem(k + h * half, nz)
                going.append(copies.start(
                    sums.at[there, :, :, :, columns], first_in.at[t, pl.ds(2 * h, 2), :, :, columns], mates_near[t]))
        yield
        wait(going)
        for t in range(half - 1):
            for h in range(2):
                for j in range(ny):
                    for k in range(nx):
                        sums[lax.rem(z + h * half, nz), j, k, :, columns] += first_in[t, 2 * h + j, k, :, columns]
        landing = [second_in.at[0, pl.ds(nx * j, nx), :, columns] for j in range(ny)]
        going = [copies.start(sums.at[across_z, j, :, :, columns], landing[j], mate_across) for j in range(ny)]
        yield
        wait(going)
        for j in range(ny):
            for k in range(nx):
                sums[z, j, k, :, columns] += second_in[0, nx * j + k, :, columns]
        going = [copies.start(sums.at[z, :, k, :, columns], near_in.at[t, :, :, columns], mates_x[t])
                 for t, k in enumerate(others_x)]
        yield
        wait(going)
        for t in range(nx - 1):
            for j in range(ny):
                sums[z, j, x, :, columns] += near_in[t, j, :, columns]
        going = [copies.start(sums.at[z, 1 - y, x, :, columns], across_in.at[:, columns], mate_y)]
        yield
        wait(going)
        kept, going = settled(start, across_in[:, columns], columns)
        going += [copies.start(final_low.at[:, columns], full.at[z, y, x, core, :, columns], peer) for peer in mates_x]
        yield
        last = [own_core(kept, columns)]
        wait(going)
        part = full.at[z, y, :, core, :, columns]
        going = [copies.start(part, part, mate_y)]
        yield
        wait(going)
        part = full.at[z, :, :, core, :, columns]
        going = [copies.start(part, part, peer) for peer in [mate_across] + mates_near]
        yield
        wait(going)
        part = full.at[across_z, :, :, core, :, columns]
        going = [copies.start(part, part, peer) for peer in mates_near]
        yield
        wait(going)
        part = full.at[:, :, :, core, :, columns]
        last.append(copies.start(part, part, mate))
        yield
        wait(last)
        block_of(start, columns)

    def chunk(start, size, x_first):
        columns = pl.ds(start, size)
        yield from enter(start, size)
        if x_first:
            going = [copies.start(sums.at[:, :, k, :, columns], first_in.at[t, :, :, :, columns], mates_x[t])
                     for t, k in enumerate(others_x)]
        else:
            going = [copies.start(sums.at[:, 1 - y, pl.ds(ny * t, ny), :, columns], first_in.at[t, :, :, :, columns], mate_y)
                     for t in range(nx // ny)]
        yield
        wait(going)
        going = []
        if x_first:
            for t in range(nx - 1):
                for i in range(nz):
                    for j in range(ny):
                        sums[i, j, x, :, columns] += first_in[t, i, j, :, columns]
            going.append(copies.start(sums.at[:, 1 - y, x, :, columns], second_in.at[0, :, :, columns], mate_y))
        else:
            for i in range(nz):
                for k in range(nx):
                    sums[i, y, k, :, columns] += first_in[k // ny, i, k % ny, :, columns]
            for t, k in enumerate(others_x):
                going.append(copies.start(sums.at[:, y, k, :, columns], second_in.at[t, :, :, columns], mates_x[t]))
        yield
        wait(going)
        for t in range(1 if x_first else nx - 1):
            for i in range(nz):
                sums[i, y, x, :, columns] += second_in[t, i, :, columns]
        going = []
        for t, k in enumerate(near_z):
            for h in range(2):
                there = lax.rem(k + h * half, nz)
                going.append(copies.start(sums.at[there, y, x, :, columns], near_in.at[t, h, :, columns], mates_near[t]))
        yield
        wait(going)
        for t in range(half - 1):
            for h in range(2):
                sums[lax.rem(z + h * half, nz), y, x, :, columns] += near_in[t, h, :, columns]
        going = [copies.start(sums.at[across_z, y, x, :, columns], across_in.at[:, columns], mate_across)]
        yield
        wait(going)
        kept, going = settled(start, across_in[:, columns], columns)
        if start < wide:
            going += [copies.start(final_low.at[:, columns], full.at[z, y, x, core, :, columns], peer)
                      for peer in [mate_across] + mates_near]
        yield
        rows_core = [own_core(kept, columns)]
        if start < wide:
            wait(going)
            part = full.at[across_z, y, x, core, :, columns]
            going = [copies.start(part, part, peer) for peer in mates_near]
            yield
            wait(going)
            part = full.at[:, y, x, core, :, columns]
            going = [copies.start(part, part, peer) for peer in (mates_x if x_first else [mate_y])]
            yield
            wait(going)
            part = full.at[:, y, :, core, :, columns] if x_first else full.at[:, :, x, core, :, columns]
            going = [copies.start(part, part, peer) for peer in ([mate_y] if x_first else mates_x)]
            yield
            wait(going)
            part = full.at[:, :, :, core, :, columns]
            rows_core.append(copies.start(part, part, mate))
        yield
        wait(rows_core)
        if start < wide:
            block_of(start, columns)

    rounds = [[chunk_z(*c[:2]) if c[2] == "z" and c[0] < wide else chunk(*c[:2], c[2] != "y") for c in some] for some in chunks]
    begun, active = [], []
    while rounds or begun or active:
        active += begun
        begun = rounds.pop(0) if rounds else []
        for going in begun:
            next(going)
        for going in active[::-1]:
            try:
                next(going)
            except StopIteration:
                active.remove(going)
    going = [copies.start(squares, held.at[k + 1], peer) for k, peer in enumerate(others)]
    held[0] = squares[...]
    wait(going + outgoing)
    size[...] = jnp.sqrt(jnp.sum(held[...], axis=0) / (width * width) + 1e-06)


def settle(spatial, reduce, head, mask, left_root, roots):
    nz, nx, n = lax.axis_size("chan") // 2, lax.axis_size("batch") // 2, lax.axis_size("chan")
    blocks, own_rows, width = left_root.shape
    rows = width // (4 * nz * nx)
    total = spatial.shape[1] + reduce.shape[1] + head.shape[1]
    wide = spatial.shape[1] + reduce.shape[1]
    split = lambda a: a.reshape(nz, 2, nx, 2, rows, a.shape[1])
    f32, low = jnp.float32, jnp.bfloat16
    kinds = ORDERS if nx == 2 and nz == 4 else ("xy",)
    chunks, start = [], 0
    while start < total:
        some = [(start + i * width, width, kind) for i, kind in enumerate(kinds[len(chunks) % len(kinds)])]
        chunks.append([c for c in some if c[0] < total])
        start += len(some) * width
    near = nz // 2 - 1
    first = max(nx - 1, nx // 2)
    count = (total // width) * (4 + first + max(nx - 1, 1) + 2 * near + 1 + (nx - 1) + 1 + near + 1 + near + nx + 1) + n
    product = jax.ShapeDtypeStruct((blocks, own_rows, width), f32)
    padded = (blocks + 7) // 8 * 8
    own, left_part, right_part, outer, size = pl.pallas_call(
        functools.partial(settle_kernel, chunks),
        out_shape=(
            jax.ShapeDtypeStruct((nx, 2, rows, total), f32), product, product, product,
            jax.ShapeDtypeStruct((padded, 128), f32),
        ),
        in_specs=[ANY, ANY, ANY, VMEM, VMEM, ANY],
        out_specs=(ANY,) * 4 + (VMEM,),
        scratch_shapes=[
            pltpu.VMEM((nz, 2, nx, 2, rows, wide), low),
            pltpu.VMEM(roots.shape, low),
            pltpu.VMEM(product.shape, f32),
            pltpu.VMEM(product.shape, f32),
            pltpu.VMEM(product.shape, f32),
            pltpu.VMEM((padded, 128), f32),
            pltpu.VMEM((n, padded, 128), f32),
            pltpu.VMEM((nz, 2, nx, rows, total), f32),
            pltpu.VMEM((nz, 2, nx, rows, total), f32),
            pltpu.VMEM((first, nz, 2, rows, total), f32),
            pltpu.VMEM((max(nx - 1, 1), nz, rows, total), f32),
            pltpu.VMEM((near, 2, rows, total), f32),
            pltpu.VMEM((rows, total), f32),
            pltpu.VMEM((rows, total), f32),
            pltpu.VMEM((rows, wide), low),
            DMA((count,)), DMA((count,)), DMA((7 * (total // width) + 4,)),
        ],
        compiler_params=pltpu.CompilerParams(collective_id=1, has_side_effects=True, vmem_limit_bytes=60 << 20),
        name="settle",
    )(split(spatial), split(reduce), split(head), mask, left_root, roots)
    return own.reshape(own_rows, total), left_part, right_part, outer, size


def finish_kernel(
    tiles_one, own, head_a, head_b, left_part, right_part, outer, size, left_stats, right_stats,
    reduce_weight, spatial_weight, reduce_mask, spatial_mask, head_weight, head_first, head_second,
    reduce_grad, spatial_grad, reduce_new, spatial_new, left_new, right_new, head_new, head_first_new, head_second_new,
):
    t = pl.program_id(0)
    left_new[0] = 0.95 * left_stats[0] + left_part[0]
    right_new[0] = 0.95 * right_stats[0] + right_part[0]
    step = outer[0] / jnp.concatenate([size[pl.ds(t, 1), :]] * (outer.shape[-1] // 128), axis=1)

    def leave(weight, mask, grad, new):
        grad[...] = own[...]
        new[...] = weight[...] - 0.02 * mask[...].astype(jnp.float32) * (step + 0.1 * weight[...])

    @pl.when(t < tiles_one)
    def _():
        leave(reduce_weight, reduce_mask, reduce_grad, reduce_new)

    @pl.when(t >= tiles_one)
    def _():
        leave(spatial_weight, spatial_mask, spatial_grad, spatial_new)

    @pl.when(t == 0)
    def _():
        head_grad = jnp.concatenate([head_a[...], head_b[...]], axis=1)[:, : head_weight.shape[1]]
        head_new[...], head_first_new[...], head_second_new[...] = adam_step(
            head_weight[...], head_grad, head_first[...], head_second[...], 0.04, 0.1)


def finish(own, left_part, right_part, outer, size, left_stats, right_stats,
           reduce_weight, spatial_weight, reduce_mask, spatial_mask, head_weight, head_first, head_second):
    blocks, rows, width = left_stats.shape
    tiles_one, taps = reduce_weight.shape[1] // width, spatial_weight.shape[1] // width
    columns = lambda index: pl.BlockSpec((rows, width), lambda t: (0, index(t)))
    of_block = pl.BlockSpec((1, rows, width), lambda t: (t, 0, 0))
    whole = lambda a: pl.BlockSpec(a.shape, lambda t: (0, 0))
    of_reduce = columns(lambda t: jnp.minimum(t, tiles_one - 1))
    of_spatial = columns(lambda t: jnp.maximum(t - tiles_one, 0))
    like = lambda a: jax.ShapeDtypeStruct(a.shape, jnp.float32)
    return pl.pallas_call(
        functools.partial(finish_kernel, tiles_one),
        grid=(blocks,),
        out_shape=(like(reduce_weight), like(spatial_weight), like(reduce_weight), like(spatial_weight),
                   like(left_stats), like(left_stats), like(head_weight), like(head_weight), like(head_weight)),
        in_specs=[
            columns(lambda t: jnp.where(t < tiles_one, taps + t, t - tiles_one)),
            columns(lambda t: taps + tiles_one), columns(lambda t: taps + tiles_one + 1),
            of_block, of_block, of_block, whole(size), of_block, of_block,
            of_reduce, of_spatial, of_reduce, of_spatial, whole(head_weight), whole(head_weight), whole(head_weight),
        ],
        out_specs=(of_reduce, of_spatial, of_reduce, of_spatial, of_block, of_block,
                   whole(head_weight), whole(head_weight), whole(head_weight)),
        compiler_params=pltpu.CompilerParams(vmem_limit_bytes=60 << 20),
        name="finish",
    )(own, own, own, left_part, right_part, outer, size, left_stats, right_stats,
      reduce_weight, spatial_weight, reduce_mask, spatial_mask, head_weight, head_first, head_second)


def silu_slope(pre):
    sigma = jax.nn.sigmoid(pre)
    return sigma * (1.0 + pre * (1.0 - sigma))


def adam_step(param, grad, first, second, rate, decay):
    first = 0.9 * first + 0.1 * grad
    second = 0.999 * second + 0.001 * grad * grad
    mhat = first / (1.0 - 0.9**STEP)
    vhat = second / (1.0 - 0.999**STEP)
    return (param - rate * (mhat / (jnp.sqrt(vhat) + 1e-08) + decay * param), first, second)


def own_part(array, axis, name="chan"):
    size = array.shape[axis] // lax.axis_size(name)
    return lax.dynamic_slice_in_dim(array, lax.axis_index(name) * size, size, axis)


def body(
    images,
    pixel_mask,
    labels,
    reduce_weight,
    reduce_mask,
    spatial_weight,
    spatial_mask,
    head_weight,
    head_bias,
    norm_params,
    left_stats,
    right_stats,
    left_root,
    input_side_roots,
    head_first,
    head_second,
    bias_first,
    bias_second,
    norm_first,
    norm_second,
):
    n = lax.axis_size("chan")
    pixels, channels = images.shape[1:]
    side = SIDE
    rows_out, c_in = reduce_weight.shape
    width = left_stats.shape[2]
    classes = head_weight.shape[1]
    padded = 1024
    slots = images.shape[0] // n
    low = jnp.bfloat16
    f32 = jnp.float32
    reduce_float = reduce_mask.astype(f32)
    spatial_float = spatial_mask.astype(f32)

    spread_out = lambda a: jnp.broadcast_to(a[:, None], (a.shape[0], 128))
    by_pixel = images.reshape(n, slots, pixels, channels).transpose(0, 2, 1, 3)
    weights = jnp.concatenate(
        [(spatial_weight * spatial_float).astype(low), (reduce_weight * reduce_float).astype(low),
         jnp.pad(head_weight.astype(low), ((0, 0), (0, padded - classes)))], axis=1)
    roots = input_side_roots.astype(low).transpose(1, 0, 2).reshape(rows_out, -1)
    norms = lax.dynamic_update_slice_in_dim(
        jnp.zeros((8, width), f32), jnp.pad(norm_params, ((0, 4), (0, 0))), lax.axis_index("chan") * rows_out, 1)
    mask_own = own_part(pixel_mask, 0).astype(f32)
    filled = jnp.sum(mask_own, axis=1)
    spatial_local, reduce_local, head_local, sums_two, sums_one, roots_full = local_step(
        by_pixel, weights, roots, norms, spread_out(mask_own.T.reshape(-1)), spread_out(own_part(labels, 0)),
        spread_out((filled > 0.0).astype(f32)), spread_out(jnp.maximum(filled, 1.0)),
        jnp.pad(head_bias, (0, padded - classes), constant_values=-1e30)[None])

    mask_rows = jnp.concatenate([spatial_float, reduce_float, jnp.ones((rows_out, padded), f32)], axis=1)
    own, *products = settle(spatial_local, reduce_local, head_local, own_part(mask_rows, 0, "batch"), left_root, roots_full)
    of_norms = jnp.stack([a.reshape(-1) for a in (sums_one[4:], sums_one[:4], sums_two[4:8], sums_two[:4])])
    norm_gain_gradient = own_part(of_norms, 1)
    of_head = sums_two[8:].reshape(-1)
    bias_grad = of_head[:classes]
    loss_sum, slot_count = of_head[-1], of_head[-2]
    (reduce_grad, spatial_grad, reduce_new, spatial_new, left_new, right_new, head_new, head_first_new,
     head_second_new) = finish(
        own, *products, left_stats, right_stats, reduce_weight, spatial_weight, reduce_mask, spatial_mask,
        head_weight, head_first, head_second)
    bias_new, bias_first_new, bias_second_new = adam_step(head_bias, bias_grad, bias_first, bias_second, 0.1, 0.0)
    norm_new, norm_first_new, norm_second_new = adam_step(
        norm_params, norm_gain_gradient, norm_first, norm_second, 0.1, 0.0)
    return (
        loss_sum,
        slot_count,
        reduce_grad,
        spatial_grad,
        reduce_new,
        spatial_new,
        left_new,
        right_new,
        head_new,
        head_first_new,
        head_second_new,
        bias_new,
        bias_first_new,
        bias_second_new,
        norm_new,
        norm_first_new,
        norm_second_new,
    )


FULL_PRECISION = lax.Precision.HIGHEST
BOTH = ("chan", "batch")


def conv_grid(grid, taps, spec):
    return lax.conv_general_dilated(
        grid, taps, (1, 1), ((1, 1), (1, 1)), dimension_numbers=spec,
        preferred_element_type=jnp.float32,
    )


def plain_norm_forward(pre_norm, gain, shift, valid):
    first_sum = jnp.sum(pre_norm * valid, axis=(0, 1))
    second_sum = jnp.sum(pre_norm * pre_norm * valid, axis=(0, 1))
    first_sum, second_sum, count = lax.psum((first_sum, second_sum, jnp.sum(valid)), BOTH)
    mean = first_sum / count
    scale = lax.rsqrt(second_sum / count - mean * mean + EPS)
    normed = (pre_norm - mean) * scale
    pre = gain * normed + shift
    return (jax.nn.silu(pre) * valid, (normed, pre, scale, count))


def plain_norm_backward(grad_act, kept, gain, valid):
    normed, pre, scale, count = kept
    d_pre = grad_act * valid * silu_slope(pre)
    shift_gradient, gain_grad = lax.psum(
        (jnp.sum(d_pre, axis=(0, 1)), jnp.sum(d_pre * normed, axis=(0, 1))), BOTH
    )
    d_input = gain * scale / count * (count * d_pre - shift_gradient - normed * gain_grad) * valid
    return (d_input, gain_grad, shift_gradient)


def plain_own_part(array, parts, axis=0):
    size = array.shape[axis] // parts
    return lax.dynamic_slice_in_dim(array, lax.axis_index("chan") * size, size, axis)


def plain_body(
    images,
    pixel_mask,
    labels,
    reduce_weight,
    reduce_mask,
    spatial_weight,
    spatial_mask,
    head_weight,
    head_bias,
    norm_params,
    left_stats,
    right_stats,
    left_root,
    input_side_roots,
    head_first,
    head_second,
    bias_first,
    bias_second,
    norm_first,
    norm_second,
):
    parts = lax.axis_size("chan")
    pixels = images.shape[1]
    side = SIDE
    rows_out = reduce_weight.shape[0]
    width = left_stats.shape[2]
    classes = head_weight.shape[1]
    own_images = lax.all_to_all(images, "chan", 0, 2, tiled=True)
    slots = own_images.shape[0]
    reduce_float = reduce_mask.astype(jnp.float32)
    spatial_float = spatial_mask.astype(jnp.float32)
    gather = lambda a, axis: lax.all_gather(a, "chan", axis=axis, tiled=True)
    reduce_low = gather((reduce_weight * reduce_float).astype(jnp.bfloat16), 0)
    spatial_low = gather((spatial_weight * spatial_float).astype(jnp.bfloat16), 0)
    head_low = gather(head_weight.astype(jnp.bfloat16), 0)
    norm_full = gather(norm_params, 1)
    right_factor_full = gather(input_side_roots, 1)
    valid = plain_own_part(pixel_mask, parts).astype(jnp.float32)[:, :, None]
    own_labels = plain_own_part(labels, parts)
    filled = jnp.sum(valid[:, :, 0], axis=1)
    divisor = jnp.maximum(filled, 1.0)
    used = (filled > 0.0).astype(jnp.float32)
    taps = spatial_low.reshape(width, 3, 3, width)
    first_pre = jnp.einsum("spc,oc->spo", own_images, reduce_low, preferred_element_type=jnp.float32)
    first_act, first_kept = plain_norm_forward(first_pre, norm_full[0], norm_full[1], valid)
    hidden = first_act.astype(jnp.bfloat16).reshape(slots, side, side, width)
    second_pre = conv_grid(hidden, taps, ("NHWC", "OHWI", "NHWC")).reshape(slots, pixels, width)
    second_act, second_kept = plain_norm_forward(second_pre, norm_full[2], norm_full[3], valid)
    pooled = (jnp.sum(second_act, axis=1) / divisor[:, None]).astype(jnp.bfloat16)
    logits = jnp.dot(pooled, head_low, preferred_element_type=jnp.float32) + head_bias
    onehot = (jnp.arange(classes)[None, :] == own_labels[:, None]).astype(jnp.float32)
    log_total = jax.nn.logsumexp(logits, axis=1)
    picked = jnp.sum(onehot * logits, axis=1)
    loss_local = jnp.sum(used * (log_total - picked))
    d_logits = (used[:, None] * (jnp.exp(logits - log_total[:, None]) - onehot) / SLOTS_DEV).astype(
        jnp.bfloat16
    )
    head_grad = jnp.einsum("so,sc->oc", pooled, d_logits, preferred_element_type=jnp.float32)
    bias_grad = jnp.sum(d_logits.astype(jnp.float32), axis=0)
    d_pooled = jnp.einsum("sc,oc->so", d_logits, head_low, preferred_element_type=jnp.float32)
    d_act = jnp.broadcast_to((d_pooled / divisor[:, None])[:, None, :], second_act.shape)
    d_second, gain_two, shift_two = plain_norm_backward(d_act, second_kept, norm_full[2], valid)
    d_second = d_second.astype(jnp.bfloat16).reshape(slots, side, side, width)
    spatial_local = lax.conv_general_dilated(
        hidden, d_second, (1, 1), ((1, 1), (1, 1)), dimension_numbers=("CHWN", "IHWO", "NHWC"),
        preferred_element_type=jnp.float32,
    )
    spatial_local = spatial_local.transpose(3, 1, 2, 0).reshape(width, 9 * width)
    d_hidden = conv_grid(
        d_second, taps[:, ::-1, ::-1, :], ("NHWC", "IHWO", "NHWC")
    ).reshape(slots, pixels, width)
    d_first, gain_one, shift_one = plain_norm_backward(d_hidden, first_kept, norm_full[0], valid)
    d_first = d_first.astype(jnp.bfloat16)
    reduce_local = jnp.einsum("spc,spo->oc", own_images, d_first, preferred_element_type=jnp.float32)
    scatter = lambda a: lax.psum_scatter(a, "chan", scatter_dimension=0, tiled=True)
    reduce_grad, spatial_grad, head_grad = scatter(reduce_local), scatter(spatial_local), scatter(head_grad)
    reduce_grad, spatial_grad, head_grad = lax.psum((reduce_grad, spatial_grad, head_grad), "batch")
    reduce_grad = reduce_grad * reduce_float
    spatial_grad = spatial_grad * spatial_float
    bias_grad, loss_sum, slot_count = lax.psum((bias_grad, loss_local, jnp.sum(used)), BOTH)
    norm_gain_gradient = plain_own_part(jnp.stack([gain_one, shift_one, gain_two, shift_two], axis=0), parts, 1)
    tiles_one = reduce_weight.shape[1] // width
    blocks = jnp.concatenate(
        [
            reduce_grad.reshape(rows_out, tiles_one, width).transpose(1, 0, 2),
            spatial_grad.reshape(rows_out, 9, width).transpose(1, 0, 2),
        ],
        axis=0,
    )
    blocks_full = gather(blocks, 1)
    left_new = 0.95 * left_stats + jnp.einsum(
        "tak,tbk->tab", blocks, blocks_full, precision=FULL_PRECISION
    )
    own_columns = plain_own_part(blocks_full, parts, 2)
    right_new = 0.95 * right_stats + jnp.einsum(
        "tki,tkb->tib", own_columns, blocks_full, precision=FULL_PRECISION
    )
    matrix_product = jnp.einsum("tak,tkb->tab", left_root, blocks_full, precision=FULL_PRECISION)
    matrix_product = jnp.einsum(
        "ghk,gkl->ghl", matrix_product, right_factor_full, precision=FULL_PRECISION
    )
    squares = lax.psum(jnp.sum(matrix_product * matrix_product, axis=(1, 2)), "chan")
    step = matrix_product / jnp.sqrt(squares / (width * width) + 1e-06)[:, None, None]
    step_one = step[:tiles_one].transpose(1, 0, 2).reshape(rows_out, tiles_one * width)
    step_two = step[tiles_one:].transpose(1, 0, 2).reshape(rows_out, 9 * width)
    reduce_new = reduce_weight - 0.02 * reduce_float * (step_one + 0.1 * reduce_weight)
    spatial_new = spatial_weight - 0.02 * spatial_float * (step_two + 0.1 * spatial_weight)
    head_new, head_first_new, head_second_new = adam_step(
        head_weight, head_grad, head_first, head_second, 0.04, 0.1
    )
    bias_new, bias_first_new, bias_second_new = adam_step(
        head_bias, bias_grad, bias_first, bias_second, 0.1, 0.0
    )
    norm_new, norm_first_new, norm_second_new = adam_step(
        norm_params, norm_gain_gradient, norm_first, norm_second, 0.1, 0.0
    )
    return (
        loss_sum,
        slot_count,
        reduce_grad,
        spatial_grad,
        reduce_new,
        spatial_new,
        left_new,
        right_new,
        head_new,
        head_first_new,
        head_second_new,
        bias_new,
        bias_first_new,
        bias_second_new,
        norm_new,
        norm_first_new,
        norm_second_new,
    )


def solution(mesh):
    in_specs = (
        P("batch", None, "chan"),
        P("batch", None),
        P("batch"),
        P("chan", None),
        P("chan", None),
        P("chan", None),
        P("chan", None),
        P("chan", None),
        P(),
        P(None, "chan"),
        P(None, "chan", None),
        P(None, "chan", None),
        P(None, "chan", None),
        P(None, "chan", None),
        P("chan", None),
        P("chan", None),
        P(),
        P(),
        P(None, "chan"),
        P(None, "chan"),
    )
    out_specs = (
        P(),
        P(),
        P("chan", None),
        P("chan", None),
        P("chan", None),
        P("chan", None),
        P(None, "chan", None),
        P(None, "chan", None),
        P("chan", None),
        P("chan", None),
        P("chan", None),
        P(),
        P(),
        P(),
        P(None, "chan"),
        P(None, "chan"),
        P(None, "chan"),
    )
    chan, batch = mesh.shape["chan"], mesh.shape["batch"]
    fits = chan % 4 == 0 and batch % 2 == 0 and WIDTH % (16 * chan * batch) == 0 and SLOTS_DEV % (16 * chan) == 0
    return jax.shard_map(body if fits else plain_body, mesh=mesh, in_specs=in_specs, out_specs=out_specs, check_vma=False)
```

```python
import functools

import jax
import jax.numpy as jnp
from jax import lax
from jax.experimental import pallas as pl
from jax.experimental.pallas import tpu as pltpu
from jax.sharding import PartitionSpec as P

SIDE = 7
SLOTS_DEV = 384
STEP = 10
ORDERS = ("xyz", "xy")

WIDTH = 512
EPS = 1e-05
MESH = pl.DeviceIdType.MESH
ANY = pl.BlockSpec(memory_space=pl.ANY)
VMEM = pl.BlockSpec(memory_space=pltpu.VMEM)
DMA = pltpu.SemaphoreType.DMA
SMALL = 8


def place():
    c, b = lax.axis_index("chan"), lax.axis_index("batch")
    nz, nx = lax.axis_size("chan") // 2, lax.axis_size("batch") // 2
    return (c // 2, lax.rem(c, 2), b // 2, lax.rem(b, 2)), (nz, 2, nx, 2)


def at(z, y, x, core):
    return {"chan": z * 2 + y, "batch": x * 2 + core}


def turned(index, size):
    return [lax.rem(index + k, size) for k in range(1, size)]


def greet(peers):
    barrier = pltpu.get_barrier_semaphore()
    for peer in peers:
        pl.semaphore_signal(barrier, inc=1, device_id=peer, device_id_type=MESH)
    pl.semaphore_wait(barrier, len(peers))


class Copies:
    def __init__(self, send, recv):
        self.send, self.recv, self.used = send, recv, 0

    def start(self, source, target, peer):
        copy = pltpu.make_async_remote_copy(
            source, target, self.send.at[self.used], self.recv.at[self.used],
            device_id=peer, device_id_type=MESH,
        )
        self.used += 1
        copy.start()
        return copy


def dot(left, right, left_dim, right_dim):
    return lax.dot_general(left, right, (((left_dim,), (right_dim,)), ((), ())), preferred_element_type=jnp.float32)


def sigmoid(value):
    return 1.0 / (1.0 + jnp.exp(-value))


def packed(row):
    return jnp.concatenate([row[:, i : i + 128] for i in range(0, row.shape[1], 128)], axis=0)


def unpacked(block):
    return jnp.concatenate([block[i : i + 1] for i in range(block.shape[0])], axis=1)


def step_kernel(
    images, weights, roots, norms, valid, labels, used, divisor, bias,
    taps_out, reduce_out, head_out, totals_out, weights_out, roots_out,
    own_images, first, second, hidden_pad, grad_pad, turned_grad, taps, reduce_low, head_low,
    norms_held, pack_one, pack_two, pack_three, pack_four, held_one, held_two, held_three, held_four,
    tap_sums, core_in, first_in, partial, pooling, pooled_low, d_logits, d_act, head_buf, grad_buf, send, recv, local,
):
    (z, y, x, core), (nz, ny, nx, nc) = place()
    c, n = lax.axis_index("chan"), lax.axis_size("chan")
    f32, low = jnp.float32, jnp.bfloat16
    slots = used.shape[0]
    side = SIDE
    line = side * slots
    wide_line = (side + 1) * slots
    pixels = side * side
    rim = (side + 2) * slots
    body_rows = side * wide_line
    width = first.shape[1]
    depth = own_images.shape[-1]
    everyone = [
        at(lax.rem(z + i, nz), lax.rem(y + j, ny), lax.rem(x + k, nx), lax.rem(core + m, nc))
        for i in range(nz) for j in range(ny) for k in range(nx) for m in range(nc) if i + j + k + m
    ]
    greet(everyone)
    copies = Copies(send, recv)
    others = turned(c, n)
    across_z = lax.rem(z + nz // 2, nz)
    near_z = [z // (nz // 2) * (nz // 2) + lax.rem(lax.rem(z, nz // 2) + k, nz // 2) for k in range(1, nz // 2)]
    mate, mate_y = at(z, y, x, 1 - core), at(z, 1 - y, x, core)
    mates_x = [at(z, y, k, core) for k in turned(x, nx)]

    def begin_z(source, target, sem):
        keep = pltpu.make_async_copy(source.at[x, core], target.at[z, y, x, core], local.at[sem])
        keep.start()
        peers = [at(k, y, x, core) for k in [across_z] + near_z]
        return [keep] + [copies.start(source.at[x, core], target.at[z, y, x, core], peer) for peer in peers]

    def pass_z(target, begun):
        for copy in begun:
            copy.wait()
        part = target.at[across_z, y, x, core]
        return [copies.start(part, part, at(k, y, x, core)) for k in near_z]

    weights_z = pass_z(weights_out, begin_z(weights, weights_out, 0))
    norm_copies = [copies.start(norms, norms_held.at[k + 1], {"chan": other}) for k, other in enumerate(others)]
    image_copies = [[copies.start(images.at[k, j], own_images.at[c, j, pl.ds(0, line)], {"chan": k}) for k in others]
                    for j in range(side)]
    own = pltpu.make_async_copy(images.at[c], own_images.at[c, :, pl.ds(0, line)], local.at[2])
    own.start()
    norms_held[0] = norms[...]

    def clear(i, _):
        rows = pl.ds(pl.multiple_of(i * slots, slots), slots)
        hidden_pad[rows, :] = jnp.zeros((slots, width), low)
        grad_pad[rows, :] = jnp.zeros((slots, width), low)
        return 0

    lax.fori_loop(0, hidden_pad.shape[0] // slots, clear, 0)
    for k in range(n):
        for j in range(side):
            own_images[k, j, pl.ds(line, slots), :] = jnp.zeros((slots, depth), low)

    for copy in weights_z:
        copy.wait()
    part = weights_out.at[:, y, x, core]
    copies.start(part, part, mate_y).wait()
    part = weights_out.at[:, :, x, core]
    along_x = [copies.start(part, part, peer) for peer in mates_x]
    for copy in along_x:
        copy.wait()
    part = weights_out.at[:, :, :, core]
    copies.start(part, part, mate).wait()
    fetched = []
    start = 0
    for j, held in enumerate((taps, reduce_low, head_low)):
        size = held.shape[-1]
        copy = pltpu.make_async_copy(weights_out.at[:, :, :, :, :, pl.ds(start, size)], held, local.at[3 + j])
        copy.start()
        fetched.append(copy)
        start += size
    for copy in fetched:
        copy.wait()
    taps, reduce_low, head_low = (held.reshape(width, held.shape[-1]) for held in (taps, reduce_low, head_low))
    for copy in norm_copies:
        copy.wait()
    norm_rows = jnp.sum(norms_held[...], axis=0)
    gain_one, shift_one, gain_two, shift_two = (norm_rows[i : i + 1] for i in range(4))

    def line_rows(j):
        return pl.ds(pl.multiple_of(j * line, slots), line)

    def pixel_rows(p):
        return pl.ds(pl.multiple_of(p * slots, slots), slots)

    def padded_pixel(p):
        j = p // side
        return pl.ds(pl.multiple_of(rim + (p + j) * slots, slots), slots)

    def across(block):
        return jnp.concatenate([block] * (width // 128), axis=1)

    def fold(value):
        return jnp.sum(value.reshape(-1, 8, width), axis=0)

    def total_of(index):
        return jnp.sum(partial[index], axis=0, keepdims=True)

    def exchange(pack, held):
        pack_copies = [copies.start(pack, held.at[k + 1], peer) for k, peer in enumerate(everyone)]
        held[0] = pack[...]
        return pack_copies

    def settled(pack_copies, held):
        for copy in pack_copies:
            copy.wait()
        return jnp.sum(held[...], axis=0)

    def add_to_sums(ref):
        def add(p, _):
            value = ref[pixel_rows(p), :]
            kept = value * across(valid[pixel_rows(p), :])
            partial[0] += fold(kept)
            partial[1] += fold(kept * value)
            return 0

        return add

    own.wait()
    partial[...] = jnp.zeros(partial.shape, f32)
    for j in range(side):
        for copy in image_copies[j]:
            copy.wait()
        block = jnp.concatenate([own_images[k, j, pl.ds(0, line), :] for k in range(n)], axis=1)
        first[pl.ds(j * line, line), :] = dot(block, reduce_low[...], 1, 1)
        lax.fori_loop(j * side, (j + 1) * side, add_to_sums(first), 0)
    all_valid = jnp.sum(valid[...], axis=0, keepdims=True)
    pack_one[...] = jnp.concatenate(
        [packed(total_of(0)), packed(total_of(1)), all_valid, jnp.zeros((7, 128), f32)], axis=0)
    stats = settled(exchange(pack_one, held_one), held_one)
    rows = width // 128
    count = jnp.concatenate([stats[2 * rows : 2 * rows + 1]] * rows, axis=1)

    def norm_of(stats):
        mean = unpacked(stats[:rows]) / count
        scale = lax.rsqrt(unpacked(stats[rows : 2 * rows]) / count - mean * mean + EPS)
        return mean, scale

    mean_one, scale_one = norm_of(stats)
    roots_z = begin_z(roots, roots_out, 1)

    def activate(p, _):
        normed = (first[pixel_rows(p), :] - mean_one) * scale_one
        pre = gain_one * normed + shift_one
        act = pre * sigmoid(pre) * across(valid[pixel_rows(p), :])
        hidden_pad[padded_pixel(p), :] = act.astype(low)
        return 0

    lax.fori_loop(0, pixels, activate, 0)

    def conv_line(j, _):
        value = None
        for t in range(9):
            offset = (t // 3 - 1) * wide_line + (t % 3 - 1) * slots
            rows_in = pl.ds(pl.multiple_of(rim + j * wide_line + offset, slots), line)
            term = dot(hidden_pad[rows_in, :], taps[:, t * width : (t + 1) * width], 1, 1)
            value = term if value is None else value + term
        second[line_rows(j), :] = value
        return 0

    lax.fori_loop(0, side, conv_line, 0)
    roots_z = pass_z(roots_out, roots_z)
    partial[...] = jnp.zeros(partial.shape, f32)
    lax.fori_loop(0, pixels, add_to_sums(second), 0)
    pack_two[...] = jnp.concatenate([packed(total_of(0)), packed(total_of(1))], axis=0)
    stats = settled(exchange(pack_two, held_two), held_two)
    mean_two, scale_two = norm_of(stats)
    for copy in roots_z:
        copy.wait()
    across_half = roots_out.shape[-1] // 2
    left, right = pl.ds(0, across_half), pl.ds(across_half, across_half)
    part = roots_out.at[:, y, x, core, :, left]
    roots_a = [copies.start(part, part, peer) for peer in mates_x]
    part = roots_out.at[:, y, x, core, :, right]
    roots_b = [copies.start(part, part, mate_y)]

    pooling[...] = jnp.zeros(pooling.shape, f32)

    def pool(p, _):
        normed = (second[pixel_rows(p), :] - mean_two) * scale_two
        pre = gain_two * normed + shift_two
        sigma = sigmoid(pre)
        kept = across(valid[pixel_rows(p), :])
        slope = sigma * (1.0 + pre * (1.0 - sigma)) * kept
        pooling[0] += pre * sigma * kept
        pooling[1] += slope
        pooling[2] += slope * normed
        return 0

    lax.fori_loop(0, pixels, pool, 0)
    divide = across(divisor[...])
    pooled_low[...] = (pooling[0] / divide).astype(low)
    logits = dot(pooled_low[...], head_low[...], 1, 0) + bias[...]
    classes = logits.shape[1]
    index = lax.broadcasted_iota(jnp.int32, (slots, classes), 1)
    onehot = (index == labels[:, :1]).astype(f32)
    top = jnp.max(logits, axis=1, keepdims=True)
    log_total = jnp.log(jnp.sum(jnp.exp(logits - top), axis=1, keepdims=True)) + top
    picked = jnp.sum(onehot * logits, axis=1, keepdims=True)
    use = used[:, :1]
    loss = jnp.sum(use * (log_total - picked))
    d_logits[...] = (use * (jnp.exp(logits - log_total) - onehot) / SLOTS_DEV).astype(low)
    bias_sum = jnp.sum(d_logits[...].astype(f32), axis=0, keepdims=True)
    half = width // 2

    def to_pooled(m, _):
        rows_in = pl.ds(pl.multiple_of(m * half, half), half)
        d_act[:, rows_in] = dot(d_logits[...], head_low[rows_in, :], 1, 1) / across(divisor[...])[:, :half]
        return 0

    lax.fori_loop(0, 2, to_pooled, 0)
    at_class = lax.broadcasted_iota(jnp.int32, (1, classes), 1)
    bias_sum = jnp.where(at_class == classes - 1, loss, jnp.where(at_class == classes - 2, jnp.sum(use), bias_sum))
    pack_three[...] = jnp.concatenate(
        [packed(jnp.sum(d_act[...] * pooling[1], axis=0, keepdims=True)),
         packed(jnp.sum(d_act[...] * pooling[2], axis=0, keepdims=True)), packed(bias_sum)], axis=0)
    going = exchange(pack_three, held_three)

    def to_head(m, _):
        columns = pl.ds(pl.multiple_of(m * (classes // 2), 128), classes // 2)
        head_buf[:, columns] = dot(pooled_low[...], d_logits[:, columns], 0, 0)
        return 0

    lax.fori_loop(0, 2, to_head, 0)
    head_copy = pltpu.make_async_copy(head_buf, head_out, local.at[6])
    head_copy.start()
    totals_two = settled(going, held_three)
    shift_grad, gain_grad = unpacked(totals_two[:rows]), unpacked(totals_two[rows : 2 * rows])
    factor = gain_two * scale_two / count
    for copy in roots_a:
        copy.wait()
    part = roots_out.at[:, y, :, core, :, left]
    roots_a = [copies.start(part, part, mate_y)]
    for copy in roots_b:
        copy.wait()
    part = roots_out.at[:, :, x, core, :, right]
    roots_b = [copies.start(part, part, peer) for peer in mates_x]

    def leave_second(p, _):
        normed = (second[pixel_rows(p), :] - mean_two) * scale_two
        pre = gain_two * normed + shift_two
        sigma = sigmoid(pre)
        kept = across(valid[pixel_rows(p), :])
        d_pre = d_act[...] * kept * (sigma * (1.0 + pre * (1.0 - sigma)))
        d_z = factor * (count * d_pre - shift_grad - normed * gain_grad) * kept
        grad_pad[padded_pixel(p), :] = d_z.astype(low)
        return 0

    lax.fori_loop(0, pixels, leave_second, 0)

    partial[...] = jnp.zeros(partial.shape, f32)

    def spread_line(j, _):
        value = None
        for t in range(9):
            offset = (t // 3 - 1) * wide_line + (t % 3 - 1) * slots
            rows_in = pl.ds(pl.multiple_of(rim + j * wide_line - offset, slots), line)
            term = dot(grad_pad[rows_in, :], taps[:, t * width : (t + 1) * width], 1, 0)
            value = term if value is None else value + term
        second[line_rows(j), :] = value
        return 0

    lax.fori_loop(0, side, spread_line, 0)
    def enter_first(p, _):
        normed = (first[pixel_rows(p), :] - mean_one) * scale_one
        pre = gain_one * normed + shift_one
        sigma = sigmoid(pre)
        d_pre = second[pixel_rows(p), :] * across(valid[pixel_rows(p), :]) * (sigma * (1.0 + pre * (1.0 - sigma)))
        second[pixel_rows(p), :] = d_pre
        partial[0] += fold(d_pre)
        partial[1] += fold(d_pre * normed)
        return 0

    lax.fori_loop(0, pixels, enter_first, 0)
    pack_four[...] = jnp.concatenate([packed(total_of(0)), packed(total_of(1))], axis=0)
    going = exchange(pack_four, held_four)

    def turn(j, _):
        rows_in = pl.ds(pl.multiple_of(rim + j * wide_line, slots), wide_line)
        turned_grad[:, pl.ds(pl.multiple_of(j * wide_line, 128), wide_line)] = grad_pad[rows_in, :].T
        return 0

    lax.fori_loop(0, side, turn, 0)

    def leave(slot, target, sem):
        copy = pltpu.make_async_copy(grad_buf.at[slot], target, local.at[sem])
        copy.start()
        return copy

    half = nz // 2
    near = z // half * half + lax.rem(z + 1, half)
    kinds = "".join(chunk_rounds(9))
    core_going, first_going = [], []

    def part_of(t, mine):
        if kinds[t] == "x":
            return [(tap_sums.at[t, :, :, x if mine else lax.rem(x + 1, nx)], first_in.at[t])]
        if kinds[t] == "y":
            return [(tap_sums.at[t, :, y if mine else 1 - y], first_in.at[t])]
        return [(tap_sums.at[t, (z // half * half + lax.rem(z, half) if mine else near) % half + h * half],
                 first_in.at[t, pl.ds(2 * h, 2)]) for h in range(2)]

    def over_core(t):
        core_going[t].wait()
        for i in range(nz):
            tap_sums[t, i] += core_in[t, i]
        peer = {"x": at(z, y, lax.rem(x + 1, nx), core), "y": mate_y, "z": at(near, y, x, core)}[kinds[t]]
        first_going.append([copies.start(source, target, peer) for source, target in part_of(t, False)])

    for t in range(9):
        offset = (t // 3 - 1) * wide_line + (t % 3 - 1) * slots
        slot = t % 2
        shifted = hidden_pad.at[pl.ds(rim + offset, body_rows)]
        grad_buf[slot] = dot(turned_grad[...], shifted[...], 1, 0).reshape(grad_buf.shape[1:])
        core_going.append(copies.start(grad_buf.at[slot, :, :, :, 1 - core], core_in.at[t], mate))
        for i in range(nz):
            tap_sums[t, i] = grad_buf[slot, i, :, :, core]
        if t:
            over_core(t - 1)
    over_core(8)
    leaving = []

    for copy in roots_a + roots_b:
        copy.wait()
    part = roots_out.at[:, :, :, core]
    roots_core = copies.start(part, part, mate)
    totals_one = settled(going, held_four)
    shift_sum, gain_sum = unpacked(totals_one[:rows]), unpacked(totals_one[rows : 2 * rows])
    factor_one = gain_one * scale_one / count

    def leave_first(p, _):
        normed = (first[pixel_rows(p), :] - mean_one) * scale_one
        kept = across(valid[pixel_rows(p), :])
        d_z = factor_one * (count * second[pixel_rows(p), :] - shift_sum - normed * gain_sum) * kept
        grad_pad[padded_pixel(p), :] = d_z.astype(low)
        return 0

    lax.fori_loop(0, pixels, leave_first, 0)
    lax.fori_loop(0, side, turn, 0)
    per = width // depth
    for t in range(n // per):
        slot = (9 + t) % 2
        if t >= 2:
            leaving[t - 2].wait()
        block = jnp.concatenate([own_images[t * per + k].reshape(body_rows, depth) for k in range(per)], axis=1)
        grad_buf[slot] = dot(turned_grad[...], block, 1, 0).reshape(grad_buf.shape[1:])
        leaving.append(leave(slot, reduce_out.at[:, :, :, :, :, pl.ds(t * width, width)], 7 + slot))
    taps_going = []
    for t in range(9):
        for copy in first_going[t]:
            copy.wait()
        for h, (kept, landed) in enumerate(part_of(t, True)):
            kept[...] += landed[...]
            copy = pltpu.make_async_copy(
                kept, taps_out.at[t, pl.ds(2 * h, 2)] if kinds[t] == "z" else taps_out.at[t], local.at[9 + 2 * t + h])
            copy.start()
            taps_going.append(copy)
    for copy in taps_going:
        copy.wait()
    totals_out[...] = jnp.concatenate([totals_two, totals_one], axis=0)
    head_copy.wait()
    roots_core.wait()
    for copy in leaving[-2:]:
        copy.wait()


def local_step(images, weights, roots, norms, valid, labels, used, divisor, bias):
    n, nb = lax.axis_size("chan"), lax.axis_size("batch")
    nz, nx = n // 2, nb // 2
    slots, width = used.shape[0], norms.shape[1]
    line, depth, classes = SIDE * slots, images.shape[-1], bias.shape[1]
    f32, low = jnp.float32, jnp.bfloat16
    rows = weights.shape[0] // nb
    grids = ((SIDE * (SIDE + 1) + 2 * (SIDE + 2)) * slots, width)
    shape = jax.ShapeDtypeStruct
    gathered = lambda a: shape((nz, 2, nx, 2, rows, a.shape[1]), a.dtype)
    quarters = lambda a: a.reshape(nx, 2, rows, a.shape[1])
    held = lambda k: pltpu.VMEM((n * nb, k, 128), f32)
    pack = lambda k: pltpu.VMEM((k, 128), f32)
    count = 2 * (nz - 1) + (SIDE + 1) * (n - 1) + (1 + (nx - 1) + 1) + (2 * nx + 1) + 4 * (n * nb - 1) + 27
    two = 2 * width // 128
    three = two + classes // 128
    weight = lambda size: pltpu.VMEM((nz, 2, nx, 2, rows, size), low)
    spatial, reduce, head, totals, weights_full, roots_full = pl.pallas_call(
        step_kernel,
        out_shape=(
            shape((9, nz, 2, rows, width), f32),
            shape((nz, 2, nx, 2, rows, n * depth), f32),
            shape((width, classes), f32),
            shape((two + three, 128), f32),
            gathered(weights),
            gathered(roots),
        ),
        in_specs=[ANY, ANY, ANY, VMEM, VMEM, VMEM, VMEM, VMEM, VMEM],
        out_specs=(ANY, ANY, ANY, VMEM, ANY, ANY),
        scratch_shapes=[
            pltpu.VMEM((n, SIDE, line + slots, depth), low),
            pltpu.VMEM((SIDE * line, width), f32),
            pltpu.VMEM((SIDE * line, width), f32),
            pltpu.VMEM(grids, low),
            pltpu.VMEM(grids, low),
            pltpu.VMEM((width, SIDE * (line + slots)), low),
            weight(9 * width), weight(n * depth), weight(classes),
            pltpu.VMEM((n,) + norms.shape, f32),
            pack(two + 8), pack(two), pack(three), pack(two),
            held(two + 8), held(two), held(three), held(two),
            pltpu.VMEM((9, nz, 2, nx, rows, width), f32),
            pltpu.VMEM((9, nz, 2, nx, rows, width), f32),
            pltpu.VMEM((9, nz, 2, rows, width), f32),
            pltpu.VMEM((2, 8, width), f32),
            pltpu.VMEM((3, slots, width), f32),
            pltpu.VMEM((slots, width), low),
            pltpu.VMEM((slots, classes), low),
            pltpu.VMEM((slots, width), f32),
            pltpu.VMEM((width, classes), f32),
            pltpu.VMEM((2, nz, 2, nx, 2, rows, width), f32),
            DMA((count,)), DMA((count,)), DMA((27,)),
        ],
        compiler_params=pltpu.CompilerParams(collective_id=0, has_side_effects=True, vmem_limit_bytes=60 << 20),
        name="step",
    )(images.reshape(n, SIDE, line, depth), quarters(weights), quarters(roots), norms, valid, labels, used, divisor, bias)
    return spatial, reduce, head, totals[:three], totals[three:], roots_full.reshape(width, roots.shape[1])


def chunk_rounds(count):
    rounds = []
    while count > 0:
        rounds.append(ORDERS[len(rounds) % len(ORDERS)][:count])
        count -= len(rounds[-1])
    return rounds


def settle_kernel(
    chunks, taps, reduce, head, mask, left_root, roots, own, left_part, right_part, outer_out, size,
    full, factors, lefts, rights, outers, squares, held, sums, core_in, first_in, second_in, near_in, across_in,
    final, final_low, send, recv, local,
):
    (z, y, x, core), (nz, ny, nx, nc) = place()
    half = nz // 2
    across_z = lax.rem(z + half, nz)
    base_z = z // half * half
    near_z = [base_z + lax.rem(lax.rem(z, half) + k, half) for k in range(1, half)]
    others_x = turned(x, nx)
    mate, mate_y = at(z, y, x, 1 - core), at(z, 1 - y, x, core)
    mates_x = [at(z, y, k, core) for k in others_x]
    mates_near = [at(k, y, x, core) for k in near_z]
    mate_across = at(across_z, y, x, core)
    c, n = lax.axis_index("chan"), lax.axis_size("chan")
    others = [{"chan": k} for k in turned(c, n)]
    greet(others + mates_x + [mate])
    copies = Copies(send, recv)
    f32, low = jnp.float32, jnp.bfloat16
    rows, width = left_root.shape[1:]
    tiles_one = reduce.shape[-1] // width
    n_taps = taps.shape[0]
    sources = ((reduce, n_taps * width), (head, n_taps * width + reduce.shape[-1]))
    wide = n_taps * width + reduce.shape[-1]
    used_local = [0]

    def keep(source, target):
        copy = pltpu.make_async_copy(source, target, local.at[used_local[0]])
        used_local[0] += 1
        copy.start()
        return copy

    roots_in = [keep(roots, factors)]
    pick = (lax.broadcasted_iota(jnp.int32, (rows, width), 1)
            == lax.broadcasted_iota(jnp.int32, (rows, width), 0) + c * rows).astype(low)
    squares[...] = jnp.zeros(squares.shape, f32)
    outgoing = []

    def two_parts(value):
        high = value.astype(low)
        return [high, (value - high.astype(f32)).astype(low)]

    def multiply(t, columns):
        grad = full[:, :, :, :, :, columns].reshape(width, width)
        mine = full[z, y, :, :, :, columns].reshape(rows, width)
        first = dot(jnp.concatenate([mine, pick], axis=0), grad, 1, 1)
        lefts[t] = first[:rows]
        second = dot(jnp.concatenate([first[rows:].astype(low)] + two_parts(left_root[t]), axis=0), grad, 1, 0)
        rights[t] = second[:rows]
        inner = second[rows : 2 * rows] + second[2 * rows :]
        third = dot(jnp.concatenate(two_parts(inner), axis=0), factors[:, t * width : (t + 1) * width], 1, 0)
        value = third[:rows] + third[rows:]
        outers[t] = value
        squares[t : t + 1, :] = jnp.full((1, 128), jnp.sum(value * value), f32)
        outgoing.extend(keep(a.at[t], b.at[t]) for a, b in ((lefts, left_part), (rights, right_part), (outers, outer_out)))

    def wait(going):
        for copy in going:
            copy.wait()

    def enter(start, size):
        columns = pl.ds(start, size)
        going = []
        for source, first_column in sources:
            begin, end = max(start, first_column), min(start + size, first_column + source.shape[-1])
            if begin < end:
                taken, landed = pl.ds(begin - first_column, end - begin), pl.ds(begin, end - begin)
                going.append(copies.start(source.at[:, :, :, 1 - core, :, taken], core_in.at[:, :, :, :, landed], mate))
                going.append(keep(source.at[:, :, :, core, :, taken], sums.at[:, :, :, :, landed]))
        yield
        wait(going)
        for i in range(nz):
            for j in range(ny):
                for k in range(nx):
                    sums[i, j, k, :, columns] += core_in[i, j, k, :, columns]

    def settled(start, last_in, columns):
        total = (sums[z, y, x, :, columns] + last_in) * mask[:, columns]
        final[:, columns] = total
        kept = [keep(final.at[:, columns], own.at[x, core, :, columns])]
        kept += [copies.start(final.at[:, columns], own.at[x, core, :, columns], peer) for peer in mates_x]
        if start < wide:
            final_low[:, columns] = total.astype(low)
            return kept, [keep(final_low.at[:, columns], full.at[z, y, x, core, :, columns])]
        return kept, []

    def own_core(kept, columns):
        wait(kept)
        part = own.at[:, core, :, columns]
        return copies.start(part, part, mate)

    def block_of(start, columns):
        t = start // width
        if roots_in:
            roots_in.pop().wait()
        multiply(t + tiles_one if t < n_taps else t - n_taps, columns)

    def chunk_z(start, size):
        columns = pl.ds(start, size)
        if start < n_taps * width:
            going = [keep(taps.at[start // width, pl.ds(2 * h, 2)], sums.at[lax.rem(z, half) + h * half, :, :, :, columns])
                     for h in range(2)]
            yield
            wait(going)
        else:
            yield from enter(start, size)
            going = []
            for t, k in enumerate(near_z):
                for h in range(2):
                    there = lax.rem(k, half) + h * half
                    going.append(copies.start(
                        sums.at[there, :, :, :, columns], first_in.at[t, pl.ds(2 * h, 2), :, :, columns], mates_near[t]))
            yield
            wait(going)
            for t in range(half - 1):
                for h in range(2):
                    for j in range(ny):
                        for k in range(nx):
                            sums[lax.rem(z, half) + h * half, j, k, :, columns] += first_in[t, 2 * h + j, k, :, columns]
        landing = [second_in.at[0, pl.ds(nx * j, nx), :, columns] for j in range(ny)]
        going = [copies.start(sums.at[across_z, j, :, :, columns], landing[j], mate_across) for j in range(ny)]
        yield
        wait(going)
        for j in range(ny):
            for k in range(nx):
                sums[z, j, k, :, columns] += second_in[0, nx * j + k, :, columns]
        going = [copies.start(sums.at[z, :, k, :, columns], near_in.at[t, :, :, columns], mates_x[t])
                 for t, k in enumerate(others_x)]
        yield
        wait(going)
        for t in range(nx - 1):
            for j in range(ny):
                sums[z, j, x, :, columns] += near_in[t, j, :, columns]
        going = [copies.start(sums.at[z, 1 - y, x, :, columns], across_in.at[:, columns], mate_y)]
        yield
        wait(going)
        kept, going = settled(start, across_in[:, columns], columns)
        going += [copies.start(final_low.at[:, columns], full.at[z, y, x, core, :, columns], peer) for peer in mates_x]
        yield
        last = [own_core(kept, columns)]
        wait(going)
        part = full.at[z, y, :, core, :, columns]
        going = [copies.start(part, part, mate_y)]
        yield
        wait(going)
        part = full.at[z, :, :, core, :, columns]
        going = [copies.start(part, part, peer) for peer in [mate_across] + mates_near]
        yield
        wait(going)
        part = full.at[across_z, :, :, core, :, columns]
        going = [copies.start(part, part, peer) for peer in mates_near]
        yield
        wait(going)
        part = full.at[:, :, :, core, :, columns]
        last.append(copies.start(part, part, mate))
        yield
        wait(last)
        block_of(start, columns)

    def chunk(start, size, x_first):
        columns = pl.ds(start, size)
        if start < n_taps * width:
            going = [keep(taps.at[start // width], sums.at[:, :, x, :, columns] if x_first else sums.at[:, y, :, :, columns])]
            yield
            wait(going)
        else:
            yield from enter(start, size)
            if x_first:
                going = [copies.start(sums.at[:, :, k, :, columns], first_in.at[t, :, :, :, columns], mates_x[t])
                         for t, k in enumerate(others_x)]
            else:
                going = [copies.start(sums.at[:, 1 - y, :, :, columns], first_in.at[0, :, :, :, columns], mate_y)]
            yield
            wait(going)
            for i in range(nz):
                for j in range(2):
                    if x_first:
                        sums[i, j, x, :, columns] += first_in[0, i, j, :, columns]
                    else:
                        sums[i, y, j, :, columns] += first_in[0, i, j, :, columns]
        going = []
        if x_first:
            going.append(copies.start(sums.at[:, 1 - y, x, :, columns], second_in.at[0, :, :, columns], mate_y))
        else:
            for t, k in enumerate(others_x):
                going.append(copies.start(sums.at[:, y, k, :, columns], second_in.at[t, :, :, columns], mates_x[t]))
        yield
        wait(going)
        for t in range(1 if x_first else nx - 1):
            for i in range(nz):
                sums[i, y, x, :, columns] += second_in[t, i, :, columns]
        going = []
        for t, k in enumerate(near_z):
            for h in range(2):
                there = lax.rem(k + h * half, nz)
                going.append(copies.start(sums.at[there, y, x, :, columns], near_in.at[t, h, :, columns], mates_near[t]))
        yield
        wait(going)
        for t in range(half - 1):
            for h in range(2):
                sums[lax.rem(z + h * half, nz), y, x, :, columns] += near_in[t, h, :, columns]
        going = [copies.start(sums.at[across_z, y, x, :, columns], across_in.at[:, columns], mate_across)]
        yield
        wait(going)
        kept, going = settled(start, across_in[:, columns], columns)
        if start < wide:
            going += [copies.start(final_low.at[:, columns], full.at[z, y, x, core, :, columns], peer)
                      for peer in [mate_across] + mates_near]
        yield
        rows_core = [own_core(kept, columns)]
        if start < wide:
            wait(going)
            part = full.at[across_z, y, x, core, :, columns]
            going = [copies.start(part, part, peer) for peer in mates_near]
            yield
            wait(going)
            part = full.at[:, y, x, core, :, columns]
            going = [copies.start(part, part, peer) for peer in (mates_x if x_first else [mate_y])]
            yield
            wait(going)
            part = full.at[:, y, :, core, :, columns] if x_first else full.at[:, :, x, core, :, columns]
            going = [copies.start(part, part, peer) for peer in ([mate_y] if x_first else mates_x)]
            yield
            wait(going)
            part = full.at[:, :, :, core, :, columns]
            rows_core.append(copies.start(part, part, mate))
        yield
        wait(rows_core)
        if start < wide:
            block_of(start, columns)

    rounds = [[chunk_z(*c[:2]) if c[2] == "z" and c[0] < wide else chunk(*c[:2], c[2] != "y") for c in some] for some in chunks]
    begun, active = [], []
    while rounds or begun or active:
        active += begun
        begun = rounds.pop(0) if rounds else []
        for going in begun:
            next(going)
        for going in active[::-1]:
            try:
                next(going)
            except StopIteration:
                active.remove(going)
    going = [copies.start(squares, held.at[k + 1], peer) for k, peer in enumerate(others)]
    held[0] = squares[...]
    wait(going + outgoing)
    size[...] = jnp.sqrt(jnp.sum(held[...], axis=0) / (width * width) + 1e-06)


def settle(taps, reduce, head, mask, left_root, roots):
    nz, nx, n = lax.axis_size("chan") // 2, lax.axis_size("batch") // 2, lax.axis_size("chan")
    blocks, own_rows, width = left_root.shape
    rows = width // (4 * nz * nx)
    wide = taps.shape[0] * width + reduce.shape[-1]
    total = wide + head.shape[1]
    split = lambda a: a.reshape(nz, 2, nx, 2, rows, a.shape[1])
    f32, low = jnp.float32, jnp.bfloat16
    chunks, start = [], 0
    for kinds in chunk_rounds(total // width):
        chunks.append([(start + i * width, width, kind) for i, kind in enumerate(kinds)])
        start += len(kinds) * width
    near = nz // 2 - 1
    first = max(nx - 1, nx // 2)
    count = (total // width) * (4 + first + max(nx - 1, 1) + 2 * near + 1 + (nx - 1) + 1 + near + 1 + near + nx + 1) + n
    product = jax.ShapeDtypeStruct((blocks, own_rows, width), f32)
    padded = (blocks + 7) // 8 * 8
    own, left_part, right_part, outer, size = pl.pallas_call(
        functools.partial(settle_kernel, chunks),
        out_shape=(
            jax.ShapeDtypeStruct((nx, 2, rows, total), f32), product, product, product,
            jax.ShapeDtypeStruct((padded, 128), f32),
        ),
        in_specs=[ANY, ANY, ANY, VMEM, VMEM, ANY],
        out_specs=(ANY,) * 4 + (VMEM,),
        scratch_shapes=[
            pltpu.VMEM((nz, 2, nx, 2, rows, wide), low),
            pltpu.VMEM(roots.shape, low),
            pltpu.VMEM(product.shape, f32),
            pltpu.VMEM(product.shape, f32),
            pltpu.VMEM(product.shape, f32),
            pltpu.VMEM((padded, 128), f32),
            pltpu.VMEM((n, padded, 128), f32),
            pltpu.VMEM((nz, 2, nx, rows, total), f32),
            pltpu.VMEM((nz, 2, nx, rows, total), f32),
            pltpu.VMEM((first, nz, 2, rows, total), f32),
            pltpu.VMEM((max(nx - 1, 1), nz, rows, total), f32),
            pltpu.VMEM((near, 2, rows, total), f32),
            pltpu.VMEM((rows, total), f32),
            pltpu.VMEM((rows, total), f32),
            pltpu.VMEM((rows, wide), low),
            DMA((count,)), DMA((count,)), DMA((7 * (total // width) + 4,)),
        ],
        compiler_params=pltpu.CompilerParams(collective_id=1, has_side_effects=True, vmem_limit_bytes=60 << 20),
        name="settle",
    )(taps, reduce, split(head), mask, left_root, roots)
    return own.reshape(own_rows, total), left_part, right_part, outer, size


def finish_kernel(
    tiles_one, own, head_a, head_b, left_part, right_part, outer, size, left_stats, right_stats,
    reduce_weight, spatial_weight, reduce_mask, spatial_mask, head_weight, head_first, head_second,
    reduce_grad, spatial_grad, reduce_new, spatial_new, left_new, right_new, head_new, head_first_new, head_second_new,
):
    t = pl.program_id(0)
    left_new[0] = 0.95 * left_stats[0] + left_part[0]
    right_new[0] = 0.95 * right_stats[0] + right_part[0]
    step = outer[0] / jnp.concatenate([size[pl.ds(t, 1), :]] * (outer.shape[-1] // 128), axis=1)

    def leave(weight, mask, grad, new):
        grad[...] = own[...]
        new[...] = weight[...] - 0.02 * mask[...].astype(jnp.float32) * (step + 0.1 * weight[...])

    @pl.when(t < tiles_one)
    def _():
        leave(reduce_weight, reduce_mask, reduce_grad, reduce_new)

    @pl.when(t >= tiles_one)
    def _():
        leave(spatial_weight, spatial_mask, spatial_grad, spatial_new)

    @pl.when(t == 0)
    def _():
        head_grad = jnp.concatenate([head_a[...], head_b[...]], axis=1)[:, : head_weight.shape[1]]
        head_new[...], head_first_new[...], head_second_new[...] = adam_step(
            head_weight[...], head_grad, head_first[...], head_second[...], 0.04, 0.1)


def finish(own, left_part, right_part, outer, size, left_stats, right_stats,
           reduce_weight, spatial_weight, reduce_mask, spatial_mask, head_weight, head_first, head_second):
    blocks, rows, width = left_stats.shape
    tiles_one, taps = reduce_weight.shape[1] // width, spatial_weight.shape[1] // width
    columns = lambda index: pl.BlockSpec((rows, width), lambda t: (0, index(t)))
    of_block = pl.BlockSpec((1, rows, width), lambda t: (t, 0, 0))
    whole = lambda a: pl.BlockSpec(a.shape, lambda t: (0, 0))
    of_reduce = columns(lambda t: jnp.minimum(t, tiles_one - 1))
    of_spatial = columns(lambda t: jnp.maximum(t - tiles_one, 0))
    like = lambda a: jax.ShapeDtypeStruct(a.shape, jnp.float32)
    return pl.pallas_call(
        functools.partial(finish_kernel, tiles_one),
        grid=(blocks,),
        out_shape=(like(reduce_weight), like(spatial_weight), like(reduce_weight), like(spatial_weight),
                   like(left_stats), like(left_stats), like(head_weight), like(head_weight), like(head_weight)),
        in_specs=[
            columns(lambda t: jnp.where(t < tiles_one, taps + t, t - tiles_one)),
            columns(lambda t: taps + tiles_one), columns(lambda t: taps + tiles_one + 1),
            of_block, of_block, of_block, whole(size), of_block, of_block,
            of_reduce, of_spatial, of_reduce, of_spatial, whole(head_weight), whole(head_weight), whole(head_weight),
        ],
        out_specs=(of_reduce, of_spatial, of_reduce, of_spatial, of_block, of_block,
                   whole(head_weight), whole(head_weight), whole(head_weight)),
        compiler_params=pltpu.CompilerParams(vmem_limit_bytes=60 << 20),
        name="finish",
    )(own, own, own, left_part, right_part, outer, size, left_stats, right_stats,
      reduce_weight, spatial_weight, reduce_mask, spatial_mask, head_weight, head_first, head_second)


def silu_slope(pre):
    sigma = jax.nn.sigmoid(pre)
    return sigma * (1.0 + pre * (1.0 - sigma))


def adam_step(param, grad, first, second, rate, decay):
    first = 0.9 * first + 0.1 * grad
    second = 0.999 * second + 0.001 * grad * grad
    mhat = first / (1.0 - 0.9**STEP)
    vhat = second / (1.0 - 0.999**STEP)
    return (param - rate * (mhat / (jnp.sqrt(vhat) + 1e-08) + decay * param), first, second)


def own_part(array, axis, name="chan"):
    size = array.shape[axis] // lax.axis_size(name)
    return lax.dynamic_slice_in_dim(array, lax.axis_index(name) * size, size, axis)


def body(
    images,
    pixel_mask,
    labels,
    reduce_weight,
    reduce_mask,
    spatial_weight,
    spatial_mask,
    head_weight,
    head_bias,
    norm_params,
    left_stats,
    right_stats,
    left_root,
    input_side_roots,
    head_first,
    head_second,
    bias_first,
    bias_second,
    norm_first,
    norm_second,
):
    n = lax.axis_size("chan")
    pixels, channels = images.shape[1:]
    side = SIDE
    rows_out, c_in = reduce_weight.shape
    width = left_stats.shape[2]
    classes = head_weight.shape[1]
    padded = 1024
    slots = images.shape[0] // n
    low = jnp.bfloat16
    f32 = jnp.float32
    reduce_float = reduce_mask.astype(f32)
    spatial_float = spatial_mask.astype(f32)

    spread_out = lambda a: jnp.broadcast_to(a[:, None], (a.shape[0], 128))
    by_pixel = images.reshape(n, slots, pixels, channels).transpose(0, 2, 1, 3)
    weights = jnp.concatenate(
        [(spatial_weight * spatial_float).astype(low), (reduce_weight * reduce_float).astype(low),
         jnp.pad(head_weight.astype(low), ((0, 0), (0, padded - classes)))], axis=1)
    roots = input_side_roots.astype(low).transpose(1, 0, 2).reshape(rows_out, -1)
    norms = lax.dynamic_update_slice_in_dim(
        jnp.zeros((8, width), f32), jnp.pad(norm_params, ((0, 4), (0, 0))), lax.axis_index("chan") * rows_out, 1)
    mask_own = own_part(pixel_mask, 0).astype(f32)
    filled = jnp.sum(mask_own, axis=1)
    taps_local, reduce_local, head_local, sums_two, sums_one, roots_full = local_step(
        by_pixel, weights, roots, norms, spread_out(mask_own.T.reshape(-1)), spread_out(own_part(labels, 0)),
        spread_out((filled > 0.0).astype(f32)), spread_out(jnp.maximum(filled, 1.0)),
        jnp.pad(head_bias, (0, padded - classes), constant_values=-1e30)[None])

    mask_rows = jnp.concatenate([spatial_float, reduce_float, jnp.ones((rows_out, padded), f32)], axis=1)
    own, *products = settle(taps_local, reduce_local, head_local, own_part(mask_rows, 0, "batch"), left_root, roots_full)
    of_norms = jnp.stack([a.reshape(-1) for a in (sums_one[4:], sums_one[:4], sums_two[4:8], sums_two[:4])])
    norm_gain_gradient = own_part(of_norms, 1)
    of_head = sums_two[8:].reshape(-1)
    bias_grad = of_head[:classes]
    loss_sum, slot_count = of_head[-1], of_head[-2]
    (reduce_grad, spatial_grad, reduce_new, spatial_new, left_new, right_new, head_new, head_first_new,
     head_second_new) = finish(
        own, *products, left_stats, right_stats, reduce_weight, spatial_weight, reduce_mask, spatial_mask,
        head_weight, head_first, head_second)
    bias_new, bias_first_new, bias_second_new = adam_step(head_bias, bias_grad, bias_first, bias_second, 0.1, 0.0)
    norm_new, norm_first_new, norm_second_new = adam_step(
        norm_params, norm_gain_gradient, norm_first, norm_second, 0.1, 0.0)
    return (
        loss_sum,
        slot_count,
        reduce_grad,
        spatial_grad,
        reduce_new,
        spatial_new,
        left_new,
        right_new,
        head_new,
        head_first_new,
        head_second_new,
        bias_new,
        bias_first_new,
        bias_second_new,
        norm_new,
        norm_first_new,
        norm_second_new,
    )


FULL_PRECISION = lax.Precision.HIGHEST
BOTH = ("chan", "batch")


def conv_grid(grid, taps, spec):
    return lax.conv_general_dilated(
        grid, taps, (1, 1), ((1, 1), (1, 1)), dimension_numbers=spec,
        preferred_element_type=jnp.float32,
    )


def plain_norm_forward(pre_norm, gain, shift, valid):
    first_sum = jnp.sum(pre_norm * valid, axis=(0, 1))
    second_sum = jnp.sum(pre_norm * pre_norm * valid, axis=(0, 1))
    first_sum, second_sum, count = lax.psum((first_sum, second_sum, jnp.sum(valid)), BOTH)
    mean = first_sum / count
    scale = lax.rsqrt(second_sum / count - mean * mean + EPS)
    normed = (pre_norm - mean) * scale
    pre = gain * normed + shift
    return (jax.nn.silu(pre) * valid, (normed, pre, scale, count))


def plain_norm_backward(grad_act, kept, gain, valid):
    normed, pre, scale, count = kept
    d_pre = grad_act * valid * silu_slope(pre)
    shift_gradient, gain_grad = lax.psum(
        (jnp.sum(d_pre, axis=(0, 1)), jnp.sum(d_pre * normed, axis=(0, 1))), BOTH
    )
    d_input = gain * scale / count * (count * d_pre - shift_gradient - normed * gain_grad) * valid
    return (d_input, gain_grad, shift_gradient)


def plain_own_part(array, parts, axis=0):
    size = array.shape[axis] // parts
    return lax.dynamic_slice_in_dim(array, lax.axis_index("chan") * size, size, axis)


def plain_body(
    images,
    pixel_mask,
    labels,
    reduce_weight,
    reduce_mask,
    spatial_weight,
    spatial_mask,
    head_weight,
    head_bias,
    norm_params,
    left_stats,
    right_stats,
    left_root,
    input_side_roots,
    head_first,
    head_second,
    bias_first,
    bias_second,
    norm_first,
    norm_second,
):
    parts = lax.axis_size("chan")
    pixels = images.shape[1]
    side = SIDE
    rows_out = reduce_weight.shape[0]
    width = left_stats.shape[2]
    classes = head_weight.shape[1]
    own_images = lax.all_to_all(images, "chan", 0, 2, tiled=True)
    slots = own_images.shape[0]
    reduce_float = reduce_mask.astype(jnp.float32)
    spatial_float = spatial_mask.astype(jnp.float32)
    gather = lambda a, axis: lax.all_gather(a, "chan", axis=axis, tiled=True)
    reduce_low = gather((reduce_weight * reduce_float).astype(jnp.bfloat16), 0)
    spatial_low = gather((spatial_weight * spatial_float).astype(jnp.bfloat16), 0)
    head_low = gather(head_weight.astype(jnp.bfloat16), 0)
    norm_full = gather(norm_params, 1)
    right_factor_full = gather(input_side_roots, 1)
    valid = plain_own_part(pixel_mask, parts).astype(jnp.float32)[:, :, None]
    own_labels = plain_own_part(labels, parts)
    filled = jnp.sum(valid[:, :, 0], axis=1)
    divisor = jnp.maximum(filled, 1.0)
    used = (filled > 0.0).astype(jnp.float32)
    taps = spatial_low.reshape(width, 3, 3, width)
    first_pre = jnp.einsum("spc,oc->spo", own_images, reduce_low, preferred_element_type=jnp.float32)
    first_act, first_kept = plain_norm_forward(first_pre, norm_full[0], norm_full[1], valid)
    hidden = first_act.astype(jnp.bfloat16).reshape(slots, side, side, width)
    second_pre = conv_grid(hidden, taps, ("NHWC", "OHWI", "NHWC")).reshape(slots, pixels, width)
    second_act, second_kept = plain_norm_forward(second_pre, norm_full[2], norm_full[3], valid)
    pooled = (jnp.sum(second_act, axis=1) / divisor[:, None]).astype(jnp.bfloat16)
    logits = jnp.dot(pooled, head_low, preferred_element_type=jnp.float32) + head_bias
    onehot = (jnp.arange(classes)[None, :] == own_labels[:, None]).astype(jnp.float32)
    log_total = jax.nn.logsumexp(logits, axis=1)
    picked = jnp.sum(onehot * logits, axis=1)
    loss_local = jnp.sum(used * (log_total - picked))
    d_logits = (used[:, None] * (jnp.exp(logits - log_total[:, None]) - onehot) / SLOTS_DEV).astype(
        jnp.bfloat16
    )
    head_grad = jnp.einsum("so,sc->oc", pooled, d_logits, preferred_element_type=jnp.float32)
    bias_grad = jnp.sum(d_logits.astype(jnp.float32), axis=0)
    d_pooled = jnp.einsum("sc,oc->so", d_logits, head_low, preferred_element_type=jnp.float32)
    d_act = jnp.broadcast_to((d_pooled / divisor[:, None])[:, None, :], second_act.shape)
    d_second, gain_two, shift_two = plain_norm_backward(d_act, second_kept, norm_full[2], valid)
    d_second = d_second.astype(jnp.bfloat16).reshape(slots, side, side, width)
    spatial_local = lax.conv_general_dilated(
        hidden, d_second, (1, 1), ((1, 1), (1, 1)), dimension_numbers=("CHWN", "IHWO", "NHWC"),
        preferred_element_type=jnp.float32,
    )
    spatial_local = spatial_local.transpose(3, 1, 2, 0).reshape(width, 9 * width)
    d_hidden = conv_grid(
        d_second, taps[:, ::-1, ::-1, :], ("NHWC", "IHWO", "NHWC")
    ).reshape(slots, pixels, width)
    d_first, gain_one, shift_one = plain_norm_backward(d_hidden, first_kept, norm_full[0], valid)
    d_first = d_first.astype(jnp.bfloat16)
    reduce_local = jnp.einsum("spc,spo->oc", own_images, d_first, preferred_element_type=jnp.float32)
    scatter = lambda a: lax.psum_scatter(a, "chan", scatter_dimension=0, tiled=True)
    reduce_grad, spatial_grad, head_grad = scatter(reduce_local), scatter(spatial_local), scatter(head_grad)
    reduce_grad, spatial_grad, head_grad = lax.psum((reduce_grad, spatial_grad, head_grad), "batch")
    reduce_grad = reduce_grad * reduce_float
    spatial_grad = spatial_grad * spatial_float
    bias_grad, loss_sum, slot_count = lax.psum((bias_grad, loss_local, jnp.sum(used)), BOTH)
    norm_gain_gradient = plain_own_part(jnp.stack([gain_one, shift_one, gain_two, shift_two], axis=0), parts, 1)
    tiles_one = reduce_weight.shape[1] // width
    blocks = jnp.concatenate(
        [
            reduce_grad.reshape(rows_out, tiles_one, width).transpose(1, 0, 2),
            spatial_grad.reshape(rows_out, 9, width).transpose(1, 0, 2),
        ],
        axis=0,
    )
    blocks_full = gather(blocks, 1)
    left_new = 0.95 * left_stats + jnp.einsum(
        "tak,tbk->tab", blocks, blocks_full, precision=FULL_PRECISION
    )
    own_columns = plain_own_part(blocks_full, parts, 2)
    right_new = 0.95 * right_stats + jnp.einsum(
        "tki,tkb->tib", own_columns, blocks_full, precision=FULL_PRECISION
    )
    matrix_product = jnp.einsum("tak,tkb->tab", left_root, blocks_full, precision=FULL_PRECISION)
    matrix_product = jnp.einsum(
        "ghk,gkl->ghl", matrix_product, right_factor_full, precision=FULL_PRECISION
    )
    squares = lax.psum(jnp.sum(matrix_product * matrix_product, axis=(1, 2)), "chan")
    step = matrix_product / jnp.sqrt(squares / (width * width) + 1e-06)[:, None, None]
    step_one = step[:tiles_one].transpose(1, 0, 2).reshape(rows_out, tiles_one * width)
    step_two = step[tiles_one:].transpose(1, 0, 2).reshape(rows_out, 9 * width)
    reduce_new = reduce_weight - 0.02 * reduce_float * (step_one + 0.1 * reduce_weight)
    spatial_new = spatial_weight - 0.02 * spatial_float * (step_two + 0.1 * spatial_weight)
    head_new, head_first_new, head_second_new = adam_step(
        head_weight, head_grad, head_first, head_second, 0.04, 0.1
    )
    bias_new, bias_first_new, bias_second_new = adam_step(
        head_bias, bias_grad, bias_first, bias_second, 0.1, 0.0
    )
    norm_new, norm_first_new, norm_second_new = adam_step(
        norm_params, norm_gain_gradient, norm_first, norm_second, 0.1, 0.0
    )
    return (
        loss_sum,
        slot_count,
        reduce_grad,
        spatial_grad,
        reduce_new,
        spatial_new,
        left_new,
        right_new,
        head_new,
        head_first_new,
        head_second_new,
        bias_new,
        bias_first_new,
        bias_second_new,
        norm_new,
        norm_first_new,
        norm_second_new,
    )


def solution(mesh):
    in_specs = (
        P("batch", None, "chan"),
        P("batch", None),
        P("batch"),
        P("chan", None),
        P("chan", None),
        P("chan", None),
        P("chan", None),
        P("chan", None),
        P(),
        P(None, "chan"),
        P(None, "chan", None),
        P(None, "chan", None),
        P(None, "chan", None),
        P(None, "chan", None),
        P("chan", None),
        P("chan", None),
        P(),
        P(),
        P(None, "chan"),
        P(None, "chan"),
    )
    out_specs = (
        P(),
        P(),
        P("chan", None),
        P("chan", None),
        P("chan", None),
        P("chan", None),
        P(None, "chan", None),
        P(None, "chan", None),
        P("chan", None),
        P("chan", None),
        P("chan", None),
        P(),
        P(),
        P(),
        P(None, "chan"),
        P(None, "chan"),
        P(None, "chan"),
    )
    chan, batch = mesh.shape["chan"], mesh.shape["batch"]
    fits = chan == 8 and batch == 4 and WIDTH % (16 * chan * batch) == 0 and SLOTS_DEV % (16 * chan) == 0
    return jax.shard_map(body if fits else plain_body, mesh=mesh, in_specs=in_specs, out_specs=out_specs, check_vma=False)
```

```python
import functools

import jax
import jax.numpy as jnp
from jax import lax
from jax.experimental import pallas as pl
from jax.experimental.pallas import tpu as pltpu
from jax.sharding import PartitionSpec as P

SIDE = 7
SLOTS_DEV = 384
STEP = 10
ORDERS = ("xyz", "xy")

WIDTH = 512
EPS = 1e-05
MESH = pl.DeviceIdType.MESH
ANY = pl.BlockSpec(memory_space=pl.ANY)
VMEM = pl.BlockSpec(memory_space=pltpu.VMEM)
DMA = pltpu.SemaphoreType.DMA
SMALL = 8


def place():
    c, b = lax.axis_index("chan"), lax.axis_index("batch")
    nz, nx = lax.axis_size("chan") // 2, lax.axis_size("batch") // 2
    return (c // 2, lax.rem(c, 2), b // 2, lax.rem(b, 2)), (nz, 2, nx, 2)


def at(z, y, x, core):
    return {"chan": z * 2 + y, "batch": x * 2 + core}


def turned(index, size):
    return [lax.rem(index + k, size) for k in range(1, size)]


def greet(peers):
    barrier = pltpu.get_barrier_semaphore()
    for peer in peers:
        pl.semaphore_signal(barrier, inc=1, device_id=peer, device_id_type=MESH)
    pl.semaphore_wait(barrier, len(peers))


class Copies:
    def __init__(self, send, recv):
        self.send, self.recv, self.used = send, recv, 0

    def start(self, source, target, peer):
        copy = pltpu.make_async_remote_copy(
            source, target, self.send.at[self.used], self.recv.at[self.used],
            device_id=peer, device_id_type=MESH,
        )
        self.used += 1
        copy.start()
        return copy


def dot(left, right, left_dim, right_dim):
    return lax.dot_general(left, right, (((left_dim,), (right_dim,)), ((), ())), preferred_element_type=jnp.float32)


def sigmoid(value):
    return 1.0 / (1.0 + jnp.exp(-value))


def packed(row):
    return jnp.concatenate([row[:, i : i + 128] for i in range(0, row.shape[1], 128)], axis=0)


def unpacked(block):
    return jnp.concatenate([block[i : i + 1] for i in range(block.shape[0])], axis=1)


def step_kernel(
    images, weights, roots, own_norms, pixel_mask, all_labels, bias,
    taps_out, reduce_out, head_out, totals_out, weights_out, roots_out,
    own_images, first, second, hidden_pad, grad_pad, turned_grad, taps, reduce_low, head_low,
    valid, used, divisor, norms, norms_held, pack_one, pack_two, pack_three, pack_four, held_one, held_two, held_three, held_four,
    tap_sums, core_in, first_in, partial, pooling, pooled_low, d_logits, d_act, head_buf, grad_buf, send, recv, local,
):
    (z, y, x, core), (nz, ny, nx, nc) = place()
    c, n = lax.axis_index("chan"), lax.axis_size("chan")
    f32, low = jnp.float32, jnp.bfloat16
    slots = used.shape[0]
    side = SIDE
    line = side * slots
    wide_line = (side + 1) * slots
    pixels = side * side
    rim = (side + 2) * slots
    body_rows = side * wide_line
    width = first.shape[1]
    depth = own_images.shape[-1]
    everyone = [
        at(lax.rem(z + i, nz), lax.rem(y + j, ny), lax.rem(x + k, nx), lax.rem(core + m, nc))
        for i in range(nz) for j in range(ny) for k in range(nx) for m in range(nc) if i + j + k + m
    ]
    greet(everyone)
    copies = Copies(send, recv)
    others = turned(c, n)
    across_z = lax.rem(z + nz // 2, nz)
    near_z = [z // (nz // 2) * (nz // 2) + lax.rem(lax.rem(z, nz // 2) + k, nz // 2) for k in range(1, nz // 2)]
    mate, mate_y = at(z, y, x, 1 - core), at(z, 1 - y, x, core)
    mates_x = [at(z, y, k, core) for k in turned(x, nx)]

    def begin_z(source, target, sem):
        keep = pltpu.make_async_copy(source.at[x, core], target.at[z, y, x, core], local.at[sem])
        keep.start()
        peers = [at(k, y, x, core) for k in [across_z] + near_z]
        return [keep] + [copies.start(source.at[x, core], target.at[z, y, x, core], peer) for peer in peers]

    def pass_z(target, begun):
        for copy in begun:
            copy.wait()
        part = target.at[across_z, y, x, core]
        return [copies.start(part, part, at(k, y, x, core)) for k in near_z]

    lane = lax.broadcasted_iota(jnp.int32, norms.shape, 1)
    own_width = own_norms.shape[1]
    mine = (lane >= c * own_width) & (lane < (c + 1) * own_width)
    norms[...] = jnp.where(mine, jnp.concatenate([own_norms[...]] * n, axis=1), 0.0)

    weights_z = pass_z(weights_out, begin_z(weights, weights_out, 0))
    norm_copies = [copies.start(norms, norms_held.at[k + 1], {"chan": other}) for k, other in enumerate(others)]
    image_copies = [[copies.start(images.at[k, j], own_images.at[c, j, pl.ds(0, line)], {"chan": k}) for k in others]
                    for j in range(side)]
    own = pltpu.make_async_copy(images.at[c], own_images.at[c, :, pl.ds(0, line)], local.at[2])
    own.start()
    norms_held[0] = norms[...]

    own_slots = pl.ds(pl.multiple_of(c * slots, slots), slots)
    mask = pixel_mask[own_slots, :].astype(f32)
    for p in range(pixels):
        valid[p * slots : (p + 1) * slots, :] = jnp.broadcast_to(mask[:, p : p + 1], (slots, 128))
    filled = jnp.broadcast_to(jnp.sum(mask, axis=1, keepdims=True), (slots, 128))
    used[...] = (filled > 0.0).astype(f32)
    divisor[...] = jnp.maximum(filled, 1.0)

    def clear(i, _):
        rows = pl.ds(pl.multiple_of(i * slots, slots), slots)
        hidden_pad[rows, :] = jnp.zeros((slots, width), low)
        grad_pad[rows, :] = jnp.zeros((slots, width), low)
        return 0

    lax.fori_loop(0, hidden_pad.shape[0] // slots, clear, 0)
    for k in range(n):
        for j in range(side):
            own_images[k, j, pl.ds(line, slots), :] = jnp.zeros((slots, depth), low)

    for copy in weights_z:
        copy.wait()
    part = weights_out.at[:, y, x, core]
    copies.start(part, part, mate_y).wait()
    part = weights_out.at[:, :, x, core]
    along_x = [copies.start(part, part, peer) for peer in mates_x]
    for copy in along_x:
        copy.wait()
    part = weights_out.at[:, :, :, core]
    copies.start(part, part, mate).wait()
    fetched = []
    start = 0
    for j, held in enumerate((taps, reduce_low, head_low)):
        size = held.shape[-1]
        copy = pltpu.make_async_copy(weights_out.at[:, :, :, :, :, pl.ds(start, size)], held, local.at[3 + j])
        copy.start()
        fetched.append(copy)
        start += size
    for copy in fetched:
        copy.wait()
    taps, reduce_low, head_low = (held.reshape(width, held.shape[-1]) for held in (taps, reduce_low, head_low))
    for copy in norm_copies:
        copy.wait()
    norm_rows = jnp.sum(norms_held[...], axis=0)
    gain_one, shift_one, gain_two, shift_two = (norm_rows[i : i + 1] for i in range(4))

    def line_rows(j):
        return pl.ds(pl.multiple_of(j * line, slots), line)

    def pixel_rows(p):
        return pl.ds(pl.multiple_of(p * slots, slots), slots)

    def padded_pixel(p):
        j = p // side
        return pl.ds(pl.multiple_of(rim + (p + j) * slots, slots), slots)

    def across(block):
        return jnp.concatenate([block] * (width // 128), axis=1)

    def fold(value):
        return jnp.sum(value.reshape(-1, 8, width), axis=0)

    def total_of(index):
        return jnp.sum(partial[index], axis=0, keepdims=True)

    def exchange(pack, held):
        pack_copies = [copies.start(pack, held.at[k + 1], peer) for k, peer in enumerate(everyone)]
        held[0] = pack[...]
        return pack_copies

    def settled(pack_copies, held):
        for copy in pack_copies:
            copy.wait()
        return jnp.sum(held[...], axis=0)

    def add_to_sums(ref):
        def add(p, _):
            value = ref[pixel_rows(p), :]
            kept = value * across(valid[pixel_rows(p), :])
            partial[0] += fold(kept)
            partial[1] += fold(kept * value)
            return 0

        return add

    own.wait()
    partial[...] = jnp.zeros(partial.shape, f32)
    for j in range(side):
        for copy in image_copies[j]:
            copy.wait()
        block = jnp.concatenate([own_images[k, j, pl.ds(0, line), :] for k in range(n)], axis=1)
        first[pl.ds(j * line, line), :] = dot(block, reduce_low[...], 1, 1)
        lax.fori_loop(j * side, (j + 1) * side, add_to_sums(first), 0)
    all_valid = jnp.sum(valid[...], axis=0, keepdims=True)
    pack_one[...] = jnp.concatenate(
        [packed(total_of(0)), packed(total_of(1)), all_valid, jnp.zeros((7, 128), f32)], axis=0)
    stats = settled(exchange(pack_one, held_one), held_one)
    rows = width // 128
    count = jnp.concatenate([stats[2 * rows : 2 * rows + 1]] * rows, axis=1)

    def norm_of(stats):
        mean = unpacked(stats[:rows]) / count
        scale = lax.rsqrt(unpacked(stats[rows : 2 * rows]) / count - mean * mean + EPS)
        return mean, scale

    mean_one, scale_one = norm_of(stats)
    roots_z = begin_z(roots, roots_out, 1)

    def activate(p, _):
        normed = (first[pixel_rows(p), :] - mean_one) * scale_one
        pre = gain_one * normed + shift_one
        act = pre * sigmoid(pre) * across(valid[pixel_rows(p), :])
        hidden_pad[padded_pixel(p), :] = act.astype(low)
        return 0

    lax.fori_loop(0, pixels, activate, 0)

    def conv_line(j, _):
        value = None
        for t in range(9):
            offset = (t // 3 - 1) * wide_line + (t % 3 - 1) * slots
            rows_in = pl.ds(pl.multiple_of(rim + j * wide_line + offset, slots), line)
            term = dot(hidden_pad[rows_in, :], taps[:, t * width : (t + 1) * width], 1, 1)
            value = term if value is None else value + term
        second[line_rows(j), :] = value
        return 0

    lax.fori_loop(0, side, conv_line, 0)
    roots_z = pass_z(roots_out, roots_z)
    partial[...] = jnp.zeros(partial.shape, f32)
    lax.fori_loop(0, pixels, add_to_sums(second), 0)
    pack_two[...] = jnp.concatenate([packed(total_of(0)), packed(total_of(1))], axis=0)
    stats = settled(exchange(pack_two, held_two), held_two)
    mean_two, scale_two = norm_of(stats)
    for copy in roots_z:
        copy.wait()
    across_half = roots_out.shape[-1] // 2
    left, right = pl.ds(0, across_half), pl.ds(across_half, across_half)
    part = roots_out.at[:, y, x, core, :, left]
    roots_a = [copies.start(part, part, peer) for peer in mates_x]
    part = roots_out.at[:, y, x, core, :, right]
    roots_b = [copies.start(part, part, mate_y)]

    pooling[...] = jnp.zeros(pooling.shape, f32)

    def pool(p, _):
        normed = (second[pixel_rows(p), :] - mean_two) * scale_two
        pre = gain_two * normed + shift_two
        sigma = sigmoid(pre)
        kept = across(valid[pixel_rows(p), :])
        slope = sigma * (1.0 + pre * (1.0 - sigma)) * kept
        pooling[0] += pre * sigma * kept
        pooling[1] += slope
        pooling[2] += slope * normed
        return 0

    lax.fori_loop(0, pixels, pool, 0)
    divide = across(divisor[...])
    pooled_low[...] = (pooling[0] / divide).astype(low)
    logits = dot(pooled_low[...], head_low[...], 1, 0) + bias[...]
    classes = logits.shape[1]
    index = lax.broadcasted_iota(jnp.int32, (slots, classes), 1)
    onehot = (index == all_labels[own_slots, :]).astype(f32)
    top = jnp.max(logits, axis=1, keepdims=True)
    log_total = jnp.log(jnp.sum(jnp.exp(logits - top), axis=1, keepdims=True)) + top
    picked = jnp.sum(onehot * logits, axis=1, keepdims=True)
    use = used[:, :1]
    loss = jnp.sum(use * (log_total - picked))
    d_logits[...] = (use * (jnp.exp(logits - log_total) - onehot) / SLOTS_DEV).astype(low)
    bias_sum = jnp.sum(d_logits[...].astype(f32), axis=0, keepdims=True)
    half = width // 2

    def to_pooled(m, _):
        rows_in = pl.ds(pl.multiple_of(m * half, half), half)
        d_act[:, rows_in] = dot(d_logits[...], head_low[rows_in, :], 1, 1) / across(divisor[...])[:, :half]
        return 0

    lax.fori_loop(0, 2, to_pooled, 0)
    at_class = lax.broadcasted_iota(jnp.int32, (1, classes), 1)
    bias_sum = jnp.where(at_class == classes - 1, loss, jnp.where(at_class == classes - 2, jnp.sum(use), bias_sum))
    pack_three[...] = jnp.concatenate(
        [packed(jnp.sum(d_act[...] * pooling[1], axis=0, keepdims=True)),
         packed(jnp.sum(d_act[...] * pooling[2], axis=0, keepdims=True)), packed(bias_sum)], axis=0)
    going = exchange(pack_three, held_three)

    def to_head(m, _):
        columns = pl.ds(pl.multiple_of(m * (classes // 2), 128), classes // 2)
        head_buf[:, columns] = dot(pooled_low[...], d_logits[:, columns], 0, 0)
        return 0

    lax.fori_loop(0, 2, to_head, 0)
    head_copy = pltpu.make_async_copy(head_buf, head_out, local.at[6])
    head_copy.start()
    totals_two = settled(going, held_three)
    shift_grad, gain_grad = unpacked(totals_two[:rows]), unpacked(totals_two[rows : 2 * rows])
    factor = gain_two * scale_two / count
    for copy in roots_a:
        copy.wait()
    part = roots_out.at[:, y, :, core, :, left]
    roots_a = [copies.start(part, part, mate_y)]
    for copy in roots_b:
        copy.wait()
    part = roots_out.at[:, :, x, core, :, right]
    roots_b = [copies.start(part, part, peer) for peer in mates_x]

    def leave_second(p, _):
        normed = (second[pixel_rows(p), :] - mean_two) * scale_two
        pre = gain_two * normed + shift_two
        sigma = sigmoid(pre)
        kept = across(valid[pixel_rows(p), :])
        d_pre = d_act[...] * kept * (sigma * (1.0 + pre * (1.0 - sigma)))
        d_z = factor * (count * d_pre - shift_grad - normed * gain_grad) * kept
        grad_pad[padded_pixel(p), :] = d_z.astype(low)
        return 0

    lax.fori_loop(0, pixels, leave_second, 0)

    partial[...] = jnp.zeros(partial.shape, f32)

    def spread_line(j, _):
        value = None
        for t in range(9):
            offset = (t // 3 - 1) * wide_line + (t % 3 - 1) * slots
            rows_in = pl.ds(pl.multiple_of(rim + j * wide_line - offset, slots), line)
            term = dot(grad_pad[rows_in, :], taps[:, t * width : (t + 1) * width], 1, 0)
            value = term if value is None else value + term
        second[line_rows(j), :] = value
        return 0

    lax.fori_loop(0, side, spread_line, 0)
    def enter_first(p, _):
        normed = (first[pixel_rows(p), :] - mean_one) * scale_one
        pre = gain_one * normed + shift_one
        sigma = sigmoid(pre)
        d_pre = second[pixel_rows(p), :] * across(valid[pixel_rows(p), :]) * (sigma * (1.0 + pre * (1.0 - sigma)))
        second[pixel_rows(p), :] = d_pre
        partial[0] += fold(d_pre)
        partial[1] += fold(d_pre * normed)
        return 0

    lax.fori_loop(0, pixels, enter_first, 0)
    pack_four[...] = jnp.concatenate([packed(total_of(0)), packed(total_of(1))], axis=0)
    going = exchange(pack_four, held_four)

    def turn(j, _):
        rows_in = pl.ds(pl.multiple_of(rim + j * wide_line, slots), wide_line)
        turned_grad[:, pl.ds(pl.multiple_of(j * wide_line, 128), wide_line)] = grad_pad[rows_in, :].T
        return 0

    lax.fori_loop(0, side, turn, 0)

    def leave(slot, target, sem):
        copy = pltpu.make_async_copy(grad_buf.at[slot], target, local.at[sem])
        copy.start()
        return copy

    half = nz // 2
    near = z // half * half + lax.rem(z + 1, half)
    kinds = "".join(chunk_rounds(9))
    core_going, first_going = [], []

    def part_of(t, mine):
        if kinds[t] == "x":
            return [(tap_sums.at[t, :, :, x if mine else lax.rem(x + 1, nx)], first_in.at[t])]
        if kinds[t] == "y":
            return [(tap_sums.at[t, :, y if mine else 1 - y], first_in.at[t])]
        return [(tap_sums.at[t, (z // half * half + lax.rem(z, half) if mine else near) % half + h * half],
                 first_in.at[t, pl.ds(2 * h, 2)]) for h in range(2)]

    def over_core(t):
        core_going[t].wait()
        for i in range(nz):
            tap_sums[t, i] += core_in[t, i]
        peer = {"x": at(z, y, lax.rem(x + 1, nx), core), "y": mate_y, "z": at(near, y, x, core)}[kinds[t]]
        first_going.append([copies.start(source, target, peer) for source, target in part_of(t, False)])

    for t in range(9):
        offset = (t // 3 - 1) * wide_line + (t % 3 - 1) * slots
        slot = t % 2
        shifted = hidden_pad.at[pl.ds(rim + offset, body_rows)]
        grad_buf[slot] = dot(turned_grad[...], shifted[...], 1, 0).reshape(grad_buf.shape[1:])
        core_going.append(copies.start(grad_buf.at[slot, :, :, :, 1 - core], core_in.at[t], mate))
        for i in range(nz):
            tap_sums[t, i] = grad_buf[slot, i, :, :, core]
        if t:
            over_core(t - 1)
    over_core(8)
    leaving = []

    for copy in roots_a + roots_b:
        copy.wait()
    part = roots_out.at[:, :, :, core]
    roots_core = copies.start(part, part, mate)
    totals_one = settled(going, held_four)
    shift_sum, gain_sum = unpacked(totals_one[:rows]), unpacked(totals_one[rows : 2 * rows])
    factor_one = gain_one * scale_one / count

    def leave_first(p, _):
        normed = (first[pixel_rows(p), :] - mean_one) * scale_one
        kept = across(valid[pixel_rows(p), :])
        d_z = factor_one * (count * second[pixel_rows(p), :] - shift_sum - normed * gain_sum) * kept
        grad_pad[padded_pixel(p), :] = d_z.astype(low)
        return 0

    lax.fori_loop(0, pixels, leave_first, 0)
    lax.fori_loop(0, side, turn, 0)
    per = width // depth
    for t in range(n // per):
        slot = (9 + t) % 2
        if t >= 2:
            leaving[t - 2].wait()
        block = jnp.concatenate([own_images[t * per + k].reshape(body_rows, depth) for k in range(per)], axis=1)
        grad_buf[slot] = dot(turned_grad[...], block, 1, 0).reshape(grad_buf.shape[1:])
        leaving.append(leave(slot, reduce_out.at[:, :, :, :, :, pl.ds(t * width, width)], 7 + slot))
    taps_going = []
    for t in range(9):
        for copy in first_going[t]:
            copy.wait()
        for h, (kept, landed) in enumerate(part_of(t, True)):
            kept[...] += landed[...]
            copy = pltpu.make_async_copy(
                kept, taps_out.at[t, pl.ds(2 * h, 2)] if kinds[t] == "z" else taps_out.at[t], local.at[9 + 2 * t + h])
            copy.start()
            taps_going.append(copy)
    for copy in taps_going:
        copy.wait()
    totals_out[...] = jnp.concatenate([totals_two, totals_one], axis=0)
    head_copy.wait()
    roots_core.wait()
    for copy in leaving[-2:]:
        copy.wait()


def local_step(images, weights, roots, norms, pixel_mask, labels, bias):
    n, nb = lax.axis_size("chan"), lax.axis_size("batch")
    nz, nx = n // 2, nb // 2
    slots, width = pixel_mask.shape[0] // n, norms.shape[1] * n
    line, depth, classes = SIDE * slots, images.shape[-1], bias.shape[1]
    f32, low = jnp.float32, jnp.bfloat16
    rows = weights.shape[0] // nb
    grids = ((SIDE * (SIDE + 1) + 2 * (SIDE + 2)) * slots, width)
    shape = jax.ShapeDtypeStruct
    gathered = lambda a: shape((nz, 2, nx, 2, rows, a.shape[1]), a.dtype)
    quarters = lambda a: a.reshape(nx, 2, rows, a.shape[1])
    held = lambda k: pltpu.VMEM((n * nb, k, 128), f32)
    pack = lambda k: pltpu.VMEM((k, 128), f32)
    count = 2 * (nz - 1) + (SIDE + 1) * (n - 1) + (1 + (nx - 1) + 1) + (2 * nx + 1) + 4 * (n * nb - 1) + 27
    two = 2 * width // 128
    three = two + classes // 128
    weight = lambda size: pltpu.VMEM((nz, 2, nx, 2, rows, size), low)
    spatial, reduce, head, totals, weights_full, roots_full = pl.pallas_call(
        step_kernel,
        out_shape=(
            shape((9, nz, 2, rows, width), f32),
            shape((nz, 2, nx, 2, rows, n * depth), f32),
            shape((width, classes), f32),
            shape((two + three, 128), f32),
            gathered(weights),
            gathered(roots),
        ),
        in_specs=[ANY, ANY, ANY, VMEM, VMEM, VMEM, VMEM],
        out_specs=(ANY, ANY, ANY, VMEM, ANY, ANY),
        scratch_shapes=[
            pltpu.VMEM((n, SIDE, line + slots, depth), low),
            pltpu.VMEM((SIDE * line, width), f32),
            pltpu.VMEM((SIDE * line, width), f32),
            pltpu.VMEM(grids, low),
            pltpu.VMEM(grids, low),
            pltpu.VMEM((width, SIDE * (line + slots)), low),
            weight(9 * width), weight(n * depth), weight(classes),
            pltpu.VMEM((SIDE * line, 128), f32),
            pltpu.VMEM((slots, 128), f32),
            pltpu.VMEM((slots, 128), f32),
            pltpu.VMEM((norms.shape[0], width), f32),
            pltpu.VMEM((n, norms.shape[0], width), f32),
            pack(two + 8), pack(two), pack(three), pack(two),
            held(two + 8), held(two), held(three), held(two),
            pltpu.VMEM((9, nz, 2, nx, rows, width), f32),
            pltpu.VMEM((9, nz, 2, nx, rows, width), f32),
            pltpu.VMEM((9, nz, 2, rows, width), f32),
            pltpu.VMEM((2, 8, width), f32),
            pltpu.VMEM((3, slots, width), f32),
            pltpu.VMEM((slots, width), low),
            pltpu.VMEM((slots, classes), low),
            pltpu.VMEM((slots, width), f32),
            pltpu.VMEM((width, classes), f32),
            pltpu.VMEM((2, nz, 2, nx, 2, rows, width), f32),
            DMA((count,)), DMA((count,)), DMA((27,)),
        ],
        compiler_params=pltpu.CompilerParams(collective_id=0, has_side_effects=True, vmem_limit_bytes=60 << 20),
        name="step",
    )(images.reshape(n, SIDE, line, depth), quarters(weights), quarters(roots), norms, pixel_mask, labels, bias)
    return spatial, reduce, head, totals[:three], totals[three:], roots_full.reshape(width, roots.shape[1])


def chunk_rounds(count):
    rounds = []
    while count > 0:
        rounds.append(ORDERS[len(rounds) % len(ORDERS)][:count])
        count -= len(rounds[-1])
    return rounds


def settle_kernel(
    chunks, taps, reduce, head, mask, left_root, roots, own, left_part, right_part, outer_out, size,
    full, factors, lefts, rights, outers, squares, held, sums, core_in, first_in, second_in, near_in, across_in,
    final, final_low, send, recv, local,
):
    (z, y, x, core), (nz, ny, nx, nc) = place()
    half = nz // 2
    across_z = lax.rem(z + half, nz)
    base_z = z // half * half
    near_z = [base_z + lax.rem(lax.rem(z, half) + k, half) for k in range(1, half)]
    others_x = turned(x, nx)
    mate, mate_y = at(z, y, x, 1 - core), at(z, 1 - y, x, core)
    mates_x = [at(z, y, k, core) for k in others_x]
    mates_near = [at(k, y, x, core) for k in near_z]
    mate_across = at(across_z, y, x, core)
    c, n = lax.axis_index("chan"), lax.axis_size("chan")
    others = [{"chan": k} for k in turned(c, n)]
    greet(others + mates_x + [mate])
    copies = Copies(send, recv)
    f32, low = jnp.float32, jnp.bfloat16
    rows, width = left_root.shape[1:]
    tiles_one = reduce.shape[-1] // width
    n_taps = taps.shape[0]
    sources = ((reduce, n_taps * width), (head, n_taps * width + reduce.shape[-1]))
    wide = n_taps * width + reduce.shape[-1]
    used_local = [0]

    def keep(source, target):
        copy = pltpu.make_async_copy(source, target, local.at[used_local[0]])
        used_local[0] += 1
        copy.start()
        return copy

    roots_in = [keep(roots, factors)]
    pick = (lax.broadcasted_iota(jnp.int32, (rows, width), 1)
            == lax.broadcasted_iota(jnp.int32, (rows, width), 0) + c * rows).astype(low)
    squares[...] = jnp.zeros(squares.shape, f32)
    outgoing = []

    def two_parts(value):
        high = value.astype(low)
        return [high, (value - high.astype(f32)).astype(low)]

    def multiply(t, columns):
        grad = full[:, :, :, :, :, columns].reshape(width, width)
        mine = full[z, y, :, :, :, columns].reshape(rows, width)
        first = dot(jnp.concatenate([mine, pick], axis=0), grad, 1, 1)
        lefts[t] = first[:rows]
        second = dot(jnp.concatenate([first[rows:].astype(low)] + two_parts(left_root[t]), axis=0), grad, 1, 0)
        rights[t] = second[:rows]
        inner = second[rows : 2 * rows] + second[2 * rows :]
        third = dot(jnp.concatenate(two_parts(inner), axis=0), factors[:, t * width : (t + 1) * width], 1, 0)
        value = third[:rows] + third[rows:]
        outers[t] = value
        squares[t : t + 1, :] = jnp.full((1, 128), jnp.sum(value * value), f32)
        outgoing.extend(keep(a.at[t], b.at[t]) for a, b in ((lefts, left_part), (rights, right_part), (outers, outer_out)))

    def wait(going):
        for copy in going:
            copy.wait()

    def enter(start, size):
        columns = pl.ds(start, size)
        going = []
        for source, first_column in sources:
            begin, end = max(start, first_column), min(start + size, first_column + source.shape[-1])
            if begin < end:
                taken, landed = pl.ds(begin - first_column, end - begin), pl.ds(begin, end - begin)
                going.append(copies.start(source.at[:, :, :, 1 - core, :, taken], core_in.at[:, :, :, :, landed], mate))
                going.append(keep(source.at[:, :, :, core, :, taken], sums.at[:, :, :, :, landed]))
        yield
        wait(going)
        for i in range(nz):
            for j in range(ny):
                for k in range(nx):
                    sums[i, j, k, :, columns] += core_in[i, j, k, :, columns]

    def settled(start, last_in, columns):
        total = (sums[z, y, x, :, columns] + last_in) * mask[:, columns]
        final[:, columns] = total
        kept = [keep(final.at[:, columns], own.at[x, core, :, columns])]
        kept += [copies.start(final.at[:, columns], own.at[x, core, :, columns], peer) for peer in mates_x]
        if start < wide:
            final_low[:, columns] = total.astype(low)
            return kept, [keep(final_low.at[:, columns], full.at[z, y, x, core, :, columns])]
        return kept, []

    def own_core(kept, columns):
        wait(kept)
        part = own.at[:, core, :, columns]
        return copies.start(part, part, mate)

    def block_of(start, columns):
        t = start // width
        if roots_in:
            roots_in.pop().wait()
        multiply(t + tiles_one if t < n_taps else t - n_taps, columns)

    def chunk_z(start, size):
        columns = pl.ds(start, size)
        if start < n_taps * width:
            going = [keep(taps.at[start // width, pl.ds(2 * h, 2)], sums.at[lax.rem(z, half) + h * half, :, :, :, columns])
                     for h in range(2)]
            yield
            wait(going)
        else:
            yield from enter(start, size)
            going = []
            for t, k in enumerate(near_z):
                for h in range(2):
                    there = lax.rem(k, half) + h * half
                    going.append(copies.start(
                        sums.at[there, :, :, :, columns], first_in.at[t, pl.ds(2 * h, 2), :, :, columns], mates_near[t]))
            yield
            wait(going)
            for t in range(half - 1):
                for h in range(2):
                    for j in range(ny):
                        for k in range(nx):
                            sums[lax.rem(z, half) + h * half, j, k, :, columns] += first_in[t, 2 * h + j, k, :, columns]
        landing = [second_in.at[0, pl.ds(nx * j, nx), :, columns] for j in range(ny)]
        going = [copies.start(sums.at[across_z, j, :, :, columns], landing[j], mate_across) for j in range(ny)]
        yield
        wait(going)
        for j in range(ny):
            for k in range(nx):
                sums[z, j, k, :, columns] += second_in[0, nx * j + k, :, columns]
        going = [copies.start(sums.at[z, :, k, :, columns], near_in.at[t, :, :, columns], mates_x[t])
                 for t, k in enumerate(others_x)]
        yield
        wait(going)
        for t in range(nx - 1):
            for j in range(ny):
                sums[z, j, x, :, columns] += near_in[t, j, :, columns]
        going = [copies.start(sums.at[z, 1 - y, x, :, columns], across_in.at[:, columns], mate_y)]
        yield
        wait(going)
        kept, going = settled(start, across_in[:, columns], columns)
        going += [copies.start(final_low.at[:, columns], full.at[z, y, x, core, :, columns], peer) for peer in mates_x]
        yield
        last = [own_core(kept, columns)]
        wait(going)
        part = full.at[z, y, :, core, :, columns]
        going = [copies.start(part, part, mate_y)]
        yield
        wait(going)
        part = full.at[z, :, :, core, :, columns]
        going = [copies.start(part, part, peer) for peer in [mate_across] + mates_near]
        yield
        wait(going)
        part = full.at[across_z, :, :, core, :, columns]
        going = [copies.start(part, part, peer) for peer in mates_near]
        yield
        wait(going)
        part = full.at[:, :, :, core, :, columns]
        last.append(copies.start(part, part, mate))
        yield
        wait(last)
        block_of(start, columns)

    def chunk(start, size, x_first):
        columns = pl.ds(start, size)
        if start < n_taps * width:
            going = [keep(taps.at[start // width], sums.at[:, :, x, :, columns] if x_first else sums.at[:, y, :, :, columns])]
            yield
            wait(going)
        else:
            yield from enter(start, size)
            if x_first:
                going = [copies.start(sums.at[:, :, k, :, columns], first_in.at[t, :, :, :, columns], mates_x[t])
                         for t, k in enumerate(others_x)]
            else:
                going = [copies.start(sums.at[:, 1 - y, :, :, columns], first_in.at[0, :, :, :, columns], mate_y)]
            yield
            wait(going)
            for i in range(nz):
                for j in range(2):
                    if x_first:
                        sums[i, j, x, :, columns] += first_in[0, i, j, :, columns]
                    else:
                        sums[i, y, j, :, columns] += first_in[0, i, j, :, columns]
        going = []
        if x_first:
            going.append(copies.start(sums.at[:, 1 - y, x, :, columns], second_in.at[0, :, :, columns], mate_y))
        else:
            for t, k in enumerate(others_x):
                going.append(copies.start(sums.at[:, y, k, :, columns], second_in.at[t, :, :, columns], mates_x[t]))
        yield
        wait(going)
        for t in range(1 if x_first else nx - 1):
            for i in range(nz):
                sums[i, y, x, :, columns] += second_in[t, i, :, columns]
        going = []
        for t, k in enumerate(near_z):
            for h in range(2):
                there = lax.rem(k + h * half, nz)
                going.append(copies.start(sums.at[there, y, x, :, columns], near_in.at[t, h, :, columns], mates_near[t]))
        yield
        wait(going)
        for t in range(half - 1):
            for h in range(2):
                sums[lax.rem(z + h * half, nz), y, x, :, columns] += near_in[t, h, :, columns]
        going = [copies.start(sums.at[across_z, y, x, :, columns], across_in.at[:, columns], mate_across)]
        yield
        wait(going)
        kept, going = settled(start, across_in[:, columns], columns)
        if start < wide:
            going += [copies.start(final_low.at[:, columns], full.at[z, y, x, core, :, columns], peer)
                      for peer in [mate_across] + mates_near]
        yield
        rows_core = [own_core(kept, columns)]
        if start < wide:
            wait(going)
            part = full.at[across_z, y, x, core, :, columns]
            going = [copies.start(part, part, peer) for peer in mates_near]
            yield
            wait(going)
            part = full.at[:, y, x, core, :, columns]
            going = [copies.start(part, part, peer) for peer in (mates_x if x_first else [mate_y])]
            yield
            wait(going)
            part = full.at[:, y, :, core, :, columns] if x_first else full.at[:, :, x, core, :, columns]
            going = [copies.start(part, part, peer) for peer in ([mate_y] if x_first else mates_x)]
            yield
            wait(going)
            part = full.at[:, :, :, core, :, columns]
            rows_core.append(copies.start(part, part, mate))
        yield
        wait(rows_core)
        if start < wide:
            block_of(start, columns)

    rounds = [[chunk_z(*c[:2]) if c[2] == "z" and c[0] < wide else chunk(*c[:2], c[2] != "y") for c in some] for some in chunks]
    begun, active = [], []
    while rounds or begun or active:
        active += begun
        begun = rounds.pop(0) if rounds else []
        for going in begun:
            next(going)
        for going in active[::-1]:
            try:
                next(going)
            except StopIteration:
                active.remove(going)
    going = [copies.start(squares, held.at[k + 1], peer) for k, peer in enumerate(others)]
    held[0] = squares[...]
    wait(going + outgoing)
    size[...] = jnp.sqrt(jnp.sum(held[...], axis=0) / (width * width) + 1e-06)


def settle(taps, reduce, head, mask, left_root, roots):
    nz, nx, n = lax.axis_size("chan") // 2, lax.axis_size("batch") // 2, lax.axis_size("chan")
    blocks, own_rows, width = left_root.shape
    rows = width // (4 * nz * nx)
    wide = taps.shape[0] * width + reduce.shape[-1]
    total = wide + head.shape[1]
    split = lambda a: a.reshape(nz, 2, nx, 2, rows, a.shape[1])
    f32, low = jnp.float32, jnp.bfloat16
    chunks, start = [], 0
    for kinds in chunk_rounds(total // width):
        chunks.append([(start + i * width, width, kind) for i, kind in enumerate(kinds)])
        start += len(kinds) * width
    near = nz // 2 - 1
    first = max(nx - 1, nx // 2)
    count = (total // width) * (4 + first + max(nx - 1, 1) + 2 * near + 1 + (nx - 1) + 1 + near + 1 + near + nx + 1) + n
    product = jax.ShapeDtypeStruct((blocks, own_rows, width), f32)
    padded = (blocks + 7) // 8 * 8
    own, left_part, right_part, outer, size = pl.pallas_call(
        functools.partial(settle_kernel, chunks),
        out_shape=(
            jax.ShapeDtypeStruct((nx, 2, rows, total), f32), product, product, product,
            jax.ShapeDtypeStruct((padded, 128), f32),
        ),
        in_specs=[ANY, ANY, ANY, VMEM, VMEM, ANY],
        out_specs=(ANY,) * 4 + (VMEM,),
        scratch_shapes=[
            pltpu.VMEM((nz, 2, nx, 2, rows, wide), low),
            pltpu.VMEM(roots.shape, low),
            pltpu.VMEM(product.shape, f32),
            pltpu.VMEM(product.shape, f32),
            pltpu.VMEM(product.shape, f32),
            pltpu.VMEM((padded, 128), f32),
            pltpu.VMEM((n, padded, 128), f32),
            pltpu.VMEM((nz, 2, nx, rows, total), f32),
            pltpu.VMEM((nz, 2, nx, rows, total), f32),
            pltpu.VMEM((first, nz, 2, rows, total), f32),
            pltpu.VMEM((max(nx - 1, 1), nz, rows, total), f32),
            pltpu.VMEM((near, 2, rows, total), f32),
            pltpu.VMEM((rows, total), f32),
            pltpu.VMEM((rows, total), f32),
            pltpu.VMEM((rows, wide), low),
            DMA((count,)), DMA((count,)), DMA((7 * (total // width) + 4,)),
        ],
        compiler_params=pltpu.CompilerParams(collective_id=1, has_side_effects=True, vmem_limit_bytes=60 << 20),
        name="settle",
    )(taps, reduce, split(head), mask, left_root, roots)
    return own.reshape(own_rows, total), left_part, right_part, outer, size


def finish_kernel(
    size, head_weight, head_first, head_second,
    own, left_part, right_part, outer, left_stats, right_stats, reduce_weight, spatial_weight, reduce_mask, spatial_mask,
    head_new, head_first_new, head_second_new,
    reduce_grad, spatial_grad, reduce_new, spatial_new, left_new, right_new,
    own_rows, lefts, rights, outers, left_kept, right_kept, weights, masks, arrive, leave,
):
    blocks, rows, width = outers.shape
    c_in, taps = reduce_weight.shape[1], spatial_weight.shape[1]
    tiles_one = c_in // width
    groups = [(0, tiles_one)] + [(t, min(t + 3, blocks)) for t in range(tiles_one, blocks, 3)]
    every = [pltpu.make_async_copy(own, own_rows, arrive.at[0, 7])]
    coming = []
    for g, (begin, end) in enumerate(groups):
        some, columns = pl.ds(begin, end - begin), pl.ds(begin * width, (end - begin) * width)
        theirs = pl.ds((begin if g == 0 else begin - tiles_one) * width, (end - begin) * width)
        pairs = [(a.at[some], b.at[some]) for a, b in (
            (left_part, lefts), (right_part, rights), (outer, outers), (left_stats, left_kept), (right_stats, right_kept))]
        pairs += [((reduce_weight if g == 0 else spatial_weight).at[:, theirs], weights.at[:, columns]),
                  ((reduce_mask if g == 0 else spatial_mask).at[:, theirs], masks.at[:, columns])]
        coming.append([pltpu.make_async_copy(a, b, arrive.at[g, i]) for i, (a, b) in enumerate(pairs)])
    for copy in every + [copy for group in coming for copy in group]:
        copy.start()
    going = []

    def out(source, target):
        copy = pltpu.make_async_copy(source, target, leave.at[len(going)])
        copy.start()
        going.append(copy)

    every[0].wait()
    out(own_rows.at[:, pl.ds(0, taps)], spatial_grad)
    out(own_rows.at[:, pl.ds(taps, c_in)], reduce_grad)
    head_grad = own_rows[:, taps + c_in : taps + c_in + head_weight.shape[1]]
    head_new[...], head_first_new[...], head_second_new[...] = adam_step(
        head_weight[...], head_grad, head_first[...], head_second[...], 0.04, 0.1)
    for g, (begin, end) in enumerate(groups):
        for copy in coming[g]:
            copy.wait()

        def block(t, _):
            columns = pl.ds(pl.multiple_of(t * width, width), width)
            lefts[t] = 0.95 * left_kept[t] + lefts[t]
            rights[t] = 0.95 * right_kept[t] + rights[t]
            step = outers[t] / jnp.concatenate([size[pl.ds(t, 1), :]] * (width // 128), axis=1)
            weight = weights[:, columns]
            weights[:, columns] = weight - 0.02 * masks[:, columns].astype(jnp.float32) * (step + 0.1 * weight)
            return 0

        lax.fori_loop(begin, end, block, 0)
        some, columns = pl.ds(begin, end - begin), pl.ds(begin * width, (end - begin) * width)
        theirs = pl.ds((begin if g == 0 else begin - tiles_one) * width, (end - begin) * width)
        out(lefts.at[some], left_new.at[some])
        out(rights.at[some], right_new.at[some])
        out(weights.at[:, columns], (reduce_new if g == 0 else spatial_new).at[:, theirs])
    for copy in going:
        copy.wait()


def finish(own, left_part, right_part, outer, size, left_stats, right_stats,
           reduce_weight, spatial_weight, reduce_mask, spatial_mask, head_weight, head_first, head_second):
    blocks, rows, width = left_stats.shape
    like = lambda a: jax.ShapeDtypeStruct(a.shape, jnp.float32)
    wide = reduce_weight.shape[1] + spatial_weight.shape[1]
    products = pltpu.VMEM(left_stats.shape, jnp.float32)
    groups = 1 + -(-(spatial_weight.shape[1] // width) // 3)
    head_new, head_first_new, head_second_new, *rest = pl.pallas_call(
        finish_kernel,
        out_shape=(like(head_weight), like(head_weight), like(head_weight), like(reduce_weight), like(spatial_weight),
                   like(reduce_weight), like(spatial_weight), like(left_stats), like(left_stats)),
        in_specs=[VMEM] * 4 + [ANY] * 10,
        out_specs=(VMEM,) * 3 + (ANY,) * 6,
        scratch_shapes=[pltpu.VMEM(own.shape, jnp.float32)] + [products] * 5
        + [pltpu.VMEM((rows, wide), jnp.float32), pltpu.VMEM((rows, wide), jnp.int32),
           DMA((groups, 8)), DMA((2 + 3 * groups,))],
        compiler_params=pltpu.CompilerParams(vmem_limit_bytes=60 << 20),
        name="finish",
    )(size, head_weight, head_first, head_second, own, left_part, right_part, outer, left_stats, right_stats,
      reduce_weight, spatial_weight, reduce_mask, spatial_mask)
    return *rest, head_new, head_first_new, head_second_new


def silu_slope(pre):
    sigma = jax.nn.sigmoid(pre)
    return sigma * (1.0 + pre * (1.0 - sigma))


def adam_step(param, grad, first, second, rate, decay):
    first = 0.9 * first + 0.1 * grad
    second = 0.999 * second + 0.001 * grad * grad
    mhat = first / (1.0 - 0.9**STEP)
    vhat = second / (1.0 - 0.999**STEP)
    return (param - rate * (mhat / (jnp.sqrt(vhat) + 1e-08) + decay * param), first, second)


def own_part(array, axis, name="chan"):
    size = array.shape[axis] // lax.axis_size(name)
    return lax.dynamic_slice_in_dim(array, lax.axis_index(name) * size, size, axis)


def body(
    images,
    pixel_mask,
    labels,
    reduce_weight,
    reduce_mask,
    spatial_weight,
    spatial_mask,
    head_weight,
    head_bias,
    norm_params,
    left_stats,
    right_stats,
    left_root,
    input_side_roots,
    head_first,
    head_second,
    bias_first,
    bias_second,
    norm_first,
    norm_second,
):
    n = lax.axis_size("chan")
    pixels, channels = images.shape[1:]
    side = SIDE
    rows_out, c_in = reduce_weight.shape
    width = left_stats.shape[2]
    classes = head_weight.shape[1]
    padded = 1024
    slots = images.shape[0] // n
    low = jnp.bfloat16
    f32 = jnp.float32
    reduce_float = reduce_mask.astype(f32)
    spatial_float = spatial_mask.astype(f32)

    by_pixel = images.reshape(n, slots, pixels, channels).transpose(0, 2, 1, 3)
    weights = jnp.concatenate(
        [(spatial_weight * spatial_float).astype(low), (reduce_weight * reduce_float).astype(low),
         jnp.pad(head_weight.astype(low), ((0, 0), (0, padded - classes)))], axis=1)
    roots = input_side_roots.astype(low).transpose(1, 0, 2).reshape(rows_out, -1)
    taps_local, reduce_local, head_local, sums_two, sums_one, roots_full = local_step(
        by_pixel, weights, roots, norm_params, pixel_mask, labels[:, None],
        jnp.pad(head_bias, (0, padded - classes), constant_values=-1e30)[None])

    mask_rows = jnp.concatenate([spatial_float, reduce_float, jnp.ones((rows_out, padded), f32)], axis=1)
    own, *products = settle(taps_local, reduce_local, head_local, own_part(mask_rows, 0, "batch"), left_root, roots_full)
    of_norms = jnp.stack([a.reshape(-1) for a in (sums_one[4:], sums_one[:4], sums_two[4:8], sums_two[:4])])
    norm_gain_gradient = own_part(of_norms, 1)
    of_head = sums_two[8:].reshape(-1)
    bias_grad = of_head[:classes]
    loss_sum, slot_count = of_head[-1], of_head[-2]
    (reduce_grad, spatial_grad, reduce_new, spatial_new, left_new, right_new, head_new, head_first_new,
     head_second_new) = finish(
        own, *products, left_stats, right_stats, reduce_weight, spatial_weight, reduce_mask, spatial_mask,
        head_weight, head_first, head_second)
    bias_new, bias_first_new, bias_second_new = adam_step(head_bias, bias_grad, bias_first, bias_second, 0.1, 0.0)
    norm_new, norm_first_new, norm_second_new = adam_step(
        norm_params, norm_gain_gradient, norm_first, norm_second, 0.1, 0.0)
    return (
        loss_sum,
        slot_count,
        reduce_grad,
        spatial_grad,
        reduce_new,
        spatial_new,
        left_new,
        right_new,
        head_new,
        head_first_new,
        head_second_new,
        bias_new,
        bias_first_new,
        bias_second_new,
        norm_new,
        norm_first_new,
        norm_second_new,
    )


FULL_PRECISION = lax.Precision.HIGHEST
BOTH = ("chan", "batch")


def conv_grid(grid, taps, spec):
    return lax.conv_general_dilated(
        grid, taps, (1, 1), ((1, 1), (1, 1)), dimension_numbers=spec,
        preferred_element_type=jnp.float32,
    )


def plain_norm_forward(pre_norm, gain, shift, valid):
    first_sum = jnp.sum(pre_norm * valid, axis=(0, 1))
    second_sum = jnp.sum(pre_norm * pre_norm * valid, axis=(0, 1))
    first_sum, second_sum, count = lax.psum((first_sum, second_sum, jnp.sum(valid)), BOTH)
    mean = first_sum / count
    scale = lax.rsqrt(second_sum / count - mean * mean + EPS)
    normed = (pre_norm - mean) * scale
    pre = gain * normed + shift
    return (jax.nn.silu(pre) * valid, (normed, pre, scale, count))


def plain_norm_backward(grad_act, kept, gain, valid):
    normed, pre, scale, count = kept
    d_pre = grad_act * valid * silu_slope(pre)
    shift_gradient, gain_grad = lax.psum(
        (jnp.sum(d_pre, axis=(0, 1)), jnp.sum(d_pre * normed, axis=(0, 1))), BOTH
    )
    d_input = gain * scale / count * (count * d_pre - shift_gradient - normed * gain_grad) * valid
    return (d_input, gain_grad, shift_gradient)


def plain_own_part(array, parts, axis=0):
    size = array.shape[axis] // parts
    return lax.dynamic_slice_in_dim(array, lax.axis_index("chan") * size, size, axis)


def plain_body(
    images,
    pixel_mask,
    labels,
    reduce_weight,
    reduce_mask,
    spatial_weight,
    spatial_mask,
    head_weight,
    head_bias,
    norm_params,
    left_stats,
    right_stats,
    left_root,
    input_side_roots,
    head_first,
    head_second,
    bias_first,
    bias_second,
    norm_first,
    norm_second,
):
    parts = lax.axis_size("chan")
    pixels = images.shape[1]
    side = SIDE
    rows_out = reduce_weight.shape[0]
    width = left_stats.shape[2]
    classes = head_weight.shape[1]
    own_images = lax.all_to_all(images, "chan", 0, 2, tiled=True)
    slots = own_images.shape[0]
    reduce_float = reduce_mask.astype(jnp.float32)
    spatial_float = spatial_mask.astype(jnp.float32)
    gather = lambda a, axis: lax.all_gather(a, "chan", axis=axis, tiled=True)
    reduce_low = gather((reduce_weight * reduce_float).astype(jnp.bfloat16), 0)
    spatial_low = gather((spatial_weight * spatial_float).astype(jnp.bfloat16), 0)
    head_low = gather(head_weight.astype(jnp.bfloat16), 0)
    norm_full = gather(norm_params, 1)
    right_factor_full = gather(input_side_roots, 1)
    valid = plain_own_part(pixel_mask, parts).astype(jnp.float32)[:, :, None]
    own_labels = plain_own_part(labels, parts)
    filled = jnp.sum(valid[:, :, 0], axis=1)
    divisor = jnp.maximum(filled, 1.0)
    used = (filled > 0.0).astype(jnp.float32)
    taps = spatial_low.reshape(width, 3, 3, width)
    first_pre = jnp.einsum("spc,oc->spo", own_images, reduce_low, preferred_element_type=jnp.float32)
    first_act, first_kept = plain_norm_forward(first_pre, norm_full[0], norm_full[1], valid)
    hidden = first_act.astype(jnp.bfloat16).reshape(slots, side, side, width)
    second_pre = conv_grid(hidden, taps, ("NHWC", "OHWI", "NHWC")).reshape(slots, pixels, width)
    second_act, second_kept = plain_norm_forward(second_pre, norm_full[2], norm_full[3], valid)
    pooled = (jnp.sum(second_act, axis=1) / divisor[:, None]).astype(jnp.bfloat16)
    logits = jnp.dot(pooled, head_low, preferred_element_type=jnp.float32) + head_bias
    onehot = (jnp.arange(classes)[None, :] == own_labels[:, None]).astype(jnp.float32)
    log_total = jax.nn.logsumexp(logits, axis=1)
    picked = jnp.sum(onehot * logits, axis=1)
    loss_local = jnp.sum(used * (log_total - picked))
    d_logits = (used[:, None] * (jnp.exp(logits - log_total[:, None]) - onehot) / SLOTS_DEV).astype(
        jnp.bfloat16
    )
    head_grad = jnp.einsum("so,sc->oc", pooled, d_logits, preferred_element_type=jnp.float32)
    bias_grad = jnp.sum(d_logits.astype(jnp.float32), axis=0)
    d_pooled = jnp.einsum("sc,oc->so", d_logits, head_low, preferred_element_type=jnp.float32)
    d_act = jnp.broadcast_to((d_pooled / divisor[:, None])[:, None, :], second_act.shape)
    d_second, gain_two, shift_two = plain_norm_backward(d_act, second_kept, norm_full[2], valid)
    d_second = d_second.astype(jnp.bfloat16).reshape(slots, side, side, width)
    spatial_local = lax.conv_general_dilated(
        hidden, d_second, (1, 1), ((1, 1), (1, 1)), dimension_numbers=("CHWN", "IHWO", "NHWC"),
        preferred_element_type=jnp.float32,
    )
    spatial_local = spatial_local.transpose(3, 1, 2, 0).reshape(width, 9 * width)
    d_hidden = conv_grid(
        d_second, taps[:, ::-1, ::-1, :], ("NHWC", "IHWO", "NHWC")
    ).reshape(slots, pixels, width)
    d_first, gain_one, shift_one = plain_norm_backward(d_hidden, first_kept, norm_full[0], valid)
    d_first = d_first.astype(jnp.bfloat16)
    reduce_local = jnp.einsum("spc,spo->oc", own_images, d_first, preferred_element_type=jnp.float32)
    scatter = lambda a: lax.psum_scatter(a, "chan", scatter_dimension=0, tiled=True)
    reduce_grad, spatial_grad, head_grad = scatter(reduce_local), scatter(spatial_local), scatter(head_grad)
    reduce_grad, spatial_grad, head_grad = lax.psum((reduce_grad, spatial_grad, head_grad), "batch")
    reduce_grad = reduce_grad * reduce_float
    spatial_grad = spatial_grad * spatial_float
    bias_grad, loss_sum, slot_count = lax.psum((bias_grad, loss_local, jnp.sum(used)), BOTH)
    norm_gain_gradient = plain_own_part(jnp.stack([gain_one, shift_one, gain_two, shift_two], axis=0), parts, 1)
    tiles_one = reduce_weight.shape[1] // width
    blocks = jnp.concatenate(
        [
            reduce_grad.reshape(rows_out, tiles_one, width).transpose(1, 0, 2),
            spatial_grad.reshape(rows_out, 9, width).transpose(1, 0, 2),
        ],
        axis=0,
    )
    blocks_full = gather(blocks, 1)
    left_new = 0.95 * left_stats + jnp.einsum(
        "tak,tbk->tab", blocks, blocks_full, precision=FULL_PRECISION
    )
    own_columns = plain_own_part(blocks_full, parts, 2)
    right_new = 0.95 * right_stats + jnp.einsum(
        "tki,tkb->tib", own_columns, blocks_full, precision=FULL_PRECISION
    )
    matrix_product = jnp.einsum("tak,tkb->tab", left_root, blocks_full, precision=FULL_PRECISION)
    matrix_product = jnp.einsum(
        "ghk,gkl->ghl", matrix_product, right_factor_full, precision=FULL_PRECISION
    )
    squares = lax.psum(jnp.sum(matrix_product * matrix_product, axis=(1, 2)), "chan")
    step = matrix_product / jnp.sqrt(squares / (width * width) + 1e-06)[:, None, None]
    step_one = step[:tiles_one].transpose(1, 0, 2).reshape(rows_out, tiles_one * width)
    step_two = step[tiles_one:].transpose(1, 0, 2).reshape(rows_out, 9 * width)
    reduce_new = reduce_weight - 0.02 * reduce_float * (step_one + 0.1 * reduce_weight)
    spatial_new = spatial_weight - 0.02 * spatial_float * (step_two + 0.1 * spatial_weight)
    head_new, head_first_new, head_second_new = adam_step(
        head_weight, head_grad, head_first, head_second, 0.04, 0.1
    )
    bias_new, bias_first_new, bias_second_new = adam_step(
        head_bias, bias_grad, bias_first, bias_second, 0.1, 0.0
    )
    norm_new, norm_first_new, norm_second_new = adam_step(
        norm_params, norm_gain_gradient, norm_first, norm_second, 0.1, 0.0
    )
    return (
        loss_sum,
        slot_count,
        reduce_grad,
        spatial_grad,
        reduce_new,
        spatial_new,
        left_new,
        right_new,
        head_new,
        head_first_new,
        head_second_new,
        bias_new,
        bias_first_new,
        bias_second_new,
        norm_new,
        norm_first_new,
        norm_second_new,
    )


def solution(mesh):
    in_specs = (
        P("batch", None, "chan"),
        P("batch", None),
        P("batch"),
        P("chan", None),
        P("chan", None),
        P("chan", None),
        P("chan", None),
        P("chan", None),
        P(),
        P(None, "chan"),
        P(None, "chan", None),
        P(None, "chan", None),
        P(None, "chan", None),
        P(None, "chan", None),
        P("chan", None),
        P("chan", None),
        P(),
        P(),
        P(None, "chan"),
        P(None, "chan"),
    )
    out_specs = (
        P(),
        P(),
        P("chan", None),
        P("chan", None),
        P("chan", None),
        P("chan", None),
        P(None, "chan", None),
        P(None, "chan", None),
        P("chan", None),
        P("chan", None),
        P("chan", None),
        P(),
        P(),
        P(),
        P(None, "chan"),
        P(None, "chan"),
        P(None, "chan"),
    )
    chan, batch = mesh.shape["chan"], mesh.shape["batch"]
    fits = chan == 8 and batch == 4 and WIDTH % (16 * chan * batch) == 0 and SLOTS_DEV % (16 * chan) == 0
    return jax.shard_map(body if fits else plain_body, mesh=mesh, in_specs=in_specs, out_specs=out_specs, check_vma=False)
```

```python
import functools

import jax
import jax.numpy as jnp
from jax import lax
from jax.experimental import pallas as pl
from jax.experimental.pallas import tpu as pltpu
from jax.sharding import PartitionSpec as P

SIDE = 7
SLOTS_DEV = 384
STEP = 10
ORDERS = ("xyz", "xy")

WIDTH = 512
EPS = 1e-05
MESH = pl.DeviceIdType.MESH
ANY = pl.BlockSpec(memory_space=pl.ANY)
VMEM = pl.BlockSpec(memory_space=pltpu.VMEM)
DMA = pltpu.SemaphoreType.DMA
SMALL = 8


def place():
    c, b = lax.axis_index("chan"), lax.axis_index("batch")
    nz, nx = lax.axis_size("chan") // 2, lax.axis_size("batch") // 2
    return (c // 2, lax.rem(c, 2), b // 2, lax.rem(b, 2)), (nz, 2, nx, 2)


def at(z, y, x, core):
    return {"chan": z * 2 + y, "batch": x * 2 + core}


def turned(index, size):
    return [lax.rem(index + k, size) for k in range(1, size)]


def greet(peers):
    barrier = pltpu.get_barrier_semaphore()
    for peer in peers:
        pl.semaphore_signal(barrier, inc=1, device_id=peer, device_id_type=MESH)
    pl.semaphore_wait(barrier, len(peers))


class Copies:
    def __init__(self, send, recv):
        self.send, self.recv, self.used = send, recv, 0

    def start(self, source, target, peer):
        copy = pltpu.make_async_remote_copy(
            source, target, self.send.at[self.used], self.recv.at[self.used],
            device_id=peer, device_id_type=MESH,
        )
        self.used += 1
        copy.start()
        return copy


def dot(left, right, left_dim, right_dim):
    return lax.dot_general(left, right, (((left_dim,), (right_dim,)), ((), ())), preferred_element_type=jnp.float32)


def sigmoid(value):
    return 1.0 / (1.0 + jnp.exp(-value))


def packed(row):
    return jnp.concatenate([row[:, i : i + 128] for i in range(0, row.shape[1], 128)], axis=0)


def unpacked(block):
    return jnp.concatenate([block[i : i + 1] for i in range(block.shape[0])], axis=1)


def step_kernel(
    images, spatial_weight, spatial_mask, reduce_weight, reduce_mask, head_weight, input_roots,
    own_norms, pixel_mask, all_labels, bias,
    taps_out, reduce_out, head_out, totals_out, mask_out, weights_out, roots_out,
    raw_spatial, raw_spatial_mask, raw_reduce, raw_reduce_mask, raw_head, raw_roots, weights, roots,
    own_images, first, second, hidden_pad, grad_pad, turned_grad, taps, reduce_low, head_low,
    valid, used, divisor, norms, norms_held, pack_one, pack_two, pack_three, pack_four, held_one, held_two, held_three, held_four,
    tap_sums, core_in, first_in, partial, pooling, pooled_low, d_logits, d_act, head_buf, grad_buf, send, recv, local,
):
    (z, y, x, core), (nz, ny, nx, nc) = place()
    c, n = lax.axis_index("chan"), lax.axis_size("chan")
    f32, low = jnp.float32, jnp.bfloat16
    slots = used.shape[0]
    side = SIDE
    line = side * slots
    wide_line = (side + 1) * slots
    pixels = side * side
    rim = (side + 2) * slots
    body_rows = side * wide_line
    width = first.shape[1]
    depth = own_images.shape[-1]
    everyone = [
        at(lax.rem(z + i, nz), lax.rem(y + j, ny), lax.rem(x + k, nx), lax.rem(core + m, nc))
        for i in range(nz) for j in range(ny) for k in range(nx) for m in range(nc) if i + j + k + m
    ]
    row_count = weights.shape[0]
    quarter = pl.ds(pl.multiple_of((x * nc + core) * row_count, row_count), row_count)
    raw = ((spatial_weight, raw_spatial), (spatial_mask, raw_spatial_mask), (reduce_weight, raw_reduce),
           (reduce_mask, raw_reduce_mask), (head_weight, raw_head))
    raw = [pltpu.make_async_copy(a.at[quarter], b, local.at[9 + i]) for i, (a, b) in enumerate(raw)]
    raw.append(pltpu.make_async_copy(input_roots.at[:, quarter], raw_roots, local.at[9 + len(raw)]))
    for copy in raw:
        copy.start()
    greet(everyone)
    copies = Copies(send, recv)
    others = turned(c, n)
    for copy in raw:
        copy.wait()
    size_taps, size_reduce = raw_spatial.shape[1], raw_reduce.shape[1]
    size_both = size_taps + size_reduce
    weights[:, size_both:] = jnp.zeros((row_count, weights.shape[1] - size_both), low)
    weights[:, :size_taps] = (raw_spatial[...] * raw_spatial_mask[...].astype(f32)).astype(low)
    weights[:, size_taps:size_both] = (raw_reduce[...] * raw_reduce_mask[...].astype(f32)).astype(low)
    weights[:, size_both : size_both + raw_head.shape[1]] = raw_head[...].astype(low)
    across_z = lax.rem(z + nz // 2, nz)
    near_z = [z // (nz // 2) * (nz // 2) + lax.rem(lax.rem(z, nz // 2) + k, nz // 2) for k in range(1, nz // 2)]
    mate, mate_y = at(z, y, x, 1 - core), at(z, 1 - y, x, core)
    mates_x = [at(z, y, k, core) for k in turned(x, nx)]

    def begin_z(source, target, sem):
        keep = pltpu.make_async_copy(source, target.at[z, y, x, core], local.at[sem])
        keep.start()
        peers = [at(k, y, x, core) for k in [across_z] + near_z]
        return [keep] + [copies.start(source, target.at[z, y, x, core], peer) for peer in peers]

    def pass_z(target, begun):
        for copy in begun:
            copy.wait()
        part = target.at[across_z, y, x, core]
        return [copies.start(part, part, at(k, y, x, core)) for k in near_z]

    lane = lax.broadcasted_iota(jnp.int32, norms.shape, 1)
    own_width = own_norms.shape[1]
    mine = (lane >= c * own_width) & (lane < (c + 1) * own_width)
    norms[...] = jnp.where(mine, jnp.concatenate([own_norms[...]] * n, axis=1), 0.0)

    weights_z = pass_z(weights_out, begin_z(weights, weights_out, 0))
    norm_copies = [copies.start(norms, norms_held.at[k + 1], {"chan": other}) for k, other in enumerate(others)]
    image_copies = [[copies.start(images.at[k, j], own_images.at[c, j, pl.ds(0, line)], {"chan": k}) for k in others]
                    for j in range(side)]
    own = pltpu.make_async_copy(images.at[c], own_images.at[c, :, pl.ds(0, line)], local.at[2])
    own.start()
    norms_held[0] = norms[...]

    for t in range(raw_roots.shape[0]):
        roots[:, t * width : (t + 1) * width] = raw_roots[t].astype(low)
    mask_out[:, :size_taps] = raw_spatial_mask[...].astype(f32)
    mask_out[:, size_taps:size_both] = raw_reduce_mask[...].astype(f32)
    mask_out[:, size_both:] = jnp.ones((row_count, mask_out.shape[1] - size_both), f32)

    own_slots = pl.ds(pl.multiple_of(c * slots, slots), slots)
    mask = pixel_mask[own_slots, :].astype(f32)
    for p in range(pixels):
        valid[p * slots : (p + 1) * slots, :] = jnp.broadcast_to(mask[:, p : p + 1], (slots, 128))
    filled = jnp.broadcast_to(jnp.sum(mask, axis=1, keepdims=True), (slots, 128))
    used[...] = (filled > 0.0).astype(f32)
    divisor[...] = jnp.maximum(filled, 1.0)

    def clear(i, _):
        rows = pl.ds(pl.multiple_of(i * slots, slots), slots)
        hidden_pad[rows, :] = jnp.zeros((slots, width), low)
        grad_pad[rows, :] = jnp.zeros((slots, width), low)
        return 0

    lax.fori_loop(0, hidden_pad.shape[0] // slots, clear, 0)
    for k in range(n):
        for j in range(side):
            own_images[k, j, pl.ds(line, slots), :] = jnp.zeros((slots, depth), low)

    for copy in weights_z:
        copy.wait()
    part = weights_out.at[:, y, x, core]
    copies.start(part, part, mate_y).wait()
    part = weights_out.at[:, :, x, core]
    along_x = [copies.start(part, part, peer) for peer in mates_x]
    for copy in along_x:
        copy.wait()
    part = weights_out.at[:, :, :, core]
    copies.start(part, part, mate).wait()
    fetched = []
    start = 0
    for j, held in enumerate((taps, reduce_low, head_low)):
        size = held.shape[-1]
        copy = pltpu.make_async_copy(weights_out.at[:, :, :, :, :, pl.ds(start, size)], held, local.at[3 + j])
        copy.start()
        fetched.append(copy)
        start += size
    for copy in fetched:
        copy.wait()
    taps, reduce_low, head_low = (held.reshape(width, held.shape[-1]) for held in (taps, reduce_low, head_low))
    for copy in norm_copies:
        copy.wait()
    norm_rows = jnp.sum(norms_held[...], axis=0)
    gain_one, shift_one, gain_two, shift_two = (norm_rows[i : i + 1] for i in range(4))

    def line_rows(j):
        return pl.ds(pl.multiple_of(j * line, slots), line)

    def pixel_rows(p):
        return pl.ds(pl.multiple_of(p * slots, slots), slots)

    def padded_pixel(p):
        j = p // side
        return pl.ds(pl.multiple_of(rim + (p + j) * slots, slots), slots)

    def across(block):
        return jnp.concatenate([block] * (width // 128), axis=1)

    def fold(value):
        return jnp.sum(value.reshape(-1, 8, width), axis=0)

    def total_of(index):
        return jnp.sum(partial[index], axis=0, keepdims=True)

    def exchange(pack, held):
        pack_copies = [copies.start(pack, held.at[k + 1], peer) for k, peer in enumerate(everyone)]
        held[0] = pack[...]
        return pack_copies

    def settled(pack_copies, held):
        for copy in pack_copies:
            copy.wait()
        return jnp.sum(held[...], axis=0)

    def add_to_sums(ref):
        def add(p, _):
            value = ref[pixel_rows(p), :]
            kept = value * across(valid[pixel_rows(p), :])
            partial[0] += fold(kept)
            partial[1] += fold(kept * value)
            return 0

        return add

    own.wait()
    partial[...] = jnp.zeros(partial.shape, f32)
    for j in range(side):
        for copy in image_copies[j]:
            copy.wait()
        block = jnp.concatenate([own_images[k, j, pl.ds(0, line), :] for k in range(n)], axis=1)
        first[pl.ds(j * line, line), :] = dot(block, reduce_low[...], 1, 1)
        lax.fori_loop(j * side, (j + 1) * side, add_to_sums(first), 0)
    all_valid = jnp.sum(valid[...], axis=0, keepdims=True)
    pack_one[...] = jnp.concatenate(
        [packed(total_of(0)), packed(total_of(1)), all_valid, jnp.zeros((7, 128), f32)], axis=0)
    stats = settled(exchange(pack_one, held_one), held_one)
    rows = width // 128
    count = jnp.concatenate([stats[2 * rows : 2 * rows + 1]] * rows, axis=1)

    def norm_of(stats):
        mean = unpacked(stats[:rows]) / count
        scale = lax.rsqrt(unpacked(stats[rows : 2 * rows]) / count - mean * mean + EPS)
        return mean, scale

    mean_one, scale_one = norm_of(stats)
    roots_z = begin_z(roots, roots_out, 1)

    def activate(p, _):
        normed = (first[pixel_rows(p), :] - mean_one) * scale_one
        pre = gain_one * normed + shift_one
        act = pre * sigmoid(pre) * across(valid[pixel_rows(p), :])
        hidden_pad[padded_pixel(p), :] = act.astype(low)
        return 0

    lax.fori_loop(0, pixels, activate, 0)

    def conv_line(j, _):
        value = None
        for t in range(9):
            offset = (t // 3 - 1) * wide_line + (t % 3 - 1) * slots
            rows_in = pl.ds(pl.multiple_of(rim + j * wide_line + offset, slots), line)
            term = dot(hidden_pad[rows_in, :], taps[:, t * width : (t + 1) * width], 1, 1)
            value = term if value is None else value + term
        second[line_rows(j), :] = value
        return 0

    lax.fori_loop(0, side, conv_line, 0)
    roots_z = pass_z(roots_out, roots_z)
    partial[...] = jnp.zeros(partial.shape, f32)
    lax.fori_loop(0, pixels, add_to_sums(second), 0)
    pack_two[...] = jnp.concatenate([packed(total_of(0)), packed(total_of(1))], axis=0)
    stats = settled(exchange(pack_two, held_two), held_two)
    mean_two, scale_two = norm_of(stats)
    for copy in roots_z:
        copy.wait()
    across_half = roots_out.shape[-1] // 2
    left, right = pl.ds(0, across_half), pl.ds(across_half, across_half)
    part = roots_out.at[:, y, x, core, :, left]
    roots_a = [copies.start(part, part, peer) for peer in mates_x]
    part = roots_out.at[:, y, x, core, :, right]
    roots_b = [copies.start(part, part, mate_y)]

    pooling[...] = jnp.zeros(pooling.shape, f32)

    def pool(p, _):
        normed = (second[pixel_rows(p), :] - mean_two) * scale_two
        pre = gain_two * normed + shift_two
        sigma = sigmoid(pre)
        kept = across(valid[pixel_rows(p), :])
        slope = sigma * (1.0 + pre * (1.0 - sigma)) * kept
        pooling[0] += pre * sigma * kept
        pooling[1] += slope
        pooling[2] += slope * normed
        return 0

    lax.fori_loop(0, pixels, pool, 0)
    divide = across(divisor[...])
    pooled_low[...] = (pooling[0] / divide).astype(low)
    logits = dot(pooled_low[...], head_low[...], 1, 0) + bias[...]
    classes = logits.shape[1]
    index = lax.broadcasted_iota(jnp.int32, (slots, classes), 1)
    onehot = (index == all_labels[own_slots, :]).astype(f32)
    top = jnp.max(logits, axis=1, keepdims=True)
    log_total = jnp.log(jnp.sum(jnp.exp(logits - top), axis=1, keepdims=True)) + top
    picked = jnp.sum(onehot * logits, axis=1, keepdims=True)
    use = used[:, :1]
    loss = jnp.sum(use * (log_total - picked))
    d_logits[...] = (use * (jnp.exp(logits - log_total) - onehot) / SLOTS_DEV).astype(low)
    bias_sum = jnp.sum(d_logits[...].astype(f32), axis=0, keepdims=True)
    half = width // 2

    def to_pooled(m, _):
        rows_in = pl.ds(pl.multiple_of(m * half, half), half)
        d_act[:, rows_in] = dot(d_logits[...], head_low[rows_in, :], 1, 1) / across(divisor[...])[:, :half]
        return 0

    lax.fori_loop(0, 2, to_pooled, 0)
    at_class = lax.broadcasted_iota(jnp.int32, (1, classes), 1)
    bias_sum = jnp.where(at_class == classes - 1, loss, jnp.where(at_class == classes - 2, jnp.sum(use), bias_sum))
    pack_three[...] = jnp.concatenate(
        [packed(jnp.sum(d_act[...] * pooling[1], axis=0, keepdims=True)),
         packed(jnp.sum(d_act[...] * pooling[2], axis=0, keepdims=True)), packed(bias_sum)], axis=0)
    going = exchange(pack_three, held_three)

    def to_head(m, _):
        columns = pl.ds(pl.multiple_of(m * (classes // 2), 128), classes // 2)
        head_buf[:, columns] = dot(pooled_low[...], d_logits[:, columns], 0, 0)
        return 0

    lax.fori_loop(0, 2, to_head, 0)
    head_copy = pltpu.make_async_copy(head_buf, head_out, local.at[6])
    head_copy.start()
    totals_two = settled(going, held_three)
    shift_grad, gain_grad = unpacked(totals_two[:rows]), unpacked(totals_two[rows : 2 * rows])
    factor = gain_two * scale_two / count
    for copy in roots_a:
        copy.wait()
    part = roots_out.at[:, y, :, core, :, left]
    roots_a = [copies.start(part, part, mate_y)]
    for copy in roots_b:
        copy.wait()
    part = roots_out.at[:, :, x, core, :, right]
    roots_b = [copies.start(part, part, peer) for peer in mates_x]

    def leave_second(p, _):
        normed = (second[pixel_rows(p), :] - mean_two) * scale_two
        pre = gain_two * normed + shift_two
        sigma = sigmoid(pre)
        kept = across(valid[pixel_rows(p), :])
        d_pre = d_act[...] * kept * (sigma * (1.0 + pre * (1.0 - sigma)))
        d_z = factor * (count * d_pre - shift_grad - normed * gain_grad) * kept
        grad_pad[padded_pixel(p), :] = d_z.astype(low)
        return 0

    lax.fori_loop(0, pixels, leave_second, 0)

    partial[...] = jnp.zeros(partial.shape, f32)

    def spread_line(j, _):
        value = None
        for t in range(9):
            offset = (t // 3 - 1) * wide_line + (t % 3 - 1) * slots
            rows_in = pl.ds(pl.multiple_of(rim + j * wide_line - offset, slots), line)
            term = dot(grad_pad[rows_in, :], taps[:, t * width : (t + 1) * width], 1, 0)
            value = term if value is None else value + term
        second[line_rows(j), :] = value
        return 0

    lax.fori_loop(0, side, spread_line, 0)
    def enter_first(p, _):
        normed = (first[pixel_rows(p), :] - mean_one) * scale_one
        pre = gain_one * normed + shift_one
        sigma = sigmoid(pre)
        d_pre = second[pixel_rows(p), :] * across(valid[pixel_rows(p), :]) * (sigma * (1.0 + pre * (1.0 - sigma)))
        second[pixel_rows(p), :] = d_pre
        partial[0] += fold(d_pre)
        partial[1] += fold(d_pre * normed)
        return 0

    lax.fori_loop(0, pixels, enter_first, 0)
    pack_four[...] = jnp.concatenate([packed(total_of(0)), packed(total_of(1))], axis=0)
    going = exchange(pack_four, held_four)

    def turn(j, _):
        rows_in = pl.ds(pl.multiple_of(rim + j * wide_line, slots), wide_line)
        turned_grad[:, pl.ds(pl.multiple_of(j * wide_line, 128), wide_line)] = grad_pad[rows_in, :].T
        return 0

    lax.fori_loop(0, side, turn, 0)

    def leave(slot, target, sem):
        copy = pltpu.make_async_copy(grad_buf.at[slot], target, local.at[sem])
        copy.start()
        return copy

    half = nz // 2
    near = z // half * half + lax.rem(z + 1, half)
    kinds = "".join(chunk_rounds(9))
    core_going, first_going = [], []

    def part_of(t, mine):
        if kinds[t] == "x":
            return [(tap_sums.at[t, :, :, x if mine else lax.rem(x + 1, nx)], first_in.at[t])]
        if kinds[t] == "y":
            return [(tap_sums.at[t, :, y if mine else 1 - y], first_in.at[t])]
        return [(tap_sums.at[t, (z // half * half + lax.rem(z, half) if mine else near) % half + h * half],
                 first_in.at[t, pl.ds(2 * h, 2)]) for h in range(2)]

    def over_core(t):
        core_going[t].wait()
        for i in range(nz):
            tap_sums[t, i] += core_in[t, i]
        peer = {"x": at(z, y, lax.rem(x + 1, nx), core), "y": mate_y, "z": at(near, y, x, core)}[kinds[t]]
        first_going.append([copies.start(source, target, peer) for source, target in part_of(t, False)])

    for t in range(9):
        offset = (t // 3 - 1) * wide_line + (t % 3 - 1) * slots
        slot = t % 2
        shifted = hidden_pad.at[pl.ds(rim + offset, body_rows)]
        grad_buf[slot] = dot(turned_grad[...], shifted[...], 1, 0).reshape(grad_buf.shape[1:])
        core_going.append(copies.start(grad_buf.at[slot, :, :, :, 1 - core], core_in.at[t], mate))
        for i in range(nz):
            tap_sums[t, i] = grad_buf[slot, i, :, :, core]
        if t:
            over_core(t - 1)
    over_core(8)
    leaving = []

    for copy in roots_a + roots_b:
        copy.wait()
    part = roots_out.at[:, :, :, core]
    roots_core = copies.start(part, part, mate)
    totals_one = settled(going, held_four)
    shift_sum, gain_sum = unpacked(totals_one[:rows]), unpacked(totals_one[rows : 2 * rows])
    factor_one = gain_one * scale_one / count

    def leave_first(p, _):
        normed = (first[pixel_rows(p), :] - mean_one) * scale_one
        kept = across(valid[pixel_rows(p), :])
        d_z = factor_one * (count * second[pixel_rows(p), :] - shift_sum - normed * gain_sum) * kept
        grad_pad[padded_pixel(p), :] = d_z.astype(low)
        return 0

    lax.fori_loop(0, pixels, leave_first, 0)
    lax.fori_loop(0, side, turn, 0)
    per = width // depth
    for t in range(n // per):
        slot = (9 + t) % 2
        if t >= 2:
            leaving[t - 2].wait()
        block = jnp.concatenate([own_images[t * per + k].reshape(body_rows, depth) for k in range(per)], axis=1)
        grad_buf[slot] = dot(turned_grad[...], block, 1, 0).reshape(grad_buf.shape[1:])
        leaving.append(leave(slot, reduce_out.at[:, :, :, :, :, pl.ds(t * width, width)], 7 + slot))
    taps_going = []
    for t in range(9):
        for copy in first_going[t]:
            copy.wait()
        for h, (kept, landed) in enumerate(part_of(t, True)):
            kept[...] += landed[...]
            copy = pltpu.make_async_copy(
                kept, taps_out.at[t, pl.ds(2 * h, 2)] if kinds[t] == "z" else taps_out.at[t], local.at[9 + 2 * t + h])
            copy.start()
            taps_going.append(copy)
    for copy in taps_going:
        copy.wait()
    totals_out[...] = jnp.concatenate([totals_two, totals_one], axis=0)
    head_copy.wait()
    roots_core.wait()
    for copy in leaving[-2:]:
        copy.wait()


def local_step(images, spatial_weight, spatial_mask, reduce_weight, reduce_mask, head_weight, roots,
               norms, pixel_mask, labels, bias):
    n, nb = lax.axis_size("chan"), lax.axis_size("batch")
    nz, nx = n // 2, nb // 2
    slots, width = pixel_mask.shape[0] // n, norms.shape[1] * n
    line, depth, classes = SIDE * slots, images.shape[-1], bias.shape[1]
    f32, low = jnp.float32, jnp.bfloat16
    rows = spatial_weight.shape[0] // nb
    wide_weights, wide_roots = spatial_weight.shape[1] + reduce_weight.shape[1] + classes, roots.shape[0] * roots.shape[2]
    grids = ((SIDE * (SIDE + 1) + 2 * (SIDE + 2)) * slots, width)
    shape = jax.ShapeDtypeStruct
    gathered = lambda size: shape((nz, 2, nx, 2, rows, size), low)
    raw = lambda a: pltpu.VMEM((rows, a.shape[1]), a.dtype)
    held = lambda k: pltpu.VMEM((n * nb, k, 128), f32)
    pack = lambda k: pltpu.VMEM((k, 128), f32)
    count = 2 * (nz - 1) + (SIDE + 1) * (n - 1) + (1 + (nx - 1) + 1) + (2 * nx + 1) + 4 * (n * nb - 1) + 27
    two = 2 * width // 128
    three = two + classes // 128
    weight = lambda size: pltpu.VMEM((nz, 2, nx, 2, rows, size), low)
    taps, reduce, head, totals, mask, _, roots_full = pl.pallas_call(
        step_kernel,
        out_shape=(
            shape((9, nz, 2, rows, width), f32),
            shape((nz, 2, nx, 2, rows, n * depth), f32),
            shape((width, classes), f32),
            shape((two + three, 128), f32),
            shape((rows, wide_weights), f32),
            gathered(wide_weights),
            gathered(wide_roots),
        ),
        in_specs=[ANY] * 7 + [VMEM] * 4,
        out_specs=(ANY, ANY, ANY, VMEM, VMEM, ANY, ANY),
        scratch_shapes=[
            raw(spatial_weight), raw(spatial_mask), raw(reduce_weight), raw(reduce_mask), raw(head_weight),
            pltpu.VMEM((roots.shape[0], rows, width), f32),
            pltpu.VMEM((rows, wide_weights), low),
            pltpu.VMEM((rows, wide_roots), low),
            pltpu.VMEM((n, SIDE, line + slots, depth), low),
            pltpu.VMEM((SIDE * line, width), f32),
            pltpu.VMEM((SIDE * line, width), f32),
            pltpu.VMEM(grids, low),
            pltpu.VMEM(grids, low),
            pltpu.VMEM((width, SIDE * (line + slots)), low),
            weight(9 * width), weight(n * depth), weight(classes),
            pltpu.VMEM((SIDE * line, 128), f32),
            pltpu.VMEM((slots, 128), f32),
            pltpu.VMEM((slots, 128), f32),
            pltpu.VMEM((norms.shape[0], width), f32),
            pltpu.VMEM((n, norms.shape[0], width), f32),
            pack(two + 8), pack(two), pack(three), pack(two),
            held(two + 8), held(two), held(three), held(two),
            pltpu.VMEM((9, nz, 2, nx, rows, width), f32),
            pltpu.VMEM((9, nz, 2, nx, rows, width), f32),
            pltpu.VMEM((9, nz, 2, rows, width), f32),
            pltpu.VMEM((2, 8, width), f32),
            pltpu.VMEM((3, slots, width), f32),
            pltpu.VMEM((slots, width), low),
            pltpu.VMEM((slots, classes), low),
            pltpu.VMEM((slots, width), f32),
            pltpu.VMEM((width, classes), f32),
            pltpu.VMEM((2, nz, 2, nx, 2, rows, width), f32),
            DMA((count,)), DMA((count,)), DMA((27,)),
        ],
        compiler_params=pltpu.CompilerParams(collective_id=0, has_side_effects=True, vmem_limit_bytes=60 << 20),
        name="step",
    )(images.reshape(n, SIDE, line, depth), spatial_weight, spatial_mask, reduce_weight, reduce_mask, head_weight, roots,
      norms, pixel_mask, labels, bias)
    return taps, reduce, head, totals[:three], totals[three:], mask, roots_full.reshape(width, wide_roots)


def chunk_rounds(count):
    rounds = []
    while count > 0:
        rounds.append(ORDERS[len(rounds) % len(ORDERS)][:count])
        count -= len(rounds[-1])
    return rounds


def settle_kernel(
    chunks, taps, reduce, head, mask, left_root, roots, own, left_part, right_part, outer_out, size,
    full, factors, lefts, rights, outers, squares, held, sums, core_in, first_in, second_in, near_in, across_in,
    final, final_low, send, recv, local,
):
    (z, y, x, core), (nz, ny, nx, nc) = place()
    half = nz // 2
    across_z = lax.rem(z + half, nz)
    base_z = z // half * half
    near_z = [base_z + lax.rem(lax.rem(z, half) + k, half) for k in range(1, half)]
    others_x = turned(x, nx)
    mate, mate_y = at(z, y, x, 1 - core), at(z, 1 - y, x, core)
    mates_x = [at(z, y, k, core) for k in others_x]
    mates_near = [at(k, y, x, core) for k in near_z]
    mate_across = at(across_z, y, x, core)
    c, n = lax.axis_index("chan"), lax.axis_size("chan")
    others = [{"chan": k} for k in turned(c, n)]
    greet(others + mates_x + [mate])
    copies = Copies(send, recv)
    f32, low = jnp.float32, jnp.bfloat16
    rows, width = left_root.shape[1:]
    tiles_one = reduce.shape[-1] // width
    n_taps = taps.shape[0]
    sources = ((reduce, n_taps * width), (head, n_taps * width + reduce.shape[-1]))
    wide = n_taps * width + reduce.shape[-1]
    used_local = [0]

    def keep(source, target):
        copy = pltpu.make_async_copy(source, target, local.at[used_local[0]])
        used_local[0] += 1
        copy.start()
        return copy

    roots_in = [keep(roots, factors)]
    pick = (lax.broadcasted_iota(jnp.int32, (rows, width), 1)
            == lax.broadcasted_iota(jnp.int32, (rows, width), 0) + c * rows).astype(low)
    squares[...] = jnp.zeros(squares.shape, f32)
    outgoing = []

    def two_parts(value):
        high = value.astype(low)
        return [high, (value - high.astype(f32)).astype(low)]

    def multiply(t, columns):
        grad = full[:, :, :, :, :, columns].reshape(width, width)
        mine = full[z, y, :, :, :, columns].reshape(rows, width)
        first = dot(jnp.concatenate([mine, pick], axis=0), grad, 1, 1)
        lefts[t] = first[:rows]
        second = dot(jnp.concatenate([first[rows:].astype(low)] + two_parts(left_root[t]), axis=0), grad, 1, 0)
        rights[t] = second[:rows]
        inner = second[rows : 2 * rows] + second[2 * rows :]
        third = dot(jnp.concatenate(two_parts(inner), axis=0), factors[:, t * width : (t + 1) * width], 1, 0)
        value = third[:rows] + third[rows:]
        outers[t] = value
        squares[t : t + 1, :] = jnp.full((1, 128), jnp.sum(value * value), f32)
        outgoing.extend(keep(a.at[t], b.at[t]) for a, b in ((lefts, left_part), (rights, right_part), (outers, outer_out)))

    def wait(going):
        for copy in going:
            copy.wait()

    def enter(start, size):
        columns = pl.ds(start, size)
        going = []
        for source, first_column in sources:
            begin, end = max(start, first_column), min(start + size, first_column + source.shape[-1])
            if begin < end:
                taken, landed = pl.ds(begin - first_column, end - begin), pl.ds(begin, end - begin)
                going.append(copies.start(source.at[:, :, :, 1 - core, :, taken], core_in.at[:, :, :, :, landed], mate))
                going.append(keep(source.at[:, :, :, core, :, taken], sums.at[:, :, :, :, landed]))
        yield
        wait(going)
        for i in range(nz):
            for j in range(ny):
                for k in range(nx):
                    sums[i, j, k, :, columns] += core_in[i, j, k, :, columns]

    def settled(start, last_in, columns):
        total = (sums[z, y, x, :, columns] + last_in) * mask[:, columns]
        final[:, columns] = total
        kept = [keep(final.at[:, columns], own.at[x, core, :, columns])]
        kept += [copies.start(final.at[:, columns], own.at[x, core, :, columns], peer) for peer in mates_x]
        if start < wide:
            final_low[:, columns] = total.astype(low)
            return kept, [keep(final_low.at[:, columns], full.at[z, y, x, core, :, columns])]
        return kept, []

    def own_core(kept, columns):
        wait(kept)
        part = own.at[:, core, :, columns]
        return copies.start(part, part, mate)

    def block_of(start, columns):
        t = start // width
        if roots_in:
            roots_in.pop().wait()
        multiply(t + tiles_one if t < n_taps else t - n_taps, columns)

    def chunk_z(start, size):
        columns = pl.ds(start, size)
        if start < n_taps * width:
            going = [keep(taps.at[start // width, pl.ds(2 * h, 2)], sums.at[lax.rem(z, half) + h * half, :, :, :, columns])
                     for h in range(2)]
            yield
            wait(going)
        else:
            yield from enter(start, size)
            going = []
            for t, k in enumerate(near_z):
                for h in range(2):
                    there = lax.rem(k, half) + h * half
                    going.append(copies.start(
                        sums.at[there, :, :, :, columns], first_in.at[t, pl.ds(2 * h, 2), :, :, columns], mates_near[t]))
            yield
            wait(going)
            for t in range(half - 1):
                for h in range(2):
                    for j in range(ny):
                        for k in range(nx):
                            sums[lax.rem(z, half) + h * half, j, k, :, columns] += first_in[t, 2 * h + j, k, :, columns]
        landing = [second_in.at[0, pl.ds(nx * j, nx), :, columns] for j in range(ny)]
        going = [copies.start(sums.at[across_z, j, :, :, columns], landing[j], mate_across) for j in range(ny)]
        yield
        wait(going)
        for j in range(ny):
            for k in range(nx):
                sums[z, j, k, :, columns] += second_in[0, nx * j + k, :, columns]
        going = [copies.start(sums.at[z, :, k, :, columns], near_in.at[t, :, :, columns], mates_x[t])
                 for t, k in enumerate(others_x)]
        yield
        wait(going)
        for t in range(nx - 1):
            for j in range(ny):
                sums[z, j, x, :, columns] += near_in[t, j, :, columns]
        going = [copies.start(sums.at[z, 1 - y, x, :, columns], across_in.at[:, columns], mate_y)]
        yield
        wait(going)
        kept, going = settled(start, across_in[:, columns], columns)
        going += [copies.start(final_low.at[:, columns], full.at[z, y, x, core, :, columns], peer) for peer in mates_x]
        yield
        last = [own_core(kept, columns)]
        wait(going)
        part = full.at[z, y, :, core, :, columns]
        going = [copies.start(part, part, mate_y)]
        yield
        wait(going)
        part = full.at[z, :, :, core, :, columns]
        going = [copies.start(part, part, peer) for peer in [mate_across] + mates_near]
        yield
        wait(going)
        part = full.at[across_z, :, :, core, :, columns]
        going = [copies.start(part, part, peer) for peer in mates_near]
        yield
        wait(going)
        part = full.at[:, :, :, core, :, columns]
        last.append(copies.start(part, part, mate))
        yield
        wait(last)
        block_of(start, columns)

    def chunk(start, size, x_first):
        columns = pl.ds(start, size)
        if start < n_taps * width:
            going = [keep(taps.at[start // width], sums.at[:, :, x, :, columns] if x_first else sums.at[:, y, :, :, columns])]
            yield
            wait(going)
        else:
            yield from enter(start, size)
            if x_first:
                going = [copies.start(sums.at[:, :, k, :, columns], first_in.at[t, :, :, :, columns], mates_x[t])
                         for t, k in enumerate(others_x)]
            else:
                going = [copies.start(sums.at[:, 1 - y, :, :, columns], first_in.at[0, :, :, :, columns], mate_y)]
            yield
            wait(going)
            for i in range(nz):
                for j in range(2):
                    if x_first:
                        sums[i, j, x, :, columns] += first_in[0, i, j, :, columns]
                    else:
                        sums[i, y, j, :, columns] += first_in[0, i, j, :, columns]
        going = []
        if x_first:
            going.append(copies.start(sums.at[:, 1 - y, x, :, columns], second_in.at[0, :, :, columns], mate_y))
        else:
            for t, k in enumerate(others_x):
                going.append(copies.start(sums.at[:, y, k, :, columns], second_in.at[t, :, :, columns], mates_x[t]))
        yield
        wait(going)
        for t in range(1 if x_first else nx - 1):
            for i in range(nz):
                sums[i, y, x, :, columns] += second_in[t, i, :, columns]
        going = []
        for t, k in enumerate(near_z):
            for h in range(2):
                there = lax.rem(k + h * half, nz)
                going.append(copies.start(sums.at[there, y, x, :, columns], near_in.at[t, h, :, columns], mates_near[t]))
        yield
        wait(going)
        for t in range(half - 1):
            for h in range(2):
                sums[lax.rem(z + h * half, nz), y, x, :, columns] += near_in[t, h, :, columns]
        going = [copies.start(sums.at[across_z, y, x, :, columns], across_in.at[:, columns], mate_across)]
        yield
        wait(going)
        kept, going = settled(start, across_in[:, columns], columns)
        if start < wide:
            going += [copies.start(final_low.at[:, columns], full.at[z, y, x, core, :, columns], peer)
                      for peer in [mate_across] + mates_near]
        yield
        rows_core = [own_core(kept, columns)]
        if start < wide:
            wait(going)
            part = full.at[across_z, y, x, core, :, columns]
            going = [copies.start(part, part, peer) for peer in mates_near]
            yield
            wait(going)
            part = full.at[:, y, x, core, :, columns]
            going = [copies.start(part, part, peer) for peer in (mates_x if x_first else [mate_y])]
            yield
            wait(going)
            part = full.at[:, y, :, core, :, columns] if x_first else full.at[:, :, x, core, :, columns]
            going = [copies.start(part, part, peer) for peer in ([mate_y] if x_first else mates_x)]
            yield
            wait(going)
            part = full.at[:, :, :, core, :, columns]
            rows_core.append(copies.start(part, part, mate))
        yield
        wait(rows_core)
        if start < wide:
            block_of(start, columns)

    rounds = [[chunk_z(*c[:2]) if c[2] == "z" and c[0] < wide else chunk(*c[:2], c[2] != "y") for c in some] for some in chunks]
    begun, active = [], []
    while rounds or begun or active:
        active += begun
        begun = rounds.pop(0) if rounds else []
        for going in begun:
            next(going)
        for going in active[::-1]:
            try:
                next(going)
            except StopIteration:
                active.remove(going)
    going = [copies.start(squares, held.at[k + 1], peer) for k, peer in enumerate(others)]
    held[0] = squares[...]
    wait(going + outgoing)
    size[...] = jnp.sqrt(jnp.sum(held[...], axis=0) / (width * width) + 1e-06)


def settle(taps, reduce, head, mask, left_root, roots):
    nz, nx, n = lax.axis_size("chan") // 2, lax.axis_size("batch") // 2, lax.axis_size("chan")
    blocks, own_rows, width = left_root.shape
    rows = width // (4 * nz * nx)
    wide = taps.shape[0] * width + reduce.shape[-1]
    total = wide + head.shape[1]
    split = lambda a: a.reshape(nz, 2, nx, 2, rows, a.shape[1])
    f32, low = jnp.float32, jnp.bfloat16
    chunks, start = [], 0
    for kinds in chunk_rounds(total // width):
        chunks.append([(start + i * width, width, kind) for i, kind in enumerate(kinds)])
        start += len(kinds) * width
    near = nz // 2 - 1
    first = max(nx - 1, nx // 2)
    count = (total // width) * (4 + first + max(nx - 1, 1) + 2 * near + 1 + (nx - 1) + 1 + near + 1 + near + nx + 1) + n
    product = jax.ShapeDtypeStruct((blocks, own_rows, width), f32)
    padded = (blocks + 7) // 8 * 8
    own, left_part, right_part, outer, size = pl.pallas_call(
        functools.partial(settle_kernel, chunks),
        out_shape=(
            jax.ShapeDtypeStruct((nx, 2, rows, total), f32), product, product, product,
            jax.ShapeDtypeStruct((padded, 128), f32),
        ),
        in_specs=[ANY, ANY, ANY, VMEM, VMEM, ANY],
        out_specs=(ANY,) * 4 + (VMEM,),
        scratch_shapes=[
            pltpu.VMEM((nz, 2, nx, 2, rows, wide), low),
            pltpu.VMEM(roots.shape, low),
            pltpu.VMEM(product.shape, f32),
            pltpu.VMEM(product.shape, f32),
            pltpu.VMEM(product.shape, f32),
            pltpu.VMEM((padded, 128), f32),
            pltpu.VMEM((n, padded, 128), f32),
            pltpu.VMEM((nz, 2, nx, rows, total), f32),
            pltpu.VMEM((nz, 2, nx, rows, total), f32),
            pltpu.VMEM((first, nz, 2, rows, total), f32),
            pltpu.VMEM((max(nx - 1, 1), nz, rows, total), f32),
            pltpu.VMEM((near, 2, rows, total), f32),
            pltpu.VMEM((rows, total), f32),
            pltpu.VMEM((rows, total), f32),
            pltpu.VMEM((rows, wide), low),
            DMA((count,)), DMA((count,)), DMA((7 * (total // width) + 4,)),
        ],
        compiler_params=pltpu.CompilerParams(collective_id=1, has_side_effects=True, vmem_limit_bytes=60 << 20),
        name="settle",
    )(taps, reduce, split(head), mask, left_root, roots)
    return own.reshape(own_rows, total), left_part, right_part, outer, size


def finish_kernel(
    size, head_weight, head_first, head_second,
    own, left_part, right_part, outer, left_stats, right_stats, reduce_weight, spatial_weight, reduce_mask, spatial_mask,
    head_new, head_first_new, head_second_new,
    reduce_grad, spatial_grad, reduce_new, spatial_new, left_new, right_new,
    own_rows, lefts, rights, outers, left_kept, right_kept, weights, masks, arrive, leave,
):
    blocks, rows, width = outers.shape
    c_in, taps = reduce_weight.shape[1], spatial_weight.shape[1]
    tiles_one = c_in // width
    groups = [(0, tiles_one)] + [(t, min(t + 3, blocks)) for t in range(tiles_one, blocks, 3)]
    every = [pltpu.make_async_copy(own, own_rows, arrive.at[0, 7])]
    coming = []
    for g, (begin, end) in enumerate(groups):
        some, columns = pl.ds(begin, end - begin), pl.ds(begin * width, (end - begin) * width)
        theirs = pl.ds((begin if g == 0 else begin - tiles_one) * width, (end - begin) * width)
        pairs = [(a.at[some], b.at[some]) for a, b in (
            (left_part, lefts), (right_part, rights), (outer, outers), (left_stats, left_kept), (right_stats, right_kept))]
        pairs += [((reduce_weight if g == 0 else spatial_weight).at[:, theirs], weights.at[:, columns]),
                  ((reduce_mask if g == 0 else spatial_mask).at[:, theirs], masks.at[:, columns])]
        coming.append([pltpu.make_async_copy(a, b, arrive.at[g, i]) for i, (a, b) in enumerate(pairs)])
    for copy in every + [copy for group in coming for copy in group]:
        copy.start()
    going = []

    def out(source, target):
        copy = pltpu.make_async_copy(source, target, leave.at[len(going)])
        copy.start()
        going.append(copy)

    every[0].wait()
    out(own_rows.at[:, pl.ds(0, taps)], spatial_grad)
    out(own_rows.at[:, pl.ds(taps, c_in)], reduce_grad)
    head_grad = own_rows[:, taps + c_in : taps + c_in + head_weight.shape[1]]
    head_new[...], head_first_new[...], head_second_new[...] = adam_step(
        head_weight[...], head_grad, head_first[...], head_second[...], 0.04, 0.1)
    for g, (begin, end) in enumerate(groups):
        for copy in coming[g]:
            copy.wait()

        def block(t, _):
            columns = pl.ds(pl.multiple_of(t * width, width), width)
            lefts[t] = 0.95 * left_kept[t] + lefts[t]
            rights[t] = 0.95 * right_kept[t] + rights[t]
            step = outers[t] / jnp.concatenate([size[pl.ds(t, 1), :]] * (width // 128), axis=1)
            weight = weights[:, columns]
            weights[:, columns] = weight - 0.02 * masks[:, columns].astype(jnp.float32) * (step + 0.1 * weight)
            return 0

        lax.fori_loop(begin, end, block, 0)
        some, columns = pl.ds(begin, end - begin), pl.ds(begin * width, (end - begin) * width)
        theirs = pl.ds((begin if g == 0 else begin - tiles_one) * width, (end - begin) * width)
        out(lefts.at[some], left_new.at[some])
        out(rights.at[some], right_new.at[some])
        out(weights.at[:, columns], (reduce_new if g == 0 else spatial_new).at[:, theirs])
    for copy in going:
        copy.wait()


def finish(own, left_part, right_part, outer, size, left_stats, right_stats,
           reduce_weight, spatial_weight, reduce_mask, spatial_mask, head_weight, head_first, head_second):
    blocks, rows, width = left_stats.shape
    like = lambda a: jax.ShapeDtypeStruct(a.shape, jnp.float32)
    wide = reduce_weight.shape[1] + spatial_weight.shape[1]
    products = pltpu.VMEM(left_stats.shape, jnp.float32)
    groups = 1 + -(-(spatial_weight.shape[1] // width) // 3)
    head_new, head_first_new, head_second_new, *rest = pl.pallas_call(
        finish_kernel,
        out_shape=(like(head_weight), like(head_weight), like(head_weight), like(reduce_weight), like(spatial_weight),
                   like(reduce_weight), like(spatial_weight), like(left_stats), like(left_stats)),
        in_specs=[VMEM] * 4 + [ANY] * 10,
        out_specs=(VMEM,) * 3 + (ANY,) * 6,
        scratch_shapes=[pltpu.VMEM(own.shape, jnp.float32)] + [products] * 5
        + [pltpu.VMEM((rows, wide), jnp.float32), pltpu.VMEM((rows, wide), jnp.int32),
           DMA((groups, 8)), DMA((2 + 3 * groups,))],
        compiler_params=pltpu.CompilerParams(vmem_limit_bytes=60 << 20),
        name="finish",
    )(size, head_weight, head_first, head_second, own, left_part, right_part, outer, left_stats, right_stats,
      reduce_weight, spatial_weight, reduce_mask, spatial_mask)
    return *rest, head_new, head_first_new, head_second_new


def silu_slope(pre):
    sigma = jax.nn.sigmoid(pre)
    return sigma * (1.0 + pre * (1.0 - sigma))


def adam_step(param, grad, first, second, rate, decay):
    first = 0.9 * first + 0.1 * grad
    second = 0.999 * second + 0.001 * grad * grad
    mhat = first / (1.0 - 0.9**STEP)
    vhat = second / (1.0 - 0.999**STEP)
    return (param - rate * (mhat / (jnp.sqrt(vhat) + 1e-08) + decay * param), first, second)


def own_part(array, axis, name="chan"):
    size = array.shape[axis] // lax.axis_size(name)
    return lax.dynamic_slice_in_dim(array, lax.axis_index(name) * size, size, axis)


def body(
    images,
    pixel_mask,
    labels,
    reduce_weight,
    reduce_mask,
    spatial_weight,
    spatial_mask,
    head_weight,
    head_bias,
    norm_params,
    left_stats,
    right_stats,
    left_root,
    input_side_roots,
    head_first,
    head_second,
    bias_first,
    bias_second,
    norm_first,
    norm_second,
):
    n = lax.axis_size("chan")
    pixels, channels = images.shape[1:]
    side = SIDE
    rows_out, c_in = reduce_weight.shape
    width = left_stats.shape[2]
    classes = head_weight.shape[1]
    padded = 1024
    slots = images.shape[0] // n
    f32 = jnp.float32

    by_pixel = images.reshape(n, slots, pixels, channels).transpose(0, 2, 1, 3)
    taps_local, reduce_local, head_local, sums_two, sums_one, mask_rows, roots_full = local_step(
        by_pixel, spatial_weight, spatial_mask, reduce_weight, reduce_mask, head_weight, input_side_roots, norm_params, pixel_mask, labels[:, None],
        jnp.pad(head_bias, (0, padded - classes), constant_values=-1e30)[None])

    own, *products = settle(taps_local, reduce_local, head_local, mask_rows, left_root, roots_full)
    of_norms = jnp.stack([a.reshape(-1) for a in (sums_one[4:], sums_one[:4], sums_two[4:8], sums_two[:4])])
    norm_gain_gradient = own_part(of_norms, 1)
    of_head = sums_two[8:].reshape(-1)
    bias_grad = of_head[:classes]
    loss_sum, slot_count = of_head[-1], of_head[-2]
    (reduce_grad, spatial_grad, reduce_new, spatial_new, left_new, right_new, head_new, head_first_new,
     head_second_new) = finish(
        own, *products, left_stats, right_stats, reduce_weight, spatial_weight, reduce_mask, spatial_mask,
        head_weight, head_first, head_second)
    bias_new, bias_first_new, bias_second_new = adam_step(head_bias, bias_grad, bias_first, bias_second, 0.1, 0.0)
    norm_new, norm_first_new, norm_second_new = adam_step(
        norm_params, norm_gain_gradient, norm_first, norm_second, 0.1, 0.0)
    return (
        loss_sum,
        slot_count,
        reduce_grad,
        spatial_grad,
        reduce_new,
        spatial_new,
        left_new,
        right_new,
        head_new,
        head_first_new,
        head_second_new,
        bias_new,
        bias_first_new,
        bias_second_new,
        norm_new,
        norm_first_new,
        norm_second_new,
    )


FULL_PRECISION = lax.Precision.HIGHEST
BOTH = ("chan", "batch")


def conv_grid(grid, taps, spec):
    return lax.conv_general_dilated(
        grid, taps, (1, 1), ((1, 1), (1, 1)), dimension_numbers=spec,
        preferred_element_type=jnp.float32,
    )


def plain_norm_forward(pre_norm, gain, shift, valid):
    first_sum = jnp.sum(pre_norm * valid, axis=(0, 1))
    second_sum = jnp.sum(pre_norm * pre_norm * valid, axis=(0, 1))
    first_sum, second_sum, count = lax.psum((first_sum, second_sum, jnp.sum(valid)), BOTH)
    mean = first_sum / count
    scale = lax.rsqrt(second_sum / count - mean * mean + EPS)
    normed = (pre_norm - mean) * scale
    pre = gain * normed + shift
    return (jax.nn.silu(pre) * valid, (normed, pre, scale, count))


def plain_norm_backward(grad_act, kept, gain, valid):
    normed, pre, scale, count = kept
    d_pre = grad_act * valid * silu_slope(pre)
    shift_gradient, gain_grad = lax.psum(
        (jnp.sum(d_pre, axis=(0, 1)), jnp.sum(d_pre * normed, axis=(0, 1))), BOTH
    )
    d_input = gain * scale / count * (count * d_pre - shift_gradient - normed * gain_grad) * valid
    return (d_input, gain_grad, shift_gradient)


def plain_own_part(array, parts, axis=0):
    size = array.shape[axis] // parts
    return lax.dynamic_slice_in_dim(array, lax.axis_index("chan") * size, size, axis)


def plain_body(
    images,
    pixel_mask,
    labels,
    reduce_weight,
    reduce_mask,
    spatial_weight,
    spatial_mask,
    head_weight,
    head_bias,
    norm_params,
    left_stats,
    right_stats,
    left_root,
    input_side_roots,
    head_first,
    head_second,
    bias_first,
    bias_second,
    norm_first,
    norm_second,
):
    parts = lax.axis_size("chan")
    pixels = images.shape[1]
    side = SIDE
    rows_out = reduce_weight.shape[0]
    width = left_stats.shape[2]
    classes = head_weight.shape[1]
    own_images = lax.all_to_all(images, "chan", 0, 2, tiled=True)
    slots = own_images.shape[0]
    reduce_float = reduce_mask.astype(jnp.float32)
    spatial_float = spatial_mask.astype(jnp.float32)
    gather = lambda a, axis: lax.all_gather(a, "chan", axis=axis, tiled=True)
    reduce_low = gather((reduce_weight * reduce_float).astype(jnp.bfloat16), 0)
    spatial_low = gather((spatial_weight * spatial_float).astype(jnp.bfloat16), 0)
    head_low = gather(head_weight.astype(jnp.bfloat16), 0)
    norm_full = gather(norm_params, 1)
    right_factor_full = gather(input_side_roots, 1)
    valid = plain_own_part(pixel_mask, parts).astype(jnp.float32)[:, :, None]
    own_labels = plain_own_part(labels, parts)
    filled = jnp.sum(valid[:, :, 0], axis=1)
    divisor = jnp.maximum(filled, 1.0)
    used = (filled > 0.0).astype(jnp.float32)
    taps = spatial_low.reshape(width, 3, 3, width)
    first_pre = jnp.einsum("spc,oc->spo", own_images, reduce_low, preferred_element_type=jnp.float32)
    first_act, first_kept = plain_norm_forward(first_pre, norm_full[0], norm_full[1], valid)
    hidden = first_act.astype(jnp.bfloat16).reshape(slots, side, side, width)
    second_pre = conv_grid(hidden, taps, ("NHWC", "OHWI", "NHWC")).reshape(slots, pixels, width)
    second_act, second_kept = plain_norm_forward(second_pre, norm_full[2], norm_full[3], valid)
    pooled = (jnp.sum(second_act, axis=1) / divisor[:, None]).astype(jnp.bfloat16)
    logits = jnp.dot(pooled, head_low, preferred_element_type=jnp.float32) + head_bias
    onehot = (jnp.arange(classes)[None, :] == own_labels[:, None]).astype(jnp.float32)
    log_total = jax.nn.logsumexp(logits, axis=1)
    picked = jnp.sum(onehot * logits, axis=1)
    loss_local = jnp.sum(used * (log_total - picked))
    d_logits = (used[:, None] * (jnp.exp(logits - log_total[:, None]) - onehot) / SLOTS_DEV).astype(
        jnp.bfloat16
    )
    head_grad = jnp.einsum("so,sc->oc", pooled, d_logits, preferred_element_type=jnp.float32)
    bias_grad = jnp.sum(d_logits.astype(jnp.float32), axis=0)
    d_pooled = jnp.einsum("sc,oc->so", d_logits, head_low, preferred_element_type=jnp.float32)
    d_act = jnp.broadcast_to((d_pooled / divisor[:, None])[:, None, :], second_act.shape)
    d_second, gain_two, shift_two = plain_norm_backward(d_act, second_kept, norm_full[2], valid)
    d_second = d_second.astype(jnp.bfloat16).reshape(slots, side, side, width)
    spatial_local = lax.conv_general_dilated(
        hidden, d_second, (1, 1), ((1, 1), (1, 1)), dimension_numbers=("CHWN", "IHWO", "NHWC"),
        preferred_element_type=jnp.float32,
    )
    spatial_local = spatial_local.transpose(3, 1, 2, 0).reshape(width, 9 * width)
    d_hidden = conv_grid(
        d_second, taps[:, ::-1, ::-1, :], ("NHWC", "IHWO", "NHWC")
    ).reshape(slots, pixels, width)
    d_first, gain_one, shift_one = plain_norm_backward(d_hidden, first_kept, norm_full[0], valid)
    d_first = d_first.astype(jnp.bfloat16)
    reduce_local = jnp.einsum("spc,spo->oc", own_images, d_first, preferred_element_type=jnp.float32)
    scatter = lambda a: lax.psum_scatter(a, "chan", scatter_dimension=0, tiled=True)
    reduce_grad, spatial_grad, head_grad = scatter(reduce_local), scatter(spatial_local), scatter(head_grad)
    reduce_grad, spatial_grad, head_grad = lax.psum((reduce_grad, spatial_grad, head_grad), "batch")
    reduce_grad = reduce_grad * reduce_float
    spatial_grad = spatial_grad * spatial_float
    bias_grad, loss_sum, slot_count = lax.psum((bias_grad, loss_local, jnp.sum(used)), BOTH)
    norm_gain_gradient = plain_own_part(jnp.stack([gain_one, shift_one, gain_two, shift_two], axis=0), parts, 1)
    tiles_one = reduce_weight.shape[1] // width
    blocks = jnp.concatenate(
        [
            reduce_grad.reshape(rows_out, tiles_one, width).transpose(1, 0, 2),
            spatial_grad.reshape(rows_out, 9, width).transpose(1, 0, 2),
        ],
        axis=0,
    )
    blocks_full = gather(blocks, 1)
    left_new = 0.95 * left_stats + jnp.einsum(
        "tak,tbk->tab", blocks, blocks_full, precision=FULL_PRECISION
    )
    own_columns = plain_own_part(blocks_full, parts, 2)
    right_new = 0.95 * right_stats + jnp.einsum(
        "tki,tkb->tib", own_columns, blocks_full, precision=FULL_PRECISION
    )
    matrix_product = jnp.einsum("tak,tkb->tab", left_root, blocks_full, precision=FULL_PRECISION)
    matrix_product = jnp.einsum(
        "ghk,gkl->ghl", matrix_product, right_factor_full, precision=FULL_PRECISION
    )
    squares = lax.psum(jnp.sum(matrix_product * matrix_product, axis=(1, 2)), "chan")
    step = matrix_product / jnp.sqrt(squares / (width * width) + 1e-06)[:, None, None]
    step_one = step[:tiles_one].transpose(1, 0, 2).reshape(rows_out, tiles_one * width)
    step_two = step[tiles_one:].transpose(1, 0, 2).reshape(rows_out, 9 * width)
    reduce_new = reduce_weight - 0.02 * reduce_float * (step_one + 0.1 * reduce_weight)
    spatial_new = spatial_weight - 0.02 * spatial_float * (step_two + 0.1 * spatial_weight)
    head_new, head_first_new, head_second_new = adam_step(
        head_weight, head_grad, head_first, head_second, 0.04, 0.1
    )
    bias_new, bias_first_new, bias_second_new = adam_step(
        head_bias, bias_grad, bias_first, bias_second, 0.1, 0.0
    )
    norm_new, norm_first_new, norm_second_new = adam_step(
        norm_params, norm_gain_gradient, norm_first, norm_second, 0.1, 0.0
    )
    return (
        loss_sum,
        slot_count,
        reduce_grad,
        spatial_grad,
        reduce_new,
        spatial_new,
        left_new,
        right_new,
        head_new,
        head_first_new,
        head_second_new,
        bias_new,
        bias_first_new,
        bias_second_new,
        norm_new,
        norm_first_new,
        norm_second_new,
    )


def solution(mesh):
    in_specs = (
        P("batch", None, "chan"),
        P("batch", None),
        P("batch"),
        P("chan", None),
        P("chan", None),
        P("chan", None),
        P("chan", None),
        P("chan", None),
        P(),
        P(None, "chan"),
        P(None, "chan", None),
        P(None, "chan", None),
        P(None, "chan", None),
        P(None, "chan", None),
        P("chan", None),
        P("chan", None),
        P(),
        P(),
        P(None, "chan"),
        P(None, "chan"),
    )
    out_specs = (
        P(),
        P(),
        P("chan", None),
        P("chan", None),
        P("chan", None),
        P("chan", None),
        P(None, "chan", None),
        P(None, "chan", None),
        P("chan", None),
        P("chan", None),
        P("chan", None),
        P(),
        P(),
        P(),
        P(None, "chan"),
        P(None, "chan"),
        P(None, "chan"),
    )
    chan, batch = mesh.shape["chan"], mesh.shape["batch"]
    fits = chan == 8 and batch == 4 and WIDTH % (16 * chan * batch) == 0 and SLOTS_DEV % (16 * chan) == 0
    return jax.shard_map(body if fits else plain_body, mesh=mesh, in_specs=in_specs, out_specs=out_specs, check_vma=False)
```

```python
import functools

import jax
import jax.numpy as jnp
from jax import lax
from jax.experimental import pallas as pl
from jax.experimental.pallas import tpu as pltpu
from jax.sharding import PartitionSpec as P

SIDE = 7
SLOTS_DEV = 384
STEP = 10
ORDERS = ("xyz", "xy")

WIDTH = 512
EPS = 1e-05
MESH = pl.DeviceIdType.MESH
ANY = pl.BlockSpec(memory_space=pl.ANY)
VMEM = pl.BlockSpec(memory_space=pltpu.VMEM)
DMA = pltpu.SemaphoreType.DMA
SMALL = 8


def place():
    c, b = lax.axis_index("chan"), lax.axis_index("batch")
    nz, nx = lax.axis_size("chan") // 2, lax.axis_size("batch") // 2
    return (c // 2, lax.rem(c, 2), b // 2, lax.rem(b, 2)), (nz, 2, nx, 2)


def at(z, y, x, core):
    return {"chan": z * 2 + y, "batch": x * 2 + core}


def turned(index, size):
    return [lax.rem(index + k, size) for k in range(1, size)]


def greet(peers):
    barrier = pltpu.get_barrier_semaphore()
    for peer in peers:
        pl.semaphore_signal(barrier, inc=1, device_id=peer, device_id_type=MESH)
    return lambda: pl.semaphore_wait(barrier, len(peers))


class Copies:
    def __init__(self, send, recv):
        self.send, self.recv, self.used = send, recv, 0

    def start(self, source, target, peer):
        copy = pltpu.make_async_remote_copy(
            source, target, self.send.at[self.used], self.recv.at[self.used],
            device_id=peer, device_id_type=MESH,
        )
        self.used += 1
        copy.start()
        return copy


def dot(left, right, left_dim, right_dim):
    return lax.dot_general(left, right, (((left_dim,), (right_dim,)), ((), ())), preferred_element_type=jnp.float32)


def sigmoid(value):
    return 1.0 / (1.0 + jnp.exp(-value))


def packed(row):
    return jnp.concatenate([row[:, i : i + 128] for i in range(0, row.shape[1], 128)], axis=0)


def unpacked(block):
    return jnp.concatenate([block[i : i + 1] for i in range(block.shape[0])], axis=1)


def step_kernel(
    images, spatial_weight, spatial_mask, reduce_weight, reduce_mask, head_weight, input_roots,
    own_norms, pixel_mask, all_labels, bias,
    taps_out, reduce_out, head_out, totals_out, mask_out, weights_out, roots_out,
    raw_spatial, raw_spatial_mask, raw_reduce, raw_reduce_mask, raw_head, raw_roots, weights, roots,
    own_images, first, second, hidden_pad, grad_pad, turned_grad, taps, reduce_low, head_low,
    valid, used, divisor, norms, norms_held, pack_one, pack_two, pack_three, pack_four, held_one, held_two, held_three, held_four,
    tap_sums, core_in, first_in, partial, pooling, pooled_low, d_logits, d_act, head_buf, grad_buf, send, recv, local,
):
    (z, y, x, core), (nz, ny, nx, nc) = place()
    c, n = lax.axis_index("chan"), lax.axis_size("chan")
    f32, low = jnp.float32, jnp.bfloat16
    slots = used.shape[0]
    side = SIDE
    line = side * slots
    wide_line = (side + 1) * slots
    pixels = side * side
    rim = (side + 2) * slots
    body_rows = side * wide_line
    width = first.shape[1]
    depth = own_images.shape[-1]
    everyone = [
        at(lax.rem(z + i, nz), lax.rem(y + j, ny), lax.rem(x + k, nx), lax.rem(core + m, nc))
        for i in range(nz) for j in range(ny) for k in range(nx) for m in range(nc) if i + j + k + m
    ]
    row_count = weights.shape[0]
    quarter = pl.ds(pl.multiple_of((x * nc + core) * row_count, row_count), row_count)
    raw = ((spatial_weight, raw_spatial), (spatial_mask, raw_spatial_mask), (reduce_weight, raw_reduce),
           (reduce_mask, raw_reduce_mask), (head_weight, raw_head))
    raw = [pltpu.make_async_copy(a.at[quarter], b, local.at[9 + i]) for i, (a, b) in enumerate(raw)]
    raw.append(pltpu.make_async_copy(input_roots.at[:, quarter], raw_roots, local.at[9 + len(raw)]))
    for copy in raw:
        copy.start()
    greeted = greet(everyone)
    copies = Copies(send, recv)
    others = turned(c, n)
    for copy in raw:
        copy.wait()
    size_taps, size_reduce = raw_spatial.shape[1], raw_reduce.shape[1]
    size_both = size_taps + size_reduce
    weights[:, size_both:] = jnp.zeros((row_count, weights.shape[1] - size_both), low)
    weights[:, :size_taps] = (raw_spatial[...] * raw_spatial_mask[...].astype(f32)).astype(low)
    weights[:, size_taps:size_both] = (raw_reduce[...] * raw_reduce_mask[...].astype(f32)).astype(low)
    weights[:, size_both : size_both + raw_head.shape[1]] = raw_head[...].astype(low)
    greeted()
    across_z = lax.rem(z + nz // 2, nz)
    near_z = [z // (nz // 2) * (nz // 2) + lax.rem(lax.rem(z, nz // 2) + k, nz // 2) for k in range(1, nz // 2)]
    mate, mate_y = at(z, y, x, 1 - core), at(z, 1 - y, x, core)
    mates_x = [at(z, y, k, core) for k in turned(x, nx)]

    def begin_z(source, target, sem):
        keep = pltpu.make_async_copy(source, target.at[z, y, x, core], local.at[sem])
        keep.start()
        peers = [at(k, y, x, core) for k in [across_z] + near_z]
        return [keep] + [copies.start(source, target.at[z, y, x, core], peer) for peer in peers]

    def pass_z(target, begun):
        for copy in begun:
            copy.wait()
        part = target.at[across_z, y, x, core]
        return [copies.start(part, part, at(k, y, x, core)) for k in near_z]

    lane = lax.broadcasted_iota(jnp.int32, norms.shape, 1)
    own_width = own_norms.shape[1]
    mine = (lane >= c * own_width) & (lane < (c + 1) * own_width)
    norms[...] = jnp.where(mine, jnp.concatenate([own_norms[...]] * n, axis=1), 0.0)

    weights_z = pass_z(weights_out, begin_z(weights, weights_out, 0))
    norm_copies = [copies.start(norms, norms_held.at[k + 1], {"chan": other}) for k, other in enumerate(others)]
    image_copies = [[copies.start(images.at[k, j], own_images.at[c, j, pl.ds(0, line)], {"chan": k}) for k in others]
                    for j in range(side)]
    own = pltpu.make_async_copy(images.at[c], own_images.at[c, :, pl.ds(0, line)], local.at[2])
    own.start()
    norms_held[0] = norms[...]

    for t in range(raw_roots.shape[0]):
        roots[:, t * width : (t + 1) * width] = raw_roots[t].astype(low)
    mask_out[:, :size_taps] = raw_spatial_mask[...].astype(f32)
    mask_out[:, size_taps:size_both] = raw_reduce_mask[...].astype(f32)
    mask_out[:, size_both:] = jnp.ones((row_count, mask_out.shape[1] - size_both), f32)

    own_slots = pl.ds(pl.multiple_of(c * slots, slots), slots)
    mask = pixel_mask[own_slots, :].astype(f32)
    for p in range(pixels):
        valid[p * slots : (p + 1) * slots, :] = jnp.broadcast_to(mask[:, p : p + 1], (slots, 128))
    filled = jnp.broadcast_to(jnp.sum(mask, axis=1, keepdims=True), (slots, 128))
    used[...] = (filled > 0.0).astype(f32)
    divisor[...] = jnp.maximum(filled, 1.0)

    def clear(i, _):
        rows = pl.ds(pl.multiple_of(i * slots, slots), slots)
        hidden_pad[rows, :] = jnp.zeros((slots, width), low)
        grad_pad[rows, :] = jnp.zeros((slots, width), low)
        return 0

    lax.fori_loop(0, hidden_pad.shape[0] // slots, clear, 0)
    for k in range(n):
        for j in range(side):
            own_images[k, j, pl.ds(line, slots), :] = jnp.zeros((slots, depth), low)

    for copy in weights_z:
        copy.wait()
    part = weights_out.at[:, y, x, core]
    copies.start(part, part, mate_y).wait()
    part = weights_out.at[:, :, x, core]
    along_x = [copies.start(part, part, peer) for peer in mates_x]
    for copy in along_x:
        copy.wait()
    part = weights_out.at[:, :, :, core]
    copies.start(part, part, mate).wait()
    fetched = []
    start = 0
    for j, held in enumerate((taps, reduce_low, head_low)):
        size = held.shape[-1]
        copy = pltpu.make_async_copy(weights_out.at[:, :, :, :, :, pl.ds(start, size)], held, local.at[3 + j])
        copy.start()
        fetched.append(copy)
        start += size
    for copy in fetched:
        copy.wait()
    taps, reduce_low, head_low = (held.reshape(width, held.shape[-1]) for held in (taps, reduce_low, head_low))
    for copy in norm_copies:
        copy.wait()
    norm_rows = jnp.sum(norms_held[...], axis=0)
    gain_one, shift_one, gain_two, shift_two = (norm_rows[i : i + 1] for i in range(4))

    def line_rows(j):
        return pl.ds(pl.multiple_of(j * line, slots), line)

    def pixel_rows(p):
        return pl.ds(pl.multiple_of(p * slots, slots), slots)

    def padded_pixel(p):
        j = p // side
        return pl.ds(pl.multiple_of(rim + (p + j) * slots, slots), slots)

    def across(block):
        return jnp.concatenate([block] * (width // 128), axis=1)

    def fold(value):
        return jnp.sum(value.reshape(-1, 8, width), axis=0)

    def total_of(index):
        return jnp.sum(partial[index], axis=0, keepdims=True)

    def exchange(pack, held):
        pack_copies = [copies.start(pack, held.at[k + 1], peer) for k, peer in enumerate(everyone)]
        held[0] = pack[...]
        return pack_copies

    def settled(pack_copies, held):
        for copy in pack_copies:
            copy.wait()
        return jnp.sum(held[...], axis=0)

    def add_to_sums(ref):
        def add(p, _):
            value = ref[pixel_rows(p), :]
            kept = value * across(valid[pixel_rows(p), :])
            partial[0] += fold(kept)
            partial[1] += fold(kept * value)
            return 0

        return add

    own.wait()
    partial[...] = jnp.zeros(partial.shape, f32)
    for j in range(side):
        for copy in image_copies[j]:
            copy.wait()
        block = jnp.concatenate([own_images[k, j, pl.ds(0, line), :] for k in range(n)], axis=1)
        first[pl.ds(j * line, line), :] = dot(block, reduce_low[...], 1, 1)
        lax.fori_loop(j * side, (j + 1) * side, add_to_sums(first), 0)
    all_valid = jnp.sum(valid[...], axis=0, keepdims=True)
    pack_one[...] = jnp.concatenate(
        [packed(total_of(0)), packed(total_of(1)), all_valid, jnp.zeros((7, 128), f32)], axis=0)
    stats = settled(exchange(pack_one, held_one), held_one)
    rows = width // 128
    count = jnp.concatenate([stats[2 * rows : 2 * rows + 1]] * rows, axis=1)

    def norm_of(stats):
        mean = unpacked(stats[:rows]) / count
        scale = lax.rsqrt(unpacked(stats[rows : 2 * rows]) / count - mean * mean + EPS)
        return mean, scale

    mean_one, scale_one = norm_of(stats)
    roots_z = begin_z(roots, roots_out, 1)

    def activate(p, _):
        normed = (first[pixel_rows(p), :] - mean_one) * scale_one
        pre = gain_one * normed + shift_one
        act = pre * sigmoid(pre) * across(valid[pixel_rows(p), :])
        hidden_pad[padded_pixel(p), :] = act.astype(low)
        return 0

    lax.fori_loop(0, pixels, activate, 0)

    def conv_line(j, _):
        value = None
        for t in range(9):
            offset = (t // 3 - 1) * wide_line + (t % 3 - 1) * slots
            rows_in = pl.ds(pl.multiple_of(rim + j * wide_line + offset, slots), line)
            term = dot(hidden_pad[rows_in, :], taps[:, t * width : (t + 1) * width], 1, 1)
            value = term if value is None else value + term
        second[line_rows(j), :] = value
        return 0

    lax.fori_loop(0, side, conv_line, 0)
    roots_z = pass_z(roots_out, roots_z)
    partial[...] = jnp.zeros(partial.shape, f32)
    lax.fori_loop(0, pixels, add_to_sums(second), 0)
    pack_two[...] = jnp.concatenate([packed(total_of(0)), packed(total_of(1))], axis=0)
    stats = settled(exchange(pack_two, held_two), held_two)
    mean_two, scale_two = norm_of(stats)
    for copy in roots_z:
        copy.wait()
    across_half = roots_out.shape[-1] // 2
    left, right = pl.ds(0, across_half), pl.ds(across_half, across_half)
    part = roots_out.at[:, y, x, core, :, left]
    roots_a = [copies.start(part, part, peer) for peer in mates_x]
    part = roots_out.at[:, y, x, core, :, right]
    roots_b = [copies.start(part, part, mate_y)]

    pooling[...] = jnp.zeros(pooling.shape, f32)

    def pool(p, _):
        normed = (second[pixel_rows(p), :] - mean_two) * scale_two
        pre = gain_two * normed + shift_two
        sigma = sigmoid(pre)
        kept = across(valid[pixel_rows(p), :])
        slope = sigma * (1.0 + pre * (1.0 - sigma)) * kept
        pooling[0] += pre * sigma * kept
        pooling[1] += slope
        pooling[2] += slope * normed
        return 0

    lax.fori_loop(0, pixels, pool, 0)
    divide = across(divisor[...])
    pooled_low[...] = (pooling[0] / divide).astype(low)
    logits = dot(pooled_low[...], head_low[...], 1, 0) + bias[...]
    classes = logits.shape[1]
    index = lax.broadcasted_iota(jnp.int32, (slots, classes), 1)
    onehot = (index == all_labels[own_slots, :]).astype(f32)
    top = jnp.max(logits, axis=1, keepdims=True)
    log_total = jnp.log(jnp.sum(jnp.exp(logits - top), axis=1, keepdims=True)) + top
    picked = jnp.sum(onehot * logits, axis=1, keepdims=True)
    use = used[:, :1]
    loss = jnp.sum(use * (log_total - picked))
    d_logits[...] = (use * (jnp.exp(logits - log_total) - onehot) / SLOTS_DEV).astype(low)
    bias_sum = jnp.sum(d_logits[...].astype(f32), axis=0, keepdims=True)
    half = width // 2

    def to_pooled(m, _):
        rows_in = pl.ds(pl.multiple_of(m * half, half), half)
        d_act[:, rows_in] = dot(d_logits[...], head_low[rows_in, :], 1, 1) / across(divisor[...])[:, :half]
        return 0

    lax.fori_loop(0, 2, to_pooled, 0)
    at_class = lax.broadcasted_iota(jnp.int32, (1, classes), 1)
    bias_sum = jnp.where(at_class == classes - 1, loss, jnp.where(at_class == classes - 2, jnp.sum(use), bias_sum))
    pack_three[...] = jnp.concatenate(
        [packed(jnp.sum(d_act[...] * pooling[1], axis=0, keepdims=True)),
         packed(jnp.sum(d_act[...] * pooling[2], axis=0, keepdims=True)), packed(bias_sum)], axis=0)
    going = exchange(pack_three, held_three)

    def to_head(m, _):
        columns = pl.ds(pl.multiple_of(m * (classes // 2), 128), classes // 2)
        head_buf[:, columns] = dot(pooled_low[...], d_logits[:, columns], 0, 0)
        return 0

    lax.fori_loop(0, 2, to_head, 0)
    head_copy = pltpu.make_async_copy(head_buf, head_out, local.at[6])
    head_copy.start()
    totals_two = settled(going, held_three)
    shift_grad, gain_grad = unpacked(totals_two[:rows]), unpacked(totals_two[rows : 2 * rows])
    factor = gain_two * scale_two / count
    for copy in roots_a:
        copy.wait()
    part = roots_out.at[:, y, :, core, :, left]
    roots_a = [copies.start(part, part, mate_y)]
    for copy in roots_b:
        copy.wait()
    part = roots_out.at[:, :, x, core, :, right]
    roots_b = [copies.start(part, part, peer) for peer in mates_x]

    def leave_second(p, _):
        normed = (second[pixel_rows(p), :] - mean_two) * scale_two
        pre = gain_two * normed + shift_two
        sigma = sigmoid(pre)
        kept = across(valid[pixel_rows(p), :])
        d_pre = d_act[...] * kept * (sigma * (1.0 + pre * (1.0 - sigma)))
        d_z = factor * (count * d_pre - shift_grad - normed * gain_grad) * kept
        grad_pad[padded_pixel(p), :] = d_z.astype(low)
        return 0

    lax.fori_loop(0, pixels, leave_second, 0)

    partial[...] = jnp.zeros(partial.shape, f32)

    def spread_line(j, _):
        value = None
        for t in range(9):
            offset = (t // 3 - 1) * wide_line + (t % 3 - 1) * slots
            rows_in = pl.ds(pl.multiple_of(rim + j * wide_line - offset, slots), line)
            term = dot(grad_pad[rows_in, :], taps[:, t * width : (t + 1) * width], 1, 0)
            value = term if value is None else value + term
        second[line_rows(j), :] = value
        return 0

    lax.fori_loop(0, side, spread_line, 0)
    def enter_first(p, _):
        normed = (first[pixel_rows(p), :] - mean_one) * scale_one
        pre = gain_one * normed + shift_one
        sigma = sigmoid(pre)
        d_pre = second[pixel_rows(p), :] * across(valid[pixel_rows(p), :]) * (sigma * (1.0 + pre * (1.0 - sigma)))
        second[pixel_rows(p), :] = d_pre
        partial[0] += fold(d_pre)
        partial[1] += fold(d_pre * normed)
        return 0

    lax.fori_loop(0, pixels, enter_first, 0)
    pack_four[...] = jnp.concatenate([packed(total_of(0)), packed(total_of(1))], axis=0)
    going = exchange(pack_four, held_four)

    def turn(j, _):
        rows_in = pl.ds(pl.multiple_of(rim + j * wide_line, slots), wide_line)
        turned_grad[:, pl.ds(pl.multiple_of(j * wide_line, 128), wide_line)] = grad_pad[rows_in, :].T
        return 0

    lax.fori_loop(0, side, turn, 0)

    def leave(slot, target, sem):
        copy = pltpu.make_async_copy(grad_buf.at[slot], target, local.at[sem])
        copy.start()
        return copy

    half = nz // 2
    near = z // half * half + lax.rem(z + 1, half)
    kinds = "".join(chunk_rounds(9))
    core_going, first_going = [], []

    def part_of(t, mine):
        if kinds[t] == "x":
            return [(tap_sums.at[t, :, :, x if mine else lax.rem(x + 1, nx)], first_in.at[t])]
        if kinds[t] == "y":
            return [(tap_sums.at[t, :, y if mine else 1 - y], first_in.at[t])]
        return [(tap_sums.at[t, (z // half * half + lax.rem(z, half) if mine else near) % half + h * half],
                 first_in.at[t, pl.ds(2 * h, 2)]) for h in range(2)]

    def over_core(t):
        core_going[t].wait()
        for i in range(nz):
            tap_sums[t, i] += core_in[t, i]
        peer = {"x": at(z, y, lax.rem(x + 1, nx), core), "y": mate_y, "z": at(near, y, x, core)}[kinds[t]]
        first_going.append([copies.start(source, target, peer) for source, target in part_of(t, False)])

    for t in range(9):
        offset = (t // 3 - 1) * wide_line + (t % 3 - 1) * slots
        slot = t % 2
        shifted = hidden_pad.at[pl.ds(rim + offset, body_rows)]
        grad_buf[slot] = dot(turned_grad[...], shifted[...], 1, 0).reshape(grad_buf.shape[1:])
        core_going.append(copies.start(grad_buf.at[slot, :, :, :, 1 - core], core_in.at[t], mate))
        for i in range(nz):
            tap_sums[t, i] = grad_buf[slot, i, :, :, core]
        if t:
            over_core(t - 1)
    over_core(8)
    leaving = []

    for copy in roots_a + roots_b:
        copy.wait()
    part = roots_out.at[:, :, :, core]
    roots_core = copies.start(part, part, mate)
    totals_one = settled(going, held_four)
    shift_sum, gain_sum = unpacked(totals_one[:rows]), unpacked(totals_one[rows : 2 * rows])
    factor_one = gain_one * scale_one / count

    def leave_first(p, _):
        normed = (first[pixel_rows(p), :] - mean_one) * scale_one
        kept = across(valid[pixel_rows(p), :])
        d_z = factor_one * (count * second[pixel_rows(p), :] - shift_sum - normed * gain_sum) * kept
        grad_pad[padded_pixel(p), :] = d_z.astype(low)
        return 0

    lax.fori_loop(0, pixels, leave_first, 0)
    lax.fori_loop(0, side, turn, 0)
    per = width // depth
    for t in range(n // per):
        slot = (9 + t) % 2
        if t >= 2:
            leaving[t - 2].wait()
        block = jnp.concatenate([own_images[t * per + k].reshape(body_rows, depth) for k in range(per)], axis=1)
        grad_buf[slot] = dot(turned_grad[...], block, 1, 0).reshape(grad_buf.shape[1:])
        leaving.append(leave(slot, reduce_out.at[:, :, :, :, :, pl.ds(t * width, width)], 7 + slot))
    taps_going = []
    for t in range(9):
        for copy in first_going[t]:
            copy.wait()
        for h, (kept, landed) in enumerate(part_of(t, True)):
            kept[...] += landed[...]
            copy = pltpu.make_async_copy(
                kept, taps_out.at[t, pl.ds(2 * h, 2)] if kinds[t] == "z" else taps_out.at[t], local.at[9 + 2 * t + h])
            copy.start()
            taps_going.append(copy)
    for copy in taps_going:
        copy.wait()
    totals_out[...] = jnp.concatenate([totals_two, totals_one], axis=0)
    head_copy.wait()
    roots_core.wait()
    for copy in leaving[-2:]:
        copy.wait()


def local_step(images, spatial_weight, spatial_mask, reduce_weight, reduce_mask, head_weight, roots,
               norms, pixel_mask, labels, bias):
    n, nb = lax.axis_size("chan"), lax.axis_size("batch")
    nz, nx = n // 2, nb // 2
    slots, width = pixel_mask.shape[0] // n, norms.shape[1] * n
    line, depth, classes = SIDE * slots, images.shape[-1], bias.shape[1]
    f32, low = jnp.float32, jnp.bfloat16
    rows = spatial_weight.shape[0] // nb
    wide_weights, wide_roots = spatial_weight.shape[1] + reduce_weight.shape[1] + classes, roots.shape[0] * roots.shape[2]
    grids = ((SIDE * (SIDE + 1) + 2 * (SIDE + 2)) * slots, width)
    shape = jax.ShapeDtypeStruct
    gathered = lambda size: shape((nz, 2, nx, 2, rows, size), low)
    raw = lambda a: pltpu.VMEM((rows, a.shape[1]), a.dtype)
    held = lambda k: pltpu.VMEM((n * nb, k, 128), f32)
    pack = lambda k: pltpu.VMEM((k, 128), f32)
    count = 2 * (nz - 1) + (SIDE + 1) * (n - 1) + (1 + (nx - 1) + 1) + (2 * nx + 1) + 4 * (n * nb - 1) + 27
    two = 2 * width // 128
    three = two + classes // 128
    weight = lambda size: pltpu.VMEM((nz, 2, nx, 2, rows, size), low)
    taps, reduce, head, totals, mask, _, roots_full = pl.pallas_call(
        step_kernel,
        out_shape=(
            shape((9, nz, 2, rows, width), f32),
            shape((nz, 2, nx, 2, rows, n * depth), f32),
            shape((width, classes), f32),
            shape((two + three, 128), f32),
            shape((rows, wide_weights), f32),
            gathered(wide_weights),
            gathered(wide_roots),
        ),
        in_specs=[ANY] * 7 + [VMEM] * 4,
        out_specs=(ANY, ANY, ANY, VMEM, VMEM, ANY, ANY),
        scratch_shapes=[
            raw(spatial_weight), raw(spatial_mask), raw(reduce_weight), raw(reduce_mask), raw(head_weight),
            pltpu.VMEM((roots.shape[0], rows, width), f32),
            pltpu.VMEM((rows, wide_weights), low),
            pltpu.VMEM((rows, wide_roots), low),
            pltpu.VMEM((n, SIDE, line + slots, depth), low),
            pltpu.VMEM((SIDE * line, width), f32),
            pltpu.VMEM((SIDE * line, width), f32),
            pltpu.VMEM(grids, low),
            pltpu.VMEM(grids, low),
            pltpu.VMEM((width, SIDE * (line + slots)), low),
            weight(9 * width), weight(n * depth), weight(classes),
            pltpu.VMEM((SIDE * line, 128), f32),
            pltpu.VMEM((slots, 128), f32),
            pltpu.VMEM((slots, 128), f32),
            pltpu.VMEM((norms.shape[0], width), f32),
            pltpu.VMEM((n, norms.shape[0], width), f32),
            pack(two + 8), pack(two), pack(three), pack(two),
            held(two + 8), held(two), held(three), held(two),
            pltpu.VMEM((9, nz, 2, nx, rows, width), f32),
            pltpu.VMEM((9, nz, 2, nx, rows, width), f32),
            pltpu.VMEM((9, nz, 2, rows, width), f32),
            pltpu.VMEM((2, 8, width), f32),
            pltpu.VMEM((3, slots, width), f32),
            pltpu.VMEM((slots, width), low),
            pltpu.VMEM((slots, classes), low),
            pltpu.VMEM((slots, width), f32),
            pltpu.VMEM((width, classes), f32),
            pltpu.VMEM((2, nz, 2, nx, 2, rows, width), f32),
            DMA((count,)), DMA((count,)), DMA((27,)),
        ],
        compiler_params=pltpu.CompilerParams(collective_id=0, has_side_effects=True, vmem_limit_bytes=60 << 20),
        name="step",
    )(images.reshape(n, SIDE, line, depth), spatial_weight, spatial_mask, reduce_weight, reduce_mask, head_weight, roots,
      norms, pixel_mask, labels, bias)
    return taps, reduce, head, totals[:three], totals[three:], mask, roots_full.reshape(width, wide_roots)


def chunk_rounds(count):
    rounds = []
    while count > 0:
        rounds.append(ORDERS[len(rounds) % len(ORDERS)][:count])
        count -= len(rounds[-1])
    return rounds


def settle_kernel(
    chunks, taps, reduce, head, mask, left_root, roots, own, left_part, right_part, outer_out, size,
    full, factors, lefts, rights, outers, squares, held, sums, core_in, first_in, second_in, near_in, across_in,
    final, final_low, send, recv, local,
):
    (z, y, x, core), (nz, ny, nx, nc) = place()
    half = nz // 2
    across_z = lax.rem(z + half, nz)
    base_z = z // half * half
    near_z = [base_z + lax.rem(lax.rem(z, half) + k, half) for k in range(1, half)]
    others_x = turned(x, nx)
    mate, mate_y = at(z, y, x, 1 - core), at(z, 1 - y, x, core)
    mates_x = [at(z, y, k, core) for k in others_x]
    mates_near = [at(k, y, x, core) for k in near_z]
    mate_across = at(across_z, y, x, core)
    c, n = lax.axis_index("chan"), lax.axis_size("chan")
    others = [{"chan": k} for k in turned(c, n)]
    greeted = greet(others + mates_x + [mate])
    copies = Copies(send, recv)
    f32, low = jnp.float32, jnp.bfloat16
    rows, width = left_root.shape[1:]
    tiles_one = reduce.shape[-1] // width
    n_taps = taps.shape[0]
    sources = ((reduce, n_taps * width), (head, n_taps * width + reduce.shape[-1]))
    wide = n_taps * width + reduce.shape[-1]
    used_local = [0]

    def keep(source, target):
        copy = pltpu.make_async_copy(source, target, local.at[used_local[0]])
        used_local[0] += 1
        copy.start()
        return copy

    roots_in = [keep(roots, factors)]
    pick = (lax.broadcasted_iota(jnp.int32, (rows, width), 1)
            == lax.broadcasted_iota(jnp.int32, (rows, width), 0) + c * rows).astype(low)
    squares[...] = jnp.zeros(squares.shape, f32)
    outgoing = []

    def two_parts(value):
        high = value.astype(low)
        return [high, (value - high.astype(f32)).astype(low)]

    def multiply(t, columns):
        grad = full[:, :, :, :, :, columns].reshape(width, width)
        mine = full[z, y, :, :, :, columns].reshape(rows, width)
        first = dot(jnp.concatenate([mine, pick], axis=0), grad, 1, 1)
        lefts[t] = first[:rows]
        second = dot(jnp.concatenate([first[rows:].astype(low)] + two_parts(left_root[t]), axis=0), grad, 1, 0)
        rights[t] = second[:rows]
        inner = second[rows : 2 * rows] + second[2 * rows :]
        third = dot(jnp.concatenate(two_parts(inner), axis=0), factors[:, t * width : (t + 1) * width], 1, 0)
        value = third[:rows] + third[rows:]
        outers[t] = value
        squares[t : t + 1, :] = jnp.full((1, 128), jnp.sum(value * value), f32)
        outgoing.extend(keep(a.at[t], b.at[t]) for a, b in ((lefts, left_part), (rights, right_part), (outers, outer_out)))

    def wait(going):
        for copy in going:
            copy.wait()

    def enter(start, size):
        columns = pl.ds(start, size)
        going = []
        for source, first_column in sources:
            begin, end = max(start, first_column), min(start + size, first_column + source.shape[-1])
            if begin < end:
                taken, landed = pl.ds(begin - first_column, end - begin), pl.ds(begin, end - begin)
                going.append(copies.start(source.at[:, :, :, 1 - core, :, taken], core_in.at[:, :, :, :, landed], mate))
                going.append(keep(source.at[:, :, :, core, :, taken], sums.at[:, :, :, :, landed]))
        yield
        wait(going)
        for i in range(nz):
            for j in range(ny):
                for k in range(nx):
                    sums[i, j, k, :, columns] += core_in[i, j, k, :, columns]

    def settled(start, last_in, columns):
        total = (sums[z, y, x, :, columns] + last_in) * mask[:, columns]
        final[:, columns] = total
        kept = [keep(final.at[:, columns], own.at[x, core, :, columns])]
        kept += [copies.start(final.at[:, columns], own.at[x, core, :, columns], peer) for peer in mates_x]
        if start < wide:
            final_low[:, columns] = total.astype(low)
            return kept, [keep(final_low.at[:, columns], full.at[z, y, x, core, :, columns])]
        return kept, []

    def own_core(kept, columns):
        wait(kept)
        part = own.at[:, core, :, columns]
        return copies.start(part, part, mate)

    def block_of(start, columns):
        t = start // width
        if roots_in:
            roots_in.pop().wait()
        multiply(t + tiles_one if t < n_taps else t - n_taps, columns)

    def chunk_z(start, size):
        columns = pl.ds(start, size)
        if start < n_taps * width:
            going = [keep(taps.at[start // width, pl.ds(2 * h, 2)], sums.at[lax.rem(z, half) + h * half, :, :, :, columns])
                     for h in range(2)]
            yield
            wait(going)
        else:
            yield from enter(start, size)
            going = []
            for t, k in enumerate(near_z):
                for h in range(2):
                    there = lax.rem(k, half) + h * half
                    going.append(copies.start(
                        sums.at[there, :, :, :, columns], first_in.at[t, pl.ds(2 * h, 2), :, :, columns], mates_near[t]))
            yield
            wait(going)
            for t in range(half - 1):
                for h in range(2):
                    for j in range(ny):
                        for k in range(nx):
                            sums[lax.rem(z, half) + h * half, j, k, :, columns] += first_in[t, 2 * h + j, k, :, columns]
        landing = [second_in.at[0, pl.ds(nx * j, nx), :, columns] for j in range(ny)]
        going = [copies.start(sums.at[across_z, j, :, :, columns], landing[j], mate_across) for j in range(ny)]
        yield
        wait(going)
        for j in range(ny):
            for k in range(nx):
                sums[z, j, k, :, columns] += second_in[0, nx * j + k, :, columns]
        going = [copies.start(sums.at[z, :, k, :, columns], near_in.at[t, :, :, columns], mates_x[t])
                 for t, k in enumerate(others_x)]
        yield
        wait(going)
        for t in range(nx - 1):
            for j in range(ny):
                sums[z, j, x, :, columns] += near_in[t, j, :, columns]
        going = [copies.start(sums.at[z, 1 - y, x, :, columns], across_in.at[:, columns], mate_y)]
        yield
        wait(going)
        kept, going = settled(start, across_in[:, columns], columns)
        going += [copies.start(final_low.at[:, columns], full.at[z, y, x, core, :, columns], peer) for peer in mates_x]
        yield
        last = [own_core(kept, columns)]
        wait(going)
        part = full.at[z, y, :, core, :, columns]
        going = [copies.start(part, part, mate_y)]
        yield
        wait(going)
        part = full.at[z, :, :, core, :, columns]
        going = [copies.start(part, part, peer) for peer in [mate_across] + mates_near]
        yield
        wait(going)
        part = full.at[across_z, :, :, core, :, columns]
        going = [copies.start(part, part, peer) for peer in mates_near]
        yield
        wait(going)
        part = full.at[:, :, :, core, :, columns]
        last.append(copies.start(part, part, mate))
        yield
        wait(last)
        block_of(start, columns)

    def chunk(start, size, x_first):
        columns = pl.ds(start, size)
        if start < n_taps * width:
            going = [keep(taps.at[start // width], sums.at[:, :, x, :, columns] if x_first else sums.at[:, y, :, :, columns])]
            yield
            wait(going)
        else:
            yield from enter(start, size)
            if x_first:
                going = [copies.start(sums.at[:, :, k, :, columns], first_in.at[t, :, :, :, columns], mates_x[t])
                         for t, k in enumerate(others_x)]
            else:
                going = [copies.start(sums.at[:, 1 - y, :, :, columns], first_in.at[0, :, :, :, columns], mate_y)]
            yield
            wait(going)
            for i in range(nz):
                for j in range(2):
                    if x_first:
                        sums[i, j, x, :, columns] += first_in[0, i, j, :, columns]
                    else:
                        sums[i, y, j, :, columns] += first_in[0, i, j, :, columns]
        going = []
        if x_first:
            going.append(copies.start(sums.at[:, 1 - y, x, :, columns], second_in.at[0, :, :, columns], mate_y))
        else:
            for t, k in enumerate(others_x):
                going.append(copies.start(sums.at[:, y, k, :, columns], second_in.at[t, :, :, columns], mates_x[t]))
        yield
        wait(going)
        for t in range(1 if x_first else nx - 1):
            for i in range(nz):
                sums[i, y, x, :, columns] += second_in[t, i, :, columns]
        going = []
        for t, k in enumerate(near_z):
            for h in range(2):
                there = lax.rem(k + h * half, nz)
                going.append(copies.start(sums.at[there, y, x, :, columns], near_in.at[t, h, :, columns], mates_near[t]))
        yield
        wait(going)
        for t in range(half - 1):
            for h in range(2):
                sums[lax.rem(z + h * half, nz), y, x, :, columns] += near_in[t, h, :, columns]
        going = [copies.start(sums.at[across_z, y, x, :, columns], across_in.at[:, columns], mate_across)]
        yield
        wait(going)
        kept, going = settled(start, across_in[:, columns], columns)
        if start < wide:
            going += [copies.start(final_low.at[:, columns], full.at[z, y, x, core, :, columns], peer)
                      for peer in [mate_across] + mates_near]
        yield
        rows_core = [own_core(kept, columns)]
        if start < wide:
            wait(going)
            part = full.at[across_z, y, x, core, :, columns]
            going = [copies.start(part, part, peer) for peer in mates_near]
            yield
            wait(going)
            part = full.at[:, y, x, core, :, columns]
            going = [copies.start(part, part, peer) for peer in (mates_x if x_first else [mate_y])]
            yield
            wait(going)
            part = full.at[:, y, :, core, :, columns] if x_first else full.at[:, :, x, core, :, columns]
            going = [copies.start(part, part, peer) for peer in ([mate_y] if x_first else mates_x)]
            yield
            wait(going)
            part = full.at[:, :, :, core, :, columns]
            rows_core.append(copies.start(part, part, mate))
        yield
        wait(rows_core)
        if start < wide:
            block_of(start, columns)

    rounds = [[chunk_z(*c[:2]) if c[2] == "z" and c[0] < wide else chunk(*c[:2], c[2] != "y") for c in some] for some in chunks]
    begun, active = rounds.pop(0), []
    for going in begun:
        next(going)
    greeted()
    while rounds or begun or active:
        active += begun
        begun = rounds.pop(0) if rounds else []
        for going in begun:
            next(going)
        for going in active[::-1]:
            try:
                next(going)
            except StopIteration:
                active.remove(going)
    going = [copies.start(squares, held.at[k + 1], peer) for k, peer in enumerate(others)]
    held[0] = squares[...]
    wait(going + outgoing)
    size[...] = jnp.sqrt(jnp.sum(held[...], axis=0) / (width * width) + 1e-06)


def settle(taps, reduce, head, mask, left_root, roots):
    nz, nx, n = lax.axis_size("chan") // 2, lax.axis_size("batch") // 2, lax.axis_size("chan")
    blocks, own_rows, width = left_root.shape
    rows = width // (4 * nz * nx)
    wide = taps.shape[0] * width + reduce.shape[-1]
    total = wide + head.shape[1]
    split = lambda a: a.reshape(nz, 2, nx, 2, rows, a.shape[1])
    f32, low = jnp.float32, jnp.bfloat16
    chunks, start = [], 0
    for kinds in chunk_rounds(total // width):
        chunks.append([(start + i * width, width, kind) for i, kind in enumerate(kinds)])
        start += len(kinds) * width
    near = nz // 2 - 1
    first = max(nx - 1, nx // 2)
    count = (total // width) * (4 + first + max(nx - 1, 1) + 2 * near + 1 + (nx - 1) + 1 + near + 1 + near + nx + 1) + n
    product = jax.ShapeDtypeStruct((blocks, own_rows, width), f32)
    padded = (blocks + 7) // 8 * 8
    own, left_part, right_part, outer, size = pl.pallas_call(
        functools.partial(settle_kernel, chunks),
        out_shape=(
            jax.ShapeDtypeStruct((nx, 2, rows, total), f32), product, product, product,
            jax.ShapeDtypeStruct((padded, 128), f32),
        ),
        in_specs=[ANY, ANY, ANY, VMEM, VMEM, ANY],
        out_specs=(ANY,) * 4 + (VMEM,),
        scratch_shapes=[
            pltpu.VMEM((nz, 2, nx, 2, rows, wide), low),
            pltpu.VMEM(roots.shape, low),
            pltpu.VMEM(product.shape, f32),
            pltpu.VMEM(product.shape, f32),
            pltpu.VMEM(product.shape, f32),
            pltpu.VMEM((padded, 128), f32),
            pltpu.VMEM((n, padded, 128), f32),
            pltpu.VMEM((nz, 2, nx, rows, total), f32),
            pltpu.VMEM((nz, 2, nx, rows, total), f32),
            pltpu.VMEM((first, nz, 2, rows, total), f32),
            pltpu.VMEM((max(nx - 1, 1), nz, rows, total), f32),
            pltpu.VMEM((near, 2, rows, total), f32),
            pltpu.VMEM((rows, total), f32),
            pltpu.VMEM((rows, total), f32),
            pltpu.VMEM((rows, wide), low),
            DMA((count,)), DMA((count,)), DMA((7 * (total // width) + 4,)),
        ],
        compiler_params=pltpu.CompilerParams(collective_id=1, has_side_effects=True, vmem_limit_bytes=60 << 20),
        name="settle",
    )(taps, reduce, split(head), mask, left_root, roots)
    return own.reshape(own_rows, total), left_part, right_part, outer, size


def finish_kernel(
    size, head_weight, head_first, head_second,
    own, left_part, right_part, outer, left_stats, right_stats, reduce_weight, spatial_weight, reduce_mask, spatial_mask,
    head_new, head_first_new, head_second_new,
    reduce_grad, spatial_grad, reduce_new, spatial_new, left_new, right_new,
    own_rows, lefts, rights, outers, left_kept, right_kept, weights, masks, arrive, leave,
):
    blocks, rows, width = outers.shape
    c_in, taps = reduce_weight.shape[1], spatial_weight.shape[1]
    tiles_one = c_in // width
    groups = [(0, tiles_one)] + [(t, min(t + 3, blocks)) for t in range(tiles_one, blocks, 3)]
    every = [pltpu.make_async_copy(own, own_rows, arrive.at[0, 7])]
    coming = []
    for g, (begin, end) in enumerate(groups):
        some, columns = pl.ds(begin, end - begin), pl.ds(begin * width, (end - begin) * width)
        theirs = pl.ds((begin if g == 0 else begin - tiles_one) * width, (end - begin) * width)
        pairs = [(a.at[some], b.at[some]) for a, b in (
            (left_part, lefts), (right_part, rights), (outer, outers), (left_stats, left_kept), (right_stats, right_kept))]
        pairs += [((reduce_weight if g == 0 else spatial_weight).at[:, theirs], weights.at[:, columns]),
                  ((reduce_mask if g == 0 else spatial_mask).at[:, theirs], masks.at[:, columns])]
        coming.append([pltpu.make_async_copy(a, b, arrive.at[g, i]) for i, (a, b) in enumerate(pairs)])
    for copy in every + [copy for group in coming for copy in group]:
        copy.start()
    going = []

    def out(source, target):
        copy = pltpu.make_async_copy(source, target, leave.at[len(going)])
        copy.start()
        going.append(copy)

    every[0].wait()
    out(own_rows.at[:, pl.ds(0, taps)], spatial_grad)
    out(own_rows.at[:, pl.ds(taps, c_in)], reduce_grad)
    head_grad = own_rows[:, taps + c_in : taps + c_in + head_weight.shape[1]]
    head_new[...], head_first_new[...], head_second_new[...] = adam_step(
        head_weight[...], head_grad, head_first[...], head_second[...], 0.04, 0.1)
    for g, (begin, end) in enumerate(groups):
        for copy in coming[g]:
            copy.wait()

        def block(t, _):
            columns = pl.ds(pl.multiple_of(t * width, width), width)
            lefts[t] = 0.95 * left_kept[t] + lefts[t]
            rights[t] = 0.95 * right_kept[t] + rights[t]
            step = outers[t] / jnp.concatenate([size[pl.ds(t, 1), :]] * (width // 128), axis=1)
            weight = weights[:, columns]
            weights[:, columns] = weight - 0.02 * masks[:, columns].astype(jnp.float32) * (step + 0.1 * weight)
            return 0

        lax.fori_loop(begin, end, block, 0)
        some, columns = pl.ds(begin, end - begin), pl.ds(begin * width, (end - begin) * width)
        theirs = pl.ds((begin if g == 0 else begin - tiles_one) * width, (end - begin) * width)
        out(lefts.at[some], left_new.at[some])
        out(rights.at[some], right_new.at[some])
        out(weights.at[:, columns], (reduce_new if g == 0 else spatial_new).at[:, theirs])
    for copy in going:
        copy.wait()


def finish(own, left_part, right_part, outer, size, left_stats, right_stats,
           reduce_weight, spatial_weight, reduce_mask, spatial_mask, head_weight, head_first, head_second):
    blocks, rows, width = left_stats.shape
    like = lambda a: jax.ShapeDtypeStruct(a.shape, jnp.float32)
    wide = reduce_weight.shape[1] + spatial_weight.shape[1]
    products = pltpu.VMEM(left_stats.shape, jnp.float32)
    groups = 1 + -(-(spatial_weight.shape[1] // width) // 3)
    head_new, head_first_new, head_second_new, *rest = pl.pallas_call(
        finish_kernel,
        out_shape=(like(head_weight), like(head_weight), like(head_weight), like(reduce_weight), like(spatial_weight),
                   like(reduce_weight), like(spatial_weight), like(left_stats), like(left_stats)),
        in_specs=[VMEM] * 4 + [ANY] * 10,
        out_specs=(VMEM,) * 3 + (ANY,) * 6,
        scratch_shapes=[pltpu.VMEM(own.shape, jnp.float32)] + [products] * 5
        + [pltpu.VMEM((rows, wide), jnp.float32), pltpu.VMEM((rows, wide), jnp.int32),
           DMA((groups, 8)), DMA((2 + 3 * groups,))],
        compiler_params=pltpu.CompilerParams(vmem_limit_bytes=60 << 20),
        name="finish",
    )(size, head_weight, head_first, head_second, own, left_part, right_part, outer, left_stats, right_stats,
      reduce_weight, spatial_weight, reduce_mask, spatial_mask)
    return *rest, head_new, head_first_new, head_second_new


def silu_slope(pre):
    sigma = jax.nn.sigmoid(pre)
    return sigma * (1.0 + pre * (1.0 - sigma))


def adam_step(param, grad, first, second, rate, decay):
    first = 0.9 * first + 0.1 * grad
    second = 0.999 * second + 0.001 * grad * grad
    mhat = first / (1.0 - 0.9**STEP)
    vhat = second / (1.0 - 0.999**STEP)
    return (param - rate * (mhat / (jnp.sqrt(vhat) + 1e-08) + decay * param), first, second)


def own_part(array, axis, name="chan"):
    size = array.shape[axis] // lax.axis_size(name)
    return lax.dynamic_slice_in_dim(array, lax.axis_index(name) * size, size, axis)


def body(
    images,
    pixel_mask,
    labels,
    reduce_weight,
    reduce_mask,
    spatial_weight,
    spatial_mask,
    head_weight,
    head_bias,
    norm_params,
    left_stats,
    right_stats,
    left_root,
    input_side_roots,
    head_first,
    head_second,
    bias_first,
    bias_second,
    norm_first,
    norm_second,
):
    n = lax.axis_size("chan")
    pixels, channels = images.shape[1:]
    side = SIDE
    rows_out, c_in = reduce_weight.shape
    width = left_stats.shape[2]
    classes = head_weight.shape[1]
    padded = 1024
    slots = images.shape[0] // n
    f32 = jnp.float32

    by_pixel = images.reshape(n, slots, pixels, channels).transpose(0, 2, 1, 3)
    taps_local, reduce_local, head_local, sums_two, sums_one, mask_rows, roots_full = local_step(
        by_pixel, spatial_weight, spatial_mask, reduce_weight, reduce_mask, head_weight, input_side_roots, norm_params, pixel_mask, labels[:, None],
        jnp.pad(head_bias, (0, padded - classes), constant_values=-1e30)[None])

    own, *products = settle(taps_local, reduce_local, head_local, mask_rows, left_root, roots_full)
    of_norms = jnp.stack([a.reshape(-1) for a in (sums_one[4:], sums_one[:4], sums_two[4:8], sums_two[:4])])
    norm_gain_gradient = own_part(of_norms, 1)
    of_head = sums_two[8:].reshape(-1)
    bias_grad = of_head[:classes]
    loss_sum, slot_count = of_head[-1], of_head[-2]
    (reduce_grad, spatial_grad, reduce_new, spatial_new, left_new, right_new, head_new, head_first_new,
     head_second_new) = finish(
        own, *products, left_stats, right_stats, reduce_weight, spatial_weight, reduce_mask, spatial_mask,
        head_weight, head_first, head_second)
    bias_new, bias_first_new, bias_second_new = adam_step(head_bias, bias_grad, bias_first, bias_second, 0.1, 0.0)
    norm_new, norm_first_new, norm_second_new = adam_step(
        norm_params, norm_gain_gradient, norm_first, norm_second, 0.1, 0.0)
    return (
        loss_sum,
        slot_count,
        reduce_grad,
        spatial_grad,
        reduce_new,
        spatial_new,
        left_new,
        right_new,
        head_new,
        head_first_new,
        head_second_new,
        bias_new,
        bias_first_new,
        bias_second_new,
        norm_new,
        norm_first_new,
        norm_second_new,
    )


FULL_PRECISION = lax.Precision.HIGHEST
BOTH = ("chan", "batch")


def conv_grid(grid, taps, spec):
    return lax.conv_general_dilated(
        grid, taps, (1, 1), ((1, 1), (1, 1)), dimension_numbers=spec,
        preferred_element_type=jnp.float32,
    )


def plain_norm_forward(pre_norm, gain, shift, valid):
    first_sum = jnp.sum(pre_norm * valid, axis=(0, 1))
    second_sum = jnp.sum(pre_norm * pre_norm * valid, axis=(0, 1))
    first_sum, second_sum, count = lax.psum((first_sum, second_sum, jnp.sum(valid)), BOTH)
    mean = first_sum / count
    scale = lax.rsqrt(second_sum / count - mean * mean + EPS)
    normed = (pre_norm - mean) * scale
    pre = gain * normed + shift
    return (jax.nn.silu(pre) * valid, (normed, pre, scale, count))


def plain_norm_backward(grad_act, kept, gain, valid):
    normed, pre, scale, count = kept
    d_pre = grad_act * valid * silu_slope(pre)
    shift_gradient, gain_grad = lax.psum(
        (jnp.sum(d_pre, axis=(0, 1)), jnp.sum(d_pre * normed, axis=(0, 1))), BOTH
    )
    d_input = gain * scale / count * (count * d_pre - shift_gradient - normed * gain_grad) * valid
    return (d_input, gain_grad, shift_gradient)


def plain_own_part(array, parts, axis=0):
    size = array.shape[axis] // parts
    return lax.dynamic_slice_in_dim(array, lax.axis_index("chan") * size, size, axis)


def plain_body(
    images,
    pixel_mask,
    labels,
    reduce_weight,
    reduce_mask,
    spatial_weight,
    spatial_mask,
    head_weight,
    head_bias,
    norm_params,
    left_stats,
    right_stats,
    left_root,
    input_side_roots,
    head_first,
    head_second,
    bias_first,
    bias_second,
    norm_first,
    norm_second,
):
    parts = lax.axis_size("chan")
    pixels = images.shape[1]
    side = SIDE
    rows_out = reduce_weight.shape[0]
    width = left_stats.shape[2]
    classes = head_weight.shape[1]
    own_images = lax.all_to_all(images, "chan", 0, 2, tiled=True)
    slots = own_images.shape[0]
    reduce_float = reduce_mask.astype(jnp.float32)
    spatial_float = spatial_mask.astype(jnp.float32)
    gather = lambda a, axis: lax.all_gather(a, "chan", axis=axis, tiled=True)
    reduce_low = gather((reduce_weight * reduce_float).astype(jnp.bfloat16), 0)
    spatial_low = gather((spatial_weight * spatial_float).astype(jnp.bfloat16), 0)
    head_low = gather(head_weight.astype(jnp.bfloat16), 0)
    norm_full = gather(norm_params, 1)
    right_factor_full = gather(input_side_roots, 1)
    valid = plain_own_part(pixel_mask, parts).astype(jnp.float32)[:, :, None]
    own_labels = plain_own_part(labels, parts)
    filled = jnp.sum(valid[:, :, 0], axis=1)
    divisor = jnp.maximum(filled, 1.0)
    used = (filled > 0.0).astype(jnp.float32)
    taps = spatial_low.reshape(width, 3, 3, width)
    first_pre = jnp.einsum("spc,oc->spo", own_images, reduce_low, preferred_element_type=jnp.float32)
    first_act, first_kept = plain_norm_forward(first_pre, norm_full[0], norm_full[1], valid)
    hidden = first_act.astype(jnp.bfloat16).reshape(slots, side, side, width)
    second_pre = conv_grid(hidden, taps, ("NHWC", "OHWI", "NHWC")).reshape(slots, pixels, width)
    second_act, second_kept = plain_norm_forward(second_pre, norm_full[2], norm_full[3], valid)
    pooled = (jnp.sum(second_act, axis=1) / divisor[:, None]).astype(jnp.bfloat16)
    logits = jnp.dot(pooled, head_low, preferred_element_type=jnp.float32) + head_bias
    onehot = (jnp.arange(classes)[None, :] == own_labels[:, None]).astype(jnp.float32)
    log_total = jax.nn.logsumexp(logits, axis=1)
    picked = jnp.sum(onehot * logits, axis=1)
    loss_local = jnp.sum(used * (log_total - picked))
    d_logits = (used[:, None] * (jnp.exp(logits - log_total[:, None]) - onehot) / SLOTS_DEV).astype(
        jnp.bfloat16
    )
    head_grad = jnp.einsum("so,sc->oc", pooled, d_logits, preferred_element_type=jnp.float32)
    bias_grad = jnp.sum(d_logits.astype(jnp.float32), axis=0)
    d_pooled = jnp.einsum("sc,oc->so", d_logits, head_low, preferred_element_type=jnp.float32)
    d_act = jnp.broadcast_to((d_pooled / divisor[:, None])[:, None, :], second_act.shape)
    d_second, gain_two, shift_two = plain_norm_backward(d_act, second_kept, norm_full[2], valid)
    d_second = d_second.astype(jnp.bfloat16).reshape(slots, side, side, width)
    spatial_local = lax.conv_general_dilated(
        hidden, d_second, (1, 1), ((1, 1), (1, 1)), dimension_numbers=("CHWN", "IHWO", "NHWC"),
        preferred_element_type=jnp.float32,
    )
    spatial_local = spatial_local.transpose(3, 1, 2, 0).reshape(width, 9 * width)
    d_hidden = conv_grid(
        d_second, taps[:, ::-1, ::-1, :], ("NHWC", "IHWO", "NHWC")
    ).reshape(slots, pixels, width)
    d_first, gain_one, shift_one = plain_norm_backward(d_hidden, first_kept, norm_full[0], valid)
    d_first = d_first.astype(jnp.bfloat16)
    reduce_local = jnp.einsum("spc,spo->oc", own_images, d_first, preferred_element_type=jnp.float32)
    scatter = lambda a: lax.psum_scatter(a, "chan", scatter_dimension=0, tiled=True)
    reduce_grad, spatial_grad, head_grad = scatter(reduce_local), scatter(spatial_local), scatter(head_grad)
    reduce_grad, spatial_grad, head_grad = lax.psum((reduce_grad, spatial_grad, head_grad), "batch")
    reduce_grad = reduce_grad * reduce_float
    spatial_grad = spatial_grad * spatial_float
    bias_grad, loss_sum, slot_count = lax.psum((bias_grad, loss_local, jnp.sum(used)), BOTH)
    norm_gain_gradient = plain_own_part(jnp.stack([gain_one, shift_one, gain_two, shift_two], axis=0), parts, 1)
    tiles_one = reduce_weight.shape[1] // width
    blocks = jnp.concatenate(
        [
            reduce_grad.reshape(rows_out, tiles_one, width).transpose(1, 0, 2),
            spatial_grad.reshape(rows_out, 9, width).transpose(1, 0, 2),
        ],
        axis=0,
    )
    blocks_full = gather(blocks, 1)
    left_new = 0.95 * left_stats + jnp.einsum(
        "tak,tbk->tab", blocks, blocks_full, precision=FULL_PRECISION
    )
    own_columns = plain_own_part(blocks_full, parts, 2)
    right_new = 0.95 * right_stats + jnp.einsum(
        "tki,tkb->tib", own_columns, blocks_full, precision=FULL_PRECISION
    )
    matrix_product = jnp.einsum("tak,tkb->tab", left_root, blocks_full, precision=FULL_PRECISION)
    matrix_product = jnp.einsum(
        "ghk,gkl->ghl", matrix_product, right_factor_full, precision=FULL_PRECISION
    )
    squares = lax.psum(jnp.sum(matrix_product * matrix_product, axis=(1, 2)), "chan")
    step = matrix_product / jnp.sqrt(squares / (width * width) + 1e-06)[:, None, None]
    step_one = step[:tiles_one].transpose(1, 0, 2).reshape(rows_out, tiles_one * width)
    step_two = step[tiles_one:].transpose(1, 0, 2).reshape(rows_out, 9 * width)
    reduce_new = reduce_weight - 0.02 * reduce_float * (step_one + 0.1 * reduce_weight)
    spatial_new = spatial_weight - 0.02 * spatial_float * (step_two + 0.1 * spatial_weight)
    head_new, head_first_new, head_second_new = adam_step(
        head_weight, head_grad, head_first, head_second, 0.04, 0.1
    )
    bias_new, bias_first_new, bias_second_new = adam_step(
        head_bias, bias_grad, bias_first, bias_second, 0.1, 0.0
    )
    norm_new, norm_first_new, norm_second_new = adam_step(
        norm_params, norm_gain_gradient, norm_first, norm_second, 0.1, 0.0
    )
    return (
        loss_sum,
        slot_count,
        reduce_grad,
        spatial_grad,
        reduce_new,
        spatial_new,
        left_new,
        right_new,
        head_new,
        head_first_new,
        head_second_new,
        bias_new,
        bias_first_new,
        bias_second_new,
        norm_new,
        norm_first_new,
        norm_second_new,
    )


def solution(mesh):
    in_specs = (
        P("batch", None, "chan"),
        P("batch", None),
        P("batch"),
        P("chan", None),
        P("chan", None),
        P("chan", None),
        P("chan", None),
        P("chan", None),
        P(),
        P(None, "chan"),
        P(None, "chan", None),
        P(None, "chan", None),
        P(None, "chan", None),
        P(None, "chan", None),
        P("chan", None),
        P("chan", None),
        P(),
        P(),
        P(None, "chan"),
        P(None, "chan"),
    )
    out_specs = (
        P(),
        P(),
        P("chan", None),
        P("chan", None),
        P("chan", None),
        P("chan", None),
        P(None, "chan", None),
        P(None, "chan", None),
        P("chan", None),
        P("chan", None),
        P("chan", None),
        P(),
        P(),
        P(),
        P(None, "chan"),
        P(None, "chan"),
        P(None, "chan"),
    )
    chan, batch = mesh.shape["chan"], mesh.shape["batch"]
    fits = chan == 8 and batch == 4 and WIDTH % (16 * chan * batch) == 0 and SLOTS_DEV % (16 * chan) == 0
    return jax.shard_map(body if fits else plain_body, mesh=mesh, in_specs=in_specs, out_specs=out_specs, check_vma=False)
```

```python
import functools

import jax
import jax.numpy as jnp
from jax import lax
from jax.experimental import pallas as pl
from jax.experimental.pallas import tpu as pltpu
from jax.sharding import PartitionSpec as P

SIDE = 7
SLOTS_DEV = 384
STEP = 10
ORDERS = ("xyz", "xy")

WIDTH = 512
EPS = 1e-05
MESH = pl.DeviceIdType.MESH
ANY = pl.BlockSpec(memory_space=pl.ANY)
VMEM = pl.BlockSpec(memory_space=pltpu.VMEM)
DMA = pltpu.SemaphoreType.DMA
SMALL = 8


def place():
    c, b = lax.axis_index("chan"), lax.axis_index("batch")
    nz, nx = lax.axis_size("chan") // 2, lax.axis_size("batch") // 2
    return (c // 2, lax.rem(c, 2), b // 2, lax.rem(b, 2)), (nz, 2, nx, 2)


def at(z, y, x, core):
    return {"chan": z * 2 + y, "batch": x * 2 + core}


def turned(index, size):
    return [lax.rem(index + k, size) for k in range(1, size)]


def greet(peers):
    barrier = pltpu.get_barrier_semaphore()
    for peer in peers:
        pl.semaphore_signal(barrier, inc=1, device_id=peer, device_id_type=MESH)
    return lambda: pl.semaphore_wait(barrier, len(peers))


class Copies:
    def __init__(self, send, recv):
        self.send, self.recv, self.used = send, recv, 0

    def start(self, source, target, peer):
        copy = pltpu.make_async_remote_copy(
            source, target, self.send.at[self.used], self.recv.at[self.used],
            device_id=peer, device_id_type=MESH,
        )
        self.used += 1
        copy.start()
        return copy


def dot(left, right, left_dim, right_dim):
    return lax.dot_general(left, right, (((left_dim,), (right_dim,)), ((), ())), preferred_element_type=jnp.float32)


def sigmoid(value):
    return 1.0 / (1.0 + jnp.exp(-value))


def packed(row):
    return jnp.concatenate([row[:, i : i + 128] for i in range(0, row.shape[1], 128)], axis=0)


def unpacked(block):
    return jnp.concatenate([block[i : i + 1] for i in range(block.shape[0])], axis=1)


def step_kernel(
    images, spatial_weight, spatial_mask, reduce_weight, reduce_mask, head_weight, input_roots,
    own_norms, pixel_mask, all_labels, bias,
    taps_out, reduce_out, head_out, totals_out, mask_out, weights_out, roots_out,
    raw_spatial, raw_spatial_mask, raw_reduce, raw_reduce_mask, raw_head, raw_roots, weights, roots,
    own_images, first, second, hidden_pad, grad_pad, turned_grad, taps, reduce_low, head_low,
    valid, used, divisor, norms, norms_held, pack_one, pack_two, pack_three, pack_four, held_one, held_two, held_three, held_four,
    tap_sums, core_in, first_in, partial, pooling, pooled_low, d_logits, d_act, head_buf, grad_buf, send, recv, local,
):
    (z, y, x, core), (nz, ny, nx, nc) = place()
    c, n = lax.axis_index("chan"), lax.axis_size("chan")
    f32, low = jnp.float32, jnp.bfloat16
    slots = used.shape[0]
    side = SIDE
    line = side * slots
    wide_line = (side + 1) * slots
    pixels = side * side
    rim = (side + 2) * slots
    body_rows = side * wide_line
    width = first.shape[1]
    depth = own_images.shape[-1]
    everyone = [
        at(lax.rem(z + i, nz), lax.rem(y + j, ny), lax.rem(x + k, nx), lax.rem(core + m, nc))
        for i in range(nz) for j in range(ny) for k in range(nx) for m in range(nc) if i + j + k + m
    ]
    row_count = weights.shape[0]
    quarter = pl.ds(pl.multiple_of((x * nc + core) * row_count, row_count), row_count)
    raw = ((spatial_weight, raw_spatial), (spatial_mask, raw_spatial_mask), (reduce_weight, raw_reduce),
           (reduce_mask, raw_reduce_mask), (head_weight, raw_head))
    raw = [pltpu.make_async_copy(a.at[quarter], b, local.at[9 + i]) for i, (a, b) in enumerate(raw)]
    raw.append(pltpu.make_async_copy(input_roots.at[:, quarter], raw_roots, local.at[9 + len(raw)]))
    for copy in raw:
        copy.start()
    greeted = greet(everyone)
    copies = Copies(send, recv)
    others = turned(c, n)
    for copy in raw:
        copy.wait()
    size_taps, size_reduce = raw_spatial.shape[1], raw_reduce.shape[1]
    size_both = size_taps + size_reduce
    weights[:, size_both:] = jnp.zeros((row_count, weights.shape[1] - size_both), low)
    weights[:, :size_taps] = (raw_spatial[...] * raw_spatial_mask[...].astype(f32)).astype(low)
    weights[:, size_taps:size_both] = (raw_reduce[...] * raw_reduce_mask[...].astype(f32)).astype(low)
    weights[:, size_both : size_both + raw_head.shape[1]] = raw_head[...].astype(low)
    greeted()
    across_z = lax.rem(z + nz // 2, nz)
    near_z = [z // (nz // 2) * (nz // 2) + lax.rem(lax.rem(z, nz // 2) + k, nz // 2) for k in range(1, nz // 2)]
    mate, mate_y = at(z, y, x, 1 - core), at(z, 1 - y, x, core)
    mates_x = [at(z, y, k, core) for k in turned(x, nx)]

    def begin_z(source, target, sem):
        keep = pltpu.make_async_copy(source, target.at[z, y, x, core], local.at[sem])
        keep.start()
        peers = [at(k, y, x, core) for k in [across_z] + near_z]
        return [keep] + [copies.start(source, target.at[z, y, x, core], peer) for peer in peers]

    def pass_z(target, begun):
        for copy in begun:
            copy.wait()
        part = target.at[across_z, y, x, core]
        return [copies.start(part, part, at(k, y, x, core)) for k in near_z]

    lane = lax.broadcasted_iota(jnp.int32, norms.shape, 1)
    own_width = own_norms.shape[1]
    mine = (lane >= c * own_width) & (lane < (c + 1) * own_width)
    norms[...] = jnp.where(mine, jnp.concatenate([own_norms[...]] * n, axis=1), 0.0)

    weights_z = pass_z(weights_out, begin_z(weights, weights_out, 0))
    norm_copies = [copies.start(norms, norms_held.at[k + 1], {"chan": other}) for k, other in enumerate(others)]
    image_copies = [[copies.start(images.at[k, j], own_images.at[c, j, pl.ds(0, line)], {"chan": k}) for k in others]
                    for j in range(side)]
    own = pltpu.make_async_copy(images.at[c], own_images.at[c, :, pl.ds(0, line)], local.at[2])
    own.start()
    norms_held[0] = norms[...]

    for t in range(raw_roots.shape[0]):
        roots[:, t * width : (t + 1) * width] = raw_roots[t].astype(low)
    mask_out[:, :size_taps] = raw_spatial_mask[...].astype(f32)
    mask_out[:, size_taps:size_both] = raw_reduce_mask[...].astype(f32)
    mask_out[:, size_both:] = jnp.ones((row_count, mask_out.shape[1] - size_both), f32)

    own_slots = pl.ds(pl.multiple_of(c * slots, slots), slots)
    mask = pixel_mask[own_slots, :].astype(f32)
    for p in range(pixels):
        valid[p * slots : (p + 1) * slots, :] = jnp.broadcast_to(mask[:, p : p + 1], (slots, 128))
    filled = jnp.broadcast_to(jnp.sum(mask, axis=1, keepdims=True), (slots, 128))
    used[...] = (filled > 0.0).astype(f32)
    divisor[...] = jnp.maximum(filled, 1.0)

    def clear(i, _):
        rows = pl.ds(pl.multiple_of(i * slots, slots), slots)
        hidden_pad[rows, :] = jnp.zeros((slots, width), low)
        grad_pad[rows, :] = jnp.zeros((slots, width), low)
        return 0

    lax.fori_loop(0, hidden_pad.shape[0] // slots, clear, 0)
    for k in range(n):
        for j in range(side):
            own_images[k, j, pl.ds(line, slots), :] = jnp.zeros((slots, depth), low)

    for copy in weights_z:
        copy.wait()
    part = weights_out.at[:, y, x, core]
    copies.start(part, part, mate_y).wait()
    part = weights_out.at[:, :, x, core]
    along_x = [copies.start(part, part, peer) for peer in mates_x]
    for copy in along_x:
        copy.wait()
    part = weights_out.at[:, :, :, core]
    copies.start(part, part, mate).wait()
    fetched = []
    start = 0
    for j, held in enumerate((taps, reduce_low, head_low)):
        size = held.shape[-1]
        copy = pltpu.make_async_copy(weights_out.at[:, :, :, :, :, pl.ds(start, size)], held, local.at[3 + j])
        copy.start()
        fetched.append(copy)
        start += size
    for copy in fetched:
        copy.wait()
    taps, reduce_low, head_low = (held.reshape(width, held.shape[-1]) for held in (taps, reduce_low, head_low))
    for copy in norm_copies:
        copy.wait()
    norm_rows = jnp.sum(norms_held[...], axis=0)
    gain_one, shift_one, gain_two, shift_two = (norm_rows[i : i + 1] for i in range(4))

    def line_rows(j):
        return pl.ds(pl.multiple_of(j * line, slots), line)

    def pixel_rows(p):
        return pl.ds(pl.multiple_of(p * slots, slots), slots)

    def padded_pixel(p):
        j = p // side
        return pl.ds(pl.multiple_of(rim + (p + j) * slots, slots), slots)

    def across(block):
        return jnp.concatenate([block] * (width // 128), axis=1)

    def fold(value):
        return jnp.sum(value.reshape(-1, 8, width), axis=0)

    def total_of(index):
        return jnp.sum(partial[index], axis=0, keepdims=True)

    def exchange(pack, held):
        pack_copies = [copies.start(pack, held.at[k + 1], peer) for k, peer in enumerate(everyone)]
        held[0] = pack[...]
        return pack_copies

    def settled(pack_copies, held):
        for copy in pack_copies:
            copy.wait()
        return jnp.sum(held[...], axis=0)

    def add_to_sums(ref):
        def add(p, _):
            value = ref[pixel_rows(p), :]
            kept = value * across(valid[pixel_rows(p), :])
            partial[0] += fold(kept)
            partial[1] += fold(kept * value)
            return 0

        return add

    own.wait()
    partial[...] = jnp.zeros(partial.shape, f32)
    for j in range(side):
        for copy in image_copies[j]:
            copy.wait()
        block = jnp.concatenate([own_images[k, j, pl.ds(0, line), :] for k in range(n)], axis=1)
        first[pl.ds(j * line, line), :] = dot(block, reduce_low[...], 1, 1)
        lax.fori_loop(j * side, (j + 1) * side, add_to_sums(first), 0)
    all_valid = jnp.sum(valid[...], axis=0, keepdims=True)
    pack_one[...] = jnp.concatenate(
        [packed(total_of(0)), packed(total_of(1)), all_valid, jnp.zeros((7, 128), f32)], axis=0)
    stats = settled(exchange(pack_one, held_one), held_one)
    rows = width // 128
    count = jnp.concatenate([stats[2 * rows : 2 * rows + 1]] * rows, axis=1)

    def norm_of(stats):
        mean = unpacked(stats[:rows]) / count
        scale = lax.rsqrt(unpacked(stats[rows : 2 * rows]) / count - mean * mean + EPS)
        return mean, scale

    mean_one, scale_one = norm_of(stats)
    roots_z = begin_z(roots, roots_out, 1)

    def activate(p, _):
        normed = (first[pixel_rows(p), :] - mean_one) * scale_one
        pre = gain_one * normed + shift_one
        act = pre * sigmoid(pre) * across(valid[pixel_rows(p), :])
        hidden_pad[padded_pixel(p), :] = act.astype(low)
        return 0

    lax.fori_loop(0, pixels, activate, 0)

    def conv_line(j, _):
        value = None
        for t in range(9):
            offset = (t // 3 - 1) * wide_line + (t % 3 - 1) * slots
            rows_in = pl.ds(pl.multiple_of(rim + j * wide_line + offset, slots), line)
            term = dot(hidden_pad[rows_in, :], taps[:, t * width : (t + 1) * width], 1, 1)
            value = term if value is None else value + term
        second[line_rows(j), :] = value
        return 0

    lax.fori_loop(0, side, conv_line, 0)
    roots_z = pass_z(roots_out, roots_z)
    partial[...] = jnp.zeros(partial.shape, f32)
    lax.fori_loop(0, pixels, add_to_sums(second), 0)
    pack_two[...] = jnp.concatenate([packed(total_of(0)), packed(total_of(1))], axis=0)
    stats = settled(exchange(pack_two, held_two), held_two)
    mean_two, scale_two = norm_of(stats)
    for copy in roots_z:
        copy.wait()
    across_half = roots_out.shape[-1] // 2
    left, right = pl.ds(0, across_half), pl.ds(across_half, across_half)
    part = roots_out.at[:, y, x, core, :, left]
    roots_a = [copies.start(part, part, peer) for peer in mates_x]
    part = roots_out.at[:, y, x, core, :, right]
    roots_b = [copies.start(part, part, mate_y)]

    pooling[...] = jnp.zeros(pooling.shape, f32)

    def pool(p, _):
        normed = (second[pixel_rows(p), :] - mean_two) * scale_two
        pre = gain_two * normed + shift_two
        sigma = sigmoid(pre)
        kept = across(valid[pixel_rows(p), :])
        slope = sigma * (1.0 + pre * (1.0 - sigma)) * kept
        pooling[0] += pre * sigma * kept
        pooling[1] += slope
        pooling[2] += slope * normed
        return 0

    lax.fori_loop(0, pixels, pool, 0)
    divide = across(divisor[...])
    pooled_low[...] = (pooling[0] / divide).astype(low)
    logits = dot(pooled_low[...], head_low[...], 1, 0) + bias[...]
    classes = logits.shape[1]
    index = lax.broadcasted_iota(jnp.int32, (slots, classes), 1)
    onehot = (index == all_labels[own_slots, :]).astype(f32)
    top = jnp.max(logits, axis=1, keepdims=True)
    log_total = jnp.log(jnp.sum(jnp.exp(logits - top), axis=1, keepdims=True)) + top
    picked = jnp.sum(onehot * logits, axis=1, keepdims=True)
    use = used[:, :1]
    loss = jnp.sum(use * (log_total - picked))
    d_logits[...] = (use * (jnp.exp(logits - log_total) - onehot) / SLOTS_DEV).astype(low)
    bias_sum = jnp.sum(d_logits[...].astype(f32), axis=0, keepdims=True)
    half = width // 2

    def to_pooled(m, _):
        rows_in = pl.ds(pl.multiple_of(m * half, half), half)
        d_act[:, rows_in] = dot(d_logits[...], head_low[rows_in, :], 1, 1) / across(divisor[...])[:, :half]
        return 0

    lax.fori_loop(0, 2, to_pooled, 0)
    at_class = lax.broadcasted_iota(jnp.int32, (1, classes), 1)
    bias_sum = jnp.where(at_class == classes - 1, loss, jnp.where(at_class == classes - 2, jnp.sum(use), bias_sum))
    pack_three[...] = jnp.concatenate(
        [packed(jnp.sum(d_act[...] * pooling[1], axis=0, keepdims=True)),
         packed(jnp.sum(d_act[...] * pooling[2], axis=0, keepdims=True)), packed(bias_sum)], axis=0)
    going = exchange(pack_three, held_three)

    def to_head(m, _):
        columns = pl.ds(pl.multiple_of(m * (classes // 2), 128), classes // 2)
        head_buf[:, columns] = dot(pooled_low[...], d_logits[:, columns], 0, 0)
        return 0

    lax.fori_loop(0, 2, to_head, 0)
    head_copy = pltpu.make_async_copy(head_buf, head_out, local.at[6])
    head_copy.start()
    totals_two = settled(going, held_three)
    shift_grad, gain_grad = unpacked(totals_two[:rows]), unpacked(totals_two[rows : 2 * rows])
    factor = gain_two * scale_two / count
    for copy in roots_a:
        copy.wait()
    part = roots_out.at[:, y, :, core, :, left]
    roots_a = [copies.start(part, part, mate_y)]
    for copy in roots_b:
        copy.wait()
    part = roots_out.at[:, :, x, core, :, right]
    roots_b = [copies.start(part, part, peer) for peer in mates_x]

    def leave_second(p, _):
        normed = (second[pixel_rows(p), :] - mean_two) * scale_two
        pre = gain_two * normed + shift_two
        sigma = sigmoid(pre)
        kept = across(valid[pixel_rows(p), :])
        d_pre = d_act[...] * kept * (sigma * (1.0 + pre * (1.0 - sigma)))
        d_z = factor * (count * d_pre - shift_grad - normed * gain_grad) * kept
        grad_pad[padded_pixel(p), :] = d_z.astype(low)
        return 0

    lax.fori_loop(0, pixels, leave_second, 0)

    partial[...] = jnp.zeros(partial.shape, f32)

    def spread_line(j, _):
        value = None
        for t in range(9):
            offset = (t // 3 - 1) * wide_line + (t % 3 - 1) * slots
            rows_in = pl.ds(pl.multiple_of(rim + j * wide_line - offset, slots), line)
            term = dot(grad_pad[rows_in, :], taps[:, t * width : (t + 1) * width], 1, 0)
            value = term if value is None else value + term
        second[line_rows(j), :] = value
        return 0

    lax.fori_loop(0, side, spread_line, 0)
    def enter_first(p, _):
        normed = (first[pixel_rows(p), :] - mean_one) * scale_one
        pre = gain_one * normed + shift_one
        sigma = sigmoid(pre)
        d_pre = second[pixel_rows(p), :] * across(valid[pixel_rows(p), :]) * (sigma * (1.0 + pre * (1.0 - sigma)))
        second[pixel_rows(p), :] = d_pre
        partial[0] += fold(d_pre)
        partial[1] += fold(d_pre * normed)
        return 0

    lax.fori_loop(0, pixels, enter_first, 0)
    pack_four[...] = jnp.concatenate([packed(total_of(0)), packed(total_of(1))], axis=0)
    going = exchange(pack_four, held_four)

    def turn(j, _):
        rows_in = pl.ds(pl.multiple_of(rim + j * wide_line, slots), wide_line)
        turned_grad[:, pl.ds(pl.multiple_of(j * wide_line, 128), wide_line)] = grad_pad[rows_in, :].T
        return 0

    lax.fori_loop(0, side, turn, 0)

    def leave(slot, target, sem):
        copy = pltpu.make_async_copy(grad_buf.at[slot], target, local.at[sem])
        copy.start()
        return copy

    half = nz // 2
    near = z // half * half + lax.rem(z + 1, half)
    kinds = "".join(chunk_rounds(9))
    core_going, first_going = [], []

    def part_of(t, mine):
        if kinds[t] == "x":
            return [(tap_sums.at[t, :, :, x if mine else lax.rem(x + 1, nx)], first_in.at[t])]
        if kinds[t] == "y":
            return [(tap_sums.at[t, :, y if mine else 1 - y], first_in.at[t])]
        return [(tap_sums.at[t, (z // half * half + lax.rem(z, half) if mine else near) % half + h * half],
                 first_in.at[t, pl.ds(2 * h, 2)]) for h in range(2)]

    def over_core(t):
        core_going[t].wait()
        for i in range(nz):
            tap_sums[t, i] += core_in[t, i]
        peer = {"x": at(z, y, lax.rem(x + 1, nx), core), "y": mate_y, "z": at(near, y, x, core)}[kinds[t]]
        first_going.append([copies.start(source, target, peer) for source, target in part_of(t, False)])

    for t in range(9):
        offset = (t // 3 - 1) * wide_line + (t % 3 - 1) * slots
        slot = t % 2
        shifted = hidden_pad.at[pl.ds(rim + offset, body_rows)]
        grad_buf[slot] = dot(turned_grad[...], shifted[...], 1, 0).reshape(grad_buf.shape[1:])
        core_going.append(copies.start(grad_buf.at[slot, :, :, :, 1 - core], core_in.at[t], mate))
        for i in range(nz):
            tap_sums[t, i] = grad_buf[slot, i, :, :, core]
        if t:
            over_core(t - 1)
    over_core(8)
    leaving = []

    for copy in roots_a + roots_b:
        copy.wait()
    part = roots_out.at[:, :, :, core]
    roots_core = copies.start(part, part, mate)
    totals_one = settled(going, held_four)
    shift_sum, gain_sum = unpacked(totals_one[:rows]), unpacked(totals_one[rows : 2 * rows])
    factor_one = gain_one * scale_one / count

    def leave_first(p, _):
        normed = (first[pixel_rows(p), :] - mean_one) * scale_one
        kept = across(valid[pixel_rows(p), :])
        d_z = factor_one * (count * second[pixel_rows(p), :] - shift_sum - normed * gain_sum) * kept
        grad_pad[padded_pixel(p), :] = d_z.astype(low)
        return 0

    lax.fori_loop(0, pixels, leave_first, 0)
    lax.fori_loop(0, side, turn, 0)
    per = width // depth
    for t in range(n // per):
        slot = (9 + t) % 2
        if t >= 2:
            leaving[t - 2].wait()
        block = jnp.concatenate([own_images[t * per + k].reshape(body_rows, depth) for k in range(per)], axis=1)
        grad_buf[slot] = dot(turned_grad[...], block, 1, 0).reshape(grad_buf.shape[1:])
        leaving.append(leave(slot, reduce_out.at[:, :, :, :, :, pl.ds(t * width, width)], 7 + slot))
    taps_going = []
    for t in range(9):
        for copy in first_going[t]:
            copy.wait()
        for h, (kept, landed) in enumerate(part_of(t, True)):
            kept[...] += landed[...]
            copy = pltpu.make_async_copy(
                kept, taps_out.at[t, pl.ds(2 * h, 2)] if kinds[t] == "z" else taps_out.at[t], local.at[9 + 2 * t + h])
            copy.start()
            taps_going.append(copy)
    for copy in taps_going:
        copy.wait()
    totals_out[...] = jnp.concatenate([totals_two, totals_one], axis=0)
    head_copy.wait()
    roots_core.wait()
    for copy in leaving[-2:]:
        copy.wait()


def local_step(images, spatial_weight, spatial_mask, reduce_weight, reduce_mask, head_weight, roots,
               norms, pixel_mask, labels, bias):
    n, nb = lax.axis_size("chan"), lax.axis_size("batch")
    nz, nx = n // 2, nb // 2
    slots, width = pixel_mask.shape[0] // n, norms.shape[1] * n
    line, depth, classes = SIDE * slots, images.shape[-1], bias.shape[1]
    f32, low = jnp.float32, jnp.bfloat16
    rows = spatial_weight.shape[0] // nb
    wide_weights, wide_roots = spatial_weight.shape[1] + reduce_weight.shape[1] + classes, roots.shape[0] * roots.shape[2]
    grids = ((SIDE * (SIDE + 1) + 2 * (SIDE + 2)) * slots, width)
    shape = jax.ShapeDtypeStruct
    gathered = lambda size: shape((nz, 2, nx, 2, rows, size), low)
    raw = lambda a: pltpu.VMEM((rows, a.shape[1]), a.dtype)
    held = lambda k: pltpu.VMEM((n * nb, k, 128), f32)
    pack = lambda k: pltpu.VMEM((k, 128), f32)
    count = 2 * (nz - 1) + (SIDE + 1) * (n - 1) + (1 + (nx - 1) + 1) + (2 * nx + 1) + 4 * (n * nb - 1) + 27
    two = 2 * width // 128
    three = two + classes // 128
    weight = lambda size: pltpu.VMEM((nz, 2, nx, 2, rows, size), low)
    taps, reduce, head, totals, mask, _, roots_full = pl.pallas_call(
        step_kernel,
        out_shape=(
            shape((9, nz, 2, rows, width), f32),
            shape((nz, 2, nx, 2, rows, n * depth), f32),
            shape((width, classes), f32),
            shape((two + three, 128), f32),
            shape((rows, wide_weights), f32),
            gathered(wide_weights),
            gathered(wide_roots),
        ),
        in_specs=[ANY] * 7 + [VMEM] * 4,
        out_specs=(ANY, ANY, ANY, VMEM, VMEM, ANY, ANY),
        scratch_shapes=[
            raw(spatial_weight), raw(spatial_mask), raw(reduce_weight), raw(reduce_mask), raw(head_weight),
            pltpu.VMEM((roots.shape[0], rows, width), f32),
            pltpu.VMEM((rows, wide_weights), low),
            pltpu.VMEM((rows, wide_roots), low),
            pltpu.VMEM((n, SIDE, line + slots, depth), low),
            pltpu.VMEM((SIDE * line, width), f32),
            pltpu.VMEM((SIDE * line, width), f32),
            pltpu.VMEM(grids, low),
            pltpu.VMEM(grids, low),
            pltpu.VMEM((width, SIDE * (line + slots)), low),
            weight(9 * width), weight(n * depth), weight(classes),
            pltpu.VMEM((SIDE * line, 128), f32),
            pltpu.VMEM((slots, 128), f32),
            pltpu.VMEM((slots, 128), f32),
            pltpu.VMEM((norms.shape[0], width), f32),
            pltpu.VMEM((n, norms.shape[0], width), f32),
            pack(two + 8), pack(two), pack(three), pack(two),
            held(two + 8), held(two), held(three), held(two),
            pltpu.VMEM((9, nz, 2, nx, rows, width), f32),
            pltpu.VMEM((9, nz, 2, nx, rows, width), f32),
            pltpu.VMEM((9, nz, 2, rows, width), f32),
            pltpu.VMEM((2, 8, width), f32),
            pltpu.VMEM((3, slots, width), f32),
            pltpu.VMEM((slots, width), low),
            pltpu.VMEM((slots, classes), low),
            pltpu.VMEM((slots, width), f32),
            pltpu.VMEM((width, classes), f32),
            pltpu.VMEM((2, nz, 2, nx, 2, rows, width), f32),
            DMA((count,)), DMA((count,)), DMA((27,)),
        ],
        compiler_params=pltpu.CompilerParams(collective_id=0, has_side_effects=True, vmem_limit_bytes=60 << 20),
        name="step",
    )(images.reshape(n, SIDE, line, depth), spatial_weight, spatial_mask, reduce_weight, reduce_mask, head_weight, roots,
      norms, pixel_mask, labels, bias)
    return taps, reduce, head, totals[:three], totals[three:], mask, roots_full.reshape(width, wide_roots)


def chunk_rounds(count):
    rounds = []
    while count > 0:
        rounds.append(ORDERS[len(rounds) % len(ORDERS)][:count])
        count -= len(rounds[-1])
    return rounds


def settle_kernel(
    chunks, taps, reduce, head, mask, left_root, roots, own, left_part, right_part, outer_out, size,
    full, factors, lefts, rights, outers, squares, held, sums, core_in, first_in, second_in, near_in, across_in,
    final, final_low, send, recv, local,
):
    (z, y, x, core), (nz, ny, nx, nc) = place()
    half = nz // 2
    across_z = lax.rem(z + half, nz)
    base_z = z // half * half
    near_z = [base_z + lax.rem(lax.rem(z, half) + k, half) for k in range(1, half)]
    others_x = turned(x, nx)
    mate, mate_y = at(z, y, x, 1 - core), at(z, 1 - y, x, core)
    mates_x = [at(z, y, k, core) for k in others_x]
    mates_near = [at(k, y, x, core) for k in near_z]
    mate_across = at(across_z, y, x, core)
    c, n = lax.axis_index("chan"), lax.axis_size("chan")
    others = [{"chan": k} for k in turned(c, n)]
    greeted = greet(others + mates_x + [mate])
    copies = Copies(send, recv)
    f32, low = jnp.float32, jnp.bfloat16
    rows, width = left_root.shape[1:]
    tiles_one = reduce.shape[-1] // width
    n_taps = taps.shape[0]
    sources = ((reduce, n_taps * width), (head, n_taps * width + reduce.shape[-1]))
    wide = n_taps * width + reduce.shape[-1]
    used_local = [0]

    def keep(source, target):
        copy = pltpu.make_async_copy(source, target, local.at[used_local[0]])
        used_local[0] += 1
        copy.start()
        return copy

    roots_in = [keep(roots, factors)]
    pick = (lax.broadcasted_iota(jnp.int32, (rows, width), 1)
            == lax.broadcasted_iota(jnp.int32, (rows, width), 0) + c * rows).astype(low)
    squares[...] = jnp.zeros(squares.shape, f32)
    outgoing = []

    def two_parts(value):
        high = value.astype(low)
        return [high, (value - high.astype(f32)).astype(low)]

    def multiply(t, columns):
        grad = full[:, :, :, :, :, columns].reshape(width, width)
        mine = full[z, y, :, :, :, columns].reshape(rows, width)
        first = dot(jnp.concatenate([mine, pick], axis=0), grad, 1, 1)
        lefts[t] = first[:rows]
        second = dot(jnp.concatenate([first[rows:].astype(low)] + two_parts(left_root[t]), axis=0), grad, 1, 0)
        rights[t] = second[:rows]
        inner = second[rows : 2 * rows] + second[2 * rows :]
        third = dot(jnp.concatenate(two_parts(inner), axis=0), factors[:, t * width : (t + 1) * width], 1, 0)
        value = third[:rows] + third[rows:]
        outers[t] = value
        squares[t : t + 1, :] = jnp.full((1, 128), jnp.sum(value * value), f32)
        outgoing.extend(keep(a.at[t], b.at[t]) for a, b in ((lefts, left_part), (rights, right_part), (outers, outer_out)))

    def wait(going):
        for copy in going:
            copy.wait()

    def enter(start, size):
        columns = pl.ds(start, size)
        going = []
        for source, first_column in sources:
            begin, end = max(start, first_column), min(start + size, first_column + source.shape[-1])
            if begin < end:
                taken, landed = pl.ds(begin - first_column, end - begin), pl.ds(begin, end - begin)
                going.append(copies.start(source.at[:, :, :, 1 - core, :, taken], core_in.at[:, :, :, :, landed], mate))
                going.append(keep(source.at[:, :, :, core, :, taken], sums.at[:, :, :, :, landed]))
        yield
        wait(going)
        for i in range(nz):
            for j in range(ny):
                for k in range(nx):
                    sums[i, j, k, :, columns] += core_in[i, j, k, :, columns]

    def settled(start, last_in, columns):
        total = (sums[z, y, x, :, columns] + last_in) * mask[:, columns]
        final[:, columns] = total
        kept = [keep(final.at[:, columns], own.at[x, core, :, columns])]
        kept += [copies.start(final.at[:, columns], own.at[x, core, :, columns], peer) for peer in mates_x]
        if start < wide:
            final_low[:, columns] = total.astype(low)
            return kept, [keep(final_low.at[:, columns], full.at[z, y, x, core, :, columns])]
        return kept, []

    def own_core(kept, columns):
        wait(kept)
        part = own.at[:, core, :, columns]
        return copies.start(part, part, mate)

    def block_of(start, columns):
        t = start // width
        if roots_in:
            roots_in.pop().wait()
        multiply(t + tiles_one if t < n_taps else t - n_taps, columns)

    def chunk_z(start, size):
        columns = pl.ds(start, size)
        if start < n_taps * width:
            going = [keep(taps.at[start // width, pl.ds(2 * h, 2)], sums.at[lax.rem(z, half) + h * half, :, :, :, columns])
                     for h in range(2)]
            yield
            wait(going)
        else:
            yield from enter(start, size)
            going = []
            for t, k in enumerate(near_z):
                for h in range(2):
                    there = lax.rem(k, half) + h * half
                    going.append(copies.start(
                        sums.at[there, :, :, :, columns], first_in.at[t, pl.ds(2 * h, 2), :, :, columns], mates_near[t]))
            yield
            wait(going)
            for t in range(half - 1):
                for h in range(2):
                    for j in range(ny):
                        for k in range(nx):
                            sums[lax.rem(z, half) + h * half, j, k, :, columns] += first_in[t, 2 * h + j, k, :, columns]
        landing = [second_in.at[0, pl.ds(nx * j, nx), :, columns] for j in range(ny)]
        going = [copies.start(sums.at[across_z, j, :, :, columns], landing[j], mate_across) for j in range(ny)]
        yield
        wait(going)
        for j in range(ny):
            for k in range(nx):
                sums[z, j, k, :, columns] += second_in[0, nx * j + k, :, columns]
        going = [copies.start(sums.at[z, :, k, :, columns], near_in.at[t, :, :, columns], mates_x[t])
                 for t, k in enumerate(others_x)]
        yield
        wait(going)
        for t in range(nx - 1):
            for j in range(ny):
                sums[z, j, x, :, columns] += near_in[t, j, :, columns]
        going = [copies.start(sums.at[z, 1 - y, x, :, columns], across_in.at[:, columns], mate_y)]
        yield
        wait(going)
        kept, going = settled(start, across_in[:, columns], columns)
        going += [copies.start(final_low.at[:, columns], full.at[z, y, x, core, :, columns], peer) for peer in mates_x]
        yield
        last = [own_core(kept, columns)]
        wait(going)
        part = full.at[z, y, :, core, :, columns]
        going = [copies.start(part, part, mate_y)]
        yield
        wait(going)
        part = full.at[z, :, :, core, :, columns]
        going = [copies.start(part, part, peer) for peer in [mate_across] + mates_near]
        yield
        wait(going)
        part = full.at[across_z, :, :, core, :, columns]
        going = [copies.start(part, part, peer) for peer in mates_near]
        yield
        wait(going)
        part = full.at[:, :, :, core, :, columns]
        last.append(copies.start(part, part, mate))
        yield
        wait(last)
        block_of(start, columns)

    def chunk(start, size, x_first):
        columns = pl.ds(start, size)
        if start < n_taps * width:
            going = [keep(taps.at[start // width], sums.at[:, :, x, :, columns] if x_first else sums.at[:, y, :, :, columns])]
            yield
            wait(going)
        else:
            yield from enter(start, size)
            if x_first:
                going = [copies.start(sums.at[:, :, k, :, columns], first_in.at[t, :, :, :, columns], mates_x[t])
                         for t, k in enumerate(others_x)]
            else:
                going = [copies.start(sums.at[:, 1 - y, :, :, columns], first_in.at[0, :, :, :, columns], mate_y)]
            yield
            wait(going)
            for i in range(nz):
                for j in range(2):
                    if x_first:
                        sums[i, j, x, :, columns] += first_in[0, i, j, :, columns]
                    else:
                        sums[i, y, j, :, columns] += first_in[0, i, j, :, columns]
        going = []
        if x_first:
            going.append(copies.start(sums.at[:, 1 - y, x, :, columns], second_in.at[0, :, :, columns], mate_y))
        else:
            for t, k in enumerate(others_x):
                going.append(copies.start(sums.at[:, y, k, :, columns], second_in.at[t, :, :, columns], mates_x[t]))
        yield
        wait(going)
        for t in range(1 if x_first else nx - 1):
            for i in range(nz):
                sums[i, y, x, :, columns] += second_in[t, i, :, columns]
        going = []
        for t, k in enumerate(near_z):
            for h in range(2):
                there = lax.rem(k + h * half, nz)
                going.append(copies.start(sums.at[there, y, x, :, columns], near_in.at[t, h, :, columns], mates_near[t]))
        yield
        wait(going)
        for t in range(half - 1):
            for h in range(2):
                sums[lax.rem(z + h * half, nz), y, x, :, columns] += near_in[t, h, :, columns]
        going = [copies.start(sums.at[across_z, y, x, :, columns], across_in.at[:, columns], mate_across)]
        yield
        wait(going)
        kept, going = settled(start, across_in[:, columns], columns)
        if start < wide:
            going += [copies.start(final_low.at[:, columns], full.at[z, y, x, core, :, columns], peer)
                      for peer in [mate_across] + mates_near]
        yield
        rows_core = [own_core(kept, columns)]
        if start < wide:
            wait(going)
            part = full.at[across_z, y, x, core, :, columns]
            going = [copies.start(part, part, peer) for peer in mates_near]
            yield
            wait(going)
            part = full.at[:, y, x, core, :, columns]
            going = [copies.start(part, part, peer) for peer in (mates_x if x_first else [mate_y])]
            yield
            wait(going)
            part = full.at[:, y, :, core, :, columns] if x_first else full.at[:, :, x, core, :, columns]
            going = [copies.start(part, part, peer) for peer in ([mate_y] if x_first else mates_x)]
            yield
            wait(going)
            part = full.at[:, :, :, core, :, columns]
            rows_core.append(copies.start(part, part, mate))
        yield
        wait(rows_core)
        if start < wide:
            block_of(start, columns)

    rounds = [[chunk_z(*c[:2]) if c[2] == "z" and c[0] < wide else chunk(*c[:2], c[2] != "y") for c in some] for some in chunks]
    begun, active = rounds.pop(0), []
    for going in begun:
        next(going)
    greeted()
    while rounds or begun or active:
        active += begun
        begun = rounds.pop(0) if rounds else []
        for going in begun:
            next(going)
        for going in active[::-1]:
            try:
                next(going)
            except StopIteration:
                active.remove(going)
    going = [copies.start(squares, held.at[k + 1], peer) for k, peer in enumerate(others)]
    held[0] = squares[...]
    wait(going + outgoing)
    size[...] = jnp.sqrt(jnp.sum(held[...], axis=0) / (width * width) + 1e-06)


def settle(taps, reduce, head, mask, left_root, roots):
    nz, nx, n = lax.axis_size("chan") // 2, lax.axis_size("batch") // 2, lax.axis_size("chan")
    blocks, own_rows, width = left_root.shape
    rows = width // (4 * nz * nx)
    wide = taps.shape[0] * width + reduce.shape[-1]
    total = wide + head.shape[1]
    split = lambda a: a.reshape(nz, 2, nx, 2, rows, a.shape[1])
    f32, low = jnp.float32, jnp.bfloat16
    chunks, start = [], 0
    for kinds in chunk_rounds(total // width):
        chunks.append([(start + i * width, width, kind) for i, kind in enumerate(kinds)])
        start += len(kinds) * width
    near = nz // 2 - 1
    first = max(nx - 1, nx // 2)
    count = (total // width) * (4 + first + max(nx - 1, 1) + 2 * near + 1 + (nx - 1) + 1 + near + 1 + near + nx + 1) + n
    product = jax.ShapeDtypeStruct((blocks, own_rows, width), f32)
    padded = (blocks + 7) // 8 * 8
    own, left_part, right_part, outer, size = pl.pallas_call(
        functools.partial(settle_kernel, chunks),
        out_shape=(
            jax.ShapeDtypeStruct((nx, 2, rows, total), f32), product, product, product,
            jax.ShapeDtypeStruct((padded, 128), f32),
        ),
        in_specs=[ANY, ANY, ANY, VMEM, VMEM, ANY],
        out_specs=(ANY,) * 4 + (VMEM,),
        scratch_shapes=[
            pltpu.VMEM((nz, 2, nx, 2, rows, wide), low),
            pltpu.VMEM(roots.shape, low),
            pltpu.VMEM(product.shape, f32),
            pltpu.VMEM(product.shape, f32),
            pltpu.VMEM(product.shape, f32),
            pltpu.VMEM((padded, 128), f32),
            pltpu.VMEM((n, padded, 128), f32),
            pltpu.VMEM((nz, 2, nx, rows, total), f32),
            pltpu.VMEM((nz, 2, nx, rows, total), f32),
            pltpu.VMEM((first, nz, 2, rows, total), f32),
            pltpu.VMEM((max(nx - 1, 1), nz, rows, total), f32),
            pltpu.VMEM((near, 2, rows, total), f32),
            pltpu.VMEM((rows, total), f32),
            pltpu.VMEM((rows, total), f32),
            pltpu.VMEM((rows, wide), low),
            DMA((count,)), DMA((count,)), DMA((7 * (total // width) + 4,)),
        ],
        compiler_params=pltpu.CompilerParams(collective_id=1, has_side_effects=True, vmem_limit_bytes=60 << 20),
        name="settle",
    )(taps, reduce, split(head), mask, left_root, roots)
    return own.reshape(own_rows, total), left_part, right_part, outer, size


def finish_kernel(
    size, head_weight, head_first, head_second,
    own, left_part, right_part, outer, left_stats, right_stats, reduce_weight, spatial_weight, reduce_mask, spatial_mask,
    head_new, head_first_new, head_second_new,
    reduce_grad, spatial_grad, reduce_new, spatial_new, left_new, right_new,
    own_rows, lefts, rights, outers, left_kept, right_kept, weights, masks, arrive, leave,
):
    blocks, rows, width = outers.shape
    c_in, taps = reduce_weight.shape[1], spatial_weight.shape[1]
    tiles_one = c_in // width
    groups = [(0, tiles_one)] + [(t, min(t + 2, blocks)) for t in range(tiles_one, blocks, 2)]
    every = [pltpu.make_async_copy(own, own_rows, arrive.at[0, 7])]
    coming = []
    for g, (begin, end) in enumerate(groups):
        some, columns = pl.ds(begin, end - begin), pl.ds(begin * width, (end - begin) * width)
        theirs = pl.ds((begin if g == 0 else begin - tiles_one) * width, (end - begin) * width)
        pairs = [(a.at[some], b.at[some]) for a, b in (
            (left_part, lefts), (right_part, rights), (outer, outers), (left_stats, left_kept), (right_stats, right_kept))]
        pairs += [((reduce_weight if g == 0 else spatial_weight).at[:, theirs], weights.at[:, columns]),
                  ((reduce_mask if g == 0 else spatial_mask).at[:, theirs], masks.at[:, columns])]
        coming.append([pltpu.make_async_copy(a, b, arrive.at[g, i]) for i, (a, b) in enumerate(pairs)])
    for copy in every + [copy for group in coming for copy in group]:
        copy.start()
    going = []

    def out(source, target):
        copy = pltpu.make_async_copy(source, target, leave.at[len(going)])
        copy.start()
        going.append(copy)

    every[0].wait()
    out(own_rows.at[:, pl.ds(0, taps)], spatial_grad)
    out(own_rows.at[:, pl.ds(taps, c_in)], reduce_grad)
    head_grad = own_rows[:, taps + c_in : taps + c_in + head_weight.shape[1]]
    head_new[...], head_first_new[...], head_second_new[...] = adam_step(
        head_weight[...], head_grad, head_first[...], head_second[...], 0.04, 0.1)
    for g, (begin, end) in enumerate(groups):
        for copy in coming[g]:
            copy.wait()

        def block(t, _):
            columns = pl.ds(pl.multiple_of(t * width, width), width)
            lefts[t] = 0.95 * left_kept[t] + lefts[t]
            rights[t] = 0.95 * right_kept[t] + rights[t]
            step = outers[t] / jnp.concatenate([size[pl.ds(t, 1), :]] * (width // 128), axis=1)
            weight = weights[:, columns]
            weights[:, columns] = weight - 0.02 * masks[:, columns].astype(jnp.float32) * (step + 0.1 * weight)
            return 0

        lax.fori_loop(begin, end, block, 0)
        some, columns = pl.ds(begin, end - begin), pl.ds(begin * width, (end - begin) * width)
        theirs = pl.ds((begin if g == 0 else begin - tiles_one) * width, (end - begin) * width)
        out(lefts.at[some], left_new.at[some])
        out(rights.at[some], right_new.at[some])
        out(weights.at[:, columns], (reduce_new if g == 0 else spatial_new).at[:, theirs])
    for copy in going:
        copy.wait()


def finish(own, left_part, right_part, outer, size, left_stats, right_stats,
           reduce_weight, spatial_weight, reduce_mask, spatial_mask, head_weight, head_first, head_second):
    blocks, rows, width = left_stats.shape
    like = lambda a: jax.ShapeDtypeStruct(a.shape, jnp.float32)
    wide = reduce_weight.shape[1] + spatial_weight.shape[1]
    products = pltpu.VMEM(left_stats.shape, jnp.float32)
    groups = 1 + -(-(spatial_weight.shape[1] // width) // 2)
    head_new, head_first_new, head_second_new, *rest = pl.pallas_call(
        finish_kernel,
        out_shape=(like(head_weight), like(head_weight), like(head_weight), like(reduce_weight), like(spatial_weight),
                   like(reduce_weight), like(spatial_weight), like(left_stats), like(left_stats)),
        in_specs=[VMEM] * 4 + [ANY] * 10,
        out_specs=(VMEM,) * 3 + (ANY,) * 6,
        scratch_shapes=[pltpu.VMEM(own.shape, jnp.float32)] + [products] * 5
        + [pltpu.VMEM((rows, wide), jnp.float32), pltpu.VMEM((rows, wide), jnp.int32),
           DMA((groups, 8)), DMA((2 + 3 * groups,))],
        compiler_params=pltpu.CompilerParams(vmem_limit_bytes=60 << 20),
        name="finish",
    )(size, head_weight, head_first, head_second, own, left_part, right_part, outer, left_stats, right_stats,
      reduce_weight, spatial_weight, reduce_mask, spatial_mask)
    return *rest, head_new, head_first_new, head_second_new


def silu_slope(pre):
    sigma = jax.nn.sigmoid(pre)
    return sigma * (1.0 + pre * (1.0 - sigma))


def adam_step(param, grad, first, second, rate, decay):
    first = 0.9 * first + 0.1 * grad
    second = 0.999 * second + 0.001 * grad * grad
    mhat = first / (1.0 - 0.9**STEP)
    vhat = second / (1.0 - 0.999**STEP)
    return (param - rate * (mhat / (jnp.sqrt(vhat) + 1e-08) + decay * param), first, second)


def own_part(array, axis, name="chan"):
    size = array.shape[axis] // lax.axis_size(name)
    return lax.dynamic_slice_in_dim(array, lax.axis_index(name) * size, size, axis)


def body(
    images,
    pixel_mask,
    labels,
    reduce_weight,
    reduce_mask,
    spatial_weight,
    spatial_mask,
    head_weight,
    head_bias,
    norm_params,
    left_stats,
    right_stats,
    left_root,
    input_side_roots,
    head_first,
    head_second,
    bias_first,
    bias_second,
    norm_first,
    norm_second,
):
    n = lax.axis_size("chan")
    pixels, channels = images.shape[1:]
    side = SIDE
    rows_out, c_in = reduce_weight.shape
    width = left_stats.shape[2]
    classes = head_weight.shape[1]
    padded = 1024
    slots = images.shape[0] // n
    f32 = jnp.float32

    by_pixel = images.reshape(n, slots, pixels, channels).transpose(0, 2, 1, 3)
    taps_local, reduce_local, head_local, sums_two, sums_one, mask_rows, roots_full = local_step(
        by_pixel, spatial_weight, spatial_mask, reduce_weight, reduce_mask, head_weight, input_side_roots, norm_params, pixel_mask, labels[:, None],
        jnp.pad(head_bias, (0, padded - classes), constant_values=-1e30)[None])

    own, *products = settle(taps_local, reduce_local, head_local, mask_rows, left_root, roots_full)
    of_norms = jnp.stack([a.reshape(-1) for a in (sums_one[4:], sums_one[:4], sums_two[4:8], sums_two[:4])])
    norm_gain_gradient = own_part(of_norms, 1)
    of_head = sums_two[8:].reshape(-1)
    bias_grad = of_head[:classes]
    loss_sum, slot_count = of_head[-1], of_head[-2]
    (reduce_grad, spatial_grad, reduce_new, spatial_new, left_new, right_new, head_new, head_first_new,
     head_second_new) = finish(
        own, *products, left_stats, right_stats, reduce_weight, spatial_weight, reduce_mask, spatial_mask,
        head_weight, head_first, head_second)
    bias_new, bias_first_new, bias_second_new = adam_step(head_bias, bias_grad, bias_first, bias_second, 0.1, 0.0)
    norm_new, norm_first_new, norm_second_new = adam_step(
        norm_params, norm_gain_gradient, norm_first, norm_second, 0.1, 0.0)
    return (
        loss_sum,
        slot_count,
        reduce_grad,
        spatial_grad,
        reduce_new,
        spatial_new,
        left_new,
        right_new,
        head_new,
        head_first_new,
        head_second_new,
        bias_new,
        bias_first_new,
        bias_second_new,
        norm_new,
        norm_first_new,
        norm_second_new,
    )


FULL_PRECISION = lax.Precision.HIGHEST
BOTH = ("chan", "batch")


def conv_grid(grid, taps, spec):
    return lax.conv_general_dilated(
        grid, taps, (1, 1), ((1, 1), (1, 1)), dimension_numbers=spec,
        preferred_element_type=jnp.float32,
    )


def plain_norm_forward(pre_norm, gain, shift, valid):
    first_sum = jnp.sum(pre_norm * valid, axis=(0, 1))
    second_sum = jnp.sum(pre_norm * pre_norm * valid, axis=(0, 1))
    first_sum, second_sum, count = lax.psum((first_sum, second_sum, jnp.sum(valid)), BOTH)
    mean = first_sum / count
    scale = lax.rsqrt(second_sum / count - mean * mean + EPS)
    normed = (pre_norm - mean) * scale
    pre = gain * normed + shift
    return (jax.nn.silu(pre) * valid, (normed, pre, scale, count))


def plain_norm_backward(grad_act, kept, gain, valid):
    normed, pre, scale, count = kept
    d_pre = grad_act * valid * silu_slope(pre)
    shift_gradient, gain_grad = lax.psum(
        (jnp.sum(d_pre, axis=(0, 1)), jnp.sum(d_pre * normed, axis=(0, 1))), BOTH
    )
    d_input = gain * scale / count * (count * d_pre - shift_gradient - normed * gain_grad) * valid
    return (d_input, gain_grad, shift_gradient)


def plain_own_part(array, parts, axis=0):
    size = array.shape[axis] // parts
    return lax.dynamic_slice_in_dim(array, lax.axis_index("chan") * size, size, axis)


def plain_body(
    images,
    pixel_mask,
    labels,
    reduce_weight,
    reduce_mask,
    spatial_weight,
    spatial_mask,
    head_weight,
    head_bias,
    norm_params,
    left_stats,
    right_stats,
    left_root,
    input_side_roots,
    head_first,
    head_second,
    bias_first,
    bias_second,
    norm_first,
    norm_second,
):
    parts = lax.axis_size("chan")
    pixels = images.shape[1]
    side = SIDE
    rows_out = reduce_weight.shape[0]
    width = left_stats.shape[2]
    classes = head_weight.shape[1]
    own_images = lax.all_to_all(images, "chan", 0, 2, tiled=True)
    slots = own_images.shape[0]
    reduce_float = reduce_mask.astype(jnp.float32)
    spatial_float = spatial_mask.astype(jnp.float32)
    gather = lambda a, axis: lax.all_gather(a, "chan", axis=axis, tiled=True)
    reduce_low = gather((reduce_weight * reduce_float).astype(jnp.bfloat16), 0)
    spatial_low = gather((spatial_weight * spatial_float).astype(jnp.bfloat16), 0)
    head_low = gather(head_weight.astype(jnp.bfloat16), 0)
    norm_full = gather(norm_params, 1)
    right_factor_full = gather(input_side_roots, 1)
    valid = plain_own_part(pixel_mask, parts).astype(jnp.float32)[:, :, None]
    own_labels = plain_own_part(labels, parts)
    filled = jnp.sum(valid[:, :, 0], axis=1)
    divisor = jnp.maximum(filled, 1.0)
    used = (filled > 0.0).astype(jnp.float32)
    taps = spatial_low.reshape(width, 3, 3, width)
    first_pre = jnp.einsum("spc,oc->spo", own_images, reduce_low, preferred_element_type=jnp.float32)
    first_act, first_kept = plain_norm_forward(first_pre, norm_full[0], norm_full[1], valid)
    hidden = first_act.astype(jnp.bfloat16).reshape(slots, side, side, width)
    second_pre = conv_grid(hidden, taps, ("NHWC", "OHWI", "NHWC")).reshape(slots, pixels, width)
    second_act, second_kept = plain_norm_forward(second_pre, norm_full[2], norm_full[3], valid)
    pooled = (jnp.sum(second_act, axis=1) / divisor[:, None]).astype(jnp.bfloat16)
    logits = jnp.dot(pooled, head_low, preferred_element_type=jnp.float32) + head_bias
    onehot = (jnp.arange(classes)[None, :] == own_labels[:, None]).astype(jnp.float32)
    log_total = jax.nn.logsumexp(logits, axis=1)
    picked = jnp.sum(onehot * logits, axis=1)
    loss_local = jnp.sum(used * (log_total - picked))
    d_logits = (used[:, None] * (jnp.exp(logits - log_total[:, None]) - onehot) / SLOTS_DEV).astype(
        jnp.bfloat16
    )
    head_grad = jnp.einsum("so,sc->oc", pooled, d_logits, preferred_element_type=jnp.float32)
    bias_grad = jnp.sum(d_logits.astype(jnp.float32), axis=0)
    d_pooled = jnp.einsum("sc,oc->so", d_logits, head_low, preferred_element_type=jnp.float32)
    d_act = jnp.broadcast_to((d_pooled / divisor[:, None])[:, None, :], second_act.shape)
    d_second, gain_two, shift_two = plain_norm_backward(d_act, second_kept, norm_full[2], valid)
    d_second = d_second.astype(jnp.bfloat16).reshape(slots, side, side, width)
    spatial_local = lax.conv_general_dilated(
        hidden, d_second, (1, 1), ((1, 1), (1, 1)), dimension_numbers=("CHWN", "IHWO", "NHWC"),
        preferred_element_type=jnp.float32,
    )
    spatial_local = spatial_local.transpose(3, 1, 2, 0).reshape(width, 9 * width)
    d_hidden = conv_grid(
        d_second, taps[:, ::-1, ::-1, :], ("NHWC", "IHWO", "NHWC")
    ).reshape(slots, pixels, width)
    d_first, gain_one, shift_one = plain_norm_backward(d_hidden, first_kept, norm_full[0], valid)
    d_first = d_first.astype(jnp.bfloat16)
    reduce_local = jnp.einsum("spc,spo->oc", own_images, d_first, preferred_element_type=jnp.float32)
    scatter = lambda a: lax.psum_scatter(a, "chan", scatter_dimension=0, tiled=True)
    reduce_grad, spatial_grad, head_grad = scatter(reduce_local), scatter(spatial_local), scatter(head_grad)
    reduce_grad, spatial_grad, head_grad = lax.psum((reduce_grad, spatial_grad, head_grad), "batch")
    reduce_grad = reduce_grad * reduce_float
    spatial_grad = spatial_grad * spatial_float
    bias_grad, loss_sum, slot_count = lax.psum((bias_grad, loss_local, jnp.sum(used)), BOTH)
    norm_gain_gradient = plain_own_part(jnp.stack([gain_one, shift_one, gain_two, shift_two], axis=0), parts, 1)
    tiles_one = reduce_weight.shape[1] // width
    blocks = jnp.concatenate(
        [
            reduce_grad.reshape(rows_out, tiles_one, width).transpose(1, 0, 2),
            spatial_grad.reshape(rows_out, 9, width).transpose(1, 0, 2),
        ],
        axis=0,
    )
    blocks_full = gather(blocks, 1)
    left_new = 0.95 * left_stats + jnp.einsum(
        "tak,tbk->tab", blocks, blocks_full, precision=FULL_PRECISION
    )
    own_columns = plain_own_part(blocks_full, parts, 2)
    right_new = 0.95 * right_stats + jnp.einsum(
        "tki,tkb->tib", own_columns, blocks_full, precision=FULL_PRECISION
    )
    matrix_product = jnp.einsum("tak,tkb->tab", left_root, blocks_full, precision=FULL_PRECISION)
    matrix_product = jnp.einsum(
        "ghk,gkl->ghl", matrix_product, right_factor_full, precision=FULL_PRECISION
    )
    squares = lax.psum(jnp.sum(matrix_product * matrix_product, axis=(1, 2)), "chan")
    step = matrix_product / jnp.sqrt(squares / (width * width) + 1e-06)[:, None, None]
    step_one = step[:tiles_one].transpose(1, 0, 2).reshape(rows_out, tiles_one * width)
    step_two = step[tiles_one:].transpose(1, 0, 2).reshape(rows_out, 9 * width)
    reduce_new = reduce_weight - 0.02 * reduce_float * (step_one + 0.1 * reduce_weight)
    spatial_new = spatial_weight - 0.02 * spatial_float * (step_two + 0.1 * spatial_weight)
    head_new, head_first_new, head_second_new = adam_step(
        head_weight, head_grad, head_first, head_second, 0.04, 0.1
    )
    bias_new, bias_first_new, bias_second_new = adam_step(
        head_bias, bias_grad, bias_first, bias_second, 0.1, 0.0
    )
    norm_new, norm_first_new, norm_second_new = adam_step(
        norm_params, norm_gain_gradient, norm_first, norm_second, 0.1, 0.0
    )
    return (
        loss_sum,
        slot_count,
        reduce_grad,
        spatial_grad,
        reduce_new,
        spatial_new,
        left_new,
        right_new,
        head_new,
        head_first_new,
        head_second_new,
        bias_new,
        bias_first_new,
        bias_second_new,
        norm_new,
        norm_first_new,
        norm_second_new,
    )


def solution(mesh):
    in_specs = (
        P("batch", None, "chan"),
        P("batch", None),
        P("batch"),
        P("chan", None),
        P("chan", None),
        P("chan", None),
        P("chan", None),
        P("chan", None),
        P(),
        P(None, "chan"),
        P(None, "chan", None),
        P(None, "chan", None),
        P(None, "chan", None),
        P(None, "chan", None),
        P("chan", None),
        P("chan", None),
        P(),
        P(),
        P(None, "chan"),
        P(None, "chan"),
    )
    out_specs = (
        P(),
        P(),
        P("chan", None),
        P("chan", None),
        P("chan", None),
        P("chan", None),
        P(None, "chan", None),
        P(None, "chan", None),
        P("chan", None),
        P("chan", None),
        P("chan", None),
        P(),
        P(),
        P(),
        P(None, "chan"),
        P(None, "chan"),
        P(None, "chan"),
    )
    chan, batch = mesh.shape["chan"], mesh.shape["batch"]
    fits = chan == 8 and batch == 4 and WIDTH % (16 * chan * batch) == 0 and SLOTS_DEV % (16 * chan) == 0
    return jax.shard_map(body if fits else plain_body, mesh=mesh, in_specs=in_specs, out_specs=out_specs, check_vma=False)
```
